32 devices in a mesh: dp: 8 (over z, x), tensor: 4 (over y, core).
Axes of the slice: x: 2, y: 2, z: 4, core: 2. Of those that a mesh axis runs over, the one named last changes fastest.
Arguments:
- tokens: bfloat16 [8192, 768], P(('dp', 'tensor')), may hold values from -6 to 6
- node_counts: int32 [64], P('dp'), may hold values from 4 to 42
- edge_counts: int32 [64], P('dp'), may hold values from 0 to 84
- ln1_gain: float32 [768], replicated, may hold values from 0.25 to 1.75
- ln1_bias: float32 [768], replicated, may hold values from -3 to 3
- qkv_weight: bfloat16 [3, 768, 768], P(None, 'tensor'), may hold values from -0.3125 to 0.3125
- out_weight: bfloat16 [768, 768], P('tensor'), may hold values from -0.875 to 0.875
- ln2_gain: float32 [768], replicated, may hold values from 0.25 to 1.75
- ln2_bias: float32 [768], replicated, may hold values from -3 to 3
- fc1_weight: bfloat16 [768, 768], P('tensor'), may hold values from -0.21875 to 0.21875
- fc1_bias: bfloat16 [768], P('tensor'), may hold values from -3 to 3
- fc2_weight: bfloat16 [768, 768], P('tensor'), may hold values from -0.3125 to 0.3125
- out_grad: bfloat16 [8192, 768], P(('dp', 'tensor')), may hold values from -6 to 6
Outputs:
- result: bfloat16 [8192, 768], P(('dp', 'tensor'))
- grad_tokens: bfloat16 [8192, 768], P(('dp', 'tensor'))
- grad_ln1_gain: float32 [768], replicated
- grad_ln1_bias: float32 [768], replicated
- grad_qkv_weight: float32 [3, 768, 768], P(None, 'tensor')
- grad_out_weight: float32 [768, 768], P('tensor')
- grad_ln2_gain: float32 [768], replicated
- grad_ln2_bias: float32 [768], replicated
- grad_fc1_weight: float32 [768, 768], P('tensor')
- grad_fc1_bias: float32 [768], P('tensor')
- grad_fc2_weight: float32 [768, 768], P('tensor')
The draws below stay inside these ranges and needn't reach their ends.
All inputs are finite; a program needn't handle non-finite values.
Results may differ from the reference program's by a relative error of at most 0.019.
Values may be sent and summed in bfloat16 or wider, within the bound.
No kernel may reach another device: no remote copies, remote signals or barrier semaphores. Data moves between devices by JAX's collectives and lax.ppermute only.
A program may use at most 64 MiB of HBM per device.

```python
import jax
import jax.numpy as jnp
from jax import lax

D = 768
HEADS = 32
HEAD_DIM = 24
FF = 768
LEN = 128
MOL_DEV = 8
MOLS = 64
TOKENS = 8192
N_DP = 8


def draw_out_grad(key, part):
    key = jax.random.fold_in(key, 7)
    row_share = jnp.arange(TOKENS, dtype=jnp.float32)[:, None] / TOKENS
    random_part = jnp.clip(jax.random.normal(key, (TOKENS, D), jnp.float32), -4.0, 4.0)
    growth = (1.0 + 2.0 * row_share) / 2.0
    return (random_part * growth).astype(jnp.bfloat16)


def set_ends(array, key, least, high):
    extent = array.shape
    place = [jax.random.randint(jax.random.fold_in(key, axis), (), 0, extent[axis]) for axis in range(len(extent))]
    array = array.at[tuple(place)].set(least)
    longest = extent.index(max(extent))
    place[longest] = (place[longest] + 1) % extent[longest]
    return array.at[tuple(place)].set(high)


def block_scale(rng, shape, shards, low, largest):
    factor_of, own = 1.0, jax.random.fold_in(rng, 6)
    for axis_at, shards_of in shards:
        steps = jnp.exp(jax.random.uniform(jax.random.fold_in(own, axis_at), (shards_of,), jnp.float32, low / len(shards), largest / len(shards)))
        factor_of = factor_of * jnp.repeat(steps, shape[axis_at] // shards_of).reshape([-1 if axis == axis_at else 1 for axis in range(len(shape))])
    return factor_of


def centred(key, shape, spread, reach, shards=(), held_as=jnp.bfloat16):
    entries = spread * jax.random.normal(key, shape, jnp.float32)
    if shards:
        entries = entries * block_scale(key, shape, shards, -0.22, 0.18)
    return jnp.clip(entries, -reach, reach).astype(held_as)


def setup_inputs(seed: int = 0) -> dict:
    seeds = jax.random.split(jax.random.key(seed), 14)
    return {
        "tokens": centred(seeds[0], (TOKENS, D), 1.0, 6.0, ((0, 32),)),
        "node_counts": set_ends(jax.random.randint(seeds[1], (MOLS,), 4, 43), jax.random.fold_in(seeds[1], 1), 4, 42).astype(jnp.int32),
        "edge_counts": set_ends(jax.random.randint(seeds[2], (MOLS,), 0, 85), jax.random.fold_in(seeds[2], 1), 0, 84).astype(jnp.int32),
        "ln1_gain": jnp.clip(1.0 + 0.15 * jax.random.normal(seeds[3], (D,), jnp.float32), 0.25, 1.75),
        "ln1_bias": centred(seeds[4], (D,), 0.5, 3.0, (), jnp.float32),
        "qkv_weight": centred(seeds[5], (3, D, D), (D // 2) ** -0.5, 0.3125, ((1, 4),)),
        "out_weight": centred(seeds[6], (D, D), (D // 16) ** -0.5, 0.875, ((0, 4),)),
        "ln2_gain": jnp.clip(1.0 + 0.15 * jax.random.normal(seeds[7], (D,), jnp.float32), 0.25, 1.75),
        "ln2_bias": centred(seeds[8], (D,), 0.5, 3.0, (), jnp.float32),
        "fc1_weight": centred(seeds[9], (FF, D), D ** -0.5, 0.21875, ((0, 4),)),
        "fc1_bias": centred(seeds[10], (FF,), 0.5, 3.0, ((0, 4),)),
        "fc2_weight": centred(seeds[11], (FF, D), (FF // 2) ** -0.5, 0.3125, ((0, 4),)),
        "out_grad": draw_out_grad(jax.random.fold_in(seeds[13], 71), 0),
    }


EPSILON = 1e-05
HIGHEST = lax.Precision.HIGHEST

@jax.custom_vjp
def low(v):
    return lax.optimization_barrier(v.astype(jnp.bfloat16)).astype(jnp.float32)

@jax.custom_vjp
def low_back(v):
    return v

def low_keep(v):
    return (low(v), None)

def low_pass(kept, grad):
    return (grad,)

def back_keep(v):
    return (v, None)

def back_low(kept, grad):
    return (low(grad),)
low.defvjp(low_keep, low_pass)
low_back.defvjp(back_keep, back_low)

def layer_norm(values, gain_values, shifts):
    average = lax.optimization_barrier(jnp.mean(values, axis=-1, keepdims=True))
    centered = values - average
    variance = lax.optimization_barrier(jnp.mean(centered * centered, axis=-1, keepdims=True))
    return centered * lax.rsqrt(variance + EPSILON) * gain_values + shifts

def block_forward(params, token_rows, valid_keys):
    ln1_gain, ln1_bias, qkv_weight, out_weight, ln2_gain, ln2_bias, fc1_weight, fc1_bias, fc2_weight = params
    molecules = valid_keys.shape[0]
    normed_one = low(layer_norm(token_rows, ln1_gain, ln1_bias))
    projected = jnp.einsum('td,ced->cte', normed_one, qkv_weight, precision=HIGHEST)
    projected = low_back(low(projected))
    shaped = projected.reshape(3, molecules, LEN, HEADS, HEAD_DIM)
    scores = jnp.einsum('mqhd,mkhd->mhqk', shaped[0], shaped[1], precision=HIGHEST) * HEAD_DIM ** (-0.5)
    scores = low_back(scores)
    scores = jnp.where(valid_keys[:, None, None, :], scores, -1000000000.0)
    probabilities = low(jax.nn.softmax(scores, axis=-1))
    attended = jnp.einsum('mhqk,mkhd->mqhd', probabilities, shaped[2], precision=HIGHEST)
    attended = low_back(low(attended.reshape(molecules * LEN, D)))
    branch_one = low_back(jnp.dot(attended, out_weight, precision=HIGHEST))
    hidden = token_rows + branch_one
    normed_two = low(layer_norm(hidden, ln2_gain, ln2_bias))
    inner_values = low_back(jnp.einsum('td,fd->tf', normed_two, fc1_weight, precision=HIGHEST) + fc1_bias)
    activated = low(jax.nn.gelu(inner_values, approximate=False))
    branch_two = low_back(jnp.dot(activated, fc2_weight, precision=HIGHEST))
    return hidden + branch_two

def reference(tokens, node_counts, edge_counts, ln1_gain, ln1_bias, qkv_weight, out_weight, ln2_gain, ln2_bias, fc1_weight, fc1_bias, fc2_weight, out_grad):
    params = tuple((weight_array.astype(jnp.float32) for weight_array in (ln1_gain, ln1_bias, qkv_weight, out_weight, ln2_gain, ln2_bias, fc1_weight, fc1_bias, fc2_weight)))
    molecules = node_counts.shape[0]
    group_size = MOL_DEV * min(N_DP, 4)
    blocks = molecules // group_size
    positions = jnp.arange(LEN, dtype=jnp.int32)
    valid_keys = positions[None, :] < (1 + node_counts + edge_counts)[:, None]
    block_masks = valid_keys.reshape(blocks, group_size, LEN)
    token_rows = tokens.astype(jnp.float32).reshape(blocks, group_size * LEN, D)

    def forward(weights, inputs):

        def one_block(block_pair):
            return block_forward(weights, block_pair[0], block_pair[1])
        return lax.map(jax.checkpoint(one_block), (inputs, block_masks))
    outputs, pullback = jax.vjp(forward, params, token_rows)
    weight_grads, input_grads = pullback(out_grad.astype(jnp.float32).reshape(blocks, group_size * LEN, D))
    return (outputs.reshape(TOKENS, D).astype(jnp.bfloat16), input_grads.reshape(TOKENS, D).astype(jnp.bfloat16), weight_grads[0].astype(jnp.float32), weight_grads[1].astype(jnp.float32), weight_grads[2].astype(jnp.float32), weight_grads[3].astype(jnp.float32), weight_grads[4].astype(jnp.float32), weight_grads[5].astype(jnp.float32), weight_grads[6].astype(jnp.float32), weight_grads[7].astype(jnp.float32), weight_grads[8].astype(jnp.float32))
```

```python
import functools

import jax
import jax.numpy as jnp
from jax import lax
from jax.experimental import pallas as pl
from jax.experimental.pallas import tpu as pltpu
from jax.sharding import PartitionSpec as P

HEAD_DIM = 24
LEN = 128
PAIR = 2 * HEAD_DIM
EPSILON = 1e-05
SCALE = HEAD_DIM ** (-0.5)
LOG2E = 1.4426950408889634
F32 = jnp.float32
BF16 = jnp.bfloat16
VMEM_LIMIT = 48 * 1024 * 1024


def dot_nn(a, b):
    return lax.dot_general(a, b, (((1,), (0,)), ((), ())), preferred_element_type=F32)


def dot_nt(a, b):
    return lax.dot_general(a, b, (((1,), (1,)), ((), ())), preferred_element_type=F32)


def dot_tn(a, b):
    return lax.dot_general(a, b, (((0,), (0,)), ((), ())), preferred_element_type=F32)


def normalise(v):
    centered = v - jnp.mean(v, axis=-1, keepdims=True)
    r = lax.rsqrt(jnp.mean(centered * centered, axis=-1, keepdims=True) + EPSILON)
    return centered * r, r


def norm_back(da, gain, xh, r):
    e = da * gain
    return r * (
        e - jnp.mean(e, axis=-1, keepdims=True) - xh * jnp.mean(e * xh, axis=-1, keepdims=True)
    )


def pair_blocks(rows):
    none = jnp.zeros((HEAD_DIM, LEN), F32)
    left = jnp.concatenate([rows[:HEAD_DIM], none], axis=0)
    right = jnp.concatenate([none, rows[HEAD_DIM:]], axis=0)
    return jnp.concatenate([left, right], axis=1).astype(BF16)


def pair_window(i, width):
    low = (PAIR * i) // LEN * LEN
    low = min(low, width - 2 * LEN)
    return low, PAIR * i - low


def placed(block, before):
    parts = []
    if before:
        parts.append(jnp.zeros((before, 2 * LEN), BF16))
    parts.append(block)
    after = 2 * LEN - PAIR - before
    if after:
        parts.append(jnp.zeros((after, 2 * LEN), BF16))
    return jnp.concatenate(parts, axis=0)


def diagonal(both):
    return jnp.concatenate([both[:HEAD_DIM, :LEN], both[HEAD_DIM:, LEN:]], axis=0)


def attention_kernel(
    aliased, place_ref, nodes_ref, edges_ref, x_ref, gain_ref, bias_ref, w_ref, *refs
):
    a1_ref, qt_ref, kt_ref, v_ref, p_ref, ot_ref, o_ref = refs[aliased:]
    width = w_ref.shape[1]
    mol = place_ref[0] + pl.program_id(0)
    count = 1 + nodes_ref[mol] + edges_ref[mol]
    xh, _ = normalise(x_ref[...].astype(F32))
    a1 = (xh * gain_ref[...] + bias_ref[...]).astype(BF16)
    a1_ref[...] = a1
    qt = dot_nt(w_ref[0], a1).astype(BF16)
    vt = dot_nt(w_ref[2], a1).astype(BF16)
    keys = dot_nt(a1, w_ref[1]).astype(BF16)
    qt_ref[...] = qt
    kt_ref[...] = dot_nt(w_ref[1], a1).astype(BF16)
    v_ref[...] = dot_nt(a1, w_ref[2]).astype(BF16)
    valid = lax.broadcasted_iota(jnp.int32, (LEN, 2 * LEN), 0) < count
    for i in range(width // PAIR):
        low, before = pair_window(i, width)
        rows = slice(PAIR * i, PAIR * (i + 1))
        rhs = placed(pair_blocks(qt[rows].astype(F32)), before)
        s = dot_nn(keys[:, low : low + 2 * LEN], rhs)
        s = jnp.where(valid, s, -1e30)
        e = jnp.exp2((s - jnp.max(s, axis=0, keepdims=True)) * (SCALE * LOG2E))
        p = (e * (1.0 / jnp.sum(e, axis=0, keepdims=True))).astype(BF16)
        p_ref[0, i] = p
        ot_ref[rows, :] = diagonal(dot_nn(vt[rows], p)).astype(BF16)
    o_ref[...] = ot_ref[...].T


def attention(place, nodes, edges, x, gain, bias, w, kept, first, total):
    width, d = w.shape[1:]
    mols = x.shape[0] // LEN
    pairs = width // PAIR
    at = lambda i, *_: (first + i, 0)
    lanes = lambda i, *_: (0, first + i)
    fixed = lambda *_: (0, 0)
    outs = [
        (jax.ShapeDtypeStruct((total * LEN, d), BF16), pl.BlockSpec((LEN, d), at)),
        (jax.ShapeDtypeStruct((width, total * LEN), BF16), pl.BlockSpec((width, LEN), lanes)),
        (jax.ShapeDtypeStruct((width, total * LEN), BF16), pl.BlockSpec((width, LEN), lanes)),
        (jax.ShapeDtypeStruct((total * LEN, width), BF16), pl.BlockSpec((LEN, width), at)),
        (
            jax.ShapeDtypeStruct((total, pairs, LEN, 2 * LEN), BF16),
            pl.BlockSpec((1, pairs, LEN, 2 * LEN), lambda i, *_: (first + i, 0, 0, 0)),
        ),
        (jax.ShapeDtypeStruct((width, total * LEN), BF16), pl.BlockSpec((width, LEN), lanes)),
        (
            jax.ShapeDtypeStruct((mols * LEN, width), BF16),
            pl.BlockSpec((LEN, width), lambda i, *_: (i, 0)),
        ),
    ]
    return pl.pallas_call(
        functools.partial(attention_kernel, len(kept)),
        grid_spec=pltpu.PrefetchScalarGridSpec(
            num_scalar_prefetch=3,
            grid=(mols,),
            in_specs=[
                pl.BlockSpec((LEN, d), lambda i, *_: (i, 0)),
                pl.BlockSpec((1, d), fixed),
                pl.BlockSpec((1, d), fixed),
                pl.BlockSpec((3, width, d), lambda *_: (0, 0, 0)),
            ]
            + [pl.BlockSpec(memory_space=pl.ANY)] * len(kept),
            out_specs=[spec for _, spec in outs],
        ),
        out_shape=[shape for shape, _ in outs],
        input_output_aliases={7 + j: j for j in range(len(kept))},
        compiler_params=pltpu.CompilerParams(vmem_limit_bytes=VMEM_LIMIT),
        cost_estimate=pl.CostEstimate(
            flops=mols * LEN * width * (10 * d + 8 * LEN),
            bytes_accessed=w.size * 2 + mols * LEN * (d * 4 + width * 20),
            transcendentals=mols * pairs * 2 * LEN * LEN,
        ),
        name="attention_forward",
    )(place, nodes, edges, x, gain, bias, w, *kept)


def feed_kernel(
    half, x0, x1, oa0, oa1, ob0, ob1, g0, g1, wa_ref, wb_ref, gain_ref, bias_ref, fc1_ref, b1_ref,
    fc2_ref, h_ref, a2_ref, z_ref, du_ref,
):
    own = pl.program_id(0) < half

    def body(x, oa, ob, g):
        branch = dot_nn(oa[...], wa_ref[...]) + dot_nn(ob[...], wb_ref[...])
        h = x[...].astype(F32) + branch
        h_ref[...] = h
        xh, _ = normalise(h)
        a2 = (xh * gain_ref[...] + bias_ref[...]).astype(BF16)
        a2_ref[...] = a2
        u = dot_nt(a2, fc1_ref[...]) + b1_ref[...]
        phi = 0.5 * (1.0 + lax.erf(u * (0.5**0.5)))
        z_ref[...] = (u * phi).astype(BF16)
        slope = phi + u * (jnp.exp(-0.5 * u * u) * 0.3989422804014327)
        du_ref[...] = (dot_nt(g[...], fc2_ref[...]) * slope).astype(BF16)

    pl.when(own)(lambda: body(x0, oa0, ob0, g0))
    pl.when(jnp.logical_not(own))(lambda: body(x1, oa1, ob1, g1))


def feed(xs, oas, obs, gs, wa, wb, gain, bias, fc1, b1, fc2):
    rows, d = xs[0].shape
    width = wa.shape[0]
    block = LEN
    half = rows // block
    mine = lambda i: (jnp.minimum(i, half - 1), 0)
    theirs = lambda i: (jnp.maximum(i - half, 0), 0)
    fixed = lambda i: (0, 0)
    pair = lambda cols: [pl.BlockSpec((block, cols), mine), pl.BlockSpec((block, cols), theirs)]
    here = lambda cols: pl.BlockSpec((block, cols), lambda i: (i, 0))
    whole = lambda a: pl.BlockSpec(a.shape, fixed)
    return pl.pallas_call(
        functools.partial(feed_kernel, half),
        grid=(2 * half,),
        in_specs=pair(d) + pair(width) + pair(width) + pair(d)
        + [whole(a) for a in (wa, wb, gain, bias, fc1, b1, fc2)],
        out_specs=[here(d), here(d), here(width), here(width)],
        out_shape=[
            jax.ShapeDtypeStruct((2 * rows, d), F32),
            jax.ShapeDtypeStruct((2 * rows, d), BF16),
            jax.ShapeDtypeStruct((2 * rows, width), BF16),
            jax.ShapeDtypeStruct((2 * rows, width), BF16),
        ],
        compiler_params=pltpu.CompilerParams(vmem_limit_bytes=VMEM_LIMIT),
        cost_estimate=pl.CostEstimate(
            flops=2 * rows * d * width * 8, bytes_accessed=rows * d * 24, transcendentals=4 * rows * width
        ),
        name="feed_forward",
    )(*xs, *oas, *obs, *gs, wa, wb, gain, bias, fc1, b1, fc2)


def feed_grads_kernel(z_ref, du_ref, a2_ref, g0, g1, fc2_ref, h_ref, keep_ref, send_ref, sums_ref,
                      mine_ref, theirs_ref):
    rows = g0.shape[0]
    shard = fc2_ref.shape[0] // 2
    z = z_ref[...]
    du = du_ref[...]
    mine_ref[...] = h_ref[...] + dot_nn(z[:rows], fc2_ref[...])
    theirs_ref[...] = dot_nn(z[rows:], fc2_ref[...]).astype(BF16)
    first = dot_tn(du, a2_ref[...]).astype(BF16)
    keep_ref[:shard] = first[:shard]
    send_ref[:shard] = first[shard:]
    second = (dot_tn(z[:rows], g0[...]) + dot_tn(z[rows:], g1[...])).astype(BF16)
    keep_ref[shard:] = second[:shard]
    send_ref[shard:] = second[shard:]
    sums_ref[...] = jnp.sum(du.astype(F32), axis=0, keepdims=True)


def feed_grads(z, du, a2, gs, fc2, h):
    rows, d = gs[0].shape
    width = z.shape[1]
    whole = lambda a: pl.BlockSpec(a.shape, lambda i: (0, 0))
    shapes = [
        jax.ShapeDtypeStruct((width, d), BF16),
        jax.ShapeDtypeStruct((width, d), BF16),
        jax.ShapeDtypeStruct((1, width), F32),
        jax.ShapeDtypeStruct((rows, d), F32),
        jax.ShapeDtypeStruct((rows, d), BF16),
    ]
    return pl.pallas_call(
        feed_grads_kernel,
        grid=(1,),
        in_specs=[whole(z), whole(du), whole(a2), whole(gs[0]), whole(gs[1]), whole(fc2),
                  pl.BlockSpec((rows, d), lambda i: (0, 0))],
        out_specs=[whole(s) for s in shapes],
        out_shape=shapes,
        compiler_params=pltpu.CompilerParams(vmem_limit_bytes=VMEM_LIMIT),
        cost_estimate=pl.CostEstimate(
            flops=2 * rows * d * width * 6, bytes_accessed=rows * d * 18, transcendentals=0
        ),
        name="feed_grads",
    )(z, du, a2, *gs, fc2, h)


def backward_kernel(
    half, du0, du1, dr0, dr1, fa_ref, fb_ref, h_ref, g0, g1, gain_ref, wo_ref, ot_ref, p_ref, qt_ref,
    kt_ref, v_ref, a1_ref, w_ref, keep_ref, send_ref, dh_ref, sums_ref, mine_ref, theirs_ref,
    dp_ref, gh_ref,
):
    step = pl.program_id(0)
    own = step < half
    width = wo_ref.shape[0]
    shard = width // 2
    here = pl.ds(pl.multiple_of(step * LEN, LEN), LEN)

    @pl.when(step == 0)
    def _():
        sums_ref[...] = jnp.zeros_like(sums_ref)

    du = jnp.where(own, du0[...].astype(F32), du1[...].astype(F32)).astype(BF16)
    dr = jnp.where(own, dr0[...].astype(F32), dr1[...].astype(F32)).astype(BF16)
    g = jnp.where(own, g0[...].astype(F32), g1[...].astype(F32))
    da2 = dot_nn(du, fa_ref[...]) + dot_nn(dr, fb_ref[...])
    xh, r = normalise(h_ref[...])
    dh = g + norm_back(da2, gain_ref[...], xh, r)

    @pl.when(own)
    def _():
        dh_ref[...] = dh
        sums_ref[0:1] += jnp.sum(da2 * xh, axis=0, keepdims=True)
        sums_ref[1:2] += jnp.sum(da2, axis=0, keepdims=True)

    gh = dh.astype(BF16)
    gh_ref[here, :] = gh
    dot = dot_nt(wo_ref[...], gh).astype(BF16)
    for i in range(width // PAIR):
        low, before = pair_window(i, width)
        rows = slice(PAIR * i, PAIR * (i + 1))
        do_pair = pair_blocks(dot[rows].astype(F32))
        q_pair = pair_blocks(qt_ref[rows, :].astype(F32))
        pb = p_ref[0, i]
        p = pb.astype(F32)
        dp = dot_nn(v_ref[:, low : low + 2 * LEN], placed(do_pair, before)) * p
        ds = (dp - p * jnp.sum(dp, axis=0, keepdims=True)).astype(BF16)
        dq = diagonal(dot_nn(kt_ref[rows, :], ds)) * SCALE
        dk = dot_nt(q_pair, ds) * SCALE
        dv = dot_nt(do_pair, pb)
        dp_ref[pl.ds(PAIR * i, PAIR), here] = dq.astype(BF16)
        dp_ref[pl.ds(width + PAIR * i, PAIR), here] = dk.astype(BF16)
        dp_ref[pl.ds(2 * width + PAIR * i, PAIR), here] = dv.astype(BF16)
    da1 = dot_tn(dp_ref[:, here], w_ref[...])

    @pl.when(own)
    def _():
        mine_ref[...] = da1

    @pl.when(jnp.logical_not(own))
    def _():
        theirs_ref[...] = da1.astype(BF16)

    @pl.when(step == 2 * half - 1)
    def _():
        a1 = a1_ref[...]
        for c in range(3):
            for s, ref in enumerate((keep_ref, send_ref)):
                at = c * width + s * shard
                ref[c] = dot_nn(dp_ref[at : at + shard, :], a1).astype(BF16)
        for s, ref in enumerate((keep_ref, send_ref)):
            ref[3] = dot_nn(ot_ref[s * shard : (s + 1) * shard, :], gh_ref[...]).astype(BF16)


def backward(dus, drs, fa, fb, h, gs, gain, wo, ot, p, qt, kt, v, a1, w):
    rows, d = gs[0].shape
    width = wo.shape[0]
    half = rows // LEN
    pairs = width // PAIR
    mine = lambda i: (jnp.minimum(i, half - 1), 0)
    theirs = lambda i: (jnp.maximum(i - half, 0), 0)
    lanes = lambda i: (0, i)
    pair = lambda cols: [pl.BlockSpec((LEN, cols), mine), pl.BlockSpec((LEN, cols), theirs)]
    whole = lambda a: pl.BlockSpec(a.shape, lambda i, n=len(a.shape): (0,) * n)
    w = w.reshape(3 * width, d)
    shapes = [
        jax.ShapeDtypeStruct((4, width // 2, d), BF16),
        jax.ShapeDtypeStruct((4, width // 2, d), BF16),
        jax.ShapeDtypeStruct((rows, d), F32),
        jax.ShapeDtypeStruct((8, d), F32),
        jax.ShapeDtypeStruct((rows, d), F32),
        jax.ShapeDtypeStruct((rows, d), BF16),
    ]
    return pl.pallas_call(
        functools.partial(backward_kernel, half),
        grid=(2 * half,),
        in_specs=[
            pl.BlockSpec((LEN, width), mine),
            pl.BlockSpec((LEN, width), lambda i: (jnp.maximum(i, half), 0)),
            pl.BlockSpec((LEN, width), lambda i: (jnp.minimum(i, half - 1) + half, 0)),
            pl.BlockSpec((LEN, width), theirs),
            whole(fa),
            whole(fb),
            pl.BlockSpec((LEN, d), lambda i: (i, 0)),
        ]
        + pair(d)
        + [
            whole(gain),
            whole(wo),
            whole(ot),
            pl.BlockSpec((1, pairs, LEN, 2 * LEN), lambda i: (i, 0, 0, 0)),
            pl.BlockSpec((width, LEN), lanes),
            pl.BlockSpec((width, LEN), lanes),
            pl.BlockSpec((LEN, width), lambda i: (i, 0)),
            whole(a1),
            whole(w),
        ],
        out_specs=[
            whole(shapes[0]),
            whole(shapes[1]),
            pl.BlockSpec((LEN, d), mine),
            whole(shapes[3]),
            pl.BlockSpec((LEN, d), mine),
            pl.BlockSpec((LEN, d), theirs),
        ],
        out_shape=shapes,
        scratch_shapes=[
            pltpu.VMEM((3 * width, 2 * rows), BF16),
            pltpu.VMEM((2 * rows, d), BF16),
        ],
        compiler_params=pltpu.CompilerParams(vmem_limit_bytes=VMEM_LIMIT),
        cost_estimate=pl.CostEstimate(
            flops=2 * rows * d * width * 22, bytes_accessed=rows * d * 40, transcendentals=0
        ),
        name="attention_backward",
    )(dus, dus, drs, drs, fa, fb, h, *gs, gain, wo, ot, p, qt, kt, v, a1, w)


def input_norm_kernel(x_ref, gain_ref, mine_ref, got_ref, dh_ref, sums_ref, bias_ref, out_ref, vec_ref):
    xh, r = normalise(x_ref[...].astype(F32))
    da1 = mine_ref[...] + got_ref[...].astype(F32)
    out_ref[...] = (dh_ref[...] + norm_back(da1, gain_ref[...], xh, r)).astype(BF16)
    d = x_ref.shape[1]
    bias = bias_ref[...]
    rows = [
        jnp.sum(da1 * xh, axis=0, keepdims=True),
        jnp.sum(da1, axis=0, keepdims=True),
        sums_ref[0:2],
        jnp.concatenate([bias, jnp.zeros((1, d - bias.shape[1]), F32)], axis=1),
        jnp.zeros((11, d), F32),
    ]
    vec_ref[...] = jnp.concatenate(rows, axis=0).astype(BF16)


def input_norm(x, gain, mine, got, dh, sums, bias):
    rows, d = x.shape
    args = (x, gain, mine, got, dh, sums, bias)
    whole = lambda a: pl.BlockSpec(a.shape, lambda i: (0, 0))
    shapes = [jax.ShapeDtypeStruct((rows, d), BF16), jax.ShapeDtypeStruct((16, d), BF16)]
    return pl.pallas_call(
        input_norm_kernel,
        grid=(1,),
        in_specs=[whole(a) for a in args],
        out_specs=[whole(s) for s in shapes],
        out_shape=shapes,
        compiler_params=pltpu.CompilerParams(vmem_limit_bytes=VMEM_LIMIT),
        cost_estimate=pl.CostEstimate(
            flops=rows * d * 20, bytes_accessed=rows * d * 14, transcendentals=0
        ),
        name="input_norm",
    )(*args)


def add(a, b):
    return (a.astype(F32) + b.astype(F32)).astype(BF16)


def local(
    n_dp, n_tensor, tokens, node_counts, edge_counts, ln1_gain, ln1_bias, qkv_weight, out_weight,
    ln2_gain, ln2_bias, fc1_weight, fc1_bias, fc2_weight, out_grad,
):
    d = tokens.shape[1]
    mols = tokens.shape[0] // LEN
    dp_at = lax.axis_index("dp")
    tensor_at = lax.axis_index("tensor")

    def swap_core(a):
        return lax.ppermute(a, "tensor", [(t, t ^ 1) for t in range(n_tensor)])

    def swap_y(a):
        return lax.ppermute(a, "tensor", [(t, t ^ 2) for t in range(n_tensor)])

    def swap_dp(a, mask0, mask1):
        pairs = [
            (p * n_tensor + t, (p ^ (mask1 if t % 2 else mask0)) * n_tensor + t)
            for p in range(n_dp)
            for t in range(n_tensor)
        ]
        return lax.ppermute(a, ("dp", "tensor"), pairs)

    row = lambda v: v.reshape(1, -1).astype(F32)
    g1, b1, g2, b2 = row(ln1_gain), row(ln1_bias), row(ln2_gain), row(ln2_bias)

    both = lambda a, axis=0: jnp.concatenate([a, swap_core(a)], axis=axis)
    place = jnp.stack([tensor_at * mols, (tensor_at ^ 2) * mols]).astype(jnp.int32)

    x_got = swap_y(tokens)
    w_qkv = both(qkv_weight, 1)
    w_out = both(out_weight)
    w_fc1 = both(fc1_weight)
    w_fc2 = both(fc2_weight)
    b_fc1 = both(fc1_bias)

    total = 2 * mols
    kept = attention(place[:1], node_counts, edge_counts, tokens, g1, b1, w_qkv, (), 0, total)
    o_own = kept[6]
    x_got, g_src, w_src = lax.optimization_barrier(
        (x_got, out_grad, jnp.concatenate([out_weight, fc1_weight], axis=0))
    )
    o_own_got = swap_y(o_own)
    kept = attention(place[1:], node_counts, edge_counts, x_got, g1, b1, w_qkv, kept[:6], mols, total)
    a1, qt, kt, v, p, ot, o_theirs = kept
    o_theirs_got = swap_y(o_theirs)
    w_got = both(swap_y(w_src))
    shard = out_weight.shape[0]
    w_out_got = jnp.concatenate([w_got[:shard], w_got[2 * shard : 3 * shard]], axis=0)
    w_fc1_got = jnp.concatenate([w_got[shard : 2 * shard], w_got[3 * shard :]], axis=0)
    g_got = swap_y(g_src)

    gs = (out_grad, g_got)
    h, a2, z, du = feed(
        (tokens, x_got), (o_own, o_theirs), (o_theirs_got, o_own_got), gs, w_out, w_out_got, g2, b2,
        w_fc1, row(b_fc1), w_fc2,
    )
    du_got = swap_y(du)
    fc_keep, fc_send, bias_sums, res_mine, res_theirs = feed_grads(z, du, a2, gs, w_fc2, h)
    res_got = swap_y(res_theirs)
    result = (res_mine + res_got.astype(F32)).astype(BF16)

    keep, send, dh, sums, da1_mine, da1_theirs = backward(
        du, du_got, w_fc1, w_fc1_got, h, gs, g2, w_out, ot, p, qt, kt, v, a1, w_qkv
    )
    grad_tokens, vec = input_norm(tokens, g1, da1_mine, swap_y(da1_theirs), dh, sums, bias_sums)
    vec_got = swap_y(vec)
    same = lax.broadcasted_iota(jnp.int32, vec.shape, 0) < 4
    vec = jnp.where(same, add(vec, vec_got), vec)
    vec_got = swap_core(vec)
    turned = jnp.concatenate(
        [vec_got[:, shard : 2 * shard], vec_got[:, :shard], vec_got[:, 2 * shard :]], axis=1
    )
    vec = add(vec, jnp.where(same, vec_got, turned))

    core = tensor_at % 2
    bit0 = dp_at % 2
    bit1 = (dp_at // 2 + dp_at // 4) % 2
    first = jnp.where(core == 0, bit0, bit1)
    second = jnp.where(core == 0, bit1, bit0)

    def pick(a, at):
        return lax.dynamic_index_in_dim(a, at, 0, False)

    def ordered(at, here, there):
        return jnp.where(at == 0, jnp.stack([here, there]), jnp.stack([there, here]))

    def sum_dp(a, extra=None):
        a = a.reshape(2, 2, -1, d)
        s = add(pick(a, first), swap_dp(pick(a, 1 - first), 1, 2))
        s = add(pick(s, second), swap_dp(pick(s, 1 - second), 2, 1))
        size = s.shape[0]
        if extra is not None:
            s = jnp.concatenate([s, extra], axis=0)
        far = [(4 << k) for k in range(n_dp.bit_length()) if (4 << k) < n_dp]
        for bit in far:
            mask = 6 if bit == 4 else bit
            s = add(s, swap_dp(s, mask, mask))
        got = swap_dp(s, 2, 1)
        if extra is not None:
            extra = add(s[size:], got[size:])
            s, got = s[:size], got[:size]
        s = ordered(second, s, got)
        if extra is None:
            got = swap_dp(s, 1, 2)
        else:
            got = swap_dp(jnp.concatenate([s.reshape(2 * size, d), extra], axis=0), 1, 2)
            extra = add(extra, got[2 * size :])
            got = got[: 2 * size].reshape(2, size, d)
        return ordered(first, s, got).astype(F32), extra

    fc, _ = sum_dp(add(fc_keep, swap_core(fc_send)))
    fc = fc.reshape(2, shard, d)
    rest, vec = sum_dp(add(keep, swap_core(send)), vec)
    rest = rest.reshape(4, shard, d)
    vec = vec.astype(F32)
    return (
        result, grad_tokens, vec[0], vec[1], rest[:3], rest[3], vec[2], vec[3], fc[0], vec[4, :shard],
        fc[1],
    )


def solution(mesh):
    in_specs = (
        P(("dp", "tensor"), None),
        P("dp"),
        P("dp"),
        P(),
        P(),
        P(None, "tensor", None),
        P("tensor", None),
        P(),
        P(),
        P("tensor", None),
        P("tensor"),
        P("tensor", None),
        P(("dp", "tensor"), None),
    )
    out_specs = (
        P(("dp", "tensor"), None),
        P(("dp", "tensor"), None),
        P(),
        P(),
        P(None, "tensor", None),
        P("tensor", None),
        P(),
        P(),
        P("tensor", None),
        P("tensor"),
        P("tensor", None),
    )
    step = functools.partial(local, mesh.shape["dp"], mesh.shape["tensor"])
    return jax.shard_map(step, mesh=mesh, in_specs=in_specs, out_specs=out_specs, check_vma=False)
```

```python
import functools

import jax
import jax.numpy as jnp
from jax import lax
from jax.experimental import pallas as pl
from jax.experimental.pallas import tpu as pltpu
from jax.sharding import PartitionSpec as P

HEAD_DIM = 24
LEN = 128
PAIR = 2 * HEAD_DIM
EPSILON = 1e-05
SCALE = HEAD_DIM ** (-0.5)
LOG2E = 1.4426950408889634
F32 = jnp.float32
BF16 = jnp.bfloat16
VMEM_LIMIT = 24 * 1024 * 1024


def dot_nn(a, b):
    return lax.dot_general(a, b, (((1,), (0,)), ((), ())), preferred_element_type=F32)


def dot_nt(a, b):
    return lax.dot_general(a, b, (((1,), (1,)), ((), ())), preferred_element_type=F32)


def dot_tn(a, b):
    return lax.dot_general(a, b, (((0,), (0,)), ((), ())), preferred_element_type=F32)


def normalise(v):
    centered = v - jnp.mean(v, axis=-1, keepdims=True)
    r = lax.rsqrt(jnp.mean(centered * centered, axis=-1, keepdims=True) + EPSILON)
    return centered * r, r


def norm_back(da, gain, xh, r):
    e = da * gain
    return r * (
        e - jnp.mean(e, axis=-1, keepdims=True) - xh * jnp.mean(e * xh, axis=-1, keepdims=True)
    )


def pair_blocks(rows):
    rows = rows.astype(F32)
    none = jnp.zeros((HEAD_DIM, LEN), F32)
    left = jnp.concatenate([rows[:HEAD_DIM], none], axis=0)
    right = jnp.concatenate([none, rows[HEAD_DIM:]], axis=0)
    return jnp.concatenate([left, right], axis=1).astype(BF16)


def pair_window(i, width):
    low = min(PAIR * i // LEN * LEN, width - 2 * LEN)
    return low, PAIR * i - low


def placed(block, before):
    parts = []
    if before:
        parts.append(jnp.zeros((before, 2 * LEN), BF16))
    parts.append(block)
    after = 2 * LEN - PAIR - before
    if after:
        parts.append(jnp.zeros((after, 2 * LEN), BF16))
    return jnp.concatenate(parts, axis=0)


def diagonal(both):
    return jnp.concatenate([both[:HEAD_DIM, :LEN], both[HEAD_DIM:, LEN:]], axis=0)


def call(kernel, name, args, shapes, flops, scalars=0, scratch=()):
    size = lambda a: a.size * a.dtype.itemsize
    return pl.pallas_call(
        kernel,
        in_specs=[
            pl.BlockSpec(memory_space=pltpu.SMEM if j < scalars else pltpu.VMEM)
            for j in range(len(args))
        ],
        out_specs=[pl.BlockSpec(memory_space=pltpu.VMEM) for _ in shapes],
        out_shape=shapes,
        scratch_shapes=list(scratch),
        compiler_params=pltpu.CompilerParams(vmem_limit_bytes=VMEM_LIMIT),
        cost_estimate=pl.CostEstimate(
            flops=flops,
            bytes_accessed=sum(map(size, args)) + sum(map(size, shapes)),
            transcendentals=0,
        ),
        name=name,
    )(*args)


def attention_body(place_ref, nodes_ref, edges_ref, x_ref, gain_ref, bias_ref, w_ref, outs):
    a1_ref, qt_ref, kt_ref, v_ref, p_ref, ot_ref, o_ref = outs
    width = w_ref.shape[1]
    mols = x_ref.shape[0] // LEN
    pairs = width // PAIR
    xh, _ = normalise(x_ref[...].astype(F32))
    a1 = (xh * gain_ref[...] + bias_ref[...]).astype(BF16)
    a1_ref[...] = a1
    qt = dot_nt(w_ref[0], a1).astype(BF16)
    keys = dot_nt(a1, w_ref[1]).astype(BF16)
    vt = dot_nt(w_ref[2], a1).astype(BF16)
    qt_ref[...] = qt
    every = [(m, i) for m in range(mols) for i in range(pairs)]
    lanes = lambda m: slice(LEN * m, LEN * (m + 1))
    rows = lambda i: slice(PAIR * i, PAIR * (i + 1))
    scores, probs = {}, {}
    for m, i in every:
        low, before = pair_window(i, width)
        rhs = placed(pair_blocks(qt[rows(i), lanes(m)]), before)
        scores[m, i] = dot_nn(keys[lanes(m), low : low + 2 * LEN], rhs)
    for m in range(mols):
        mol = place_ref[0] + m
        count = 1 + nodes_ref[mol] + edges_ref[mol]
        valid = lax.broadcasted_iota(jnp.int32, (LEN, 2 * LEN), 0) < count
        for i in range(pairs):
            s = jnp.where(valid, scores[m, i], -1e30)
            e = jnp.exp2((s - jnp.max(s, axis=0, keepdims=True)) * (SCALE * LOG2E))
            p = (e * (1.0 / jnp.sum(e, axis=0, keepdims=True))).astype(BF16)
            p_ref[m, i] = p
            probs[m, i] = p
    for m, i in every:
        both = dot_nn(vt[rows(i), lanes(m)], probs[m, i])
        ot_ref[rows(i), lanes(m)] = diagonal(both).astype(BF16)
    o_ref[...] = ot_ref[...].T
    kt_ref[...] = dot_nt(w_ref[1], a1).astype(BF16)
    v_ref[...] = dot_nt(a1, w_ref[2]).astype(BF16)


def attention(place, nodes, edges, x, gain, bias, w):
    rows, d = x.shape
    width = w.shape[1]
    pairs = width // PAIR
    shape = lambda *s: jax.ShapeDtypeStruct(s, BF16)

    def kernel(*refs):
        attention_body(*refs[:7], refs[7:])

    return call(
        kernel, "attention_forward", (place, nodes, edges, x, gain, bias, w),
        [shape(rows, d), shape(width, rows), shape(width, rows), shape(rows, width),
         shape(rows // LEN, pairs, LEN, 2 * LEN), shape(width, rows), shape(rows, width)],
        rows * width * (10 * d + 8 * LEN), scalars=3,
    )


def feed_body(x, oa, ob, g, wo_ref, gain_ref, bias_ref, fc1_ref, b1_ref, fc2_ref, h_ref, a2_ref, z_ref,
              du_ref):
    h = x.astype(F32) + dot_nn(jnp.concatenate([oa, ob], axis=1), wo_ref[...])
    h_ref[...] = h
    xh, _ = normalise(h)
    a2 = (xh * gain_ref[...] + bias_ref[...]).astype(BF16)
    a2_ref[...] = a2
    u = dot_nt(a2, fc1_ref[: fc2_ref.shape[0]]) + b1_ref[...]
    dz = dot_nt(g, fc2_ref[...])
    phi = 0.5 * (1.0 + lax.erf(u * (0.5**0.5)))
    slope = phi + u * (jnp.exp(-0.5 * u * u) * 0.3989422804014327)
    du_ref[...] = (dz * slope).astype(BF16)
    z_ref[...] = (u * phi).astype(BF16)


def feed(x, oa, got, wo, gain, bias, fc1, b1, fc2):
    rows, d = x.shape
    width = fc2.shape[0]
    got = got if isinstance(got, tuple) else (got,)

    def kernel(x_ref, oa_ref, *refs):
        if len(got) == 2:
            g, ob = refs[0][...], refs[1][...]
        else:
            g, ob = refs[0][:, :d], refs[0][:, d:]
        feed_body(x_ref[...], oa_ref[...], ob, g, *refs[len(got) :])

    shape = jax.ShapeDtypeStruct
    return call(
        kernel, "feed_forward", (x, oa, *got, wo, gain, bias, fc1, b1, fc2),
        [shape((rows, d), F32), shape((rows, d), BF16), shape((rows, width), BF16),
         shape((rows, width), BF16)],
        8 * rows * d * width,
    )


def backward_body(du_ref, dr_ref, fc1_ref, h_ref, g_ref, gain_ref, wo_ref, p_ref, qt_ref, kt_ref, v_ref,
                  gh_ref, dp_ref, dh_ref, sums_ref):
    width, d = kt_ref.shape[0], h_ref.shape[1]
    mols = h_ref.shape[0] // LEN
    pairs = width // PAIR
    du = jnp.concatenate([du_ref[...], dr_ref[...]], axis=1)
    da2 = dot_nn(du, fc1_ref[...])
    xh, r = normalise(h_ref[...])
    dh = g_ref[:, :d].astype(F32) + norm_back(da2, gain_ref[...], xh, r)
    if dh_ref is not None:
        dh_ref[...] = dh
        sums_ref[0:1] = jnp.sum(da2 * xh, axis=0, keepdims=True)
        sums_ref[1:2] = jnp.sum(da2, axis=0, keepdims=True)
    gh = dh.astype(BF16)
    gh_ref[...] = gh
    dot = dot_nt(wo_ref[:width], gh).astype(BF16)
    every = [(m, i) for m in range(mols) for i in range(pairs)]
    lanes = lambda m: slice(LEN * m, LEN * (m + 1))
    rows = lambda i: slice(PAIR * i, PAIR * (i + 1))
    dps, dss, dos = {}, {}, {}
    for m, i in every:
        low, before = pair_window(i, width)
        dos[m, i] = pair_blocks(dot[rows(i), lanes(m)])
        dps[m, i] = dot_nn(v_ref[lanes(m), low : low + 2 * LEN], placed(dos[m, i], before))
    for m, i in every:
        dp_ref[pl.ds(2 * width + PAIR * i, PAIR), lanes(m)] = dot_nt(dos[m, i], p_ref[m, i]).astype(BF16)
    for m, i in every:
        p = p_ref[m, i].astype(F32)
        t = dps[m, i] * p
        dss[m, i] = (t - p * jnp.sum(t, axis=0, keepdims=True)).astype(BF16)
    for m, i in every:
        dq = diagonal(dot_nn(kt_ref[rows(i), lanes(m)], dss[m, i])) * SCALE
        dp_ref[rows(i), lanes(m)] = dq.astype(BF16)
        dk = dot_nt(pair_blocks(qt_ref[rows(i), lanes(m)]), dss[m, i]) * SCALE
        dp_ref[pl.ds(width + PAIR * i, PAIR), lanes(m)] = dk.astype(BF16)


def pack_qkv_kernel(own_ref, got_ref, out_ref):
    shard = own_ref.shape[1]
    out_ref[:, :shard] = own_ref[...]
    out_ref[:, shard:] = got_ref[...]


def pack_qkv(own, got):
    c, shard, d = own.shape
    return call(
        pack_qkv_kernel, "pack_qkv", (own, got), [jax.ShapeDtypeStruct((c, 2 * shard, d), BF16)], 0
    )[0]


def pack_rest_kernel(bit_ref, wo0, wo1, fc10, fc11, fc20, fc21, y0, y1, x0, x1,
                     wo_ref, fc1_ref, fc2_ref):
    shard = wo0.shape[0]
    for at, (a, b, c) in enumerate(((wo0, fc10, fc20), (wo1, fc11, fc21))):
        rows = slice(at * shard, (at + 1) * shard)
        wo_ref[rows] = a[...]
        fc1_ref[rows] = b[...]
        fc2_ref[rows] = c[...]

    def far(a, b):
        for at, (u, v) in enumerate(zip(a, b)):
            rows = slice((2 + at) * shard, (3 + at) * shard)
            wo_ref[rows] = u[...]
            fc1_ref[rows] = v[...]

    @pl.when(bit_ref[0] == 0)
    def _():
        far((y0, y1), (x0, x1))

    @pl.when(bit_ref[0] != 0)
    def _():
        far((x0, x1), (y0, y1))


def pack_rest(bit, *parts):
    shard, d = parts[0].shape
    shape = lambda rows: jax.ShapeDtypeStruct((rows, d), BF16)
    return call(
        pack_rest_kernel, "pack_rest", (bit, *parts),
        [shape(4 * shard), shape(4 * shard), shape(2 * shard)], 0, scalars=1,
    )


def feed_grads_kernel(z0, z1, du0, du1, a0, a1, g0, g1, fc2_ref, h_ref,
                      keep_ref, send_ref, sums_ref, mine_ref, theirs_ref):
    shard = fc2_ref.shape[0] // 2
    d = h_ref.shape[1]
    first = dot_tn(du0[...], a0[...]) + dot_tn(du1[...], a1[...])
    second = dot_tn(z0[...], g0[...]) + dot_tn(z1[...], g1[:, :d])
    for at, ref in enumerate((keep_ref, send_ref)):
        rows = slice(at * shard, (at + 1) * shard)
        ref[0] = first[rows].astype(BF16)
        ref[1] = second[rows].astype(BF16)
    sums_ref[...] = jnp.sum(du0[...].astype(F32), axis=0, keepdims=True) + jnp.sum(
        du1[...].astype(F32), axis=0, keepdims=True
    )
    mine_ref[...] = h_ref[...] + dot_nn(z0[...], fc2_ref[...])
    theirs_ref[...] = dot_nn(z1[...], fc2_ref[...]).astype(BF16)


def feed_grads(zs, dus, a2s, gs, fc2, h):
    rows, d = h.shape
    width = fc2.shape[0]
    shape = jax.ShapeDtypeStruct
    return call(
        feed_grads_kernel, "feed_grads", (*zs, *dus, *a2s, *gs, fc2, h),
        [shape((2, width // 2, d), BF16), shape((2, width // 2, d), BF16), shape((1, width), F32),
         shape((rows, d), F32), shape((rows, d), BF16)],
        12 * rows * d * width,
    )


def out_grads_kernel(ot0, ot1, gh0, gh1, keep_ref, send_ref):
    shard = ot0.shape[0] // 2
    total = dot_nn(ot0[...], gh0[...]) + dot_nn(ot1[...], gh1[...])
    keep_ref[0] = total[:shard].astype(BF16)
    send_ref[0] = total[shard:].astype(BF16)


def out_grads(ots, ghs):
    width, d = ots[0].shape[0], ghs[0].shape[1]
    shape = jax.ShapeDtypeStruct((1, width // 2, d), BF16)
    return call(
        out_grads_kernel, "out_grads", (*ots, *ghs), [shape, shape], 4 * width * d * ghs[0].shape[0]
    )


def qkv_grads_kernel(dp0, dp1, a0, a1, keep_ref, send_ref):
    shard = keep_ref.shape[1]
    a = jnp.concatenate([a0[...], a1[...]], axis=0)
    for c in range(3):
        for at, ref in enumerate((keep_ref, send_ref)):
            rows = slice((2 * c + at) * shard, (2 * c + at + 1) * shard)
            dp = jnp.concatenate([dp0[rows], dp1[rows]], axis=1)
            ref[c] = dot_nn(dp, a).astype(BF16)


def qkv_grads(dps, a1s):
    width, d = dps[0].shape[0] // 3, a1s[0].shape[1]
    shape = jax.ShapeDtypeStruct((3, width // 2, d), BF16)
    return call(
        qkv_grads_kernel, "qkv_grads", (*dps, *a1s), [shape, shape], 12 * width * d * a1s[0].shape[0]
    )


def backward(du, dr, fc1, h, g, gain, wo, p, qt, kt, v, own):
    rows, d = h.shape
    width = kt.shape[0]
    shape = jax.ShapeDtypeStruct
    shapes = [shape((rows, d), BF16), shape((3 * width, rows), BF16)]
    if own:
        shapes += [shape((rows, d), F32), shape((8, d), F32)]

    def kernel(*refs):
        backward_body(*refs[:11], *refs[11:], *(() if own else (None, None)))

    return call(
        kernel, "attention_backward", (du, dr, fc1, h, g, gain, wo, p, qt, kt, v), shapes,
        rows * width * (6 * d + 16 * LEN),
    )


def input_grads_kernel(dp0, dp1, w_ref, mine_ref, theirs_ref):
    w = w_ref[...].reshape(dp0.shape[0], w_ref.shape[2])
    theirs_ref[...] = dot_tn(dp1[...], w).astype(BF16)
    mine_ref[...] = dot_tn(dp0[...], w)


def input_grads(dps, w):
    rows, d = dps[0].shape[1], w.shape[2]
    shape = jax.ShapeDtypeStruct
    return call(
        input_grads_kernel, "input_grads", (*dps, w), [shape((rows, d), F32), shape((rows, d), BF16)],
        4 * dps[0].size * d,
    )


def input_norm_kernel(x_ref, gain_ref, mine_ref, got_ref, dh_ref, sums_ref, bias_ref, out_ref, vec_ref):
    xh, r = normalise(x_ref[...].astype(F32))
    da1 = mine_ref[...] + got_ref[...].astype(F32)
    out_ref[...] = (dh_ref[...] + norm_back(da1, gain_ref[...], xh, r)).astype(BF16)
    d = x_ref.shape[1]
    bias = bias_ref[...]
    rows = [
        jnp.sum(da1 * xh, axis=0, keepdims=True),
        jnp.sum(da1, axis=0, keepdims=True),
        sums_ref[0:2],
        jnp.concatenate([bias, jnp.zeros((1, d - bias.shape[1]), F32)], axis=1),
        jnp.zeros((11, d), F32),
    ]
    vec_ref[...] = jnp.concatenate(rows, axis=0).astype(BF16)


def input_norm(x, gain, mine, got, dh, sums, bias):
    rows, d = x.shape
    return call(
        input_norm_kernel, "input_norm", (x, gain, mine, got, dh, sums, bias),
        [jax.ShapeDtypeStruct((rows, d), BF16), jax.ShapeDtypeStruct((16, d), BF16)], rows * d * 20,
    )


def plus(a, b):
    return (a.astype(F32) + b.astype(F32)).astype(BF16)


def halve_kernel(bits_ref, mine_ref, got_ref, keep_ref, send_ref):
    at = bits_ref[0]
    keep_ref[...] = plus(mine_ref[at], got_ref[at])
    send_ref[...] = plus(mine_ref[1 - at], got_ref[1 - at])


def halve(bit, mine, got):
    shape = jax.ShapeDtypeStruct(mine.shape[1:], BF16)
    return call(halve_kernel, "sum_halves", (bit, mine, got), [shape, shape], mine.size, scalars=1)


def sum_kernel(a_ref, b_ref, out_ref):
    out_ref[...] = plus(a_ref[...], b_ref[...])


def sum_two(a, b):
    return call(sum_kernel, "sum_two", (a, b), [jax.ShapeDtypeStruct(a.shape, BF16)], a.size)[0]


def join_kernel(bits_ref, mine_ref, got_ref, out_ref):
    at = bits_ref[0]
    out_ref[at] = mine_ref[...].astype(out_ref.dtype)
    out_ref[1 - at] = got_ref[...].astype(out_ref.dtype)


def join(bit, mine, got, dtype):
    shape = jax.ShapeDtypeStruct((2, *mine.shape), dtype)
    return call(join_kernel, "join_halves", (bit, mine, got), [shape], mine.size, scalars=1)[0]


def local(
    n_dp, n_tensor, tokens, node_counts, edge_counts, ln1_gain, ln1_bias, qkv_weight, out_weight,
    ln2_gain, ln2_bias, fc1_weight, fc1_bias, fc2_weight, out_grad,
):
    d = tokens.shape[1]
    shard = out_weight.shape[0]
    mols = tokens.shape[0] // LEN
    dp_at = lax.axis_index("dp")
    tensor_at = lax.axis_index("tensor")
    core = tensor_at % 2
    bit0 = dp_at % 2
    bit1 = (dp_at // 2 + dp_at // 4) % 2
    scalar = lambda v: v.reshape(1).astype(jnp.int32)
    first = scalar(jnp.where(core == 0, bit0, bit1))
    second = scalar(jnp.where(core == 0, bit1, bit0))

    def swap_core(a):
        return lax.ppermute(a, "tensor", [(t, t ^ 1) for t in range(n_tensor)])

    def swap_y(a):
        return lax.ppermute(a, "tensor", [(t, t ^ 2) for t in range(n_tensor)])

    def swap_dp(a, mask0, mask1):
        pairs = [
            (p * n_tensor + t, (p ^ (mask1 if t % 2 else mask0)) * n_tensor + t)
            for p in range(n_dp)
            for t in range(n_tensor)
        ]
        return lax.ppermute(a, ("dp", "tensor"), pairs)

    row = lambda v: v.reshape(1, -1).astype(F32)
    g1, b1, g2, b2 = row(ln1_gain), row(ln1_bias), row(ln2_gain), row(ln2_bias)

    x_got = swap_y(tokens)
    w_qkv = pack_qkv(qkv_weight, swap_core(qkv_weight))
    far_y = swap_y(jnp.where(bit0 == 0, out_weight, fc1_weight))
    far_x = swap_dp(far_y, 1, 1)
    bias = jnp.concatenate([fc1_bias, swap_core(fc1_bias)])

    place = lambda t: scalar(t * mols)
    fwd = lambda t, x: attention(place(t), node_counts, edge_counts, x, g1, b1, w_qkv)
    a1_0, qt_0, kt_0, v_0, p_0, ot_0, o_0 = fwd(tensor_at, tokens)
    packet = swap_y(jnp.concatenate([out_grad, o_0], axis=1))
    a1_1, qt_1, kt_1, v_1, p_1, ot_1, o_1 = fwd(tensor_at ^ 2, x_got)
    o_got = swap_y(o_1)
    wo, fc1, fc2 = pack_rest(
        scalar(bit0), out_weight, swap_core(out_weight), fc1_weight, swap_core(fc1_weight),
        fc2_weight, swap_core(fc2_weight), far_y, swap_core(far_y), far_x, swap_core(far_x),
    )

    h_1, a2_1, z_1, du_1 = feed(x_got, o_1, packet, wo, g2, b2, fc1, row(bias), fc2)
    dr_0 = swap_y(du_1)
    h_0, a2_0, z_0, du_0 = feed(tokens, o_0, (out_grad, o_got), wo, g2, b2, fc1, row(bias), fc2)
    dr_1 = swap_y(du_0)
    keep_fc, send_fc, bias_sums, res_mine, res_theirs = feed_grads(
        (z_0, z_1), (du_0, du_1), (a2_0, a2_1), (out_grad, packet), fc2, h_0
    )
    result = (res_mine + swap_y(res_theirs).astype(F32)).astype(BF16)

    gh_0, dp_0, dh, sums = backward(
        du_0, dr_0, fc1, h_0, out_grad, g2, wo, p_0, qt_0, kt_0, v_0, True
    )
    gh_1, dp_1 = backward(du_1, dr_1, fc1, h_1, packet, g2, wo, p_1, qt_1, kt_1, v_1, False)
    keep_out, send_out = out_grads((ot_0, ot_1), (gh_0, gh_1))
    keep_qkv, send_qkv = qkv_grads((dp_0, dp_1), (a1_0, a1_1))
    da1_mine, da1_theirs = input_grads((dp_0, dp_1), w_qkv)
    grad_tokens, vec = input_norm(tokens, g1, da1_mine, swap_y(da1_theirs), dh, sums, bias_sums)
    vec_got = swap_y(vec)
    same = lax.broadcasted_iota(jnp.int32, vec.shape, 0) < 4
    vec = jnp.where(same, plus(vec, vec_got), vec)
    vec_got = swap_core(vec)
    turned = jnp.concatenate(
        [vec_got[:, shard : 2 * shard], vec_got[:, :shard], vec_got[:, 2 * shard :]], axis=1
    )
    vec = plus(vec, jnp.where(same, vec_got, turned))

    def sum_dp(mine, got, extra=None):
        rows = mine.shape[0] * mine.shape[1]
        size = rows // 4
        view = lambda a: a.reshape(2, rows // 2, d)
        keep, send = halve(first, view(mine), view(got))
        split = lambda a: a.reshape(2, size, d)
        keep, send = halve(second, split(keep), split(swap_dp(send, 1, 2)))
        s = sum_two(keep, swap_dp(send, 2, 1))
        if extra is not None:
            s = jnp.concatenate([s, extra], axis=0)
        for k in range(2, n_dp.bit_length() - 1):
            mask = 6 if k == 2 else 1 << k
            s = sum_two(s, swap_dp(s, mask, mask))
        got = swap_dp(s, 2, 1)
        if extra is not None:
            extra = plus(s[size:], got[size:])
            s, got = s[:size], got[:size]
        s = join(second, s, got, BF16).reshape(2 * size, d)
        if extra is None:
            got = swap_dp(s, 1, 2)
        else:
            got = swap_dp(jnp.concatenate([s, extra], axis=0), 1, 2)
            extra = plus(extra, got[2 * size :])
            got = got[: 2 * size]
        return join(first, s, got, F32).reshape(mine.shape), extra

    keep_rest = jnp.concatenate([keep_fc, keep_out], axis=0)
    rest, _ = sum_dp(keep_rest, swap_core(jnp.concatenate([send_fc, send_out], axis=0)))
    qkv, vec = sum_dp(keep_qkv, swap_core(send_qkv), vec)
    vec = vec.astype(F32)
    return (
        result, grad_tokens, vec[0], vec[1], qkv, rest[2], vec[2], vec[3], rest[0], vec[4, :shard],
        rest[1],
    )


def solution(mesh):
    tokens = P(("dp", "tensor"), None)
    rows = P("tensor", None)
    qkv = P(None, "tensor", None)
    in_specs = (
        tokens, P("dp"), P("dp"), P(), P(), qkv, rows, P(), P(), rows, P("tensor"), rows, tokens,
    )
    out_specs = (tokens, tokens, P(), P(), qkv, rows, P(), P(), rows, P("tensor"), rows)
    step = functools.partial(local, mesh.shape["dp"], mesh.shape["tensor"])
    return jax.shard_map(step, mesh=mesh, in_specs=in_specs, out_specs=out_specs, check_vma=False)
```

```python
import functools

import jax
import jax.numpy as jnp
from jax import lax
from jax.experimental import pallas as pl
from jax.experimental.pallas import tpu as pltpu
from jax.sharding import PartitionSpec as P

HEAD_DIM = 24
LEN = 128
PAIR = 2 * HEAD_DIM
EPSILON = 1e-05
SCALE = HEAD_DIM ** (-0.5)
LOG2E = 1.4426950408889634
F32 = jnp.float32
BF16 = jnp.bfloat16
MIB = 1024 * 1024


def dot_nn(a, b):
    return lax.dot_general(a, b, (((1,), (0,)), ((), ())), preferred_element_type=F32)


def dot_nt(a, b):
    return lax.dot_general(a, b, (((1,), (1,)), ((), ())), preferred_element_type=F32)


def dot_tn(a, b):
    return lax.dot_general(a, b, (((0,), (0,)), ((), ())), preferred_element_type=F32)


def normalise(v):
    centered = v - jnp.mean(v, axis=-1, keepdims=True)
    r = lax.rsqrt(jnp.mean(centered * centered, axis=-1, keepdims=True) + EPSILON)
    return centered * r, r


def norm_back(da, gain, xh, r):
    e = da * gain
    return r * (
        e - jnp.mean(e, axis=-1, keepdims=True) - xh * jnp.mean(e * xh, axis=-1, keepdims=True)
    )


def pair_blocks(rows):
    rows = rows.astype(F32)
    none = jnp.zeros((HEAD_DIM, LEN), F32)
    left = jnp.concatenate([rows[:HEAD_DIM], none], axis=0)
    right = jnp.concatenate([none, rows[HEAD_DIM:]], axis=0)
    return jnp.concatenate([left, right], axis=1).astype(BF16)


def pair_window(i, width):
    low = min(PAIR * i // LEN * LEN, width - 2 * LEN)
    return low, PAIR * i - low


def placed(block, before):
    parts = []
    if before:
        parts.append(jnp.zeros((before, 2 * LEN), BF16))
    parts.append(block)
    after = 2 * LEN - PAIR - before
    if after:
        parts.append(jnp.zeros((after, 2 * LEN), BF16))
    return jnp.concatenate(parts, axis=0)


def diagonal(both):
    return jnp.concatenate([both[:HEAD_DIM, :LEN], both[HEAD_DIM:, LEN:]], axis=0)


def call(kernel, name, args, outs, flops=0, scalars=0, far=(), direct=(), scratch=(), after=(), limit=16):
    size = lambda a: a.size * a.dtype.itemsize
    anywhere = pl.BlockSpec(memory_space=pl.ANY)
    vmem = pl.BlockSpec(memory_space=pltpu.VMEM)
    smem = pl.BlockSpec(memory_space=pltpu.SMEM)
    n = len(args)

    def body(*refs):
        kernel(*refs[:n], *refs[n + len(after) :])

    return pl.pallas_call(
        body,
        in_specs=[smem if j < scalars else anywhere if j in far else vmem for j in range(n)]
        + [anywhere] * len(after),
        out_specs=[anywhere if j in direct else vmem for j in range(len(outs))],
        out_shape=outs,
        scratch_shapes=list(scratch),
        compiler_params=pltpu.CompilerParams(vmem_limit_bytes=limit * MIB),
        cost_estimate=pl.CostEstimate(
            flops=flops,
            bytes_accessed=sum(map(size, args)) + sum(map(size, outs)),
            transcendentals=0,
        ),
        name=name,
    )(*args, *after)


def bf16(*shape):
    return jax.ShapeDtypeStruct(shape, BF16)


def f32(*shape):
    return jax.ShapeDtypeStruct(shape, F32)


def copies(sems, pairs):
    started = [pltpu.make_async_copy(a, b, sems.at[j]) for j, (a, b) in enumerate(pairs)]
    for copy in started:
        copy.start()
    return started


def finish(started):
    for copy in started:
        copy.wait()


def attention_body(place_ref, nodes_ref, edges_ref, x_ref, gain_ref, bias_ref, w_ref, a1_ref, qt_ref,
                   kt_ref, v_ref, p_ref, ot_ref, ready):
    width = w_ref.shape[1]
    mols = x_ref.shape[0] // LEN
    pairs = width // PAIR
    xh, _ = normalise(x_ref[...].astype(F32))
    a1 = (xh * gain_ref[...][None, :] + bias_ref[...][None, :]).astype(BF16)
    a1_ref[...] = a1
    ready()
    qt = dot_nt(w_ref[0], a1).astype(BF16)
    keys = dot_nt(a1, w_ref[1]).astype(BF16)
    vt = dot_nt(w_ref[2], a1).astype(BF16)
    qt_ref[...] = qt
    every = [(m, i) for m in range(mols) for i in range(pairs)]
    lanes = lambda m: slice(LEN * m, LEN * (m + 1))
    rows = lambda i: slice(PAIR * i, PAIR * (i + 1))
    scores, probs = {}, {}
    for m, i in every:
        low, before = pair_window(i, width)
        rhs = placed(pair_blocks(qt[rows(i), lanes(m)]), before)
        scores[m, i] = dot_nn(keys[lanes(m), low : low + 2 * LEN], rhs)
    for m in range(mols):
        mol = place_ref[0] + m
        count = 1 + nodes_ref[mol] + edges_ref[mol]
        valid = lax.broadcasted_iota(jnp.int32, (LEN, 2 * LEN), 0) < count
        for i in range(pairs):
            s = jnp.where(valid, scores[m, i], -1e30)
            e = jnp.exp2((s - jnp.max(s, axis=0, keepdims=True)) * (SCALE * LOG2E))
            p = (e * (1.0 / jnp.sum(e, axis=0, keepdims=True))).astype(BF16)
            p_ref[m, i] = p
            probs[m, i] = p
    for m, i in every:
        both = dot_nn(vt[rows(i), lanes(m)], probs[m, i])
        ot_ref[rows(i), lanes(m)] = diagonal(both).astype(BF16)
    kt_ref[...] = dot_nt(w_ref[1], a1).astype(BF16)
    v_ref[...] = dot_nt(a1, w_ref[2]).astype(BF16)


def attention_outs(rows, d, width):
    pairs = width // PAIR
    return [
        bf16(rows, d), bf16(width, rows), bf16(width, rows), bf16(rows, width),
        bf16(rows // LEN, pairs, LEN, 2 * LEN), bf16(width, rows),
    ]


def attention_first(place, nodes, edges, x, gain, bias, w_own, w_got, g):
    rows, d = x.shape
    shard = w_own.shape[1]
    width = 2 * shard

    def kernel(place_ref, nodes_ref, edges_ref, x_ref, gain_ref, bias_ref, own, got, g_ref, *refs):
        *kept, packet_ref, w_ref, sems = refs
        started = copies(
            sems,
            [(own, w_ref.at[:, :shard]), (got, w_ref.at[:, shard:]), (g_ref, packet_ref.at[:, :d])],
        )
        attention_body(
            place_ref, nodes_ref, edges_ref, x_ref, gain_ref, bias_ref, w_ref, *kept,
            lambda: finish(started[:2]),
        )
        packet_ref[:, d:] = kept[-1][...].T
        finish(started[2:])

    return call(
        kernel, "attention_first", (place, nodes, edges, x, gain, bias, w_own, w_got, g),
        [*attention_outs(rows, d, width), bf16(rows, d + width), bf16(3, width, d)],
        rows * width * (10 * d + 8 * LEN), scalars=3, far=(6, 7, 8),
        scratch=[pltpu.SemaphoreType.DMA((3,))],
    )


def attention_second(place, nodes, edges, x, gain, bias, w, after):
    rows, d = x.shape
    width = w.shape[1]

    def kernel(*refs):
        *refs, o_ref = refs
        attention_body(*refs, lambda: None)
        o_ref[...] = refs[-1][...].T

    return call(
        kernel, "attention_second", (place, nodes, edges, x, gain, bias, w),
        [*attention_outs(rows, d, width), bf16(rows, width)],
        rows * width * (10 * d + 8 * LEN), scalars=3, after=after,
    )


def hold(a, after):
    def kernel(a_ref, out_ref, sem):
        finish(copies(sem, [(a_ref, out_ref)]))

    return call(
        kernel, "hold", (a,), [jax.ShapeDtypeStruct(a.shape, a.dtype)], far=(0,), after=after,
        scratch=[pltpu.SemaphoreType.DMA((1,))], limit=4,
    )[0]


def pack_rest(bit, *parts):
    shard, d = parts[0].shape

    def kernel(bit_ref, wo0, wo1, fc10, fc11, fc20, fc21, y0, y1, x0, x1, wo_ref, fc1_ref, fc2_ref, sems):
        rows = lambda ref, at: ref.at[at * shard : (at + 1) * shard]
        started = copies(
            sems,
            [(wo0, rows(wo_ref, 0)), (wo1, rows(wo_ref, 1)), (fc10, rows(fc1_ref, 0)),
             (fc11, rows(fc1_ref, 1)), (fc20, rows(fc2_ref, 0)), (fc21, rows(fc2_ref, 1))],
        )

        def far(u, v):
            pairs = [(u[0], rows(wo_ref, 2)), (u[1], rows(wo_ref, 3)), (v[0], rows(fc1_ref, 2)),
                     (v[1], rows(fc1_ref, 3))]
            finish(copies(sems.at[6:], pairs))

        pl.when(bit_ref[0] == 0)(lambda: far((y0, y1), (x0, x1)))
        pl.when(bit_ref[0] != 0)(lambda: far((x0, x1), (y0, y1)))
        finish(started)

    return call(
        kernel, "pack_rest", (bit, *parts), [bf16(4 * shard, d), bf16(4 * shard, d), bf16(2 * shard, d)],
        scalars=1, far=range(1, 11), scratch=[pltpu.SemaphoreType.DMA((10,))], limit=4,
    )


def feed_body(x, oa, ob, g, wo_ref, gain_ref, bias_ref, fc1_ref, b1_ref, fc2_ref, h_ref, a2_ref, z_ref,
              du_ref):
    h = x.astype(F32) + dot_nn(jnp.concatenate([oa, ob], axis=1), wo_ref[...])
    h_ref[...] = h
    xh, _ = normalise(h)
    a2 = (xh * gain_ref[...][None, :] + bias_ref[...][None, :]).astype(BF16)
    a2_ref[...] = a2
    u = dot_nt(a2, fc1_ref[: fc2_ref.shape[0]]) + b1_ref[...]
    dz = dot_nt(g, fc2_ref[...])
    phi = 0.5 * (1.0 + lax.erf(u * (0.5**0.5)))
    slope = phi + u * (jnp.exp(-0.5 * u * u) * 0.3989422804014327)
    du_ref[...] = (dz * slope).astype(BF16)
    z_ref[...] = (u * phi).astype(BF16)


def feed(x, oa, got, wo, gain, bias, fc1, b1, fc2, after=()):
    rows, d = x.shape
    width = fc2.shape[0]
    got = got if isinstance(got, tuple) else (got,)

    def kernel(x_ref, oa_ref, *refs):
        if len(got) == 2:
            g, ob = refs[0][...], refs[1][...]
        else:
            g, ob = refs[0][:, :d], refs[0][:, d:]
        oa = oa_ref[:, oa_ref.shape[1] - width :]
        feed_body(x_ref[...], oa, ob, g, *refs[len(got) :])

    return call(
        kernel, "feed_forward", (x, oa, *got, wo, gain, bias, fc1, b1, fc2),
        [f32(rows, d), bf16(rows, d), bf16(rows, width), bf16(rows, width)],
        8 * rows * d * width, after=after,
    )


def feed_grads(zs, dus, a2s, gs, after):
    d = a2s[0].shape[1]
    width = zs[0].shape[1]
    shard = width // 2

    def kernel(z0, z1, du0, du1, a0, a1, g0, g1, keep_ref, send_ref, sums_ref):
        first = dot_tn(du0[...], a0[...]) + dot_tn(du1[...], a1[...])
        second = dot_tn(z0[...], g0[...]) + dot_tn(z1[...], g1[:, :d])
        for at, ref in enumerate((keep_ref, send_ref)):
            rows = slice(at * shard, (at + 1) * shard)
            ref[0] = first[rows].astype(BF16)
            ref[1] = second[rows].astype(BF16)
        sums_ref[...] = jnp.sum(du0[...].astype(F32), axis=0, keepdims=True) + jnp.sum(
            du1[...].astype(F32), axis=0, keepdims=True
        )

    return call(
        kernel, "feed_grads", (*zs, *dus, *a2s, *gs), [bf16(2, shard, d), bf16(2, shard, d), f32(1, width)],
        8 * zs[0].size * d, after=after,
    )


def feed_result(zs, fc2, h, after):
    rows, d = h.shape

    def kernel(z0, z1, fc2_ref, h_ref, mine_ref, theirs_ref):
        theirs_ref[...] = dot_nn(z1[...], fc2_ref[...]).astype(BF16)
        mine_ref[...] = h_ref[...] + dot_nn(z0[...], fc2_ref[...])

    return call(
        kernel, "feed_result", (*zs, fc2, h), [f32(rows, d), bf16(rows, d)], 4 * zs[0].size * d,
        after=after, limit=8,
    )


def backward_body(du_ref, dr_ref, fc1_ref, h_ref, g_ref, gain_ref, wo_ref, p_ref, qt_ref, kt_ref, v_ref,
                  gh_ref, dp_ref, dh_ref=None, sums_ref=None):
    width, d = kt_ref.shape[0], h_ref.shape[1]
    mols = h_ref.shape[0] // LEN
    pairs = width // PAIR
    du = jnp.concatenate([du_ref[...], dr_ref[...]], axis=1)
    da2 = dot_nn(du, fc1_ref[...])
    xh, r = normalise(h_ref[...])
    dh = g_ref[:, :d].astype(F32) + norm_back(da2, gain_ref[...][None, :], xh, r)
    if dh_ref is not None:
        dh_ref[...] = dh
        sums_ref[0:1] = jnp.sum(da2 * xh, axis=0, keepdims=True)
        sums_ref[1:2] = jnp.sum(da2, axis=0, keepdims=True)
    gh = dh.astype(BF16)
    gh_ref[...] = gh
    dot = dot_nt(wo_ref[:width], gh).astype(BF16)
    every = [(m, i) for m in range(mols) for i in range(pairs)]
    lanes = lambda m: slice(LEN * m, LEN * (m + 1))
    rows = lambda i: slice(PAIR * i, PAIR * (i + 1))
    dps, dss, dos = {}, {}, {}
    for m, i in every:
        low, before = pair_window(i, width)
        dos[m, i] = pair_blocks(dot[rows(i), lanes(m)])
        dps[m, i] = dot_nn(v_ref[lanes(m), low : low + 2 * LEN], placed(dos[m, i], before))
    for m, i in every:
        dp_ref[pl.ds(2 * width + PAIR * i, PAIR), lanes(m)] = dot_nt(dos[m, i], p_ref[m, i]).astype(BF16)
    for m, i in every:
        p = p_ref[m, i].astype(F32)
        t = dps[m, i] * p
        dss[m, i] = (t - p * jnp.sum(t, axis=0, keepdims=True)).astype(BF16)
    for m, i in every:
        dq = diagonal(dot_nn(kt_ref[rows(i), lanes(m)], dss[m, i])) * SCALE
        dp_ref[rows(i), lanes(m)] = dq.astype(BF16)
        dk = dot_nt(pair_blocks(qt_ref[rows(i), lanes(m)]), dss[m, i]) * SCALE
        dp_ref[pl.ds(width + PAIR * i, PAIR), lanes(m)] = dk.astype(BF16)


def backward(args, own, after=()):
    h, kt = args[3], args[9]
    rows, d = h.shape
    width = kt.shape[0]
    outs = [bf16(rows, d), bf16(3 * width, rows)]
    return call(
        backward_body, "attention_backward", args, outs + ([f32(rows, d), f32(8, d)] if own else []),
        rows * width * (6 * d + 16 * LEN), after=after,
    )


def out_grads(ots, ghs, keep, send):
    width, d = ots[0].shape[0], ghs[0].shape[1]
    shard = width // 2

    def kernel(ot0, ot1, gh0, gh1, keep2, send2, keep_ref, send_ref):
        total = dot_nn(ot0[...], gh0[...]) + dot_nn(ot1[...], gh1[...])
        for at, (two, ref) in enumerate(((keep2, keep_ref), (send2, send_ref))):
            ref[2] = total[at * shard : (at + 1) * shard].astype(BF16)
            ref[:2] = two[...]

    return call(
        kernel, "out_grads", (*ots, *ghs, keep, send), [bf16(3, shard, d), bf16(3, shard, d)],
        4 * ots[0].size * d, limit=8,
    )


def qkv_grads(dps, a1s, after):
    width, d = dps[0].shape[0] // 3, a1s[0].shape[1]
    shard = width // 2

    def kernel(dp0, dp1, a0, a1, keep_ref, send_ref):
        a = jnp.concatenate([a0[...], a1[...]], axis=0)
        for at, ref in ((1, send_ref), (0, keep_ref)):
            for c in range(3):
                rows = slice((2 * c + at) * shard, (2 * c + at + 1) * shard)
                ref[c] = dot_nn(jnp.concatenate([dp0[rows], dp1[rows]], axis=1), a).astype(BF16)

    return call(
        kernel, "qkv_grads", (*dps, *a1s), [bf16(3, shard, d), bf16(3, shard, d)],
        4 * dps[0].size * d, after=after,
    )


def input_grads(dps, w, xs, sums, bias, after):
    rows, d = xs[0].shape

    def kernel(dp0, dp1, w_ref, x0, x1, sums_ref, bias_ref, mine_ref, theirs_ref):
        w = w_ref[...].reshape(dp0.shape[0], d)
        theirs = dot_tn(dp1[...], w)
        mine = dot_tn(dp0[...], w)
        theirs_ref[:rows] = theirs.astype(BF16)
        mine_ref[...] = mine
        xh0, _ = normalise(x0[...].astype(F32))
        xh1, _ = normalise(x1[...].astype(F32))
        bias = bias_ref[...]
        vec = [
            jnp.sum(mine * xh0, axis=0, keepdims=True) + jnp.sum(theirs * xh1, axis=0, keepdims=True),
            jnp.sum(mine, axis=0, keepdims=True) + jnp.sum(theirs, axis=0, keepdims=True),
            sums_ref[0:2],
            jnp.concatenate([bias, jnp.zeros((1, d - bias.shape[1]), F32)], axis=1),
            jnp.zeros((11, d), F32),
        ]
        theirs_ref[rows:] = jnp.concatenate(vec, axis=0).astype(BF16)

    return call(
        kernel, "input_grads", (*dps, w, *xs, sums, bias), [f32(rows, d), bf16(rows + 16, d)],
        4 * dps[0].size * d, after=after,
    )


def input_norm(x, gain, mine, got, dh, after):
    rows, d = x.shape

    def kernel(x_ref, gain_ref, mine_ref, got_ref, dh_ref, out_ref):
        xh, r = normalise(x_ref[...].astype(F32))
        da1 = mine_ref[...] + got_ref[:rows].astype(F32)
        out_ref[...] = (dh_ref[...] + norm_back(da1, gain_ref[...][None, :], xh, r)).astype(BF16)

    return call(
        kernel, "input_norm", (x, gain, mine, got, dh), [bf16(rows, d)], rows * d * 20, after=after, limit=8
    )[0]


def add_result(mine, got, after):
    def kernel(mine_ref, got_ref, out_ref):
        out_ref[...] = (mine_ref[...] + got_ref[...].astype(F32)).astype(BF16)

    return call(kernel, "add_result", (mine, got), [bf16(*mine.shape)], mine.size, after=after, limit=8)[0]


def plus(*terms):
    total = terms[0].astype(F32)
    for term in terms[1:]:
        total = total + term.astype(F32)
    return total.astype(BF16)


def vector_rows(mine, got, after):
    rows, d = mine.shape

    def kernel(mine_ref, got_ref, out_ref):
        a, b = mine_ref[rows - 16 :], got_ref[rows - 16 :]
        same = lax.broadcasted_iota(jnp.int32, (16, d), 0) < 4
        out_ref[...] = plus(a, jnp.where(same, b.astype(F32), 0.0))

    return call(kernel, "vector_rows", (mine, got), [bf16(16, d)], after=after, limit=4)[0]


def sum_half(bits, mine, got, after):
    def kernel(bits_ref, mine_ref, got_ref, out_ref):
        at = 1 - bits_ref[0]
        out_ref[...] = mine_ref[at] + got_ref[at]

    return call(
        kernel, "sum_half", (bits, mine, got), [bf16(*mine.shape[1:])], mine.size, scalars=1, after=after,
        limit=8,
    )[0]


def sum_quarter(bits, mine, got, half, last, after, vec=()):
    rows, d = mine.shape[2:]

    def kernel(bits_ref, mine_ref, got_ref, half_ref, *refs):
        *refs, out_ref = refs
        first = bits_ref[0]
        at = bits_ref[1] if last else 1 - bits_ref[1]
        terms = [mine_ref[first, at], got_ref[first, at], half_ref[at]]
        out_ref[:rows] = plus(*terms, *(ref[...] for ref in refs[: len(last)]))
        if vec:
            a, b = refs[-2][...].astype(F32), refs[-1][...].astype(F32)
            shard = vec[2]
            turned = jnp.concatenate([b[:, shard : 2 * shard], b[:, :shard], b[:, 2 * shard :]], axis=1)
            same = lax.broadcasted_iota(jnp.int32, a.shape, 0) < 4
            out_ref[rows:] = plus(a, jnp.where(same, b, turned))

    args = (bits, mine, got, half, *last, *vec[:2])
    return call(
        kernel, "sum_quarter", args, [bf16(rows + (16 if vec else 0), d)], rows * d * 4, scalars=1,
        after=after, limit=8,
    )[0]


def sum_two(a, b, after):
    def kernel(a_ref, b_ref, out_ref):
        out_ref[...] = a_ref[...] + b_ref[...]

    return call(kernel, "sum_two", (a, b), [bf16(*a.shape)], a.size, after=after, limit=8)[0]


def side_by_side(mine, got, rows, after):
    extra = mine.shape[0] - rows

    def kernel(mine_ref, got_ref, out_ref):
        out_ref[:rows] = mine_ref[:rows]
        out_ref[rows : 2 * rows] = got_ref[:rows]
        if extra:
            out_ref[2 * rows :] = mine_ref[rows:] + got_ref[rows:]

    return call(
        kernel, "side_by_side", (mine, got), [bf16(2 * rows + extra, mine.shape[1])], after=after, limit=8
    )[0]


def place_sums(bits, mine, got, rows, outs, vec, after):
    d = mine.shape[1]

    def kernel(bits_ref, mine_ref, got_ref, *refs):
        out_refs, vec_refs = refs[: len(outs)], refs[len(outs) : -2]
        all_ref, sems = refs[-2:]
        for at, ref in enumerate((mine_ref, got_ref)):
            half = bits_ref[0] if at == 0 else 1 - bits_ref[0]
            for part in range(2):
                quarter = bits_ref[1] if part == 0 else 1 - bits_ref[1]
                start = pl.multiple_of((2 * half + quarter) * rows, 16)
                all_ref[pl.ds(start, rows), :] = ref[part * rows : (part + 1) * rows].astype(F32)
        pairs, start = [], 0
        for ref in out_refs:
            flat = ref if len(ref.shape) == 2 else None
            if flat is not None:
                pairs.append((all_ref.at[start : start + ref.shape[0]], ref))
                start += ref.shape[0]
            else:
                for c in range(ref.shape[0]):
                    pairs.append((all_ref.at[start : start + ref.shape[1]], ref.at[c]))
                    start += ref.shape[1]
        started = copies(sems, pairs)
        if vec:
            total = mine_ref[2 * rows :].astype(F32) + got_ref[2 * rows :].astype(F32)
            for at, (n, ref) in enumerate(zip(vec, vec_refs)):
                ref[...] = total[at, :n]
        finish(started)

    return call(
        kernel, "place_sums", (bits, mine, got), [*outs, *(f32(n) for n in vec)], 4 * rows * d, scalars=1,
        direct=range(len(outs)), after=after, limit=8,
        scratch=[pltpu.VMEM((4 * rows, d), F32), pltpu.SemaphoreType.DMA((3,))],
    )


def local(
    n_dp, n_tensor, tokens, node_counts, edge_counts, ln1_gain, ln1_bias, qkv_weight, out_weight,
    ln2_gain, ln2_bias, fc1_weight, fc1_bias, fc2_weight, out_grad,
):
    d = tokens.shape[1]
    shard = out_weight.shape[0]
    mols = tokens.shape[0] // LEN
    dp_at = lax.axis_index("dp")
    tensor_at = lax.axis_index("tensor")
    core = tensor_at % 2
    bit0 = dp_at % 2
    bit1 = (dp_at // 2 + dp_at // 4) % 2
    bits = jnp.stack([jnp.where(core == 0, bit0, bit1), jnp.where(core == 0, bit1, bit0)])
    bits = bits.astype(jnp.int32)
    scalar = lambda v: v.reshape(1).astype(jnp.int32)

    def swap_core(a):
        return lax.ppermute(a, "tensor", [(t, t ^ 1) for t in range(n_tensor)])

    def swap_y(a):
        return lax.ppermute(a, "tensor", [(t, t ^ 2) for t in range(n_tensor)])

    def swap_dp(a, mask0, mask1):
        pairs = [
            (p * n_tensor + t, (p ^ (mask1 if t % 2 else mask0)) * n_tensor + t)
            for p in range(n_dp)
            for t in range(n_tensor)
        ]
        return lax.ppermute(a, ("dp", "tensor"), pairs)

    swap_first = lambda a: swap_dp(a, 1, 2)
    swap_second = lambda a: swap_dp(a, 2, 1)
    far_masks = [6 if k == 2 else 1 << k for k in range(2, n_dp.bit_length() - 1)]

    x_got = swap_y(tokens)
    far_y = swap_y(jnp.where(bit0 == 0, out_weight, fc1_weight))
    bias = jnp.concatenate([fc1_bias, swap_core(fc1_bias)]).astype(F32).reshape(1, -1)

    place = lambda t: scalar(t * mols)
    counts = (node_counts, edge_counts)
    a1_0, qt_0, kt_0, v_0, p_0, ot_0, packet, w_qkv = attention_first(
        place(tensor_at), *counts, tokens, ln1_gain, ln1_bias, qkv_weight, swap_core(qkv_weight), out_grad
    )
    packet_got = swap_y(packet)
    far_y = hold(far_y, (a1_0,))
    far_x = swap_dp(far_y, 1, 1)
    a1_1, qt_1, kt_1, v_1, p_1, ot_1, o_1 = attention_second(
        place(tensor_at ^ 2), *counts, x_got, ln1_gain, ln1_bias, w_qkv, (a1_0,)
    )
    o_got = swap_y(o_1)
    wo, fc1, fc2 = pack_rest(
        scalar(bit0), out_weight, swap_core(out_weight), fc1_weight, swap_core(fc1_weight),
        fc2_weight, swap_core(fc2_weight), far_y, swap_core(far_y), far_x, swap_core(far_x),
    )

    ffn = (wo, ln2_gain, ln2_bias, fc1, bias, fc2)
    h_1, a2_1, z_1, du_1 = feed(x_got, o_1, packet_got, *ffn)
    dr_0 = swap_y(du_1)
    h_0, a2_0, z_0, du_0 = feed(tokens, packet, (out_grad, o_got), *ffn, after=(du_1,))
    dr_1 = swap_y(du_0)

    gh_0, dp_0, dh, sums = backward(
        (du_0, dr_0, fc1, h_0, out_grad, ln2_gain, wo, p_0, qt_0, kt_0, v_0), True
    )
    keep_fc, send_fc, bias_sums = feed_grads(
        (z_0, z_1), (du_0, du_1), (a2_0, a2_1), (out_grad, packet_got), (gh_0,)
    )
    gh_1, dp_1 = backward(
        (du_1, dr_1, fc1, h_1, packet_got, ln2_gain, wo, p_1, qt_1, kt_1, v_1), False, (keep_fc,)
    )

    keep_r, send_r = out_grads((ot_0, ot_1), (gh_0, gh_1), keep_fc, send_fc)
    got_r = swap_core(send_r)
    keep_q, send_q = qkv_grads((dp_0, dp_1), (a1_0, a1_1), (keep_r,))
    got_q = swap_core(send_q)
    half = lambda a: a.reshape(2, -1, d)
    size = 3 * shard // 4
    quarters = lambda a: a.reshape(2, 2, size, d)
    two = lambda a: a.reshape(2, size, d)

    send1_r = sum_half(bits, half(keep_r), half(got_r), (keep_q,))
    got1_r = swap_first(send1_r)
    send1_q = sum_half(bits, half(keep_q), half(got_q), (send1_r,))
    got1_q = swap_first(send1_q)
    da1_mine, da1_theirs = input_grads(
        (dp_0, dp_1), w_qkv, (tokens, x_got), sums, bias_sums, (send1_q,)
    )
    da1_got = swap_y(da1_theirs)
    view_r = (quarters(keep_r), quarters(got_r), two(got1_r))
    view_q = (quarters(keep_q), quarters(got_q), two(got1_q))
    send2_r = sum_quarter(bits, *view_r, (), (da1_theirs,))
    got2_r = swap_second(send2_r)
    res_mine, res_theirs = feed_result((z_0, z_1), fc2, h_0, (send2_r,))
    send2_q = sum_quarter(bits, *view_q, (), (send2_r,))
    got2_q = swap_second(send2_q)
    res_got = swap_y(res_theirs)
    s_r = sum_quarter(bits, *view_r, (got2_r,), (send2_q,))
    got3_r = swap_dp(s_r, far_masks[0], far_masks[0])
    vec = vector_rows(da1_theirs, da1_got, (s_r,))
    s_q = sum_quarter(bits, *view_q, (got2_q,), (s_r,), (vec, swap_core(vec), shard))
    got3_q = swap_dp(s_q, far_masks[0], far_masks[0])
    s_r = sum_two(s_r, got3_r, (s_q,))
    for mask in far_masks[1:]:
        s_r = sum_two(s_r, swap_dp(s_r, mask, mask), ())
    got4_r = swap_second(s_r)
    grad_tokens = input_norm(tokens, ln1_gain, da1_mine, da1_got, dh, (s_r,))
    s_q = sum_two(s_q, got3_q, (s_r,))
    for mask in far_masks[1:]:
        s_q = sum_two(s_q, swap_dp(s_q, mask, mask), ())
    got4_q = swap_second(s_q)
    both_r = side_by_side(s_r, got4_r, size, (s_q,))
    got5_r = swap_first(both_r)
    result = add_result(res_mine, res_got, (both_r,))
    both_q = side_by_side(s_q, got4_q, size, (both_r,))
    got5_q = swap_first(both_q)
    rows = f32(shard, d)
    grad_fc1, grad_fc2, grad_out = place_sums(bits, both_r, got5_r, size, [rows] * 3, (), (both_q,))
    grad_qkv, gain1, bias1, gain2, bias2, grad_b = place_sums(
        bits, both_q, got5_q, size, [f32(3, shard, d)], (d, d, d, d, shard), (grad_fc1,)
    )
    return (
        result, grad_tokens, gain1, bias1, grad_qkv, grad_out, gain2, bias2, grad_fc1, grad_b, grad_fc2,
    )


def solution(mesh):
    tokens = P(("dp", "tensor"), None)
    rows = P("tensor", None)
    qkv = P(None, "tensor", None)
    in_specs = (
        tokens, P("dp"), P("dp"), P(), P(), qkv, rows, P(), P(), rows, P("tensor"), rows, tokens,
    )
    out_specs = (tokens, tokens, P(), P(), qkv, rows, P(), P(), rows, P("tensor"), rows)
    step = functools.partial(local, mesh.shape["dp"], mesh.shape["tensor"])
    return jax.shard_map(step, mesh=mesh, in_specs=in_specs, out_specs=out_specs, check_vma=False)
```

```python
import functools

import jax
import jax.numpy as jnp
from jax import lax
from jax.experimental import pallas as pl
from jax.experimental.pallas import tpu as pltpu
from jax.sharding import PartitionSpec as P

HEAD_DIM = 24
LEN = 128
PAIR = 2 * HEAD_DIM
EPSILON = 1e-05
SCALE = HEAD_DIM ** (-0.5)
LOG2E = 1.4426950408889634
F32 = jnp.float32
BF16 = jnp.bfloat16
MIB = 1024 * 1024


def dot_nn(a, b):
    return lax.dot_general(a, b, (((1,), (0,)), ((), ())), preferred_element_type=F32)


def dot_nt(a, b):
    return lax.dot_general(a, b, (((1,), (1,)), ((), ())), preferred_element_type=F32)


def dot_tn(a, b):
    return lax.dot_general(a, b, (((0,), (0,)), ((), ())), preferred_element_type=F32)


def normalise(v):
    centered = v - jnp.mean(v, axis=-1, keepdims=True)
    r = lax.rsqrt(jnp.mean(centered * centered, axis=-1, keepdims=True) + EPSILON)
    return centered * r, r


def norm_back(da, gain, xh, r):
    e = da * gain
    return r * (
        e - jnp.mean(e, axis=-1, keepdims=True) - xh * jnp.mean(e * xh, axis=-1, keepdims=True)
    )


def pair_blocks(rows):
    rows = rows.astype(F32)
    none = jnp.zeros((HEAD_DIM, LEN), F32)
    left = jnp.concatenate([rows[:HEAD_DIM], none], axis=0)
    right = jnp.concatenate([none, rows[HEAD_DIM:]], axis=0)
    return jnp.concatenate([left, right], axis=1).astype(BF16)


def pair_window(i, width):
    low = min(PAIR * i // LEN * LEN, width - 2 * LEN)
    return low, PAIR * i - low


def placed(block, before):
    parts = []
    if before:
        parts.append(jnp.zeros((before, 2 * LEN), BF16))
    parts.append(block)
    after = 2 * LEN - PAIR - before
    if after:
        parts.append(jnp.zeros((after, 2 * LEN), BF16))
    return jnp.concatenate(parts, axis=0)


def diagonal(both):
    return jnp.concatenate([both[:HEAD_DIM, :LEN], both[HEAD_DIM:, LEN:]], axis=0)


class IO:
    def __init__(self, reads, writes):
        self.reads, self.writes = reads, writes
        self.started = set()

    def wait(self, *args):
        for j in args:
            if j in self.reads:
                self.reads[j].wait()

    def flush(self, *outs):
        for j in outs:
            if j in self.writes:
                self.started.add(j)
                self.writes[j].start()

    def finish(self):
        self.flush(*(j for j in self.writes if j not in self.started))
        for copy in self.writes.values():
            copy.wait()


def pinned(a):
    return pltpu.with_memory_space_constraint(a, pltpu.HBM)


class Chain:
    def __init__(self):
        self.token = None

    def call(self, kernel, name, args, outs, kinds, scratch=(), limit=16, weight=1):
        ins, out_kinds = kinds.split("-")
        assert len(ins) == len(args) and len(out_kinds) == len(outs)
        hbm = pl.BlockSpec(memory_space=pltpu.HBM)
        vmem = pl.BlockSpec(memory_space=pltpu.VMEM)
        smem = pl.BlockSpec(memory_space=pltpu.SMEM)
        spec = lambda kind: {"s": smem, "v": vmem}.get(kind, hbm)
        tokens = () if self.token is None else (self.token,)
        staged = [j for j, kind in enumerate(ins) if kind in "hcl"]
        written = [j for j, kind in enumerate(out_kinds) if kind == "w"]
        memory = lambda kind: pltpu.SMEM if kind == "c" else pltpu.VMEM
        buffers = [memory(ins[j])(args[j].shape, args[j].dtype) for j in staged]
        buffers += [pltpu.VMEM(outs[j].shape, outs[j].dtype) for j in written]
        n_in, n_out, n_buf = len(args) + len(tokens), len(outs), len(buffers)

        def body(*refs):
            arg_refs = list(refs[: len(args)])
            out_refs = list(refs[n_in : n_in + n_out])
            token_ref = refs[n_in + n_out]
            own = refs[n_in + n_out + 1 :]
            bufs, sems, extra = own[:n_buf], own[n_buf], own[n_buf + 1 :]
            reads, writes = {}, {}
            for at, j in enumerate(staged):
                reads[j] = pltpu.make_async_copy(arg_refs[j], bufs[at], sems.at[at])
                reads[j].start()
                arg_refs[j] = bufs[at]
            for at, j in enumerate(written, len(staged)):
                writes[j] = pltpu.make_async_copy(bufs[at], out_refs[j], sems.at[at])
                out_refs[j] = bufs[at]
            io = IO(reads, writes)
            io.wait(*(j for j in staged if ins[j] == "h"))
            token_ref[...] = jnp.zeros_like(token_ref)
            kernel(io, *arg_refs, *out_refs, *extra)
            io.finish()

        *results, self.token = pl.pallas_call(
            body,
            in_specs=[spec(kind) for kind in ins] + [vmem] * len(tokens),
            out_specs=[spec(kind) for kind in out_kinds] + [vmem],
            out_shape=[*outs, f32(8, 128)],
            scratch_shapes=[*buffers, pltpu.SemaphoreType.DMA((max(n_buf, 1),)), *scratch],
            compiler_params=pltpu.CompilerParams(vmem_limit_bytes=limit * MIB),
            cost_estimate=pl.CostEstimate(flops=weight * 10**10, bytes_accessed=10**8, transcendentals=0),
            name=name,
        )(*(pinned(a) if kind in "hclp" else a for a, kind in zip(args, ins)), *tokens)
        return results


def bf16(*shape):
    return jax.ShapeDtypeStruct(shape, BF16)


def f32(*shape):
    return jax.ShapeDtypeStruct(shape, F32)


def copies(sems, pairs):
    started = [pltpu.make_async_copy(a, b, sems.at[j]) for j, (a, b) in enumerate(pairs)]
    for copy in started:
        copy.start()
    return started


def finish(started):
    for copy in started:
        copy.wait()


def attention(chain, bits, place, nodes, edges, x, gain, bias, w, g=None):
    rows, d = x.shape
    width = w.shape[1] if g is None else 2 * w[0].shape[1]
    shard = width // 2
    pairs = width // PAIR
    mols = rows // LEN

    def kernel(io, bits_ref, nodes_ref, edges_ref, x_ref, gain_ref, bias_ref, *refs):
        started = []
        if g is None:
            w_ref, *refs = refs
            a1_ref, qt_ref, kt_ref, v_ref, p_ref, ot_ref, o_ref = refs
        else:
            own, got, g_ref, *refs, w_ref, sems = refs
            a1_ref, qt_ref, kt_ref, v_ref, p_ref, ot_ref, o_ref = refs
            pairs_w = [(own, w_ref.at[:, :shard]), (got, w_ref.at[:, shard:]), (g_ref, o_ref.at[:, :d])]
            started = copies(sems, pairs_w)
        xh, _ = normalise(x_ref[...].astype(F32))
        a1 = (xh * gain_ref[...][None, :] + bias_ref[...][None, :]).astype(BF16)
        a1_ref[...] = a1
        finish(started[:2])
        qt = dot_nt(w_ref[0], a1).astype(BF16)
        keys = dot_nt(a1, w_ref[1]).astype(BF16)
        vt = dot_nt(w_ref[2], a1).astype(BF16)
        qt_ref[...] = qt
        every = [(m, i) for m in range(mols) for i in range(pairs)]
        lanes = lambda m: slice(LEN * m, LEN * (m + 1))
        rows_of = lambda i: slice(PAIR * i, PAIR * (i + 1))
        scores, probs = {}, {}
        for m, i in every:
            low, before = pair_window(i, width)
            rhs = placed(pair_blocks(qt[rows_of(i), lanes(m)]), before)
            scores[m, i] = dot_nn(keys[lanes(m), low : low + 2 * LEN], rhs)
        io.wait(1, 2)
        for m in range(mols):
            mol = bits_ref[place] + m
            count = 1 + nodes_ref[mol] + edges_ref[mol]
            valid = lax.broadcasted_iota(jnp.int32, (LEN, 2 * LEN), 0) < count
            for i in range(pairs):
                s = jnp.where(valid, scores[m, i], -1e30)
                e = jnp.exp2((s - jnp.max(s, axis=0, keepdims=True)) * (SCALE * LOG2E))
                p = (e * (1.0 / jnp.sum(e, axis=0, keepdims=True))).astype(BF16)
                p_ref[m, i] = p
                probs[m, i] = p
        for m, i in every:
            both = dot_nn(vt[rows_of(i), lanes(m)], probs[m, i])
            ot_ref[rows_of(i), lanes(m)] = diagonal(both).astype(BF16)
        o_ref[:, o_ref.shape[1] - width :] = ot_ref[...].T
        kt_ref[...] = dot_nt(w_ref[1], a1).astype(BF16)
        v_ref[...] = dot_nt(a1, w_ref[2]).astype(BF16)
        finish(started[2:])

    outs = [
        bf16(rows, d), bf16(width, rows), bf16(width, rows), bf16(rows, width),
        bf16(mols, pairs, LEN, 2 * LEN), bf16(width, rows),
    ]
    args = (bits, nodes, edges, x, gain, bias)
    if g is None:
        return chain.call(
            kernel, "attention_forward", (*args, w), [*outs, bf16(rows, width)], "sccvvvv-vvvvvvv"
        )
    return chain.call(
        kernel, "attention_forward", (*args, *w, g), [*outs, bf16(rows, d + width), bf16(3, width, d)],
        "sccvvvprv-vvvvvvvv", scratch=[pltpu.SemaphoreType.DMA((3,))],
    )


def send_parts(chain, bits, out_weight, fc1_weight, fc2_weight, bias, others):
    shard, d = out_weight.shape
    n = len(others)

    def kernel(io, bits_ref, wo, fc1, fc2, bias_ref, *refs):
        others_in, (far_ref, near_ref, *others_out, sems) = refs[:n], refs[n:]
        rows = lambda at: near_ref.at[at * shard : (at + 1) * shard]
        pl.when(bits_ref[2] == 0)(lambda: finish(copies(sems, [(wo, far_ref)])))
        pl.when(bits_ref[2] != 0)(lambda: finish(copies(sems, [(fc1, far_ref)])))
        near = [(wo, rows(0)), (fc1, rows(1)), (fc2, rows(2)), (bias_ref, near_ref.at[3 * shard :])]
        finish(copies(sems, near + list(zip(others_in, others_out))))

    far, near, *others = chain.call(
        kernel, "send_parts", (bits, out_weight, fc1_weight, fc2_weight, bias, *others),
        [bf16(shard, d), bf16(3 * shard + 16, d)] + [jax.ShapeDtypeStruct(a.shape, a.dtype) for a in others],
        "spppr" + "p" * n + "-vv" + "v" * n, limit=4, scratch=[pltpu.SemaphoreType.DMA((4 + n,))],
    )
    return far, near, others


def join_arrays(chain, *parts):
    def kernel(io, *refs):
        *ins, out_ref, sems = refs
        finish(copies(sems, [(ref, out_ref.at[j]) for j, ref in enumerate(ins)]))

    return chain.call(
        kernel, "join_arrays", parts, [bf16(len(parts), *parts[0].shape)], "v" * len(parts) + "-v", limit=4,
        scratch=[pltpu.SemaphoreType.DMA((len(parts),))],
    )[0]


def pack_near(chain, near, near_got):
    d = near.shape[1]
    shard = (near.shape[0] - 16) // 3

    def kernel(io, near0, near1, fc2_ref, sems):
        rows = lambda ref, at: ref.at[at * shard : (at + 1) * shard]
        finish(copies(sems, [(rows(near0, 2), rows(fc2_ref, 0)), (rows(near1, 2), rows(fc2_ref, 1))]))

    return chain.call(
        kernel, "pack_near", (near, near_got), [bf16(2 * shard, d)], "vv-v", limit=4,
        scratch=[pltpu.SemaphoreType.DMA((2,))],
    )[0]


def pack_rest(chain, bits, near, near_got, far, far_got):
    shard, d = far.shape[1:]

    def kernel(io, bits_ref, near0, near1, far0, far1, wo_ref, fc1_ref, sems):
        rows = lambda ref, at: ref.at[at * shard : (at + 1) * shard]
        wo_at = bits_ref[2]
        pairs = []
        for at, (near_ref, far_ref) in enumerate(((near0, far0), (near1, far1))):
            pairs += [(rows(near_ref, c), rows(ref, at)) for c, ref in enumerate((wo_ref, fc1_ref))]
            pairs += [(far_ref.at[wo_at], rows(wo_ref, 2 + at)), (far_ref.at[1 - wo_at], rows(fc1_ref, 2 + at))]
        finish(copies(sems, pairs))

    return chain.call(
        kernel, "pack_rest", (bits, near, near_got, far, far_got), [bf16(4 * shard, d), bf16(4 * shard, d)],
        "svvvv-vv", limit=4, scratch=[pltpu.SemaphoreType.DMA((8,))],
    )


def feed(chain, x, oa, got, wo, gain, bias, fc1, b1, fc2, kinds):
    rows, d = x.shape
    width = fc2.shape[0]
    shard = width // 2

    def kernel(io, x_ref, oa_ref, *refs):
        if len(got) == 2:
            g, ob = refs[0][...], refs[1][...]
        else:
            g, ob = refs[0][:, :d], refs[0][:, d:]
        wo_ref, gain_ref, bias_ref, fc1_ref, b10, b11, fc2_ref, h_ref, a2_ref, z_ref, du_ref = refs[len(got) :]
        oa = oa_ref[:, oa_ref.shape[1] - width :]
        h = x_ref[...].astype(F32) + dot_nn(jnp.concatenate([oa, ob], axis=1), wo_ref[...])
        h_ref[...] = h
        xh, _ = normalise(h)
        a2 = (xh * gain_ref[...][None, :] + bias_ref[...][None, :]).astype(BF16)
        a2_ref[...] = a2
        b1 = jnp.concatenate([b[3 * shard : 3 * shard + 1, :shard] for b in (b10, b11)], axis=1).astype(F32)
        u = dot_nt(a2, fc1_ref[:width]) + b1
        dz = dot_nt(g, fc2_ref[...])
        phi = 0.5 * (1.0 + lax.erf(u * (0.5**0.5)))
        slope = phi + u * (jnp.exp(-0.5 * u * u) * 0.3989422804014327)
        du_ref[...] = (dz * slope).astype(BF16)
        z_ref[...] = (u * phi).astype(BF16)

    return chain.call(
        kernel, "feed_forward", (x, oa, *got, wo, gain, bias, fc1, *b1, fc2),
        [f32(rows, d), bf16(rows, d), bf16(rows, width), bf16(rows, width)],
        kinds + "vvvvvvv-vvvv",
    )


def feed_grads(chain, zs, dus, a2s, gs):
    d = a2s[0].shape[1]
    width = zs[0].shape[1]
    shard = width // 2

    def kernel(io, z0, z1, du0, du1, a0, a1, g0, g1, keep_ref, send_ref, sums_ref):
        first = dot_tn(du0[...], a0[...]) + dot_tn(du1[...], a1[...])
        second = dot_tn(z0[...], g0[...]) + dot_tn(z1[...], g1[:, :d])
        for at, ref in enumerate((keep_ref, send_ref)):
            rows = slice(at * shard, (at + 1) * shard)
            ref[0] = first[rows].astype(BF16)
            ref[1] = second[rows].astype(BF16)
        sums_ref[...] = jnp.sum(du0[...].astype(F32), axis=0, keepdims=True) + jnp.sum(
            du1[...].astype(F32), axis=0, keepdims=True
        )

    return chain.call(
        kernel, "feed_grads", (*zs, *dus, *a2s, *gs), [bf16(2, shard, d), bf16(2, shard, d), f32(1, width)],
        "vvvvvvvv-vvv", weight=10,
    )


def feed_result(chain, zs, fc2, h):
    rows, d = h.shape

    def kernel(io, z0, z1, fc2_ref, h_ref, mine_ref, theirs_ref):
        theirs_ref[...] = dot_nn(z1[...], fc2_ref[...]).astype(BF16)
        mine_ref[...] = h_ref[...] + dot_nn(z0[...], fc2_ref[...])

    return chain.call(
        kernel, "feed_result", (*zs, fc2, h), [f32(rows, d), bf16(rows, d)], "vvvv-vv", limit=8,
    )


def backward(chain, args, own):
    h, kt = args[3], args[9]
    rows, d = h.shape
    width = kt.shape[0]
    mols, pairs = rows // LEN, width // PAIR

    def kernel(io, du_ref, dr_ref, fc1_ref, h_ref, g_ref, gain_ref, wo_ref, p_ref, qt_ref, kt_ref, v_ref,
               gh_ref, dp_ref, dh_ref=None, sums_ref=None):
        du = jnp.concatenate([du_ref[...], dr_ref[...]], axis=1)
        da2 = dot_nn(du, fc1_ref[...])
        xh, r = normalise(h_ref[...])
        dh = g_ref[:, :d].astype(F32) + norm_back(da2, gain_ref[...][None, :], xh, r)
        if own:
            dh_ref[...] = dh
            sums_ref[0:1] = jnp.sum(da2 * xh, axis=0, keepdims=True)
            sums_ref[1:2] = jnp.sum(da2, axis=0, keepdims=True)
            io.flush(2)
        gh = dh.astype(BF16)
        gh_ref[...] = gh
        dot = dot_nt(wo_ref[:width], gh).astype(BF16)
        every = [(m, i) for m in range(mols) for i in range(pairs)]
        lanes = lambda m: slice(LEN * m, LEN * (m + 1))
        rows_of = lambda i: slice(PAIR * i, PAIR * (i + 1))
        dps, dss, dos = {}, {}, {}
        io.wait(7, 8, 9, 10)
        for m, i in every:
            low, before = pair_window(i, width)
            dos[m, i] = pair_blocks(dot[rows_of(i), lanes(m)])
            dps[m, i] = dot_nn(v_ref[lanes(m), low : low + 2 * LEN], placed(dos[m, i], before))
        for m, i in every:
            dv = dot_nt(dos[m, i], p_ref[m, i])
            dp_ref[pl.ds(2 * width + PAIR * i, PAIR), lanes(m)] = dv.astype(BF16)
        for m, i in every:
            p = p_ref[m, i].astype(F32)
            t = dps[m, i] * p
            dss[m, i] = (t - p * jnp.sum(t, axis=0, keepdims=True)).astype(BF16)
        for m, i in every:
            dq = diagonal(dot_nn(kt_ref[rows_of(i), lanes(m)], dss[m, i])) * SCALE
            dp_ref[rows_of(i), lanes(m)] = dq.astype(BF16)
            dk = dot_nt(pair_blocks(qt_ref[rows_of(i), lanes(m)]), dss[m, i]) * SCALE
            dp_ref[pl.ds(width + PAIR * i, PAIR), lanes(m)] = dk.astype(BF16)

    outs = [bf16(rows, d), bf16(3 * width, rows)] + ([f32(rows, d), f32(8, d)] if own else [])
    return chain.call(
        kernel, "attention_backward", args, outs, "v" * 11 + ("-vvvv" if own else "-vv"),
    )


def weight_grads(chain, name, shard, lefts, rights):
    d = rights[0][0].shape[1]
    args, count = [], len(lefts)
    for (u0, u1, _), (v0, v1) in zip(lefts, rights):
        args += [u0, u1, v0, v1]

    def kernel(io, *refs):
        keep_ref, send_ref = refs[-2:]
        for at, ref in ((1, send_ref), (0, keep_ref)):
            for c in range(count):
                u0, u1, v0, v1 = refs[4 * c : 4 * c + 4]
                rows = slice(lefts[c][2] + at * shard, lefts[c][2] + (at + 1) * shard)
                left = jnp.concatenate([u0[rows], u1[rows]], axis=1)
                right = jnp.concatenate([v0[...], v1[...]], axis=0)
                ref[c] = dot_nn(left, right).astype(BF16)

    return chain.call(
        kernel, name, args, [bf16(count, shard, d), bf16(count, shard, d)], "v" * len(args) + "-vv",
    )


def input_grads(chain, dps, w, xs, sums, bias):
    rows, d = xs[0].shape

    def kernel(io, dp0, dp1, w_ref, x0, x1, sums_ref, bias_ref, mine_ref, theirs_ref):
        w = w_ref[...].reshape(dp0.shape[0], d)
        theirs = dot_tn(dp1[...], w)
        theirs_ref[:rows] = theirs.astype(BF16)
        mine = dot_tn(dp0[...], w)
        mine_ref[...] = mine
        xh0, _ = normalise(x0[...].astype(F32))
        xh1, _ = normalise(x1[...].astype(F32))
        bias = bias_ref[...]
        vec = [
            jnp.sum(mine * xh0, axis=0, keepdims=True) + jnp.sum(theirs * xh1, axis=0, keepdims=True),
            jnp.sum(mine, axis=0, keepdims=True) + jnp.sum(theirs, axis=0, keepdims=True),
            sums_ref[0:2],
            jnp.concatenate([bias, jnp.zeros((1, d - bias.shape[1]), F32)], axis=1),
            jnp.zeros((11, d), F32),
        ]
        theirs_ref[rows:] = jnp.concatenate(vec, axis=0).astype(BF16)

    return chain.call(
        kernel, "input_grads", (*dps, w, *xs, sums, bias), [f32(rows, d), bf16(rows + 16, d)], "vvvvvvv-vv"
    )


def input_norm(chain, x, gain, mine, got, dh):
    rows, d = x.shape

    def kernel(io, x_ref, gain_ref, mine_ref, got_ref, dh_ref, out_ref):
        xh, r = normalise(x_ref[...].astype(F32))
        da1 = mine_ref[...] + got_ref[:rows].astype(F32)
        out_ref[...] = (dh_ref[...] + norm_back(da1, gain_ref[...][None, :], xh, r)).astype(BF16)

    return chain.call(
        kernel, "input_norm", (x, gain, mine, got, dh), [bf16(rows, d)], "vvvvv-w", limit=8
    )[0]


def add_result(chain, mine, got):
    def kernel(io, mine_ref, got_ref, out_ref):
        out_ref[...] = (mine_ref[...] + got_ref[...].astype(F32)).astype(BF16)

    return chain.call(kernel, "add_result", (mine, got), [bf16(*mine.shape)], "vv-w", limit=8)[0]


def plus(*terms):
    total = terms[0].astype(F32)
    for term in terms[1:]:
        total = total + term.astype(F32)
    return total.astype(BF16)


def vector_rows(chain, mine, got):
    rows, d = mine.shape

    def kernel(io, mine_ref, got_ref, out_ref):
        a, b = mine_ref[rows - 16 :], got_ref[rows - 16 :]
        same = lax.broadcasted_iota(jnp.int32, (16, d), 0) < 4
        out_ref[...] = plus(a, jnp.where(same, b.astype(F32), 0.0))

    return chain.call(kernel, "vector_rows", (mine, got), [bf16(16, d)], "vv-v", limit=4)[0]


def sum_half(chain, bits, mine, got):
    def kernel(io, bits_ref, mine_ref, got_ref, out_ref):
        at = 1 - bits_ref[0]
        out_ref[...] = mine_ref[at] + got_ref[at]

    return chain.call(
        kernel, "sum_half", (bits, mine, got), [bf16(*mine.shape[1:])], "svv-v", limit=8
    )[0]


def sum_quarter(chain, bits, mine, got, half, last=(), vec=()):
    rows, d = mine.shape[2:]

    def kernel(io, bits_ref, mine_ref, got_ref, half_ref, *refs):
        *refs, out_ref = refs
        first = bits_ref[0]
        at = bits_ref[1] if last else 1 - bits_ref[1]
        terms = [mine_ref[first, at], got_ref[first, at], half_ref[at]]
        out_ref[:rows] = plus(*terms, *(ref[...] for ref in refs[: len(last)]))
        if vec:
            a, b = refs[-2][...].astype(F32), refs[-1][...].astype(F32)
            shard = vec[2]
            turned = jnp.concatenate([b[:, shard : 2 * shard], b[:, :shard], b[:, 2 * shard :]], axis=1)
            same = lax.broadcasted_iota(jnp.int32, a.shape, 0) < 4
            out_ref[rows:] = plus(a, jnp.where(same, b, turned))

    args = (bits, mine, got, half, *last, *vec[:2])
    return chain.call(
        kernel, "sum_quarter", args, [bf16(rows + (16 if vec else 0), d)], "s" + "v" * (len(args) - 1) + "-v",
        limit=8,
    )[0]


def sum_two(chain, a, b):
    def kernel(io, a_ref, b_ref, out_ref):
        out_ref[...] = a_ref[...] + b_ref[...]

    return chain.call(kernel, "sum_two", (a, b), [bf16(*a.shape)], "vv-v", limit=8)[0]


def side_by_side(chain, mine, got, rows):
    extra = mine.shape[0] - rows

    def kernel(io, mine_ref, got_ref, out_ref):
        out_ref[:rows] = mine_ref[:rows]
        out_ref[rows : 2 * rows] = got_ref[:rows]
        if extra:
            out_ref[2 * rows :] = mine_ref[rows:] + got_ref[rows:]

    return chain.call(
        kernel, "side_by_side", (mine, got), [bf16(2 * rows + extra, mine.shape[1])], "vv-v", limit=8
    )[0]


def place_sums(chain, bits, mine, got, rows, outs, vec=()):
    d = mine.shape[1]

    def kernel(io, bits_ref, mine_ref, got_ref, *refs):
        out_refs, vec_refs = refs[: len(outs)], refs[len(outs) : -2]
        all_ref, sems = refs[-2:]
        for at, ref in enumerate((mine_ref, got_ref)):
            half = bits_ref[0] if at == 0 else 1 - bits_ref[0]
            for part in range(2):
                quarter = bits_ref[1] if part == 0 else 1 - bits_ref[1]
                start = pl.multiple_of((2 * half + quarter) * rows, 16)
                all_ref[pl.ds(start, rows), :] = ref[part * rows : (part + 1) * rows].astype(F32)
        pairs, start = [], 0
        for ref in out_refs:
            for piece in [ref] if len(ref.shape) == 2 else [ref.at[c] for c in range(ref.shape[0])]:
                pairs.append((all_ref.at[start : start + piece.shape[0]], piece))
                start += piece.shape[0]
        started = copies(sems, pairs)
        if vec:
            total = mine_ref[2 * rows :].astype(F32) + got_ref[2 * rows :].astype(F32)
            for at, (n, ref) in enumerate(zip(vec, vec_refs)):
                ref[...] = total[at, :n]
        finish(started)

    return chain.call(
        kernel, "place_sums", (bits, mine, got), [*outs, *(f32(n) for n in vec)],
        "svv-" + "r" * len(outs) + "v" * len(vec), limit=8,
        scratch=[pltpu.VMEM((4 * rows, d), F32), pltpu.SemaphoreType.DMA((4,))],
    )


def local(
    n_dp, n_tensor, tokens, node_counts, edge_counts, ln1_gain, ln1_bias, qkv_weight, out_weight,
    ln2_gain, ln2_bias, fc1_weight, fc1_bias, fc2_weight, out_grad,
):
    d = tokens.shape[1]
    shard = out_weight.shape[0]
    width = 2 * shard
    mols = tokens.shape[0] // LEN
    dp_at = lax.axis_index("dp")
    tensor_at = lax.axis_index("tensor")
    core = tensor_at % 2
    bit0 = dp_at % 2
    bit1 = (dp_at // 2 + dp_at // 4) % 2
    bits = jnp.stack(
        [jnp.where(core == 0, bit0, bit1), jnp.where(core == 0, bit1, bit0), bit0, tensor_at * mols,
         (tensor_at ^ 2) * mols]
    ).astype(jnp.int32)
    chain = Chain()

    def swap_core(a):
        return lax.ppermute(a, "tensor", [(t, t ^ 1) for t in range(n_tensor)])

    def swap_y(a):
        return lax.ppermute(a, "tensor", [(t, t ^ 2) for t in range(n_tensor)])

    def swap_dp(a, mask0, mask1):
        pairs = [
            (p * n_tensor + t, (p ^ (mask1 if t % 2 else mask0)) * n_tensor + t)
            for p in range(n_dp)
            for t in range(n_tensor)
        ]
        return lax.ppermute(a, ("dp", "tensor"), pairs)

    swap_first = lambda a: swap_dp(a, 1, 2)
    swap_second = lambda a: swap_dp(a, 2, 1)
    far_masks = [6 if k == 2 else 1 << k for k in range(2, n_dp.bit_length() - 1)]

    w_got = swap_core(qkv_weight)
    bias = jnp.pad(fc1_bias.reshape(1, -1), ((0, 15), (0, d - shard)))
    far_y, near, others = send_parts(
        chain, bits, out_weight, fc1_weight, fc2_weight, bias,
        (tokens, out_grad, ln1_gain, ln1_bias, ln2_gain, ln2_bias),
    )
    far_y = swap_y(far_y)
    near_got = swap_core(near)
    x_got = swap_y(others[0])
    tokens, out_grad, ln1_gain, ln1_bias, ln2_gain, ln2_bias = others

    counts = (node_counts, edge_counts)
    norm1 = (ln1_gain, ln1_bias)
    a1_0, qt_0, kt_0, v_0, p_0, ot_0, packet, w_qkv = attention(
        chain, bits, 3, *counts, tokens, *norm1, (qkv_weight, w_got), out_grad
    )
    packet_got = swap_y(packet)
    far_x = swap_dp(join_arrays(chain, far_y)[0], 1, 1)
    a1_1, qt_1, kt_1, v_1, p_1, ot_1, o_1 = attention(chain, bits, 4, *counts, x_got, *norm1, w_qkv)
    o_got = swap_y(o_1)
    far = join_arrays(chain, far_y, far_x)
    far_got = swap_core(far)
    fc2 = pack_near(chain, near, near_got)
    wo, fc1 = pack_rest(chain, bits, near, near_got, far, far_got)

    ffn = (wo, ln2_gain, ln2_bias, fc1, (near, near_got), fc2)
    h_1, a2_1, z_1, du_1 = feed(chain, x_got, o_1, (packet_got,), *ffn, "vvv")
    dr_0 = swap_y(du_1)
    h_0, a2_0, z_0, du_0 = feed(chain, tokens, packet, (out_grad, o_got), *ffn, "vvvv")
    dr_1 = swap_y(du_0)
    keep_r, send_r, bias_sums = feed_grads(
        chain, (z_0, z_1), (du_0, du_1), (a2_0, a2_1), (out_grad, packet_got)
    )
    got_r = swap_core(send_r)
    gh_0, dp_0, dh, sums = backward(
        chain, (du_0, dr_0, fc1, h_0, out_grad, ln2_gain, wo, p_0, qt_0, kt_0, v_0), True
    )

    class Sum:
        def __init__(self, count, keep, got):
            self.size = count * shard // 4
            self.keep, self.got = keep, got

        def first(self):
            half = lambda a: a.reshape(2, 2 * self.size, d)
            got = swap_first(sum_half(chain, bits, half(self.keep), half(self.got)))
            quarters = lambda a: a.reshape(2, 2, self.size, d)
            self.view = (quarters(self.keep), quarters(self.got), got.reshape(2, self.size, d))

        def second(self):
            self.last = swap_second(sum_quarter(chain, bits, *self.view))

        def third(self, vec=()):
            self.sum = sum_quarter(chain, bits, *self.view, (self.last,), vec)
            self.last = swap_dp(self.sum, far_masks[0], far_masks[0])

        def fourth(self):
            self.sum = sum_two(chain, self.sum, self.last)
            for mask in far_masks[1:]:
                self.sum = sum_two(chain, self.sum, swap_dp(self.sum, mask, mask))
            self.last = swap_second(self.sum)

        def fifth(self):
            self.both = side_by_side(chain, self.sum, self.last, self.size)
            self.last = swap_first(self.both)

        def place(self, outs, vec=()):
            return place_sums(chain, bits, self.both, self.last, self.size, outs, vec)

    r = Sum(2, keep_r, got_r)
    r.first()
    gh_1, dp_1 = backward(
        chain, (du_1, dr_1, fc1, h_1, packet_got, ln2_gain, wo, p_1, qt_1, kt_1, v_1), False
    )
    a1s = (a1_0, a1_1)
    keep_q, send_q = weight_grads(
        chain, "weight_grads", shard, [(dp_0, dp_1, c * width) for c in range(3)] + [(ot_0, ot_1, 0)],
        [a1s] * 3 + [(gh_0, gh_1)],
    )
    q = Sum(4, keep_q, swap_core(send_q))
    r.second()
    q.first()
    da1_mine, da1_theirs = input_grads(chain, (dp_0, dp_1), w_qkv, (tokens, x_got), sums, bias_sums)
    da1_got = swap_y(da1_theirs)
    r.third()
    q.second()
    r.fourth()
    vec = vector_rows(chain, da1_theirs, da1_got)
    q.third((vec, swap_core(vec), shard))
    res_mine, res_theirs = feed_result(chain, (z_0, z_1), fc2, h_0)
    res_got = swap_y(res_theirs)
    grad_tokens = input_norm(chain, tokens, ln1_gain, da1_mine, da1_got, dh)
    r.fifth()
    q.fourth()
    rows = f32(shard, d)
    grad_fc1, grad_fc2 = r.place([rows, rows])
    result = add_result(chain, res_mine, res_got)
    q.fifth()
    grad_qkv, grad_out, gain1, bias1, gain2, bias2, grad_b = q.place(
        [f32(3, shard, d), rows], (d, d, d, d, shard)
    )
    return (
        result, grad_tokens, gain1, bias1, grad_qkv, grad_out, gain2, bias2, grad_fc1, grad_b, grad_fc2,
    )


def solution(mesh):
    tokens = P(("dp", "tensor"), None)
    rows = P("tensor", None)
    qkv = P(None, "tensor", None)
    in_specs = (
        tokens, P("dp"), P("dp"), P(), P(), qkv, rows, P(), P(), rows, P("tensor"), rows, tokens,
    )
    out_specs = (tokens, tokens, P(), P(), qkv, rows, P(), P(), rows, P("tensor"), rows)
    step = functools.partial(local, mesh.shape["dp"], mesh.shape["tensor"])
    return jax.shard_map(step, mesh=mesh, in_specs=in_specs, out_specs=out_specs, check_vma=False)
```

```python
import functools

import jax
import jax.numpy as jnp
from jax import lax
from jax.experimental import pallas as pl
from jax.experimental.pallas import tpu as pltpu
from jax.sharding import PartitionSpec as P

HEAD_DIM = 24
LEN = 128
PAIR = 2 * HEAD_DIM
EPSILON = 1e-05
SCALE = HEAD_DIM ** (-0.5)
LOG2E = 1.4426950408889634
F32 = jnp.float32
BF16 = jnp.bfloat16
MIB = 1024 * 1024


def dot_nn(a, b):
    return lax.dot_general(a, b, (((1,), (0,)), ((), ())), preferred_element_type=F32)


def dot_nt(a, b):
    return lax.dot_general(a, b, (((1,), (1,)), ((), ())), preferred_element_type=F32)


def dot_tn(a, b):
    return lax.dot_general(a, b, (((0,), (0,)), ((), ())), preferred_element_type=F32)


def normalise(v):
    centered = v - jnp.mean(v, axis=-1, keepdims=True)
    r = lax.rsqrt(jnp.mean(centered * centered, axis=-1, keepdims=True) + EPSILON)
    return centered * r, r


def norm_back(da, gain, xh, r):
    e = da * gain
    return r * (
        e - jnp.mean(e, axis=-1, keepdims=True) - xh * jnp.mean(e * xh, axis=-1, keepdims=True)
    )


def pair_blocks(rows):
    rows = rows.astype(F32)
    none = jnp.zeros((HEAD_DIM, LEN), F32)
    left = jnp.concatenate([rows[:HEAD_DIM], none], axis=0)
    right = jnp.concatenate([none, rows[HEAD_DIM:]], axis=0)
    return jnp.concatenate([left, right], axis=1).astype(BF16)


def pair_window(i, width):
    low = min(PAIR * i // LEN * LEN, width - 2 * LEN)
    return low, PAIR * i - low


def placed(block, before):
    parts = []
    if before:
        parts.append(jnp.zeros((before, 2 * LEN), BF16))
    parts.append(block)
    after = 2 * LEN - PAIR - before
    if after:
        parts.append(jnp.zeros((after, 2 * LEN), BF16))
    return jnp.concatenate(parts, axis=0)


def diagonal(both):
    return jnp.concatenate([both[:HEAD_DIM, :LEN], both[HEAD_DIM:, LEN:]], axis=0)


class IO:
    def __init__(self, reads, writes):
        self.reads, self.writes = reads, writes
        self.started = set()

    def wait(self, *args):
        for j in args:
            if j in self.reads:
                self.reads[j].wait()

    def flush(self, *outs):
        for j in outs:
            if j in self.writes:
                self.started.add(j)
                self.writes[j].start()

    def finish(self):
        self.flush(*(j for j in self.writes if j not in self.started))
        for copy in self.writes.values():
            copy.wait()


def pinned(a):
    return pltpu.with_memory_space_constraint(a, pltpu.HBM)


class Chain:
    def __init__(self):
        self.token = None

    def call(self, kernel, name, args, outs, kinds, scratch=(), limit=16, weight=1):
        ins, out_kinds = kinds.split("-")
        assert len(ins) == len(args) and len(out_kinds) == len(outs)
        hbm = pl.BlockSpec(memory_space=pltpu.HBM)
        vmem = pl.BlockSpec(memory_space=pltpu.VMEM)
        smem = pl.BlockSpec(memory_space=pltpu.SMEM)
        spec = lambda kind: {"s": smem, "v": vmem}.get(kind, hbm)
        tokens = () if self.token is None else (self.token,)
        staged = [j for j, kind in enumerate(ins) if kind in "hcl"]
        written = [j for j, kind in enumerate(out_kinds) if kind == "w"]
        memory = lambda kind: pltpu.SMEM if kind == "c" else pltpu.VMEM
        buffers = [memory(ins[j])(args[j].shape, args[j].dtype) for j in staged]
        buffers += [pltpu.VMEM(outs[j].shape, outs[j].dtype) for j in written]
        n_in, n_out, n_buf = len(args) + len(tokens), len(outs), len(buffers)

        def body(*refs):
            arg_refs = list(refs[: len(args)])
            out_refs = list(refs[n_in : n_in + n_out])
            token_ref = refs[n_in + n_out]
            own = refs[n_in + n_out + 1 :]
            bufs, sems, extra = own[:n_buf], own[n_buf], own[n_buf + 1 :]
            reads, writes = {}, {}
            for at, j in enumerate(staged):
                reads[j] = pltpu.make_async_copy(arg_refs[j], bufs[at], sems.at[at])
                reads[j].start()
                arg_refs[j] = bufs[at]
            for at, j in enumerate(written, len(staged)):
                writes[j] = pltpu.make_async_copy(bufs[at], out_refs[j], sems.at[at])
                out_refs[j] = bufs[at]
            io = IO(reads, writes)
            io.wait(*(j for j in staged if ins[j] == "h"))
            token_ref[...] = jnp.zeros_like(token_ref)
            kernel(io, *arg_refs, *out_refs, *extra)
            io.finish()

        *results, self.token = pl.pallas_call(
            body,
            in_specs=[spec(kind) for kind in ins] + [vmem] * len(tokens),
            out_specs=[spec(kind) for kind in out_kinds] + [vmem],
            out_shape=[*outs, f32(8, 128)],
            scratch_shapes=[*buffers, pltpu.SemaphoreType.DMA((max(n_buf, 1),)), *scratch],
            compiler_params=pltpu.CompilerParams(vmem_limit_bytes=limit * MIB),
            cost_estimate=pl.CostEstimate(flops=weight * 10**10, bytes_accessed=10**8, transcendentals=0),
            name=name,
        )(*(pinned(a) if kind in "hclp" else a for a, kind in zip(args, ins)), *tokens)
        return results


def bf16(*shape):
    return jax.ShapeDtypeStruct(shape, BF16)


def f32(*shape):
    return jax.ShapeDtypeStruct(shape, F32)


def copies(sems, pairs):
    started = [pltpu.make_async_copy(a, b, sems.at[j]) for j, (a, b) in enumerate(pairs)]
    for copy in started:
        copy.start()
    return started


def finish(started):
    for copy in started:
        copy.wait()


def attention(chain, bits, place, nodes, edges, x, gain, bias, w, g=None, near=()):
    rows, d = x.shape
    width = w.shape[1] if g is None else 2 * w[0].shape[1]
    shard = width // 2
    pairs = width // PAIR
    mols = rows // LEN

    def kernel(io, bits_ref, nodes_ref, edges_ref, x_ref, gain_ref, bias_ref, *refs):
        started = []
        if g is None:
            w_ref, near0, near1, *refs, wo_ref, fc1_ref, fc2_ref, sems = refs
            a1_ref, qt_ref, kt_ref, v_ref, p_ref, ot_ref, o_ref = refs
            pairs_w = []
            for at, ref in enumerate((near0, near1)):
                for c, out in enumerate((wo_ref, fc1_ref, fc2_ref)):
                    part = ref.at[c * shard : (c + 1) * shard]
                    pairs_w.append((part, out.at[at * shard : (at + 1) * shard]))
            started = copies(sems, pairs_w)
        else:
            own, got, g_ref, *refs, w_ref, sems = refs
            a1_ref, qt_ref, kt_ref, v_ref, p_ref, ot_ref, o_ref = refs
            pairs_w = [(own, w_ref.at[:, :shard]), (got, w_ref.at[:, shard:]), (g_ref, o_ref.at[:, :d])]
            started = copies(sems, pairs_w)
        xh, _ = normalise(x_ref[...].astype(F32))
        a1 = (xh * gain_ref[...][None, :] + bias_ref[...][None, :]).astype(BF16)
        a1_ref[...] = a1
        if g is not None:
            finish(started[:2])
        qt = dot_nt(w_ref[0], a1).astype(BF16)
        keys = dot_nt(a1, w_ref[1]).astype(BF16)
        vt = dot_nt(w_ref[2], a1).astype(BF16)
        qt_ref[...] = qt
        every = [(m, i) for m in range(mols) for i in range(pairs)]
        lanes = lambda m: slice(LEN * m, LEN * (m + 1))
        rows_of = lambda i: slice(PAIR * i, PAIR * (i + 1))
        scores, probs = {}, {}
        for m, i in every:
            low, before = pair_window(i, width)
            rhs = placed(pair_blocks(qt[rows_of(i), lanes(m)]), before)
            scores[m, i] = dot_nn(keys[lanes(m), low : low + 2 * LEN], rhs)
        io.wait(1, 2)
        for m in range(mols):
            mol = bits_ref[place] + m
            count = 1 + nodes_ref[mol] + edges_ref[mol]
            valid = lax.broadcasted_iota(jnp.int32, (LEN, 2 * LEN), 0) < count
            for i in range(pairs):
                s = jnp.where(valid, scores[m, i], -1e30)
                e = jnp.exp2((s - jnp.max(s, axis=0, keepdims=True)) * (SCALE * LOG2E))
                p = (e * (1.0 / jnp.sum(e, axis=0, keepdims=True))).astype(BF16)
                p_ref[m, i] = p
                probs[m, i] = p
        for m, i in every:
            both = dot_nn(vt[rows_of(i), lanes(m)], probs[m, i])
            ot_ref[rows_of(i), lanes(m)] = diagonal(both).astype(BF16)
        o_ref[:, o_ref.shape[1] - width :] = ot_ref[...].T
        kt_ref[...] = dot_nt(w_ref[1], a1).astype(BF16)
        v_ref[...] = dot_nt(a1, w_ref[2]).astype(BF16)
        finish(started if g is None else started[2:])

    outs = [
        bf16(rows, d), bf16(width, rows), bf16(width, rows), bf16(rows, width),
        bf16(mols, pairs, LEN, 2 * LEN), bf16(width, rows),
    ]
    args = (bits, nodes, edges, x, gain, bias)
    if g is None:
        return chain.call(
            kernel, "attention_forward", (*args, w, *near), [*outs, bf16(rows, width)] + [bf16(width, d)] * 3,
            "sccvvvvvv-vvvvvvvvvv", scratch=[pltpu.SemaphoreType.DMA((6,))],
        )
    return chain.call(
        kernel, "attention_forward", (*args, *w, g), [*outs, bf16(rows, d + width), bf16(3, width, d)],
        "sccvvvprv-vvvvvvvv", scratch=[pltpu.SemaphoreType.DMA((3,))],
    )


def pick(chain, bits, a, b):
    def kernel(io, bits_ref, a_ref, b_ref, out_ref, sems):
        pl.when(bits_ref[2] == 0)(lambda: finish(copies(sems, [(a_ref, out_ref)])))
        pl.when(bits_ref[2] != 0)(lambda: finish(copies(sems, [(b_ref, out_ref)])))

    return chain.call(
        kernel, "pick", (bits, a, b), [bf16(*a.shape)], "spp-v", limit=4,
        scratch=[pltpu.SemaphoreType.DMA((1,))],
    )[0]


def hold(chain, a):
    def kernel(io, a_ref, out_ref, sems):
        finish(copies(sems, [(a_ref, out_ref)]))

    return chain.call(
        kernel, "hold", (a,), [bf16(*a.shape)], "v-v", limit=4, scratch=[pltpu.SemaphoreType.DMA((1,))]
    )[0]


def load(chain, out_weight, fc1_weight, fc2_weight, bias, others):
    shard, d = out_weight.shape
    n = len(others)

    def kernel(io, wo, fc1, fc2, bias_ref, *refs):
        others_in, (near_ref, *others_out, sems) = refs[:n], refs[n:]
        rows = lambda at: near_ref.at[at * shard : (at + 1) * shard]
        near = [(wo, rows(0)), (fc1, rows(1)), (fc2, rows(2)), (bias_ref, near_ref.at[3 * shard :])]
        finish(copies(sems, near + list(zip(others_in, others_out))))

    near, *others = chain.call(
        kernel, "load", (out_weight, fc1_weight, fc2_weight, bias, *others),
        [bf16(3 * shard + 16, d)] + [jax.ShapeDtypeStruct(a.shape, a.dtype) for a in others],
        "pppr" + "p" * n + "-v" + "v" * n, limit=4, scratch=[pltpu.SemaphoreType.DMA((4 + n,))],
    )
    return near, others


def feed_body(x, oa, ob, g, wo, gain_ref, bias_ref, fc1_ref, b1, fc2_ref, h_ref, a2_ref, z_ref, du_ref):
    h = x.astype(F32) + dot_nn(oa, wo[0][...]) + dot_nn(ob, wo[1][...])
    h_ref[...] = h
    xh, _ = normalise(h)
    a2 = (xh * gain_ref[...][None, :] + bias_ref[...][None, :]).astype(BF16)
    a2_ref[...] = a2
    shard = fc2_ref.shape[0] // 2
    b1 = jnp.concatenate([b[3 * shard : 3 * shard + 1, :shard] for b in b1], axis=1).astype(F32)
    u = dot_nt(a2, fc1_ref[...]) + b1
    dz = dot_nt(g, fc2_ref[...])
    phi = 0.5 * (1.0 + lax.erf(u * (0.5**0.5)))
    slope = phi + u * (jnp.exp(-0.5 * u * u) * 0.3989422804014327)
    du = (dz * slope).astype(BF16)
    z = (u * phi).astype(BF16)
    du_ref[...] = du
    z_ref[...] = z
    return a2, z, du


def feed_far(chain, bits, x, oa, packet, gain, bias, fc1, fc2, wo, near, fars):
    rows, d = x.shape
    width = fc2.shape[0]
    shard = width // 2

    def kernel(io, bits_ref, x_ref, oa_ref, packet_ref, gain_ref, bias_ref, fc1_ref, fc2_ref, wo_ref, b10, b11,
               y0, x0, y1, x1, h_ref, a2_ref, z_ref, du_ref, wo_far, fc1_far, sems):
        def both(first, second):
            pairs = []
            for at in range(2):
                here = slice(at * shard, (at + 1) * shard)
                pairs += [(first[at], wo_far.at[here]), (second[at], fc1_far.at[here])]
            finish(copies(sems, pairs))

        pl.when(bits_ref[2] == 0)(lambda: both((y0, y1), (x0, x1)))
        pl.when(bits_ref[2] != 0)(lambda: both((x0, x1), (y0, y1)))
        feed_body(
            x_ref[...], oa_ref[...], packet_ref[:, d:], packet_ref[:, :d], (wo_ref, wo_far), gain_ref, bias_ref,
            fc1_ref, (b10, b11), fc2_ref, h_ref, a2_ref, z_ref, du_ref,
        )

    return chain.call(
        kernel, "feed_far", (bits, x, oa, packet, gain, bias, fc1, fc2, wo, *near, *fars),
        [f32(rows, d), bf16(rows, d), bf16(rows, width), bf16(rows, width), bf16(width, d), bf16(width, d)],
        "s" + "v" * 14 + "-vvvvvv", scratch=[pltpu.SemaphoreType.DMA((4,))],
    )


def feed_own(chain, x, packet, g, ob, gain, bias, fc1, fc2, wos, near, far):
    rows, d = x.shape
    width = fc2.shape[0]
    shard = width // 2

    def kernel(io, x_ref, oa_ref, g_ref, ob_ref, gain_ref, bias_ref, fc1_ref, fc2_ref, wo0, wo1, b10, b11,
               z1, du1, a1, g1, h_ref, a2_ref, z_ref, du_ref, keep_ref, send_ref, sums_ref):
        a2, z, du = feed_body(
            x_ref[...], oa_ref[:, d:], ob_ref[...], g_ref[...], (wo0, wo1), gain_ref, bias_ref, fc1_ref,
            (b10, b11), fc2_ref, h_ref, a2_ref, z_ref, du_ref,
        )
        first = dot_tn(du, a2) + dot_tn(du1[...], a1[...])
        second = dot_tn(z, g_ref[...]) + dot_tn(z1[...], g1[:, :d])
        for at, ref in enumerate((keep_ref, send_ref)):
            here = slice(at * shard, (at + 1) * shard)
            ref[0] = first[here].astype(BF16)
            ref[1] = second[here].astype(BF16)
        sums_ref[...] = jnp.sum(du.astype(F32), axis=0, keepdims=True) + jnp.sum(
            du1[...].astype(F32), axis=0, keepdims=True
        )

    return chain.call(
        kernel, "feed_own", (x, packet, g, ob, gain, bias, fc1, fc2, *wos, *near, *far),
        [f32(rows, d), bf16(rows, d), bf16(rows, width), bf16(rows, width), bf16(2, shard, d),
         bf16(2, shard, d), f32(1, width)], "v" * 16 + "-vvvvvvv",
    )


def feed_result(chain, zs, fc2, h):
    rows, d = h.shape

    def kernel(io, z0, z1, fc2_ref, h_ref, mine_ref, theirs_ref):
        theirs_ref[...] = dot_nn(z1[...], fc2_ref[...]).astype(BF16)
        mine_ref[...] = h_ref[...] + dot_nn(z0[...], fc2_ref[...])

    return chain.call(
        kernel, "feed_result", (*zs, fc2, h), [f32(rows, d), bf16(rows, d)], "vvvv-vv", limit=8,
    )


def backward(chain, args, own):
    h, kt = args[4], args[10]
    rows, d = h.shape
    width = kt.shape[0]
    mols, pairs = rows // LEN, width // PAIR

    def kernel(io, du_ref, dr_ref, fc1_ref, fc1_far, h_ref, g_ref, gain_ref, wo_ref, p_ref, qt_ref, kt_ref, v_ref,
               gh_ref, dp_ref, dh_ref=None, sums_ref=None):
        da2 = dot_nn(du_ref[...], fc1_ref[...]) + dot_nn(dr_ref[...], fc1_far[...])
        xh, r = normalise(h_ref[...])
        dh = g_ref[:, :d].astype(F32) + norm_back(da2, gain_ref[...][None, :], xh, r)
        if own:
            dh_ref[...] = dh
            sums_ref[0:1] = jnp.sum(da2 * xh, axis=0, keepdims=True)
            sums_ref[1:2] = jnp.sum(da2, axis=0, keepdims=True)
            io.flush(2)
        gh = dh.astype(BF16)
        gh_ref[...] = gh
        dot = dot_nt(wo_ref[...], gh).astype(BF16)
        every = [(m, i) for m in range(mols) for i in range(pairs)]
        lanes = lambda m: slice(LEN * m, LEN * (m + 1))
        rows_of = lambda i: slice(PAIR * i, PAIR * (i + 1))
        dps, dss, dos = {}, {}, {}
        for m, i in every:
            low, before = pair_window(i, width)
            dos[m, i] = pair_blocks(dot[rows_of(i), lanes(m)])
            dps[m, i] = dot_nn(v_ref[lanes(m), low : low + 2 * LEN], placed(dos[m, i], before))
        for m, i in every:
            dv = dot_nt(dos[m, i], p_ref[m, i])
            dp_ref[pl.ds(2 * width + PAIR * i, PAIR), lanes(m)] = dv.astype(BF16)
        for m, i in every:
            p = p_ref[m, i].astype(F32)
            t = dps[m, i] * p
            dss[m, i] = (t - p * jnp.sum(t, axis=0, keepdims=True)).astype(BF16)
        for m, i in every:
            dq = diagonal(dot_nn(kt_ref[rows_of(i), lanes(m)], dss[m, i])) * SCALE
            dp_ref[rows_of(i), lanes(m)] = dq.astype(BF16)
            dk = dot_nt(pair_blocks(qt_ref[rows_of(i), lanes(m)]), dss[m, i]) * SCALE
            dp_ref[pl.ds(width + PAIR * i, PAIR), lanes(m)] = dk.astype(BF16)

    outs = [bf16(rows, d), bf16(3 * width, rows)] + ([f32(rows, d), f32(8, d)] if own else [])
    return chain.call(
        kernel, "attention_backward", args, outs, "v" * 12 + ("-vvvv" if own else "-vv"),
    )


def weight_grads(chain, name, shard, lefts, rights):
    d = rights[0][0].shape[1]
    args, count = [], len(lefts)
    for (u0, u1, _), (v0, v1) in zip(lefts, rights):
        args += [u0, u1, v0, v1]

    def kernel(io, *refs):
        keep_ref, send_ref = refs[-2:]
        for at, ref in ((1, send_ref), (0, keep_ref)):
            for c in range(count):
                u0, u1, v0, v1 = refs[4 * c : 4 * c + 4]
                rows = slice(lefts[c][2] + at * shard, lefts[c][2] + (at + 1) * shard)
                left = jnp.concatenate([u0[rows], u1[rows]], axis=1)
                right = jnp.concatenate([v0[...], v1[...]], axis=0)
                ref[c] = dot_nn(left, right).astype(BF16)

    return chain.call(
        kernel, name, args, [bf16(count, shard, d), bf16(count, shard, d)], "v" * len(args) + "-vv",
    )


def input_grads(chain, dps, w, xs, sums, bias):
    rows, d = xs[0].shape

    def kernel(io, dp0, dp1, w_ref, x0, x1, sums_ref, bias_ref, mine_ref, theirs_ref):
        w = w_ref[...].reshape(dp0.shape[0], d)
        theirs = dot_tn(dp1[...], w)
        theirs_ref[:rows] = theirs.astype(BF16)
        mine = dot_tn(dp0[...], w)
        mine_ref[...] = mine
        xh0, _ = normalise(x0[...].astype(F32))
        xh1, _ = normalise(x1[...].astype(F32))
        bias = bias_ref[...]
        vec = [
            jnp.sum(mine * xh0, axis=0, keepdims=True) + jnp.sum(theirs * xh1, axis=0, keepdims=True),
            jnp.sum(mine, axis=0, keepdims=True) + jnp.sum(theirs, axis=0, keepdims=True),
            sums_ref[0:2],
            jnp.concatenate([bias, jnp.zeros((1, d - bias.shape[1]), F32)], axis=1),
            jnp.zeros((11, d), F32),
        ]
        theirs_ref[rows:] = jnp.concatenate(vec, axis=0).astype(BF16)

    return chain.call(
        kernel, "input_grads", (*dps, w, *xs, sums, bias), [f32(rows, d), bf16(rows + 16, d)], "vvvvvvv-vv"
    )


def input_norm(chain, x, gain, mine, got, dh):
    rows, d = x.shape

    def kernel(io, x_ref, gain_ref, mine_ref, got_ref, dh_ref, out_ref):
        xh, r = normalise(x_ref[...].astype(F32))
        da1 = mine_ref[...] + got_ref[:rows].astype(F32)
        out_ref[...] = (dh_ref[...] + norm_back(da1, gain_ref[...][None, :], xh, r)).astype(BF16)

    return chain.call(
        kernel, "input_norm", (x, gain, mine, got, dh), [bf16(rows, d)], "vvvvv-w", limit=8
    )[0]


def add_result(chain, mine, got):
    def kernel(io, mine_ref, got_ref, out_ref):
        out_ref[...] = (mine_ref[...] + got_ref[...].astype(F32)).astype(BF16)

    return chain.call(kernel, "add_result", (mine, got), [bf16(*mine.shape)], "vv-w", limit=8)[0]


def plus(*terms):
    total = terms[0].astype(F32)
    for term in terms[1:]:
        total = total + term.astype(F32)
    return total.astype(BF16)


def vector_rows(chain, mine, got):
    rows, d = mine.shape

    def kernel(io, mine_ref, got_ref, out_ref):
        a, b = mine_ref[rows - 16 :], got_ref[rows - 16 :]
        same = lax.broadcasted_iota(jnp.int32, (16, d), 0) < 4
        out_ref[...] = plus(a, jnp.where(same, b.astype(F32), 0.0))

    return chain.call(kernel, "vector_rows", (mine, got), [bf16(16, d)], "vv-v", limit=4)[0]


def sum_half(chain, bits, mine, got):
    def kernel(io, bits_ref, mine_ref, got_ref, out_ref):
        at = 1 - bits_ref[0]
        out_ref[...] = mine_ref[at] + got_ref[at]

    return chain.call(
        kernel, "sum_half", (bits, mine, got), [bf16(*mine.shape[1:])], "svv-v", limit=8
    )[0]


def sum_quarter(chain, bits, mine, got, half, last=(), vec=()):
    rows, d = mine.shape[2:]

    def kernel(io, bits_ref, mine_ref, got_ref, half_ref, *refs):
        *refs, out_ref = refs
        first = bits_ref[0]
        at = bits_ref[1] if last else 1 - bits_ref[1]
        terms = [mine_ref[first, at], got_ref[first, at], half_ref[at]]
        out_ref[:rows] = plus(*terms, *(ref[...] for ref in refs[: len(last)]))
        if vec:
            a, b = refs[-2][...].astype(F32), refs[-1][...].astype(F32)
            shard = vec[2]
            turned = jnp.concatenate([b[:, shard : 2 * shard], b[:, :shard], b[:, 2 * shard :]], axis=1)
            same = lax.broadcasted_iota(jnp.int32, a.shape, 0) < 4
            out_ref[rows:] = plus(a, jnp.where(same, b, turned))

    args = (bits, mine, got, half, *last, *vec[:2])
    return chain.call(
        kernel, "sum_quarter", args, [bf16(rows + (16 if vec else 0), d)], "s" + "v" * (len(args) - 1) + "-v",
        limit=8,
    )[0]


def sum_two(chain, a, b):
    def kernel(io, a_ref, b_ref, out_ref):
        out_ref[...] = a_ref[...] + b_ref[...]

    return chain.call(kernel, "sum_two", (a, b), [bf16(*a.shape)], "vv-v", limit=8)[0]


def side_by_side(chain, mine, got, rows):
    extra = mine.shape[0] - rows

    def kernel(io, mine_ref, got_ref, out_ref):
        out_ref[:rows] = mine_ref[:rows]
        out_ref[rows : 2 * rows] = got_ref[:rows]
        if extra:
            out_ref[2 * rows :] = mine_ref[rows:] + got_ref[rows:]

    return chain.call(
        kernel, "side_by_side", (mine, got), [bf16(2 * rows + extra, mine.shape[1])], "vv-v", limit=8
    )[0]


def place_sums(chain, bits, mine, got, rows, outs, vec=()):
    d = mine.shape[1]

    def kernel(io, bits_ref, mine_ref, got_ref, *refs):
        out_refs, vec_refs = refs[: len(outs)], refs[len(outs) : -2]
        all_ref, sems = refs[-2:]
        for at, ref in enumerate((mine_ref, got_ref)):
            half = bits_ref[0] if at == 0 else 1 - bits_ref[0]
            for part in range(2):
                quarter = bits_ref[1] if part == 0 else 1 - bits_ref[1]
                start = pl.multiple_of((2 * half + quarter) * rows, 16)
                all_ref[pl.ds(start, rows), :] = ref[part * rows : (part + 1) * rows].astype(F32)
        pairs, start = [], 0
        for ref in out_refs:
            for piece in [ref] if len(ref.shape) == 2 else [ref.at[c] for c in range(ref.shape[0])]:
                pairs.append((all_ref.at[start : start + piece.shape[0]], piece))
                start += piece.shape[0]
        started = copies(sems, pairs)
        if vec:
            total = mine_ref[2 * rows :].astype(F32) + got_ref[2 * rows :].astype(F32)
            for at, (n, ref) in enumerate(zip(vec, vec_refs)):
                ref[...] = total[at, :n]
        finish(started)

    return chain.call(
        kernel, "place_sums", (bits, mine, got), [*outs, *(f32(n) for n in vec)],
        "svv-" + "r" * len(outs) + "v" * len(vec), limit=8,
        scratch=[pltpu.VMEM((4 * rows, d), F32), pltpu.SemaphoreType.DMA((4,))],
    )


def local(
    n_dp, n_tensor, tokens, node_counts, edge_counts, ln1_gain, ln1_bias, qkv_weight, out_weight,
    ln2_gain, ln2_bias, fc1_weight, fc1_bias, fc2_weight, out_grad,
):
    d = tokens.shape[1]
    shard = out_weight.shape[0]
    width = 2 * shard
    mols = tokens.shape[0] // LEN
    dp_at = lax.axis_index("dp")
    tensor_at = lax.axis_index("tensor")
    core = tensor_at % 2
    bit0 = dp_at % 2
    bit1 = (dp_at // 2 + dp_at // 4) % 2
    bits = jnp.stack(
        [jnp.where(core == 0, bit0, bit1), jnp.where(core == 0, bit1, bit0), bit0, tensor_at * mols,
         (tensor_at ^ 2) * mols]
    ).astype(jnp.int32)
    chain = Chain()

    def swap_core(a):
        return lax.ppermute(a, "tensor", [(t, t ^ 1) for t in range(n_tensor)])

    def swap_y(a):
        return lax.ppermute(a, "tensor", [(t, t ^ 2) for t in range(n_tensor)])

    def swap_dp(a, mask0, mask1):
        pairs = [
            (p * n_tensor + t, (p ^ (mask1 if t % 2 else mask0)) * n_tensor + t)
            for p in range(n_dp)
            for t in range(n_tensor)
        ]
        return lax.ppermute(a, ("dp", "tensor"), pairs)

    swap_first = lambda a: swap_dp(a, 1, 2)
    swap_second = lambda a: swap_dp(a, 2, 1)
    far_masks = [6 if k == 2 else 1 << k for k in range(2, n_dp.bit_length() - 1)]

    w_got = swap_core(qkv_weight)
    x_got = swap_y(tokens)
    far_y = swap_y(pick(chain, bits, out_weight, fc1_weight))
    bias = jnp.pad(fc1_bias.reshape(1, -1), ((0, 15), (0, d - shard)))
    near, others = load(
        chain, out_weight, fc1_weight, fc2_weight, bias,
        (tokens, out_grad, ln1_gain, ln1_bias, ln2_gain, ln2_bias),
    )
    near = (near, swap_core(near))
    tokens, out_grad, ln1_gain, ln1_bias, ln2_gain, ln2_bias = others

    counts = (node_counts, edge_counts)
    norm1 = (ln1_gain, ln1_bias)
    a1_0, qt_0, kt_0, v_0, p_0, ot_0, packet, w_qkv = attention(
        chain, bits, 3, *counts, tokens, *norm1, (qkv_weight, w_got), out_grad
    )
    packet_got = swap_y(packet)
    far_y = hold(chain, far_y)
    far_x = swap_dp(far_y, 1, 1)
    a1_1, qt_1, kt_1, v_1, p_1, ot_1, o_1, wo, fc1, fc2 = attention(
        chain, bits, 4, *counts, x_got, *norm1, w_qkv, near=near
    )
    o_got = swap_y(o_1)
    fars = (far_y, far_x, swap_core(far_y), swap_core(far_x))
    norm2 = (ln2_gain, ln2_bias)
    h_1, a2_1, z_1, du_1, wo_far, fc1_far = feed_far(
        chain, bits, x_got, o_1, packet_got, *norm2, fc1, fc2, wo, near, fars
    )
    dr_0 = swap_y(du_1)
    h_0, a2_0, z_0, du_0, keep_r, send_r, bias_sums = feed_own(
        chain, tokens, packet, out_grad, o_got, *norm2, fc1, fc2, (wo, wo_far), near,
        (z_1, du_1, a2_1, packet_got),
    )
    dr_1 = swap_y(du_0)
    got_r = swap_core(send_r)
    gh_0, dp_0, dh, sums = backward(
        chain, (du_0, dr_0, fc1, fc1_far, h_0, out_grad, ln2_gain, wo, p_0, qt_0, kt_0, v_0), True
    )

    class Sum:
        def __init__(self, count, keep, got):
            self.size = count * shard // 4
            self.keep, self.got = keep, got

        def first(self):
            half = lambda a: a.reshape(2, 2 * self.size, d)
            got = swap_first(sum_half(chain, bits, half(self.keep), half(self.got)))
            quarters = lambda a: a.reshape(2, 2, self.size, d)
            self.view = (quarters(self.keep), quarters(self.got), got.reshape(2, self.size, d))

        def second(self):
            self.last = swap_second(sum_quarter(chain, bits, *self.view))

        def third(self, vec=()):
            self.sum = sum_quarter(chain, bits, *self.view, (self.last,), vec)
            self.last = swap_dp(self.sum, far_masks[0], far_masks[0])

        def fourth(self):
            self.sum = sum_two(chain, self.sum, self.last)
            for mask in far_masks[1:]:
                self.sum = sum_two(chain, self.sum, swap_dp(self.sum, mask, mask))
            self.last = swap_second(self.sum)

        def fifth(self):
            self.both = side_by_side(chain, self.sum, self.last, self.size)
            self.last = swap_first(self.both)

        def place(self, outs, vec=()):
            return place_sums(chain, bits, self.both, self.last, self.size, outs, vec)

    r = Sum(2, keep_r, got_r)
    r.first()
    gh_1, dp_1 = backward(
        chain, (du_1, dr_1, fc1, fc1_far, h_1, packet_got, ln2_gain, wo, p_1, qt_1, kt_1, v_1), False
    )
    a1s = (a1_0, a1_1)
    keep_q, send_q = weight_grads(
        chain, "weight_grads", shard, [(dp_0, dp_1, c * width) for c in range(3)] + [(ot_0, ot_1, 0)],
        [a1s] * 3 + [(gh_0, gh_1)],
    )
    q = Sum(4, keep_q, swap_core(send_q))
    r.second()
    q.first()
    da1_mine, da1_theirs = input_grads(chain, (dp_0, dp_1), w_qkv, (tokens, x_got), sums, bias_sums)
    da1_got = swap_y(da1_theirs)
    r.third()
    q.second()
    r.fourth()
    vec = vector_rows(chain, da1_theirs, da1_got)
    q.third((vec, swap_core(vec), shard))
    res_mine, res_theirs = feed_result(chain, (z_0, z_1), fc2, h_0)
    res_got = swap_y(res_theirs)
    grad_tokens = input_norm(chain, tokens, ln1_gain, da1_mine, da1_got, dh)
    r.fifth()
    q.fourth()
    rows = f32(shard, d)
    grad_fc1, grad_fc2 = r.place([rows, rows])
    result = add_result(chain, res_mine, res_got)
    q.fifth()
    grad_qkv, grad_out, gain1, bias1, gain2, bias2, grad_b = q.place(
        [f32(3, shard, d), rows], (d, d, d, d, shard)
    )
    return (
        result, grad_tokens, gain1, bias1, grad_qkv, grad_out, gain2, bias2, grad_fc1, grad_b, grad_fc2,
    )


def solution(mesh):
    tokens = P(("dp", "tensor"), None)
    rows = P("tensor", None)
    qkv = P(None, "tensor", None)
    in_specs = (
        tokens, P("dp"), P("dp"), P(), P(), qkv, rows, P(), P(), rows, P("tensor"), rows, tokens,
    )
    out_specs = (tokens, tokens, P(), P(), qkv, rows, P(), P(), rows, P("tensor"), rows)
    step = functools.partial(local, mesh.shape["dp"], mesh.shape["tensor"])
    return jax.shard_map(step, mesh=mesh, in_specs=in_specs, out_specs=out_specs, check_vma=False)
```

```python
import functools

import jax
import jax.numpy as jnp
from jax import lax
from jax.experimental import pallas as pl
from jax.experimental.pallas import tpu as pltpu
from jax.sharding import PartitionSpec as P

HEAD_DIM = 24
LEN = 128
PAIR = 2 * HEAD_DIM
EPSILON = 1e-05
SCALE = HEAD_DIM ** (-0.5)
LOG2E = 1.4426950408889634
F32 = jnp.float32
BF16 = jnp.bfloat16
MIB = 1024 * 1024


def dot_nn(a, b):
    return lax.dot_general(a, b, (((1,), (0,)), ((), ())), preferred_element_type=F32)


def dot_nt(a, b):
    return lax.dot_general(a, b, (((1,), (1,)), ((), ())), preferred_element_type=F32)


def dot_tn(a, b):
    return lax.dot_general(a, b, (((0,), (0,)), ((), ())), preferred_element_type=F32)


def normalise(v):
    centered = v - jnp.mean(v, axis=-1, keepdims=True)
    r = lax.rsqrt(jnp.mean(centered * centered, axis=-1, keepdims=True) + EPSILON)
    return centered * r, r


def norm_back(da, gain, xh, r):
    e = da * gain
    return r * (
        e - jnp.mean(e, axis=-1, keepdims=True) - xh * jnp.mean(e * xh, axis=-1, keepdims=True)
    )


def pair_blocks(rows):
    rows = rows.astype(F32)
    none = jnp.zeros((HEAD_DIM, LEN), F32)
    left = jnp.concatenate([rows[:HEAD_DIM], none], axis=0)
    right = jnp.concatenate([none, rows[HEAD_DIM:]], axis=0)
    return jnp.concatenate([left, right], axis=1).astype(BF16)


def pair_window(i, width):
    low = min(PAIR * i // LEN * LEN, width - 2 * LEN)
    return low, PAIR * i - low


def placed(block, before):
    parts = []
    if before:
        parts.append(jnp.zeros((before, 2 * LEN), BF16))
    parts.append(block)
    after = 2 * LEN - PAIR - before
    if after:
        parts.append(jnp.zeros((after, 2 * LEN), BF16))
    return jnp.concatenate(parts, axis=0)


def diagonal(both):
    return jnp.concatenate([both[:HEAD_DIM, :LEN], both[HEAD_DIM:, LEN:]], axis=0)


COSTS = (100, 100, 100, 100, 100, 100, 100, 100, 100, 0, 0, 0, 0, 150, 0, 60, 0, 0, 30, 0, 0, 0, 0, 0, 0, 0, 0, 0, 0, 0, 0)


class IO:
    def __init__(self, reads, writes):
        self.reads, self.writes = reads, writes
        self.started = set()

    def wait(self, *args):
        for j in args:
            if j in self.reads:
                self.reads[j].wait()

    def flush(self, *outs):
        for j in outs:
            if j in self.writes:
                self.started.add(j)
                self.writes[j].start()

    def finish(self):
        self.flush(*(j for j in self.writes if j not in self.started))
        for copy in self.writes.values():
            copy.wait()


def pinned(a):
    return pltpu.with_memory_space_constraint(a, pltpu.HBM)


class Chain:
    def __init__(self):
        self.token, self.calls = None, 0

    def call(self, kernel, name, args, outs, kinds, scratch=(), limit=16, aliases={}):
        ins, out_kinds = kinds.split("-")
        cost = COSTS[min(self.calls, len(COSTS) - 1)]
        self.calls += 1
        assert len(ins) == len(args) and len(out_kinds) == len(outs)
        hbm = pl.BlockSpec(memory_space=pltpu.HBM)
        vmem = pl.BlockSpec(memory_space=pltpu.VMEM)
        smem = pl.BlockSpec(memory_space=pltpu.SMEM)
        spec = lambda kind: {"s": smem, "v": vmem}.get(kind, hbm)
        tokens = () if self.token is None else (self.token,)
        staged = [j for j, kind in enumerate(ins) if kind in "hcl"]
        written = [j for j, kind in enumerate(out_kinds) if kind == "w"]
        memory = lambda kind: pltpu.SMEM if kind == "c" else pltpu.VMEM
        buffers = [memory(ins[j])(args[j].shape, args[j].dtype) for j in staged]
        buffers += [pltpu.VMEM(outs[j].shape, outs[j].dtype) for j in written]
        n_in, n_out, n_buf = len(args) + len(tokens), len(outs), len(buffers)

        def body(*refs):
            arg_refs = list(refs[: len(args)])
            out_refs = list(refs[n_in : n_in + n_out])
            token_ref = refs[n_in + n_out]
            own = refs[n_in + n_out + 1 :]
            bufs, sems, extra = own[:n_buf], own[n_buf], own[n_buf + 1 :]
            reads, writes = {}, {}
            for at, j in enumerate(staged):
                reads[j] = pltpu.make_async_copy(arg_refs[j], bufs[at], sems.at[at])
                reads[j].start()
                arg_refs[j] = bufs[at]
            for at, j in enumerate(written, len(staged)):
                writes[j] = pltpu.make_async_copy(bufs[at], out_refs[j], sems.at[at])
                out_refs[j] = bufs[at]
            io = IO(reads, writes)
            io.wait(*(j for j in staged if ins[j] == "h"))
            token_ref[...] = jnp.zeros_like(token_ref)
            kernel(io, *arg_refs, *out_refs, *extra)
            io.finish()

        *results, self.token = pl.pallas_call(
            body,
            in_specs=[spec(kind) for kind in ins] + [vmem] * len(tokens),
            out_specs=[spec(kind) for kind in out_kinds] + [vmem],
            out_shape=[*outs, f32(8, 128)],
            input_output_aliases=aliases,
            scratch_shapes=[*buffers, pltpu.SemaphoreType.DMA((max(n_buf, 1),)), *scratch],
            compiler_params=pltpu.CompilerParams(vmem_limit_bytes=limit * MIB),
            cost_estimate=pl.CostEstimate(flops=cost * 10**8, bytes_accessed=10**8, transcendentals=0),
            name=name,
        )(*(pinned(a) if kind in "hclp" else a for a, kind in zip(args, ins)), *tokens)
        return results


def bf16(*shape):
    return jax.ShapeDtypeStruct(shape, BF16)


def f32(*shape):
    return jax.ShapeDtypeStruct(shape, F32)


def copies(sems, pairs):
    started = [pltpu.make_async_copy(a, b, sems.at[j]) for j, (a, b) in enumerate(pairs)]
    for copy in started:
        copy.start()
    return started


def finish(started):
    for copy in started:
        copy.wait()


def attention(chain, bits, place, nodes, edges, x, gain, bias, w, g=None, near=()):
    rows, d = x.shape
    width = w.shape[1] if g is None else 2 * w[0].shape[1]
    shard = width // 2
    pairs = width // PAIR
    mols = rows // LEN

    def kernel(io, bits_ref, nodes_ref, edges_ref, x_ref, gain_ref, bias_ref, *refs):
        started = []
        if g is None:
            w_ref, near0, near1, *refs, wo_ref, fc1_ref, fc2_ref, sems = refs
            a1_ref, qt_ref, kt_ref, v_ref, p_ref, ot_ref, o_ref = refs
            pairs_w = []
            for at, ref in enumerate((near0, near1)):
                for c, out in enumerate((wo_ref, fc1_ref, fc2_ref)):
                    part = ref.at[c * shard : (c + 1) * shard]
                    pairs_w.append((part, out.at[at * shard : (at + 1) * shard]))
            started = copies(sems, pairs_w)
        else:
            own, got, g_ref, *refs, w_ref, sems = refs
            a1_ref, qt_ref, kt_ref, v_ref, p_ref, ot_ref, o_ref = refs
            pairs_w = [(own, w_ref.at[:, :shard]), (got, w_ref.at[:, shard:]), (g_ref, o_ref.at[:, :d])]
            started = copies(sems, pairs_w)
        xh, _ = normalise(x_ref[...].astype(F32))
        a1 = (xh * gain_ref[...][None, :] + bias_ref[...][None, :]).astype(BF16)
        a1_ref[...] = a1
        if g is not None:
            finish(started[:2])
        qt = dot_nt(w_ref[0], a1).astype(BF16)
        keys = dot_nt(a1, w_ref[1]).astype(BF16)
        vt = dot_nt(w_ref[2], a1).astype(BF16)
        qt_ref[...] = qt
        every = [(m, i) for m in range(mols) for i in range(pairs)]
        lanes = lambda m: slice(LEN * m, LEN * (m + 1))
        rows_of = lambda i: slice(PAIR * i, PAIR * (i + 1))
        scores, probs = {}, {}
        for m, i in every:
            low, before = pair_window(i, width)
            rhs = placed(pair_blocks(qt[rows_of(i), lanes(m)]), before)
            scores[m, i] = dot_nn(keys[lanes(m), low : low + 2 * LEN], rhs)
        io.wait(1, 2)
        for m in range(mols):
            mol = bits_ref[place] + m
            count = 1 + nodes_ref[mol] + edges_ref[mol]
            valid = lax.broadcasted_iota(jnp.int32, (LEN, 2 * LEN), 0) < count
            for i in range(pairs):
                s = jnp.where(valid, scores[m, i], -1e30)
                e = jnp.exp2((s - jnp.max(s, axis=0, keepdims=True)) * (SCALE * LOG2E))
                p = (e * (1.0 / jnp.sum(e, axis=0, keepdims=True))).astype(BF16)
                p_ref[m, i] = p
                probs[m, i] = p
        for m, i in every:
            both = dot_nn(vt[rows_of(i), lanes(m)], probs[m, i])
            ot_ref[rows_of(i), lanes(m)] = diagonal(both).astype(BF16)
        o_ref[:, o_ref.shape[1] - width :] = ot_ref[...].T
        kt_ref[...] = dot_nt(w_ref[1], a1).astype(BF16)
        v_ref[...] = dot_nt(a1, w_ref[2]).astype(BF16)
        finish(started if g is None else started[2:])

    outs = [
        bf16(rows, d), bf16(width, rows), bf16(width, rows), bf16(rows, width),
        bf16(mols, pairs, LEN, 2 * LEN), bf16(width, rows),
    ]
    args = (bits, nodes, edges, x, gain, bias)
    if g is None:
        return chain.call(
            kernel, "attention_forward", (*args, w, *near), [*outs, bf16(rows, width)] + [bf16(width, d)] * 3,
            "sccvvvvvv-vvvvvvvvvv", scratch=[pltpu.SemaphoreType.DMA((6,))],
        )
    return chain.call(
        kernel, "attention_forward", (*args, *w, g), [*outs, bf16(rows, d + width), bf16(3, width, d)],
        "sccvvvprv-vvvvvvvv", scratch=[pltpu.SemaphoreType.DMA((3,))],
    )


def pick(chain, bits, a, b):
    def kernel(io, bits_ref, a_ref, b_ref, out_ref, sems):
        pl.when(bits_ref[2] == 0)(lambda: finish(copies(sems, [(a_ref, out_ref)])))
        pl.when(bits_ref[2] != 0)(lambda: finish(copies(sems, [(b_ref, out_ref)])))

    return chain.call(
        kernel, "pick", (bits, a, b), [bf16(*a.shape)], "spp-v", limit=4,
        scratch=[pltpu.SemaphoreType.DMA((1,))],
    )[0]


def hold(chain, a):
    def kernel(io, a_ref, out_ref, sems):
        finish(copies(sems, [(a_ref, out_ref)]))

    return chain.call(
        kernel, "hold", (a,), [bf16(*a.shape)], "v-v", limit=4, scratch=[pltpu.SemaphoreType.DMA((1,))]
    )[0]


def load(chain, out_weight, fc1_weight, fc2_weight, bias, others):
    shard, d = out_weight.shape
    n = len(others)

    def kernel(io, wo, fc1, fc2, bias_ref, *refs):
        others_in, (near_ref, *others_out, sems) = refs[:n], refs[n:]
        rows = lambda at: near_ref.at[at * shard : (at + 1) * shard]
        near = [(wo, rows(0)), (fc1, rows(1)), (fc2, rows(2)), (bias_ref, near_ref.at[3 * shard :])]
        finish(copies(sems, near + list(zip(others_in, others_out))))

    near, *others = chain.call(
        kernel, "load", (out_weight, fc1_weight, fc2_weight, bias, *others),
        [bf16(3 * shard + 16, d)] + [jax.ShapeDtypeStruct(a.shape, a.dtype) for a in others],
        "pppr" + "p" * n + "-v" + "v" * n, limit=4, scratch=[pltpu.SemaphoreType.DMA((4 + n,))],
    )
    return near, others


def feed_body(x, oa, ob, g, wo_ref, gain_ref, bias_ref, fc1_ref, b1, fc2_ref, h_ref, a2_ref, z_ref, du_ref):
    h = x.astype(F32) + dot_nn(jnp.concatenate([oa, ob], axis=1), wo_ref[...])
    h_ref[...] = h
    xh, _ = normalise(h)
    a2 = (xh * gain_ref[...][None, :] + bias_ref[...][None, :]).astype(BF16)
    a2_ref[...] = a2
    shard = fc2_ref.shape[0] // 2
    b1 = jnp.concatenate([b[3 * shard : 3 * shard + 1, :shard] for b in b1], axis=1).astype(F32)
    u = dot_nt(a2, fc1_ref[: 2 * shard]) + b1
    dz = dot_nt(g, fc2_ref[...])
    phi = 0.5 * (1.0 + lax.erf(u * (0.5**0.5)))
    slope = phi + u * (jnp.exp(-0.5 * u * u) * 0.3989422804014327)
    du = (dz * slope).astype(BF16)
    z = (u * phi).astype(BF16)
    du_ref[...] = du
    z_ref[...] = z
    return a2, z, du


def pack_far(chain, bits, wo, fc1, fars):
    shard, d = fars[0].shape
    width = 2 * shard

    def kernel(io, bits_ref, wo_near, fc1_near, y0, x0, y1, x1, wo_ref, fc1_ref, sems):
        near = copies(sems.at[4:], [(wo_near, wo_ref.at[:width]), (fc1_near, fc1_ref.at[:width])])

        def both(first, second):
            pairs = []
            for at in range(2):
                here = slice(width + at * shard, width + (at + 1) * shard)
                pairs += [(first[at], wo_ref.at[here]), (second[at], fc1_ref.at[here])]
            finish(copies(sems, pairs))

        pl.when(bits_ref[2] == 0)(lambda: both((y0, y1), (x0, x1)))
        pl.when(bits_ref[2] != 0)(lambda: both((x0, x1), (y0, y1)))
        finish(near)

    return chain.call(
        kernel, "pack_far", (bits, wo, fc1, *fars), [bf16(2 * width, d), bf16(2 * width, d)], "svvvvvv-vv", limit=4,
        scratch=[pltpu.SemaphoreType.DMA((6,))],
    )


def feed_far(chain, x, oa, packet, gain, bias, fc1, fc2, wo, near):
    rows, d = x.shape
    width = fc2.shape[0]

    def kernel(io, x_ref, oa_ref, packet_ref, gain_ref, bias_ref, fc1_ref, fc2_ref, wo_ref, b10, b11, *outs):
        feed_body(
            x_ref[...], oa_ref[...], packet_ref[:, d:], packet_ref[:, :d], wo_ref, gain_ref, bias_ref, fc1_ref,
            (b10, b11), fc2_ref, *outs,
        )

    return chain.call(
        kernel, "feed_far", (x, oa, packet, gain, bias, fc1, fc2, wo, *near),
        [f32(rows, d), bf16(rows, d), bf16(rows, width), bf16(rows, width)], "v" * 10 + "-vvvv",
    )


def feed_own(chain, x, packet, g, ob, gain, bias, fc1, fc2, wo, near, far):
    rows, d = x.shape
    width = fc2.shape[0]
    shard = width // 2

    def kernel(io, x_ref, oa_ref, g_ref, ob_ref, gain_ref, bias_ref, fc1_ref, fc2_ref, wo_ref, b10, b11,
               z1, du1, a1, g1, h_ref, a2_ref, z_ref, du_ref, keep_ref, send_ref, sums_ref):
        a2, z, du = feed_body(
            x_ref[...], oa_ref[:, d:], ob_ref[...], g_ref[...], wo_ref, gain_ref, bias_ref, fc1_ref, (b10, b11),
            fc2_ref, h_ref, a2_ref, z_ref, du_ref,
        )
        first = dot_tn(du, a2) + dot_tn(du1[...], a1[...])
        second = dot_tn(z, g_ref[...]) + dot_tn(z1[...], g1[:, :d])
        for at, ref in enumerate((keep_ref, send_ref)):
            here = slice(at * shard, (at + 1) * shard)
            ref[0] = first[here].astype(BF16)
            ref[1] = second[here].astype(BF16)
        sums_ref[...] = jnp.sum(du.astype(F32), axis=0, keepdims=True) + jnp.sum(
            du1[...].astype(F32), axis=0, keepdims=True
        )

    return chain.call(
        kernel, "feed_own", (x, packet, g, ob, gain, bias, fc1, fc2, wo, *near, *far),
        [f32(rows, d), bf16(rows, d), bf16(rows, width), bf16(rows, width), bf16(2, shard, d), bf16(2, shard, d),
         f32(1, width)], "v" * 15 + "-vvvvvvv",
    )


def feed_result(chain, zs, fc2, h):
    rows, d = h.shape

    def kernel(io, z0, z1, fc2_ref, h_ref, mine_ref, theirs_ref):
        theirs_ref[...] = dot_nn(z1[...], fc2_ref[...]).astype(BF16)
        mine_ref[...] = h_ref[...] + dot_nn(z0[...], fc2_ref[...])

    return chain.call(
        kernel, "feed_result", (*zs, fc2, h), [f32(rows, d), bf16(rows, d)], "vvvv-vv", limit=8,
    )


def backward(chain, args, own):
    h, kt = args[3], args[9]
    rows, d = h.shape
    width = kt.shape[0]
    mols, pairs = rows // LEN, width // PAIR

    def kernel(io, du_ref, dr_ref, fc1_ref, h_ref, g_ref, gain_ref, wo_ref, p_ref, qt_ref, kt_ref, v_ref,
               gh_ref, dp_ref, dh_ref=None, sums_ref=None):
        da2 = dot_nn(jnp.concatenate([du_ref[...], dr_ref[...]], axis=1), fc1_ref[...])
        xh, r = normalise(h_ref[...])
        dh = g_ref[:, :d].astype(F32) + norm_back(da2, gain_ref[...][None, :], xh, r)
        if own:
            dh_ref[...] = dh
            sums_ref[0:1] = jnp.sum(da2 * xh, axis=0, keepdims=True)
            sums_ref[1:2] = jnp.sum(da2, axis=0, keepdims=True)
            io.flush(2)
        gh = dh.astype(BF16)
        gh_ref[...] = gh
        dot = dot_nt(wo_ref[:width], gh).astype(BF16)
        every = [(m, i) for m in range(mols) for i in range(pairs)]
        lanes = lambda m: slice(LEN * m, LEN * (m + 1))
        rows_of = lambda i: slice(PAIR * i, PAIR * (i + 1))
        dps, dss, dos = {}, {}, {}
        for m, i in every:
            low, before = pair_window(i, width)
            dos[m, i] = pair_blocks(dot[rows_of(i), lanes(m)])
            dps[m, i] = dot_nn(v_ref[lanes(m), low : low + 2 * LEN], placed(dos[m, i], before))
        for m, i in every:
            dv = dot_nt(dos[m, i], p_ref[m, i])
            dp_ref[pl.ds(2 * width + PAIR * i, PAIR), lanes(m)] = dv.astype(BF16)
        for m, i in every:
            p = p_ref[m, i].astype(F32)
            t = dps[m, i] * p
            dss[m, i] = (t - p * jnp.sum(t, axis=0, keepdims=True)).astype(BF16)
        for m, i in every:
            dq = diagonal(dot_nn(kt_ref[rows_of(i), lanes(m)], dss[m, i])) * SCALE
            dp_ref[rows_of(i), lanes(m)] = dq.astype(BF16)
            dk = dot_nt(pair_blocks(qt_ref[rows_of(i), lanes(m)]), dss[m, i]) * SCALE
            dp_ref[pl.ds(width + PAIR * i, PAIR), lanes(m)] = dk.astype(BF16)

    outs = [bf16(rows, d), bf16(3 * width, rows)] + ([f32(rows, d), f32(8, d)] if own else [])
    return chain.call(
        kernel, "attention_backward", args, outs, "v" * 11 + ("-vvvv" if own else "-vv"),
    )


def weight_grads(chain, name, shard, at, lefts, rights):
    d = rights[0][0].shape[1]
    args, count = [], len(lefts)
    for (u0, u1, _), (v0, v1) in zip(lefts, rights):
        args += [u0, u1, v0, v1]

    def kernel(io, *refs):
        out_ref = refs[-1]
        for c in range(count):
            u0, u1, v0, v1 = refs[4 * c : 4 * c + 4]
            rows = slice(lefts[c][2] + at * shard, lefts[c][2] + (at + 1) * shard)
            left = jnp.concatenate([u0[rows], u1[rows]], axis=1)
            right = jnp.concatenate([v0[...], v1[...]], axis=0)
            out_ref[c] = dot_nn(left, right).astype(BF16)

    return chain.call(kernel, name, args, [bf16(count, shard, d)], "v" * len(args) + "-v")[0]


def input_grads(chain, dps, w, xs, sums, bias):
    rows, d = xs[0].shape

    def kernel(io, dp0, dp1, w_ref, x0, x1, sums_ref, bias_ref, mine_ref, theirs_ref):
        w = w_ref[...].reshape(dp0.shape[0], d)
        theirs = dot_tn(dp1[...], w)
        theirs_ref[:rows] = theirs.astype(BF16)
        mine = dot_tn(dp0[...], w)
        mine_ref[...] = mine
        xh0, _ = normalise(x0[...].astype(F32))
        xh1, _ = normalise(x1[...].astype(F32))
        bias = bias_ref[...]
        vec = [
            jnp.sum(mine * xh0, axis=0, keepdims=True) + jnp.sum(theirs * xh1, axis=0, keepdims=True),
            jnp.sum(mine, axis=0, keepdims=True) + jnp.sum(theirs, axis=0, keepdims=True),
            sums_ref[0:2],
            jnp.concatenate([bias, jnp.zeros((1, d - bias.shape[1]), F32)], axis=1),
            jnp.zeros((11, d), F32),
        ]
        theirs_ref[rows:] = jnp.concatenate(vec, axis=0).astype(BF16)

    return chain.call(
        kernel, "input_grads", (*dps, w, *xs, sums, bias), [f32(rows, d), bf16(rows + 16, d)], "vvvvvvv-vv"
    )


def input_norm(chain, x, gain, mine, got, dh):
    rows, d = x.shape

    def kernel(io, x_ref, gain_ref, mine_ref, got_ref, dh_ref, out_ref):
        xh, r = normalise(x_ref[...].astype(F32))
        da1 = mine_ref[...] + got_ref[:rows].astype(F32)
        out_ref[...] = (dh_ref[...] + norm_back(da1, gain_ref[...][None, :], xh, r)).astype(BF16)

    return chain.call(
        kernel, "input_norm", (x, gain, mine, got, dh), [bf16(rows, d)], "vvvvv-w", limit=8
    )[0]


def add_result(chain, mine, got):
    def kernel(io, mine_ref, got_ref, out_ref):
        out_ref[...] = (mine_ref[...] + got_ref[...].astype(F32)).astype(BF16)

    return chain.call(kernel, "add_result", (mine, got), [bf16(*mine.shape)], "vv-w", limit=8)[0]


def plus(*terms):
    total = terms[0].astype(F32)
    for term in terms[1:]:
        total = total + term.astype(F32)
    return total.astype(BF16)


def vector_rows(chain, mine, got):
    rows, d = mine.shape

    def kernel(io, mine_ref, got_ref, out_ref):
        a, b = mine_ref[rows - 16 :], got_ref[rows - 16 :]
        same = lax.broadcasted_iota(jnp.int32, (16, d), 0) < 4
        out_ref[...] = plus(a, jnp.where(same, b.astype(F32), 0.0))

    return chain.call(kernel, "vector_rows", (mine, got), [bf16(16, d)], "vv-v", limit=4)[0]


def vector_cores(chain, mine, got, shard):
    def kernel(io, mine_ref, got_ref, out_ref):
        a, b = mine_ref[...].astype(F32), got_ref[...].astype(F32)
        turned = jnp.concatenate([b[:, shard : 2 * shard], b[:, :shard], b[:, 2 * shard :]], axis=1)
        same = lax.broadcasted_iota(jnp.int32, a.shape, 0) < 4
        out_ref[...] = plus(a, jnp.where(same, b, turned))

    return chain.call(kernel, "vector_cores", (mine, got), [bf16(*mine.shape)], "vv-v", limit=4)[0]


def sum_half(chain, bits, mine, got, apart):
    def kernel(io, bits_ref, mine_ref, got_ref, *outs):
        half, quarter = 1 - bits_ref[0], bits_ref[1]
        on_ref, kept_ref = outs if apart else (outs[0].at[0], outs[0].at[1])
        on_ref[...] = mine_ref[half, 1 - quarter] + got_ref[half, 1 - quarter]
        kept_ref[...] = mine_ref[half, quarter] + got_ref[half, quarter]

    rows, d = mine.shape[2:]
    outs = [bf16(rows, d)] * 2 if apart else [bf16(2, rows, d)]
    return chain.call(kernel, "sum_half", (bits, mine, got), outs, "svv-" + "v" * len(outs), limit=8)


def sum_quarter(chain, bits, mine, got, kept, *more, vec=()):
    rows, d = mine.shape[2:]
    arrays = [a[0] if isinstance(a, tuple) else a for a in more]

    def kernel(io, bits_ref, mine_ref, got_ref, *refs):
        *refs, out_ref = refs
        half = bits_ref[0]
        quarter = bits_ref[1] if kept else 1 - bits_ref[1]
        terms = [ref[a[1]] if isinstance(a, tuple) else ref[...] for a, ref in zip(more, refs)]
        out_ref[:rows] = plus(mine_ref[half, quarter], got_ref[half, quarter], *terms)
        if vec:
            out_ref[rows:] = refs[-1][...]

    args = (bits, mine, got, *arrays, *vec)
    return chain.call(
        kernel, "sum_quarter", args, [bf16(rows + (16 if vec else 0), d)], "s" + "v" * (len(args) - 1) + "-v",
        limit=8,
    )[0]


def sum_quarter_apart(chain, bits, mine, got, *more):
    rows, d = mine.shape[2:]
    arrays = [a[0] if isinstance(a, tuple) else a for a in more]

    def kernel(io, bits_ref, mine_ref, got_ref, *refs):
        *refs, upper_ref, lower_ref = refs
        half, quarter = bits_ref[0], bits_ref[1]
        terms = [ref[a[1]] if isinstance(a, tuple) else ref[...] for a, ref in zip(more, refs)]
        total = plus(mine_ref[half, quarter], got_ref[half, quarter], *terms)
        upper_ref[...] = total[: rows // 2]
        lower_ref[...] = total[rows // 2 :]

    args = (bits, mine, got, *arrays)
    return chain.call(
        kernel, "sum_quarter", args, [bf16(rows // 2, d)] * 2, "s" + "v" * (len(args) - 1) + "-vv", limit=8
    )


def side_by_side(chain, a, b, apart):
    rows, d = a.shape

    def kernel(io, a_ref, b_ref, *outs):
        first, second = outs if apart else (outs[0].at[:rows], outs[0].at[rows:])
        first[...] = a_ref[...]
        second[...] = b_ref[...]

    outs = [bf16(rows, d)] * 2 if apart else [bf16(2 * rows, d)]
    return chain.call(kernel, "side_by_side", (a, b), outs, "vv-" + "v" * len(outs), limit=8)


def sum_pairs(chain, *pairs):
    rows = [a.shape[0] for a, _ in pairs]

    def kernel(io, *refs):
        *refs, out_ref = refs
        start = 0
        for a_ref, b_ref in zip(refs[::2], refs[1::2]):
            out_ref[start : start + a_ref.shape[0]] = a_ref[...] + b_ref[...]
            start += a_ref.shape[0]

    args = [a for pair in pairs for a in pair]
    return chain.call(
        kernel, "sum_pairs", args, [bf16(sum(rows), args[0].shape[1])], "v" * len(args) + "-v", limit=8
    )[0]


def place_sums(chain, bits, quarters, rows, targets, outs, whole=(), vec=(), skip=0):
    d = quarters[0][0].shape[1]
    n = len(outs)
    arrays = []
    for a, *_ in quarters:
        if not any(a is b for b in arrays):
            arrays.append(a)
    which = [next(k for k, b in enumerate(arrays) if b is a) for a, *_ in quarters]

    def kernel(io, bits_ref, *refs):
        refs, (buf, sems) = refs[:-2], refs[-2:]
        ins = [refs[k] for k in which]
        refs = refs[len(arrays) + len(whole) :]
        out_refs, vec_refs = refs[:n], refs[n:]

        def each(step):
            for j, (_, _, half, quarter) in enumerate(quarters):
                if j < skip:
                    continue
                half = 1 - bits_ref[0] if half else bits_ref[0]
                quarter = 1 - bits_ref[1] if quarter else bits_ref[1]
                for at, (out, index, first) in enumerate(targets):
                    ref = out_refs[out]
                    ref = ref if index is None else ref.at[index]
                    ref = ref.at[first : first + rows]
                    copy = pltpu.make_async_copy(buf.at[j], ref, sems.at[j])
                    pl.when(2 * half + quarter == at)(functools.partial(step, copy))

        starts = [start for _, start, _, _ in quarters]
        for j, ref in enumerate(ins):
            if j >= skip:
                buf[j] = ref[starts[j] : starts[j] + rows].astype(F32)
        each(lambda copy: copy.start())
        if vec:
            a, b, c, e = (ref[x + rows : x + rows + 16].astype(F32) for ref, x in zip(ins, starts))
            total = jnp.where(bits_ref[5] == 0, (a + b) + (c + e), (a + c) + (b + e))
            for at, (length, ref) in enumerate(zip(vec, vec_refs)):
                ref[...] = total[at, :length]
        each(lambda copy: copy.wait())

    return chain.call(
        kernel, "place_sums", (bits, *arrays, *whole), [*outs, *(f32(length) for length in vec)],
        "s" + "v" * len(arrays) + "p" * len(whole) + "-" + "r" * n + "v" * len(vec), limit=8,
        aliases={1 + len(arrays) + j: j for j in range(len(whole))},
        scratch=[pltpu.VMEM((len(quarters), rows, d), F32), pltpu.SemaphoreType.DMA((len(quarters),))],
    )


def local(
    n_dp, n_tensor, tokens, node_counts, edge_counts, ln1_gain, ln1_bias, qkv_weight, out_weight,
    ln2_gain, ln2_bias, fc1_weight, fc1_bias, fc2_weight, out_grad,
):
    d = tokens.shape[1]
    shard = out_weight.shape[0]
    width = 2 * shard
    mols = tokens.shape[0] // LEN
    dp_at = lax.axis_index("dp")
    tensor_at = lax.axis_index("tensor")
    core = tensor_at % 2
    bit0 = dp_at % 2
    bit1 = (dp_at // 2) % 2
    bits = jnp.stack(
        [jnp.where(core == 0, bit0, bit1), jnp.where(core == 0, bit1, bit0), bit0, tensor_at * mols,
         (tensor_at ^ 2) * mols, core]
    ).astype(jnp.int32)
    chain = Chain()

    def swap_core(a):
        return lax.ppermute(a, "tensor", [(t, t ^ 1) for t in range(n_tensor)])

    def swap_y(a):
        return lax.ppermute(a, "tensor", [(t, t ^ 2) for t in range(n_tensor)])

    def swap_dp(a, mask0, mask1):
        pairs = [
            (p * n_tensor + t, (p ^ (mask1 if t % 2 else mask0)) * n_tensor + t)
            for p in range(n_dp)
            for t in range(n_tensor)
        ]
        return lax.ppermute(a, ("dp", "tensor"), pairs)

    swap_first = lambda a: swap_dp(a, 1, 2)
    swap_second = lambda a: swap_dp(a, 2, 1)
    far_masks = [1 << k for k in range(2, n_dp.bit_length() - 1)]

    w_got = swap_core(qkv_weight)
    x_got = swap_y(tokens)
    far_y = swap_y(pick(chain, bits, out_weight, fc1_weight))
    bias = jnp.pad(fc1_bias.reshape(1, -1), ((0, 15), (0, d - shard)))
    near, others = load(
        chain, out_weight, fc1_weight, fc2_weight, bias,
        (tokens, out_grad, ln1_gain, ln1_bias, ln2_gain, ln2_bias),
    )
    near = (near, swap_core(near))
    tokens, out_grad, ln1_gain, ln1_bias, ln2_gain, ln2_bias = others

    counts = (node_counts, edge_counts)
    norm1 = (ln1_gain, ln1_bias)
    a1_0, qt_0, kt_0, v_0, p_0, ot_0, packet, w_qkv = attention(
        chain, bits, 3, *counts, tokens, *norm1, (qkv_weight, w_got), out_grad
    )
    packet_got = swap_y(packet)
    far_y = hold(chain, far_y)
    far_x = swap_dp(far_y, 1, 1)
    a1_1, qt_1, kt_1, v_1, p_1, ot_1, o_1, wo, fc1, fc2 = attention(
        chain, bits, 4, *counts, x_got, *norm1, w_qkv, near=near
    )
    o_got = swap_y(o_1)
    fars = (far_y, far_x, swap_core(far_y), swap_core(far_x))
    norm2 = (ln2_gain, ln2_bias)
    wo, fc1 = pack_far(chain, bits, wo, fc1, fars)
    h_1, a2_1, z_1, du_1 = feed_far(chain, x_got, o_1, packet_got, *norm2, fc1, fc2, wo, near)
    dr_0 = swap_y(du_1)
    h_0, a2_0, z_0, du_0, keep_r, send_r, bias_sums = feed_own(
        chain, tokens, packet, out_grad, o_got, *norm2, fc1, fc2, wo, near, (z_1, du_1, a2_1, packet_got)
    )
    dr_1 = swap_y(du_0)

    class Sum:
        def __init__(self, count, keep, got, apart, early):
            self.size = count * shard // 4
            self.apart, self.early = apart, early
            view = lambda a: a.reshape(2, 2, self.size, d)
            self.parts = (view(keep), view(got))

        def first(self):
            sent = sum_half(chain, bits, *self.parts, self.apart)
            got = [swap_first(a) for a in sent]
            self.on, self.kept = got if self.apart else ((got[0], 0), (got[0], 1))

        def second(self):
            self.got = swap_second(sum_quarter(chain, bits, *self.parts, False, self.on))

        def third(self, *vec):
            self.sum = sum_quarter(chain, bits, *self.parts, True, self.kept, self.got, vec=vec)
            self.got = swap_dp(self.sum, far_masks[0], far_masks[0])

        def third_apart(self):
            self.sums = sum_quarter_apart(chain, bits, *self.parts, self.kept, self.got)
            self.gots = [swap_dp(a, far_masks[0], far_masks[0]) for a in self.sums]
            self.halves = [None, None]

        def fourth_apart(self, at, *vec):
            self.sum, self.got = self.sums[at], self.gots[at]
            self.fourth(*vec)
            self.halves[at] = self.quarters

        def fourth(self, *vec):
            a = sum_pairs(chain, (self.sum, self.got), *vec)
            for mask in far_masks[1:]:
                a = sum_pairs(chain, (a, swap_dp(a, mask, mask)))
            b = swap_second(a)
            if self.early == 1:
                self.quarters = [(a, 0, 0, 0), (b, 0, 0, 1), (swap_first(a), 0, 1, 0), (swap_first(b), 0, 1, 1)]
            self.last = (a, b)

        def fifth(self):
            if self.early == 0:
                (a,) = side_by_side(chain, *self.last, False)
                b = swap_first(a)
                rows = a.shape[0] // 2
                self.quarters = [(a, 0, 0, 0), (a, rows, 0, 1), (b, 0, 1, 0), (b, rows, 1, 1)]
            if self.early == 2:
                a, b = side_by_side(chain, *self.last, True)
                self.quarters = [(a, 0, 0, 0), (b, 0, 0, 1), (swap_first(a), 0, 1, 0), (swap_first(b), 0, 1, 1)]

    gh_0, dp_0, dh, sums = backward(
        chain, (du_0, dr_0, fc1, h_0, out_grad, ln2_gain, wo, p_0, qt_0, kt_0, v_0), True
    )
    r = Sum(2, keep_r, swap_core(send_r), True, 1)
    r.first()
    gh_1, dp_1 = backward(
        chain, (du_1, dr_1, fc1, h_1, packet_got, ln2_gain, wo, p_1, qt_1, kt_1, v_1), False
    )
    a1s = (a1_0, a1_1)
    lefts = [(dp_0, dp_1, c * width) for c in range(3)] + [(ot_0, ot_1, 0)]
    rights = [a1s] * 3 + [(gh_0, gh_1)]
    got_q = swap_core(weight_grads(chain, "weight_grads", shard, 1, lefts, rights))
    q = Sum(4, weight_grads(chain, "weight_grads", shard, 0, lefts, rights), got_q, True, 2)
    r.second()
    q.first()
    r.third()
    da1_mine, da1_theirs = input_grads(chain, (dp_0, dp_1), w_qkv, (tokens, x_got), sums, bias_sums)
    da1_got = swap_y(da1_theirs)
    q.second()
    r.fourth()
    res_mine, res_theirs = feed_result(chain, (z_0, z_1), fc2, h_0)
    res_got = swap_y(res_theirs)
    q.third()
    vec = vector_rows(chain, da1_theirs, da1_got)
    vec_got = swap_core(vec)
    r.fifth()
    halves = [(c, None, half * shard // 2) for c in range(2) for half in range(2)]
    grad_fc1, grad_fc2 = place_sums(chain, bits, r.quarters, r.size, halves, [f32(shard, d)] * 2)
    vec = vector_cores(chain, vec, vec_got, shard)
    vec_got = swap_dp(vec, far_masks[0], far_masks[0])
    result = add_result(chain, res_mine, res_got)
    q.fourth((vec, vec_got))
    grad_tokens = input_norm(chain, tokens, ln1_gain, da1_mine, da1_got, dh)
    q.fifth()
    each = [(0, 0, 0), (0, 1, 0), (0, 2, 0), (1, None, 0)]
    outs = [f32(3, shard, d), f32(shard, d)]
    grads = place_sums(chain, bits, q.quarters[:2], q.size, each, outs)
    grads = place_sums(chain, bits, q.quarters[:3], q.size, each, outs, grads, skip=2)
    grad_qkv, grad_out, gain1, bias1, gain2, bias2, grad_b = place_sums(
        chain, bits, q.quarters, q.size, each, outs, grads, (d, d, d, d, shard), 3
    )
    return (
        result, grad_tokens, gain1, bias1, grad_qkv, grad_out, gain2, bias2, grad_fc1, grad_b, grad_fc2,
    )


def solution(mesh):
    tokens = P(("dp", "tensor"), None)
    rows = P("tensor", None)
    qkv = P(None, "tensor", None)
    in_specs = (
        tokens, P("dp"), P("dp"), P(), P(), qkv, rows, P(), P(), rows, P("tensor"), rows, tokens,
    )
    out_specs = (tokens, tokens, P(), P(), qkv, rows, P(), P(), rows, P("tensor"), rows)
    step = functools.partial(local, mesh.shape["dp"], mesh.shape["tensor"])
    return jax.shard_map(step, mesh=mesh, in_specs=in_specs, out_specs=out_specs, check_vma=False)
```

```python
import functools

import jax
import jax.numpy as jnp
from jax import lax
from jax.experimental import pallas as pl
from jax.experimental.pallas import tpu as pltpu
from jax.sharding import PartitionSpec as P

HEAD_DIM = 24
LEN = 128
PAIR = 2 * HEAD_DIM
EPSILON = 1e-05
SCALE = HEAD_DIM ** (-0.5)
LOG2E = 1.4426950408889634
F32 = jnp.float32
BF16 = jnp.bfloat16
MIB = 1024 * 1024


def dot_nn(a, b):
    return lax.dot_general(a, b, (((1,), (0,)), ((), ())), preferred_element_type=F32)


def dot_nt(a, b):
    return lax.dot_general(a, b, (((1,), (1,)), ((), ())), preferred_element_type=F32)


def dot_tn(a, b):
    return lax.dot_general(a, b, (((0,), (0,)), ((), ())), preferred_element_type=F32)


def normalise(v):
    centered = v - jnp.mean(v, axis=-1, keepdims=True)
    r = lax.rsqrt(jnp.mean(centered * centered, axis=-1, keepdims=True) + EPSILON)
    return centered * r, r


def norm_back(da, gain, xh, r):
    e = da * gain
    return r * (
        e - jnp.mean(e, axis=-1, keepdims=True) - xh * jnp.mean(e * xh, axis=-1, keepdims=True)
    )


def pair_blocks(rows):
    rows = rows.astype(F32)
    none = jnp.zeros((HEAD_DIM, LEN), F32)
    left = jnp.concatenate([rows[:HEAD_DIM], none], axis=0)
    right = jnp.concatenate([none, rows[HEAD_DIM:]], axis=0)
    return jnp.concatenate([left, right], axis=1).astype(BF16)


def pair_window(i, width):
    low = min(PAIR * i // LEN * LEN, width - 2 * LEN)
    return low, PAIR * i - low


def placed(block, before):
    parts = []
    if before:
        parts.append(jnp.zeros((before, 2 * LEN), BF16))
    parts.append(block)
    after = 2 * LEN - PAIR - before
    if after:
        parts.append(jnp.zeros((after, 2 * LEN), BF16))
    return jnp.concatenate(parts, axis=0)


def diagonal(both):
    return jnp.concatenate([both[:HEAD_DIM, :LEN], both[HEAD_DIM:, LEN:]], axis=0)


COSTS = (0, 0, 100, 0, 0, 0, 0, 0, 0, 100, 0, 0, 0, 0, 150, 0, 60, 0, 0, 30, 0, 0, 0, 0, 0, 0, 0, 0, 0, 0, 0, 0)


class IO:
    def __init__(self, reads, writes):
        self.reads, self.writes = reads, writes
        self.started = set()

    def wait(self, *args):
        for j in args:
            if j in self.reads:
                self.reads[j].wait()

    def flush(self, *outs):
        for j in outs:
            if j in self.writes:
                self.started.add(j)
                self.writes[j].start()

    def finish(self):
        self.flush(*(j for j in self.writes if j not in self.started))
        for copy in self.writes.values():
            copy.wait()


def pinned(a):
    return pltpu.with_memory_space_constraint(a, pltpu.HBM)


class Chain:
    def __init__(self):
        self.token, self.calls = None, 0

    def call(self, kernel, name, args, outs, kinds, scratch=(), limit=16, aliases={}):
        ins, out_kinds = kinds.split("-")
        cost = COSTS[min(self.calls, len(COSTS) - 1)]
        self.calls += 1
        assert len(ins) == len(args) and len(out_kinds) == len(outs)
        hbm = pl.BlockSpec(memory_space=pltpu.HBM)
        vmem = pl.BlockSpec(memory_space=pltpu.VMEM)
        smem = pl.BlockSpec(memory_space=pltpu.SMEM)
        spec = lambda kind: {"s": smem, "v": vmem}.get(kind, hbm)
        tokens = () if self.token is None else (self.token,)
        staged = [j for j, kind in enumerate(ins) if kind in "hcl"]
        written = [j for j, kind in enumerate(out_kinds) if kind == "w"]
        memory = lambda kind: pltpu.SMEM if kind == "c" else pltpu.VMEM
        buffers = [memory(ins[j])(args[j].shape, args[j].dtype) for j in staged]
        buffers += [pltpu.VMEM(outs[j].shape, outs[j].dtype) for j in written]
        n_in, n_out, n_buf = len(args) + len(tokens), len(outs), len(buffers)

        def body(*refs):
            arg_refs = list(refs[: len(args)])
            out_refs = list(refs[n_in : n_in + n_out])
            token_ref = refs[n_in + n_out]
            own = refs[n_in + n_out + 1 :]
            bufs, sems, extra = own[:n_buf], own[n_buf], own[n_buf + 1 :]
            reads, writes = {}, {}
            for at, j in enumerate(staged):
                reads[j] = pltpu.make_async_copy(arg_refs[j], bufs[at], sems.at[at])
                reads[j].start()
                arg_refs[j] = bufs[at]
            for at, j in enumerate(written, len(staged)):
                writes[j] = pltpu.make_async_copy(bufs[at], out_refs[j], sems.at[at])
                out_refs[j] = bufs[at]
            io = IO(reads, writes)
            io.wait(*(j for j in staged if ins[j] == "h"))
            token_ref[...] = jnp.zeros_like(token_ref)
            kernel(io, *arg_refs, *out_refs, *extra)
            io.finish()

        *results, self.token = pl.pallas_call(
            body,
            in_specs=[spec(kind) for kind in ins] + [vmem] * len(tokens),
            out_specs=[spec(kind) for kind in out_kinds] + [vmem],
            out_shape=[*outs, f32(8, 128)],
            input_output_aliases=aliases,
            scratch_shapes=[*buffers, pltpu.SemaphoreType.DMA((max(n_buf, 1),)), *scratch],
            compiler_params=pltpu.CompilerParams(vmem_limit_bytes=limit * MIB),
            cost_estimate=pl.CostEstimate(flops=cost * 10**8, bytes_accessed=10**8, transcendentals=0),
            name=name,
        )(*(pinned(a) if kind in "hclp" else a for a, kind in zip(args, ins)), *tokens)
        return results


def bf16(*shape):
    return jax.ShapeDtypeStruct(shape, BF16)


def f32(*shape):
    return jax.ShapeDtypeStruct(shape, F32)


def copies(sems, pairs):
    started = [pltpu.make_async_copy(a, b, sems.at[j]) for j, (a, b) in enumerate(pairs)]
    for copy in started:
        copy.start()
    return started


def finish(started):
    for copy in started:
        copy.wait()


def attention(chain, bits, place, nodes, edges, x, gain, bias, w, g=None, near=()):
    rows, d = x.shape
    width = w.shape[1] if g is None else 2 * w[0].shape[1]
    shard = width // 2
    pairs = width // PAIR
    mols = rows // LEN

    def kernel(io, bits_ref, nodes_ref, edges_ref, x_ref, gain_ref, bias_ref, *refs):
        started = []
        if g is None:
            w_ref, near0, near1, *refs, wo_ref, fc1_ref, fc2_ref, sems = refs
            a1_ref, qt_ref, kt_ref, v_ref, p_ref, ot_ref, o_ref = refs
            pairs_w = []
            for at, ref in enumerate((near0, near1)):
                for c, out in enumerate((wo_ref, fc1_ref, fc2_ref)):
                    part = ref.at[c * shard : (c + 1) * shard]
                    pairs_w.append((part, out.at[at * shard : (at + 1) * shard]))
            started = copies(sems, pairs_w)
        else:
            own, got, g_ref, *refs, w_ref, sems = refs
            a1_ref, qt_ref, kt_ref, v_ref, p_ref, ot_ref, o_ref = refs
            pairs_w = [(own, w_ref.at[:, :shard]), (got, w_ref.at[:, shard:]), (g_ref, o_ref.at[:, :d])]
            started = copies(sems, pairs_w)
        xh, _ = normalise(x_ref[...].astype(F32))
        a1 = (xh * gain_ref[...][None, :] + bias_ref[...][None, :]).astype(BF16)
        a1_ref[...] = a1
        if g is not None:
            finish(started[:2])
        qt = dot_nt(w_ref[0], a1).astype(BF16)
        keys = dot_nt(a1, w_ref[1]).astype(BF16)
        vt = dot_nt(w_ref[2], a1).astype(BF16)
        qt_ref[...] = qt
        every = [(m, i) for m in range(mols) for i in range(pairs)]
        lanes = lambda m: slice(LEN * m, LEN * (m + 1))
        rows_of = lambda i: slice(PAIR * i, PAIR * (i + 1))
        scores, probs = {}, {}
        for m, i in every:
            low, before = pair_window(i, width)
            rhs = placed(pair_blocks(qt[rows_of(i), lanes(m)]), before)
            scores[m, i] = dot_nn(keys[lanes(m), low : low + 2 * LEN], rhs)
        io.wait(1, 2)
        for m in range(mols):
            mol = bits_ref[place] + m
            count = 1 + nodes_ref[mol] + edges_ref[mol]
            valid = lax.broadcasted_iota(jnp.int32, (LEN, 2 * LEN), 0) < count
            for i in range(pairs):
                s = jnp.where(valid, scores[m, i], -1e30)
                e = jnp.exp2((s - jnp.max(s, axis=0, keepdims=True)) * (SCALE * LOG2E))
                p = (e * (1.0 / jnp.sum(e, axis=0, keepdims=True))).astype(BF16)
                p_ref[m, i] = p
                probs[m, i] = p
        for m, i in every:
            both = dot_nn(vt[rows_of(i), lanes(m)], probs[m, i])
            ot_ref[rows_of(i), lanes(m)] = diagonal(both).astype(BF16)
        o_ref[:, o_ref.shape[1] - width :] = ot_ref[...].T
        kt_ref[...] = dot_nt(w_ref[1], a1).astype(BF16)
        v_ref[...] = dot_nt(a1, w_ref[2]).astype(BF16)
        finish(started if g is None else started[2:])

    outs = [
        bf16(rows, d), bf16(width, rows), bf16(width, rows), bf16(rows, width),
        bf16(mols, pairs, LEN, 2 * LEN), bf16(width, rows),
    ]
    args = (bits, nodes, edges, x, gain, bias)
    if g is None:
        return chain.call(
            kernel, "attention_forward", (*args, w, *near), [*outs, bf16(rows, width), bf16(2 * width, d), bf16(2 * width, d), bf16(width, d)],
            "sccvvvvvv-vvvvvvvvvv", scratch=[pltpu.SemaphoreType.DMA((6,))],
        )
    return chain.call(
        kernel, "attention_forward", (*args, *w, g), [*outs, bf16(rows, d + width), bf16(3, width, d)],
        "sccvvvprv-vvvvvvvv", scratch=[pltpu.SemaphoreType.DMA((3,))],
    )


def pick(chain, bits, a, b):
    half = a.shape[0] // 2

    def kernel(io, bits_ref, a_ref, b_ref, out_ref, sems):
        which = 2 * bits_ref[2] + bits_ref[6]
        for at, ref in enumerate((a_ref.at[:half], a_ref.at[half:], b_ref.at[:half], b_ref.at[half:])):
            pl.when(which == at)(lambda ref=ref: finish(copies(sems, [(ref, out_ref)])))

    return chain.call(
        kernel, "pick", (bits, a, b), [bf16(half, a.shape[1])], "spp-v", limit=4,
        scratch=[pltpu.SemaphoreType.DMA((1,))],
    )[0]


def hold(chain, a):
    def kernel(io, a_ref, out_ref):
        out_ref[...] = a_ref[...]

    return chain.call(kernel, "hold", (a,), [bf16(*a.shape)], "v-v", limit=4)[0]


def pair_up(chain, a, b):
    def kernel(io, a_ref, b_ref, out_ref, both_ref):
        out_ref[...] = b_ref[...]
        both_ref[0] = a_ref[...]
        both_ref[1] = b_ref[...]

    return chain.call(kernel, "pair_up", (a, b), [bf16(*b.shape), bf16(2, *a.shape)], "vv-vv", limit=4)


def load(chain, out_weight, fc1_weight, fc2_weight, bias, others):
    shard, d = out_weight.shape
    n = len(others)

    def kernel(io, wo, fc1, fc2, bias_ref, *refs):
        others_in, (near_ref, *others_out, sems) = refs[:n], refs[n:]
        rows = lambda at: near_ref.at[at * shard : (at + 1) * shard]
        near = [(wo, rows(0)), (fc1, rows(1)), (fc2, rows(2)), (bias_ref, near_ref.at[3 * shard :])]
        finish(copies(sems, near + list(zip(others_in, others_out))))

    near, *others = chain.call(
        kernel, "load", (out_weight, fc1_weight, fc2_weight, bias, *others),
        [bf16(3 * shard + 16, d)] + [jax.ShapeDtypeStruct(a.shape, a.dtype) for a in others],
        "pppr" + "p" * n + "-v" + "v" * n, limit=4, scratch=[pltpu.SemaphoreType.DMA((4 + n,))],
    )
    return near, others


def feed_body(x, oa, ob, g, wo_ref, gain_ref, bias_ref, fc1_ref, b1, fc2_ref, h_ref, a2_ref, z_ref, du_ref):
    h = x.astype(F32) + dot_nn(jnp.concatenate([oa, ob], axis=1), wo_ref[...])
    h_ref[...] = h
    xh, _ = normalise(h)
    a2 = (xh * gain_ref[...][None, :] + bias_ref[...][None, :]).astype(BF16)
    a2_ref[...] = a2
    shard = fc2_ref.shape[0] // 2
    b1 = jnp.concatenate([b[3 * shard : 3 * shard + 1, :shard] for b in b1], axis=1).astype(F32)
    u = dot_nt(a2, fc1_ref[: 2 * shard]) + b1
    dz = dot_nt(g, fc2_ref[...])
    phi = 0.5 * (1.0 + lax.erf(u * (0.5**0.5)))
    slope = phi + u * (jnp.exp(-0.5 * u * u) * 0.3989422804014327)
    du = (dz * slope).astype(BF16)
    z = (u * phi).astype(BF16)
    du_ref[...] = du
    z_ref[...] = z
    return a2, z, du


def pack_far(chain, bits, wo, fc1, fars):
    half, d = fars[0].shape
    shard = 2 * half
    width = 2 * shard

    def kernel(io, bits_ref, wo_in, fc1_in, y0, pair0, xz0, y1, pair1, xz1, wo_ref, fc1_ref):
        def placed_at(which):
            for at, (y, pair, xz) in enumerate(((y0, pair0, xz0), (y1, pair1, xz1))):
                for turn, part in enumerate((y[...], pair[1], pair[0], xz[...])):
                    quarter = which ^ turn
                    row = width + at * shard + quarter % 2 * half
                    (wo_ref, fc1_ref)[quarter // 2][row : row + half] = part

        which = 2 * bits_ref[2] + bits_ref[6]
        for at in range(4):
            pl.when(which == at)(functools.partial(placed_at, at))

    return chain.call(
        kernel, "pack_far", (bits, wo, fc1, *fars), [bf16(2 * width, d), bf16(2 * width, d)], "svvvvvvvv-vv", limit=4,
        aliases={1: 0, 2: 1},
    )


def feed_far(chain, x, oa, packet, gain, bias, fc1, fc2, wo, near):
    rows, d = x.shape
    width = fc2.shape[0]

    def kernel(io, x_ref, oa_ref, packet_ref, gain_ref, bias_ref, fc1_ref, fc2_ref, wo_ref, b10, b11, *outs):
        feed_body(
            x_ref[...], oa_ref[...], packet_ref[:, d:], packet_ref[:, :d], wo_ref, gain_ref, bias_ref, fc1_ref,
            (b10, b11), fc2_ref, *outs,
        )

    return chain.call(
        kernel, "feed_far", (x, oa, packet, gain, bias, fc1, fc2, wo, *near),
        [f32(rows, d), bf16(rows, d), bf16(rows, width), bf16(rows, width)], "v" * 10 + "-vvvv",
    )


def feed_own(chain, x, packet, g, ob, gain, bias, fc1, fc2, wo, near, far):
    rows, d = x.shape
    width = fc2.shape[0]
    shard = width // 2

    def kernel(io, x_ref, oa_ref, g_ref, ob_ref, gain_ref, bias_ref, fc1_ref, fc2_ref, wo_ref, b10, b11,
               z1, du1, a1, g1, h_ref, a2_ref, z_ref, du_ref, keep_ref, send_ref, sums_ref):
        a2, z, du = feed_body(
            x_ref[...], oa_ref[:, d:], ob_ref[...], g_ref[...], wo_ref, gain_ref, bias_ref, fc1_ref, (b10, b11),
            fc2_ref, h_ref, a2_ref, z_ref, du_ref,
        )
        first = dot_tn(du, a2) + dot_tn(du1[...], a1[...])
        second = dot_tn(z, g_ref[...]) + dot_tn(z1[...], g1[:, :d])
        for at, ref in enumerate((keep_ref, send_ref)):
            here = slice(at * shard, (at + 1) * shard)
            ref[0] = first[here].astype(BF16)
            ref[1] = second[here].astype(BF16)
        sums_ref[...] = jnp.sum(du.astype(F32), axis=0, keepdims=True) + jnp.sum(
            du1[...].astype(F32), axis=0, keepdims=True
        )

    return chain.call(
        kernel, "feed_own", (x, packet, g, ob, gain, bias, fc1, fc2, wo, *near, *far),
        [f32(rows, d), bf16(rows, d), bf16(rows, width), bf16(rows, width), bf16(2, shard, d), bf16(2, shard, d),
         f32(1, width)], "v" * 15 + "-vvvvvvv",
    )


def feed_result(chain, zs, fc2, h):
    rows, d = h.shape

    def kernel(io, z0, z1, fc2_ref, h_ref, mine_ref, theirs_ref):
        theirs_ref[...] = dot_nn(z1[...], fc2_ref[...]).astype(BF16)
        mine_ref[...] = h_ref[...] + dot_nn(z0[...], fc2_ref[...])

    return chain.call(
        kernel, "feed_result", (*zs, fc2, h), [f32(rows, d), bf16(rows, d)], "vvvv-vv", limit=8,
    )


def backward(chain, args, own):
    h, kt = args[3], args[9]
    rows, d = h.shape
    width = kt.shape[0]
    mols, pairs = rows // LEN, width // PAIR

    def kernel(io, du_ref, dr_ref, fc1_ref, h_ref, g_ref, gain_ref, wo_ref, p_ref, qt_ref, kt_ref, v_ref,
               gh_ref, dp_ref, dh_ref=None, sums_ref=None):
        da2 = dot_nn(jnp.concatenate([du_ref[...], dr_ref[...]], axis=1), fc1_ref[...])
        xh, r = normalise(h_ref[...])
        dh = g_ref[:, :d].astype(F32) + norm_back(da2, gain_ref[...][None, :], xh, r)
        if own:
            dh_ref[...] = dh
            sums_ref[0:1] = jnp.sum(da2 * xh, axis=0, keepdims=True)
            sums_ref[1:2] = jnp.sum(da2, axis=0, keepdims=True)
            io.flush(2)
        gh = dh.astype(BF16)
        gh_ref[...] = gh
        dot = dot_nt(wo_ref[:width], gh).astype(BF16)
        every = [(m, i) for m in range(mols) for i in range(pairs)]
        lanes = lambda m: slice(LEN * m, LEN * (m + 1))
        rows_of = lambda i: slice(PAIR * i, PAIR * (i + 1))
        dps, dss, dos = {}, {}, {}
        for m, i in every:
            low, before = pair_window(i, width)
            dos[m, i] = pair_blocks(dot[rows_of(i), lanes(m)])
            dps[m, i] = dot_nn(v_ref[lanes(m), low : low + 2 * LEN], placed(dos[m, i], before))
        for m, i in every:
            dv = dot_nt(dos[m, i], p_ref[m, i])
            dp_ref[pl.ds(2 * width + PAIR * i, PAIR), lanes(m)] = dv.astype(BF16)
        for m, i in every:
            p = p_ref[m, i].astype(F32)
            t = dps[m, i] * p
            dss[m, i] = (t - p * jnp.sum(t, axis=0, keepdims=True)).astype(BF16)
        for m, i in every:
            dq = diagonal(dot_nn(kt_ref[rows_of(i), lanes(m)], dss[m, i])) * SCALE
            dp_ref[rows_of(i), lanes(m)] = dq.astype(BF16)
            dk = dot_nt(pair_blocks(qt_ref[rows_of(i), lanes(m)]), dss[m, i]) * SCALE
            dp_ref[pl.ds(width + PAIR * i, PAIR), lanes(m)] = dk.astype(BF16)

    outs = [bf16(rows, d), bf16(3 * width, rows)] + ([f32(rows, d), f32(8, d)] if own else [])
    return chain.call(
        kernel, "attention_backward", args, outs, "v" * 11 + ("-vvvv" if own else "-vv"),
    )


def weight_grads(chain, name, shard, at, lefts, rights):
    d = rights[0][0].shape[1]
    args, count = [], len(lefts)
    for (u0, u1, _), (v0, v1) in zip(lefts, rights):
        args += [u0, u1, v0, v1]

    def kernel(io, *refs):
        out_ref = refs[-1]
        for c in range(count):
            u0, u1, v0, v1 = refs[4 * c : 4 * c + 4]
            rows = slice(lefts[c][2] + at * shard, lefts[c][2] + (at + 1) * shard)
            left = jnp.concatenate([u0[rows], u1[rows]], axis=1)
            right = jnp.concatenate([v0[...], v1[...]], axis=0)
            out_ref[c] = dot_nn(left, right).astype(BF16)

    return chain.call(kernel, name, args, [bf16(count, shard, d)], "v" * len(args) + "-v")[0]


def input_grads(chain, dps, w, xs, sums, bias):
    rows, d = xs[0].shape

    def kernel(io, dp0, dp1, w_ref, x0, x1, sums_ref, bias_ref, mine_ref, theirs_ref):
        w = w_ref[...].reshape(dp0.shape[0], d)
        theirs = dot_tn(dp1[...], w)
        theirs_ref[:rows] = theirs.astype(BF16)
        mine = dot_tn(dp0[...], w)
        mine_ref[...] = mine
        xh0, _ = normalise(x0[...].astype(F32))
        xh1, _ = normalise(x1[...].astype(F32))
        bias = bias_ref[...]
        vec = [
            jnp.sum(mine * xh0, axis=0, keepdims=True) + jnp.sum(theirs * xh1, axis=0, keepdims=True),
            jnp.sum(mine, axis=0, keepdims=True) + jnp.sum(theirs, axis=0, keepdims=True),
            sums_ref[0:2],
            jnp.concatenate([bias, jnp.zeros((1, d - bias.shape[1]), F32)], axis=1),
            jnp.zeros((11, d), F32),
        ]
        theirs_ref[rows:] = jnp.concatenate(vec, axis=0).astype(BF16)

    return chain.call(
        kernel, "input_grads", (*dps, w, *xs, sums, bias), [f32(rows, d), bf16(rows + 16, d)], "vvvvvvv-vv"
    )


def input_norm(chain, x, gain, mine, got, dh):
    rows, d = x.shape

    def kernel(io, x_ref, gain_ref, mine_ref, got_ref, dh_ref, out_ref):
        xh, r = normalise(x_ref[...].astype(F32))
        da1 = mine_ref[...] + got_ref[:rows].astype(F32)
        out_ref[...] = (dh_ref[...] + norm_back(da1, gain_ref[...][None, :], xh, r)).astype(BF16)

    return chain.call(
        kernel, "input_norm", (x, gain, mine, got, dh), [bf16(rows, d)], "vvvvv-w", limit=8
    )[0]


def add_result(chain, mine, got):
    def kernel(io, mine_ref, got_ref, out_ref):
        out_ref[...] = (mine_ref[...] + got_ref[...].astype(F32)).astype(BF16)

    return chain.call(kernel, "add_result", (mine, got), [bf16(*mine.shape)], "vv-w", limit=8)[0]


def plus(*terms):
    total = terms[0].astype(F32)
    for term in terms[1:]:
        total = total + term.astype(F32)
    return total.astype(BF16)


def vector_rows(chain, mine, got):
    rows, d = mine.shape

    def kernel(io, mine_ref, got_ref, out_ref):
        a, b = mine_ref[rows - 16 :], got_ref[rows - 16 :]
        same = lax.broadcasted_iota(jnp.int32, (16, d), 0) < 4
        out_ref[...] = plus(a, jnp.where(same, b.astype(F32), 0.0))

    return chain.call(kernel, "vector_rows", (mine, got), [bf16(16, d)], "vv-v", limit=4)[0]


def vector_cores(chain, mine, got, shard):
    def kernel(io, mine_ref, got_ref, out_ref):
        a, b = mine_ref[...].astype(F32), got_ref[...].astype(F32)
        turned = jnp.concatenate([b[:, shard : 2 * shard], b[:, :shard], b[:, 2 * shard :]], axis=1)
        same = lax.broadcasted_iota(jnp.int32, a.shape, 0) < 4
        out_ref[...] = plus(a, jnp.where(same, b, turned))

    return chain.call(kernel, "vector_cores", (mine, got), [bf16(*mine.shape)], "vv-v", limit=4)[0]


def sum_half(chain, bits, mine, got, apart):
    def kernel(io, bits_ref, mine_ref, got_ref, *outs):
        half, quarter = 1 - bits_ref[0], bits_ref[1]
        on_ref, kept_ref = outs if apart else (outs[0].at[0], outs[0].at[1])
        on_ref[...] = mine_ref[half, 1 - quarter] + got_ref[half, 1 - quarter]
        kept_ref[...] = mine_ref[half, quarter] + got_ref[half, quarter]

    rows, d = mine.shape[2:]
    outs = [bf16(rows, d)] * 2 if apart else [bf16(2, rows, d)]
    return chain.call(kernel, "sum_half", (bits, mine, got), outs, "svv-" + "v" * len(outs), limit=8)


def sum_quarter(chain, bits, mine, got, kept, *more, vec=()):
    rows, d = mine.shape[2:]
    arrays = [a[0] if isinstance(a, tuple) else a for a in more]

    def kernel(io, bits_ref, mine_ref, got_ref, *refs):
        *refs, out_ref = refs
        half = bits_ref[0]
        quarter = bits_ref[1] if kept else 1 - bits_ref[1]
        terms = [ref[a[1]] if isinstance(a, tuple) else ref[...] for a, ref in zip(more, refs)]
        out_ref[:rows] = plus(mine_ref[half, quarter], got_ref[half, quarter], *terms)
        if vec:
            out_ref[rows:] = refs[-1][...]

    args = (bits, mine, got, *arrays, *vec)
    return chain.call(
        kernel, "sum_quarter", args, [bf16(rows + (16 if vec else 0), d)], "s" + "v" * (len(args) - 1) + "-v",
        limit=8,
    )[0]


def sum_quarter_apart(chain, bits, mine, got, *more):
    rows, d = mine.shape[2:]
    arrays = [a[0] if isinstance(a, tuple) else a for a in more]

    def kernel(io, bits_ref, mine_ref, got_ref, *refs):
        *refs, upper_ref, lower_ref = refs
        half, quarter = bits_ref[0], bits_ref[1]
        terms = [ref[a[1]] if isinstance(a, tuple) else ref[...] for a, ref in zip(more, refs)]
        total = plus(mine_ref[half, quarter], got_ref[half, quarter], *terms)
        upper_ref[...] = total[: rows // 2]
        lower_ref[...] = total[rows // 2 :]

    args = (bits, mine, got, *arrays)
    return chain.call(
        kernel, "sum_quarter", args, [bf16(rows // 2, d)] * 2, "s" + "v" * (len(args) - 1) + "-vv", limit=8
    )


def side_by_side(chain, a, b, apart):
    rows, d = a.shape

    def kernel(io, a_ref, b_ref, *outs):
        first, second = outs if apart else (outs[0].at[:rows], outs[0].at[rows:])
        first[...] = a_ref[...]
        second[...] = b_ref[...]

    outs = [bf16(rows, d)] * 2 if apart else [bf16(2 * rows, d)]
    return chain.call(kernel, "side_by_side", (a, b), outs, "vv-" + "v" * len(outs), limit=8)


def sum_pairs(chain, *pairs):
    rows = [a.shape[0] for a, _ in pairs]

    def kernel(io, *refs):
        *refs, out_ref = refs
        start = 0
        for a_ref, b_ref in zip(refs[::2], refs[1::2]):
            out_ref[start : start + a_ref.shape[0]] = a_ref[...] + b_ref[...]
            start += a_ref.shape[0]

    args = [a for pair in pairs for a in pair]
    return chain.call(
        kernel, "sum_pairs", args, [bf16(sum(rows), args[0].shape[1])], "v" * len(args) + "-v", limit=8
    )[0]


def place_sums(chain, bits, quarters, rows, targets, outs, whole=(), vec=(), skip=0):
    d = quarters[0][0].shape[1]
    n = len(outs)
    arrays = []
    for a, *_ in quarters:
        if not any(a is b for b in arrays):
            arrays.append(a)
    which = [next(k for k, b in enumerate(arrays) if b is a) for a, *_ in quarters]

    def kernel(io, bits_ref, *refs):
        refs, (buf, sems) = refs[:-2], refs[-2:]
        ins = [refs[k] for k in which]
        refs = refs[len(arrays) + len(whole) :]
        out_refs, vec_refs = refs[:n], refs[n:]

        def each(step):
            for j, (_, _, half, quarter) in enumerate(quarters):
                if j < skip:
                    continue
                half = 1 - bits_ref[0] if half else bits_ref[0]
                quarter = 1 - bits_ref[1] if quarter else bits_ref[1]
                for at, (out, index, first) in enumerate(targets):
                    ref = out_refs[out]
                    ref = ref if index is None else ref.at[index]
                    ref = ref.at[first : first + rows]
                    copy = pltpu.make_async_copy(buf.at[j], ref, sems.at[j])
                    pl.when(2 * half + quarter == at)(functools.partial(step, copy))

        starts = [start for _, start, _, _ in quarters]
        for j, ref in enumerate(ins):
            if j >= skip:
                buf[j] = ref[starts[j] : starts[j] + rows].astype(F32)
        each(lambda copy: copy.start())
        if vec:
            a, b, c, e = (ref[x + rows : x + rows + 16].astype(F32) for ref, x in zip(ins, starts))
            total = jnp.where(bits_ref[5] == 0, (a + b) + (c + e), (a + c) + (b + e))
            for at, (length, ref) in enumerate(zip(vec, vec_refs)):
                ref[...] = total[at, :length]
        each(lambda copy: copy.wait())

    return chain.call(
        kernel, "place_sums", (bits, *arrays, *whole), [*outs, *(f32(length) for length in vec)],
        "s" + "v" * len(arrays) + "p" * len(whole) + "-" + "r" * n + "v" * len(vec), limit=8,
        aliases={1 + len(arrays) + j: j for j in range(len(whole))},
        scratch=[pltpu.VMEM((len(quarters), rows, d), F32), pltpu.SemaphoreType.DMA((len(quarters),))],
    )


def local(
    n_dp, n_tensor, tokens, node_counts, edge_counts, ln1_gain, ln1_bias, qkv_weight, out_weight,
    ln2_gain, ln2_bias, fc1_weight, fc1_bias, fc2_weight, out_grad,
):
    d = tokens.shape[1]
    shard = out_weight.shape[0]
    width = 2 * shard
    mols = tokens.shape[0] // LEN
    dp_at = lax.axis_index("dp")
    tensor_at = lax.axis_index("tensor")
    core = tensor_at % 2
    bit0 = dp_at % 2
    bit1 = (dp_at // 2) % 2
    bits = jnp.stack(
        [jnp.where(core == 0, bit0, bit1), jnp.where(core == 0, bit1, bit0), bit0, tensor_at * mols,
         (tensor_at ^ 2) * mols, core, bit1]
    ).astype(jnp.int32)
    chain = Chain()

    def swap_core(a):
        return lax.ppermute(a, "tensor", [(t, t ^ 1) for t in range(n_tensor)])

    def swap_y(a):
        return lax.ppermute(a, "tensor", [(t, t ^ 2) for t in range(n_tensor)])

    def swap_dp(a, mask0, mask1):
        pairs = [
            (p * n_tensor + t, (p ^ (mask1 if t % 2 else mask0)) * n_tensor + t)
            for p in range(n_dp)
            for t in range(n_tensor)
        ]
        return lax.ppermute(a, ("dp", "tensor"), pairs)

    swap_first = lambda a: swap_dp(a, 1, 2)
    swap_second = lambda a: swap_dp(a, 2, 1)
    far_masks = [1 << k for k in range(2, n_dp.bit_length() - 1)]

    w_got = swap_core(qkv_weight)
    x_got = swap_y(tokens)
    far_y = swap_y(pick(chain, bits, out_weight, fc1_weight))
    bias = jnp.pad(fc1_bias.reshape(1, -1), ((0, 15), (0, d - shard)))
    near, others = load(
        chain, out_weight, fc1_weight, fc2_weight, bias,
        (tokens, out_grad, ln1_gain, ln1_bias, ln2_gain, ln2_bias),
    )
    near = (near, swap_core(near))
    tokens, out_grad, ln1_gain, ln1_bias, ln2_gain, ln2_bias = others

    counts = (node_counts, edge_counts)
    norm1 = (ln1_gain, ln1_bias)
    a1_0, qt_0, kt_0, v_0, p_0, ot_0, packet, w_qkv = attention(
        chain, bits, 3, *counts, tokens, *norm1, (qkv_weight, w_got), out_grad
    )
    packet_got = swap_y(packet)
    far_y = hold(chain, far_y)
    far_x, far_z = swap_dp(far_y, 1, 1), swap_dp(far_y, 2, 2)
    a1_1, qt_1, kt_1, v_1, p_1, ot_1, o_1, wo, fc1, fc2 = attention(
        chain, bits, 4, *counts, x_got, *norm1, w_qkv, near=near
    )
    o_got = swap_y(o_1)
    far_z, pair = pair_up(chain, far_x, far_z)
    far_xz = swap_dp(far_z, 1, 1)
    fars = (far_y, pair, far_xz)
    fars += tuple(swap_core(a) for a in fars)
    norm2 = (ln2_gain, ln2_bias)
    wo, fc1 = pack_far(chain, bits, wo, fc1, fars)
    h_1, a2_1, z_1, du_1 = feed_far(chain, x_got, o_1, packet_got, *norm2, fc1, fc2, wo, near)
    dr_0 = swap_y(du_1)
    h_0, a2_0, z_0, du_0, keep_r, send_r, bias_sums = feed_own(
        chain, tokens, packet, out_grad, o_got, *norm2, fc1, fc2, wo, near, (z_1, du_1, a2_1, packet_got)
    )
    dr_1 = swap_y(du_0)

    class Sum:
        def __init__(self, count, keep, got, apart, early):
            self.size = count * shard // 4
            self.apart, self.early = apart, early
            view = lambda a: a.reshape(2, 2, self.size, d)
            self.parts = (view(keep), view(got))

        def first(self):
            sent = sum_half(chain, bits, *self.parts, self.apart)
            got = [swap_first(a) for a in sent]
            self.on, self.kept = got if self.apart else ((got[0], 0), (got[0], 1))

        def second(self):
            self.got = swap_second(sum_quarter(chain, bits, *self.parts, False, self.on))

        def third(self, *vec):
            self.sum = sum_quarter(chain, bits, *self.parts, True, self.kept, self.got, vec=vec)
            self.got = swap_dp(self.sum, far_masks[0], far_masks[0])

        def third_apart(self):
            self.sums = sum_quarter_apart(chain, bits, *self.parts, self.kept, self.got)
            self.gots = [swap_dp(a, far_masks[0], far_masks[0]) for a in self.sums]
            self.halves = [None, None]

        def fourth_apart(self, at, *vec):
            self.sum, self.got = self.sums[at], self.gots[at]
            self.fourth(*vec)
            self.halves[at] = self.quarters

        def fourth(self, *vec):
            a = sum_pairs(chain, (self.sum, self.got), *vec)
            for mask in far_masks[1:]:
                a = sum_pairs(chain, (a, swap_dp(a, mask, mask)))
            b = swap_second(a)
            if self.early == 1:
                self.quarters = [(a, 0, 0, 0), (b, 0, 0, 1), (swap_first(a), 0, 1, 0), (swap_first(b), 0, 1, 1)]
            self.last = (a, b)

        def fifth(self):
            if self.early == 0:
                (a,) = side_by_side(chain, *self.last, False)
                b = swap_first(a)
                rows = a.shape[0] // 2
                self.quarters = [(a, 0, 0, 0), (a, rows, 0, 1), (b, 0, 1, 0), (b, rows, 1, 1)]
            if self.early == 2:
                a, b = side_by_side(chain, *self.last, True)
                self.quarters = [(a, 0, 0, 0), (b, 0, 0, 1), (swap_first(a), 0, 1, 0), (swap_first(b), 0, 1, 1)]

    gh_0, dp_0, dh, sums = backward(
        chain, (du_0, dr_0, fc1, h_0, out_grad, ln2_gain, wo, p_0, qt_0, kt_0, v_0), True
    )
    r = Sum(2, keep_r, swap_core(send_r), True, 1)
    r.first()
    gh_1, dp_1 = backward(
        chain, (du_1, dr_1, fc1, h_1, packet_got, ln2_gain, wo, p_1, qt_1, kt_1, v_1), False
    )
    a1s = (a1_0, a1_1)
    lefts = [(dp_0, dp_1, c * width) for c in range(3)] + [(ot_0, ot_1, 0)]
    rights = [a1s] * 3 + [(gh_0, gh_1)]
    got_q = swap_core(weight_grads(chain, "weight_grads", shard, 1, lefts, rights))
    q = Sum(4, weight_grads(chain, "weight_grads", shard, 0, lefts, rights), got_q, True, 2)
    r.second()
    q.first()
    r.third()
    q.second()
    da1_mine, da1_theirs = input_grads(chain, (dp_0, dp_1), w_qkv, (tokens, x_got), sums, bias_sums)
    da1_got = swap_y(da1_theirs)
    r.fourth()
    res_mine, res_theirs = feed_result(chain, (z_0, z_1), fc2, h_0)
    res_got = swap_y(res_theirs)
    q.third()
    vec = vector_rows(chain, da1_theirs, da1_got)
    vec_got = swap_core(vec)
    r.fifth()
    halves = [(c, None, half * shard // 2) for c in range(2) for half in range(2)]
    grad_fc1, grad_fc2 = place_sums(chain, bits, r.quarters, r.size, halves, [f32(shard, d)] * 2)
    vec = vector_cores(chain, vec, vec_got, shard)
    vec_got = swap_dp(vec, far_masks[0], far_masks[0])
    result = add_result(chain, res_mine, res_got)
    q.fourth((vec, vec_got))
    grad_tokens = input_norm(chain, tokens, ln1_gain, da1_mine, da1_got, dh)
    q.fifth()
    each = [(0, 0, 0), (0, 1, 0), (0, 2, 0), (1, None, 0)]
    outs = [f32(3, shard, d), f32(shard, d)]
    grads = place_sums(chain, bits, q.quarters[:2], q.size, each, outs)
    grads = place_sums(chain, bits, q.quarters[:3], q.size, each, outs, grads, skip=2)
    grad_qkv, grad_out, gain1, bias1, gain2, bias2, grad_b = place_sums(
        chain, bits, q.quarters, q.size, each, outs, grads, (d, d, d, d, shard), 3
    )
    return (
        result, grad_tokens, gain1, bias1, grad_qkv, grad_out, gain2, bias2, grad_fc1, grad_b, grad_fc2,
    )


def solution(mesh):
    tokens = P(("dp", "tensor"), None)
    rows = P("tensor", None)
    qkv = P(None, "tensor", None)
    in_specs = (
        tokens, P("dp"), P("dp"), P(), P(), qkv, rows, P(), P(), rows, P("tensor"), rows, tokens,
    )
    out_specs = (tokens, tokens, P(), P(), qkv, rows, P(), P(), rows, P("tensor"), rows)
    step = functools.partial(local, mesh.shape["dp"], mesh.shape["tensor"])
    return jax.shard_map(step, mesh=mesh, in_specs=in_specs, out_specs=out_specs, check_vma=False)
```

```python
import functools

import jax
import jax.numpy as jnp
from jax import lax
from jax.experimental import pallas as pl
from jax.experimental.pallas import tpu as pltpu
from jax.sharding import PartitionSpec as P

HEAD_DIM = 24
LEN = 128
PAIR = 2 * HEAD_DIM
EPSILON = 1e-05
SCALE = HEAD_DIM ** (-0.5)
LOG2E = 1.4426950408889634
F32 = jnp.float32
BF16 = jnp.bfloat16
MIB = 1024 * 1024


def dot_nn(a, b):
    return lax.dot_general(a, b, (((1,), (0,)), ((), ())), preferred_element_type=F32)


def dot_nt(a, b):
    return lax.dot_general(a, b, (((1,), (1,)), ((), ())), preferred_element_type=F32)


def dot_tn(a, b):
    return lax.dot_general(a, b, (((0,), (0,)), ((), ())), preferred_element_type=F32)


def normalise(v):
    centered = v - jnp.mean(v, axis=-1, keepdims=True)
    r = lax.rsqrt(jnp.mean(centered * centered, axis=-1, keepdims=True) + EPSILON)
    return centered * r, r


def norm_back(da, gain, xh, r):
    e = da * gain
    return r * (
        e - jnp.mean(e, axis=-1, keepdims=True) - xh * jnp.mean(e * xh, axis=-1, keepdims=True)
    )


def pair_blocks(rows):
    rows = rows.astype(F32)
    none = jnp.zeros((HEAD_DIM, LEN), F32)
    left = jnp.concatenate([rows[:HEAD_DIM], none], axis=0)
    right = jnp.concatenate([none, rows[HEAD_DIM:]], axis=0)
    return jnp.concatenate([left, right], axis=1).astype(BF16)


def pair_window(i, width):
    low = min(PAIR * i // LEN * LEN, width - 2 * LEN)
    return low, PAIR * i - low


def placed(block, before):
    parts = []
    if before:
        parts.append(jnp.zeros((before, 2 * LEN), BF16))
    parts.append(block)
    after = 2 * LEN - PAIR - before
    if after:
        parts.append(jnp.zeros((after, 2 * LEN), BF16))
    return jnp.concatenate(parts, axis=0)


def diagonal(both):
    return jnp.concatenate([both[:HEAD_DIM, :LEN], both[HEAD_DIM:, LEN:]], axis=0)


COSTS = (0, 0, 100, 0, 0, 30, 30, 0, 0, 0, 0, 100, 0, 0, 0, 200, 0, 60, 0, 0, 30, 0, 0, 0, 0, 0, 0, 0, 0, 0, 0, 0)


class IO:
    def __init__(self, reads, writes):
        self.reads, self.writes = reads, writes
        self.started = set()

    def wait(self, *args):
        for j in args:
            if j in self.reads:
                self.reads[j].wait()

    def flush(self, *outs):
        for j in outs:
            if j in self.writes:
                self.started.add(j)
                self.writes[j].start()

    def finish(self):
        self.flush(*(j for j in self.writes if j not in self.started))
        for copy in self.writes.values():
            copy.wait()


def pinned(a):
    return pltpu.with_memory_space_constraint(a, pltpu.HBM)


class Chain:
    def __init__(self):
        self.token, self.calls = None, 0

    def call(self, kernel, name, args, outs, kinds, scratch=(), limit=16, aliases={}):
        ins, out_kinds = kinds.split("-")
        cost = COSTS[min(self.calls, len(COSTS) - 1)]
        self.calls += 1
        assert len(ins) == len(args) and len(out_kinds) == len(outs)
        hbm = pl.BlockSpec(memory_space=pltpu.HBM)
        vmem = pl.BlockSpec(memory_space=pltpu.VMEM)
        smem = pl.BlockSpec(memory_space=pltpu.SMEM)
        spec = lambda kind: {"s": smem, "v": vmem}.get(kind, hbm)
        tokens = () if self.token is None else (self.token,)
        staged = [j for j, kind in enumerate(ins) if kind in "hcl"]
        written = [j for j, kind in enumerate(out_kinds) if kind == "w"]
        memory = lambda kind: pltpu.SMEM if kind == "c" else pltpu.VMEM
        buffers = [memory(ins[j])(args[j].shape, args[j].dtype) for j in staged]
        buffers += [pltpu.VMEM(outs[j].shape, outs[j].dtype) for j in written]
        n_in, n_out, n_buf = len(args) + len(tokens), len(outs), len(buffers)

        def body(*refs):
            arg_refs = list(refs[: len(args)])
            out_refs = list(refs[n_in : n_in + n_out])
            token_ref = refs[n_in + n_out]
            own = refs[n_in + n_out + 1 :]
            bufs, sems, extra = own[:n_buf], own[n_buf], own[n_buf + 1 :]
            reads, writes = {}, {}
            for at, j in enumerate(staged):
                reads[j] = pltpu.make_async_copy(arg_refs[j], bufs[at], sems.at[at])
                reads[j].start()
                arg_refs[j] = bufs[at]
            for at, j in enumerate(written, len(staged)):
                writes[j] = pltpu.make_async_copy(bufs[at], out_refs[j], sems.at[at])
                out_refs[j] = bufs[at]
            io = IO(reads, writes)
            io.wait(*(j for j in staged if ins[j] == "h"))
            token_ref[...] = jnp.zeros_like(token_ref)
            kernel(io, *arg_refs, *out_refs, *extra)
            io.finish()

        *results, self.token = pl.pallas_call(
            body,
            in_specs=[spec(kind) for kind in ins] + [vmem] * len(tokens),
            out_specs=[spec(kind) for kind in out_kinds] + [vmem],
            out_shape=[*outs, f32(8, 128)],
            input_output_aliases=aliases,
            scratch_shapes=[*buffers, pltpu.SemaphoreType.DMA((max(n_buf, 1),)), *scratch],
            compiler_params=pltpu.CompilerParams(vmem_limit_bytes=limit * MIB),
            cost_estimate=pl.CostEstimate(flops=cost * 10**8, bytes_accessed=10**8, transcendentals=0),
            name=name,
        )(*(pinned(a) if kind in "hclp" else a for a, kind in zip(args, ins)), *tokens)
        return results


def bf16(*shape):
    return jax.ShapeDtypeStruct(shape, BF16)


def f32(*shape):
    return jax.ShapeDtypeStruct(shape, F32)


def copies(sems, pairs):
    started = [pltpu.make_async_copy(a, b, sems.at[j]) for j, (a, b) in enumerate(pairs)]
    for copy in started:
        copy.start()
    return started


def finish(started):
    for copy in started:
        copy.wait()


def attention(chain, bits, place, nodes, edges, x, gain, bias, w, g=None, near=()):
    rows, d = x.shape
    width = w.shape[1] if g is None else 2 * w[0].shape[1]
    shard = width // 2
    pairs = width // PAIR
    mols = rows // LEN

    def kernel(io, bits_ref, nodes_ref, edges_ref, x_ref, gain_ref, bias_ref, *refs):
        started = []
        if g is None:
            w_ref, near0, near1, *refs, wo_ref, fc1_ref, fc2_ref, sems = refs
            a1_ref, qt_ref, kt_ref, v_ref, p_ref, ot_ref, o_ref = refs
            pairs_w = []
            for at, ref in enumerate((near0, near1)):
                for c, out in enumerate((wo_ref, fc1_ref, fc2_ref)):
                    part = ref.at[c * shard : (c + 1) * shard]
                    pairs_w.append((part, out.at[at * shard : (at + 1) * shard]))
            started = copies(sems, pairs_w)
        else:
            own, got, g_ref, *refs, w_ref, sems = refs
            a1_ref, qt_ref, kt_ref, v_ref, p_ref, ot_ref, o_ref = refs
            pairs_w = [(own, w_ref.at[:, :shard]), (got, w_ref.at[:, shard:]), (g_ref, o_ref.at[:, :d])]
            started = copies(sems, pairs_w)
        xh, _ = normalise(x_ref[...].astype(F32))
        a1 = (xh * gain_ref[...][None, :] + bias_ref[...][None, :]).astype(BF16)
        a1_ref[...] = a1
        if g is not None:
            finish(started[:2])
        qt = dot_nt(w_ref[0], a1).astype(BF16)
        keys = dot_nt(a1, w_ref[1]).astype(BF16)
        vt = dot_nt(w_ref[2], a1).astype(BF16)
        qt_ref[...] = qt
        every = [(m, i) for m in range(mols) for i in range(pairs)]
        lanes = lambda m: slice(LEN * m, LEN * (m + 1))
        rows_of = lambda i: slice(PAIR * i, PAIR * (i + 1))
        scores, probs = {}, {}
        for m, i in every:
            low, before = pair_window(i, width)
            rhs = placed(pair_blocks(qt[rows_of(i), lanes(m)]), before)
            scores[m, i] = dot_nn(keys[lanes(m), low : low + 2 * LEN], rhs)
        io.wait(1, 2)
        for m in range(mols):
            mol = bits_ref[place] + m
            count = 1 + nodes_ref[mol] + edges_ref[mol]
            valid = lax.broadcasted_iota(jnp.int32, (LEN, 2 * LEN), 0) < count
            for i in range(pairs):
                s = jnp.where(valid, scores[m, i], -1e30)
                e = jnp.exp2((s - jnp.max(s, axis=0, keepdims=True)) * (SCALE * LOG2E))
                p = (e * (1.0 / jnp.sum(e, axis=0, keepdims=True))).astype(BF16)
                p_ref[m, i] = p
                probs[m, i] = p
        for m, i in every:
            both = dot_nn(vt[rows_of(i), lanes(m)], probs[m, i])
            ot_ref[rows_of(i), lanes(m)] = diagonal(both).astype(BF16)
        o_ref[:, o_ref.shape[1] - width :] = ot_ref[...].T
        kt_ref[...] = dot_nt(w_ref[1], a1).astype(BF16)
        v_ref[...] = dot_nt(a1, w_ref[2]).astype(BF16)
        finish(started if g is None else started[2:])

    outs = [
        bf16(rows, d), bf16(width, rows), bf16(width, rows), bf16(rows, width),
        bf16(mols, pairs, LEN, 2 * LEN), bf16(width, rows),
    ]
    args = (bits, nodes, edges, x, gain, bias)
    if g is None:
        return chain.call(
            kernel, "attention_forward", (*args, w, *near), [*outs, bf16(rows, width), bf16(2 * width, d), bf16(2 * width, d), bf16(2 * width, d)],
            "sccvvvvvv-vvvvvvvvvv", scratch=[pltpu.SemaphoreType.DMA((6,))],
        )
    return chain.call(
        kernel, "attention_forward", (*args, *w, g), [*outs, bf16(rows, d + width), bf16(3, width, d)],
        "sccvvvprv-vvvvvvvv", scratch=[pltpu.SemaphoreType.DMA((3,))],
    )


def pick(chain, bits, wo, fc1, fc2, bias):
    shard, d = wo.shape
    rows = 3 * shard // 4

    def kernel(io, bits_ref, wo_ref, fc1_ref, fc2_ref, bias_ref, out_ref, sems):
        refs = (wo_ref, fc1_ref, fc2_ref)
        out_ref[rows:] = jnp.concatenate(
            [jnp.broadcast_to(bias_ref[...].astype(F32)[None, :], (16, shard)), jnp.zeros((16, d - shard), F32)], axis=1
        ).astype(BF16)

        def part(quarter):
            pairs = []
            for c, first, at, n in quarter_rows(quarter, shard):
                pairs.append((refs[c].at[first : first + n], out_ref.at[at : at + n]))
            finish(copies(sems, pairs))

        which = 2 * bits_ref[2] + bits_ref[6]
        for at in range(4):
            pl.when(which == at)(functools.partial(part, at))

    return chain.call(
        kernel, "pick", (bits, wo, fc1, fc2, bias), [bf16(rows + 16, d)], "spppv-v", limit=4,
        scratch=[pltpu.SemaphoreType.DMA((2,))],
    )[0]


def quarter_rows(quarter, shard):
    size = 3 * shard // 4
    found, at = [], 0
    while at < size:
        which, first = divmod(quarter * size + at, shard)
        n = min(size - at, shard - first)
        found.append((which, first, at, n))
        at += n
    return found


def hold(chain, a):
    rows, d = a.shape

    def kernel(io, a_ref, out_ref, short_ref):
        out_ref[...] = a_ref[...]
        short_ref[...] = a_ref[: rows - 16]

    return chain.call(kernel, "hold", (a,), [bf16(rows, d), bf16(rows - 16, d)], "v-vv", limit=4)


def pair_up(chain, a, b):
    def kernel(io, a_ref, b_ref, out_ref, both_ref):
        out_ref[...] = b_ref[...]
        both_ref[0] = a_ref[...]
        both_ref[1] = b_ref[...]

    return chain.call(kernel, "pair_up", (a, b), [bf16(*b.shape), bf16(2, *a.shape)], "vv-vv", limit=4)


def spacer(chain):
    def kernel(io):
        pass

    chain.call(kernel, "spacer", (), [], "-", limit=2)


def load(chain, out_weight, fc1_weight, fc2_weight, bias, others):
    shard, d = out_weight.shape
    n = len(others)

    def kernel(io, wo, fc1, fc2, bias_ref, *refs):
        others_in, (near_ref, *others_out, sems) = refs[:n], refs[n:]
        rows = lambda at: near_ref.at[at * shard : (at + 1) * shard]
        near = [(wo, rows(0)), (fc1, rows(1)), (fc2, rows(2)), (bias_ref, near_ref.at[3 * shard :])]
        finish(copies(sems, near + list(zip(others_in, others_out))))

    near, *others = chain.call(
        kernel, "load", (out_weight, fc1_weight, fc2_weight, bias, *others),
        [bf16(3 * shard + 16, d)] + [jax.ShapeDtypeStruct(a.shape, a.dtype) for a in others],
        "pppr" + "p" * n + "-v" + "v" * n, limit=4, scratch=[pltpu.SemaphoreType.DMA((4 + n,))],
    )
    return near, others


def feed_body(x, oa, ob, g, wo_ref, gain_ref, bias_ref, fc1_ref, b1_ref, fc2_ref, h_ref, a2_ref, z_ref, du_ref):
    h = x.astype(F32) + dot_nn(jnp.concatenate([oa, ob], axis=1), wo_ref[...])
    h_ref[...] = h
    xh, _ = normalise(h)
    a2 = (xh * gain_ref[...][None, :] + bias_ref[...][None, :]).astype(BF16)
    a2_ref[...] = a2
    u = dot_nt(a2, fc1_ref[...]) + b1_ref[...]
    dz = dot_nt(g, fc2_ref[...])
    phi = 0.5 * (1.0 + lax.erf(u * (0.5**0.5)))
    slope = phi + u * (jnp.exp(-0.5 * u * u) * 0.3989422804014327)
    du = (dz * slope).astype(BF16)
    z = (u * phi).astype(BF16)
    du_ref[...] = du
    z_ref[...] = z
    return a2, z, du


def pack_far(chain, bits, weights, fars):
    rows, d = weights[0].shape
    shard = rows // 4

    def kernel(io, bits_ref, wo_in, fc1_in, fc2_in, y0, pair0, xz0, y1, pair1, xz1, *outs):
        def placed_at(which):
            for at, (y, pair, xz) in enumerate(((y0, pair0, xz0), (y1, pair1, xz1))):
                for turn, ref in enumerate((y, pair.at[1], pair.at[0], xz)):
                    for c, first, start, n in quarter_rows(which ^ turn, shard):
                        row = (2 + at) * shard + first
                        outs[c][row : row + n] = ref[start : start + n]

        which = 2 * bits_ref[2] + bits_ref[6]
        for at in range(4):
            pl.when(which == at)(functools.partial(placed_at, at))

    return chain.call(
        kernel, "pack_far", (bits, *weights, *fars), [bf16(rows, d)] * 3, "s" + "v" * 9 + "-vvv", limit=4,
        aliases={1: 0, 2: 1, 3: 2},
    )


def feed_far(chain, x, oa, packet, gain, bias, wo, fc1, fc2, biases):
    rows, d = x.shape
    columns = fc1.shape[0]
    shard = columns // 4

    def kernel(io, x_ref, oa_ref, packet_ref, gain_ref, bias_ref, wo_ref, fc1_ref, fc2_ref, *refs):
        b_refs, (h_ref, a2_ref, z_ref, du_ref, b1_ref) = refs[:4], refs[4:]
        parts = [ref[row : row + 1, :shard].astype(F32) for ref, (_, row) in zip(b_refs, biases)]
        b1_ref[...] = jnp.concatenate(parts, axis=1)
        feed_body(
            x_ref[...], oa_ref[...], packet_ref[:, d:], packet_ref[:, :d], wo_ref, gain_ref, bias_ref, fc1_ref, b1_ref,
            fc2_ref, h_ref, a2_ref, z_ref, du_ref,
        )

    return chain.call(
        kernel, "feed_far", (x, oa, packet, gain, bias, wo, fc1, fc2, *(a for a, _ in biases)),
        [f32(rows, d), bf16(rows, d), bf16(rows, columns), bf16(rows, columns), f32(1, columns)], "v" * 12 + "-vvvvv",
    )


def feed_own(chain, x, packet, g, ob, gain, bias, wo, fc1, b1, fc2, far):
    rows, d = x.shape
    columns = fc1.shape[0]
    width = columns // 2
    shard = width // 2

    def kernel(io, x_ref, oa_ref, g_ref, ob_ref, gain_ref, bias_ref, wo_ref, fc1_ref, b1_ref, fc2_ref, z1, du1, a1, g1,
               h_ref, a2_ref, z_ref, du_ref, keep_ref, send_ref, sums_ref):
        a2, z, du = feed_body(
            x_ref[...], oa_ref[:, d:], ob_ref[...], g_ref[...], wo_ref, gain_ref, bias_ref, fc1_ref, b1_ref, fc2_ref,
            h_ref, a2_ref, z_ref, du_ref,
        )
        z, du = z[:, :width], du[:, :width]
        first = dot_tn(du, a2) + dot_tn(du1[:, :width], a1[...])
        second = dot_tn(z, g_ref[...]) + dot_tn(z1[:, :width], g1[:, :d])
        for at, ref in enumerate((keep_ref, send_ref)):
            here = slice(at * shard, (at + 1) * shard)
            ref[0] = first[here].astype(BF16)
            ref[1] = second[here].astype(BF16)
        sums_ref[...] = jnp.sum(du.astype(F32), axis=0, keepdims=True) + jnp.sum(
            du1[:, :width].astype(F32), axis=0, keepdims=True
        )

    return chain.call(
        kernel, "feed_own", (x, packet, g, ob, gain, bias, wo, fc1, b1, fc2, *far),
        [f32(rows, d), bf16(rows, d), bf16(rows, columns), bf16(rows, columns), bf16(2, shard, d), bf16(2, shard, d),
         f32(1, width)], "v" * 14 + "-vvvvvvv",
    )


def feed_result(chain, z, fc2, h):
    def kernel(io, z_ref, fc2_ref, h_ref, out_ref):
        out_ref[...] = (h_ref[...] + dot_nn(z_ref[...], fc2_ref[...])).astype(BF16)

    return chain.call(kernel, "feed_result", (z, fc2, h), [bf16(*h.shape)], "vvv-w", limit=8)[0]


def backward(chain, args, own):
    h, kt = args[2], args[8]
    rows, d = h.shape
    width = kt.shape[0]
    mols, pairs = rows // LEN, width // PAIR

    def kernel(io, du_ref, fc1_ref, h_ref, g_ref, gain_ref, wo_ref, p_ref, qt_ref, kt_ref, v_ref,
               gh_ref, dp_ref, dh_ref=None, sums_ref=None):
        da2 = dot_nn(du_ref[...], fc1_ref[...])
        xh, r = normalise(h_ref[...])
        dh = g_ref[:, :d].astype(F32) + norm_back(da2, gain_ref[...][None, :], xh, r)
        if own:
            dh_ref[...] = dh
            sums_ref[0:1] = jnp.sum(da2 * xh, axis=0, keepdims=True)
            sums_ref[1:2] = jnp.sum(da2, axis=0, keepdims=True)
            io.flush(2)
        gh = dh.astype(BF16)
        gh_ref[...] = gh
        dot = dot_nt(wo_ref[:width], gh).astype(BF16)
        every = [(m, i) for m in range(mols) for i in range(pairs)]
        lanes = lambda m: slice(LEN * m, LEN * (m + 1))
        rows_of = lambda i: slice(PAIR * i, PAIR * (i + 1))
        dps, dss, dos = {}, {}, {}
        for m, i in every:
            low, before = pair_window(i, width)
            dos[m, i] = pair_blocks(dot[rows_of(i), lanes(m)])
            dps[m, i] = dot_nn(v_ref[lanes(m), low : low + 2 * LEN], placed(dos[m, i], before))
        for m, i in every:
            dv = dot_nt(dos[m, i], p_ref[m, i])
            dp_ref[pl.ds(2 * width + PAIR * i, PAIR), lanes(m)] = dv.astype(BF16)
        for m, i in every:
            p = p_ref[m, i].astype(F32)
            t = dps[m, i] * p
            dss[m, i] = (t - p * jnp.sum(t, axis=0, keepdims=True)).astype(BF16)
        for m, i in every:
            dq = diagonal(dot_nn(kt_ref[rows_of(i), lanes(m)], dss[m, i])) * SCALE
            dp_ref[rows_of(i), lanes(m)] = dq.astype(BF16)
            dk = dot_nt(pair_blocks(qt_ref[rows_of(i), lanes(m)]), dss[m, i]) * SCALE
            dp_ref[pl.ds(width + PAIR * i, PAIR), lanes(m)] = dk.astype(BF16)

    outs = [bf16(rows, d), bf16(3 * width, rows)] + ([f32(rows, d), f32(8, d)] if own else [])
    return chain.call(
        kernel, "attention_backward", args, outs, "v" * 10 + ("-vvvv" if own else "-vv"),
    )


def weight_grads(chain, name, shard, at, lefts, rights):
    d = rights[0][0].shape[1]
    args, count = [], len(lefts)
    for (u0, u1, _), (v0, v1) in zip(lefts, rights):
        args += [u0, u1, v0, v1]

    def kernel(io, *refs):
        out_ref = refs[-1]
        for c in range(count):
            u0, u1, v0, v1 = refs[4 * c : 4 * c + 4]
            rows = slice(lefts[c][2] + at * shard, lefts[c][2] + (at + 1) * shard)
            left = jnp.concatenate([u0[rows], u1[rows]], axis=1)
            right = jnp.concatenate([v0[...], v1[...]], axis=0)
            out_ref[c] = dot_nn(left, right).astype(BF16)

    return chain.call(kernel, name, args, [bf16(count, shard, d)], "v" * len(args) + "-v")[0]


def input_grads(chain, dps, w, xs, sums, bias):
    rows, d = xs[0].shape

    def kernel(io, dp0, dp1, w_ref, x0, x1, sums_ref, bias_ref, mine_ref, theirs_ref):
        w = w_ref[...].reshape(dp0.shape[0], d)
        theirs = dot_tn(dp1[...], w)
        theirs_ref[:rows] = theirs.astype(BF16)
        mine = dot_tn(dp0[...], w)
        mine_ref[...] = mine
        xh0, _ = normalise(x0[...].astype(F32))
        xh1, _ = normalise(x1[...].astype(F32))
        bias = bias_ref[...]
        vec = [
            jnp.sum(mine * xh0, axis=0, keepdims=True) + jnp.sum(theirs * xh1, axis=0, keepdims=True),
            jnp.sum(mine, axis=0, keepdims=True) + jnp.sum(theirs, axis=0, keepdims=True),
            sums_ref[0:2],
            jnp.concatenate([bias, jnp.zeros((1, d - bias.shape[1]), F32)], axis=1),
            jnp.zeros((11, d), F32),
        ]
        theirs_ref[rows:] = jnp.concatenate(vec, axis=0).astype(BF16)

    return chain.call(
        kernel, "input_grads", (*dps, w, *xs, sums, bias), [f32(rows, d), bf16(rows + 16, d)], "vvvvvvv-vv"
    )


def input_norm(chain, x, gain, mine, got, dh):
    rows, d = x.shape

    def kernel(io, x_ref, gain_ref, mine_ref, got_ref, dh_ref, out_ref):
        xh, r = normalise(x_ref[...].astype(F32))
        da1 = mine_ref[...] + got_ref[:rows].astype(F32)
        out_ref[...] = (dh_ref[...] + norm_back(da1, gain_ref[...][None, :], xh, r)).astype(BF16)

    return chain.call(
        kernel, "input_norm", (x, gain, mine, got, dh), [bf16(rows, d)], "vvvvv-w", limit=8
    )[0]


def plus(*terms):
    total = terms[0].astype(F32)
    for term in terms[1:]:
        total = total + term.astype(F32)
    return total.astype(BF16)


def vector_rows(chain, mine, got):
    rows, d = mine.shape

    def kernel(io, mine_ref, got_ref, out_ref):
        a, b = mine_ref[rows - 16 :], got_ref[rows - 16 :]
        same = lax.broadcasted_iota(jnp.int32, (16, d), 0) < 4
        out_ref[...] = plus(a, jnp.where(same, b.astype(F32), 0.0))

    return chain.call(kernel, "vector_rows", (mine, got), [bf16(16, d)], "vv-v", limit=4)[0]


def vector_cores(chain, mine, got, shard):
    def kernel(io, mine_ref, got_ref, out_ref):
        a, b = mine_ref[...].astype(F32), got_ref[...].astype(F32)
        turned = jnp.concatenate([b[:, shard : 2 * shard], b[:, :shard], b[:, 2 * shard :]], axis=1)
        same = lax.broadcasted_iota(jnp.int32, a.shape, 0) < 4
        out_ref[...] = plus(a, jnp.where(same, b, turned))

    return chain.call(kernel, "vector_cores", (mine, got), [bf16(*mine.shape)], "vv-v", limit=4)[0]


def sum_half(chain, bits, mine, got, apart):
    def kernel(io, bits_ref, mine_ref, got_ref, *outs):
        half, quarter = 1 - bits_ref[0], bits_ref[1]
        on_ref, kept_ref = outs if apart else (outs[0].at[0], outs[0].at[1])
        on_ref[...] = mine_ref[half, 1 - quarter] + got_ref[half, 1 - quarter]
        kept_ref[...] = mine_ref[half, quarter] + got_ref[half, quarter]

    rows, d = mine.shape[2:]
    outs = [bf16(rows, d)] * 2 if apart else [bf16(2, rows, d)]
    return chain.call(kernel, "sum_half", (bits, mine, got), outs, "svv-" + "v" * len(outs), limit=8)


def sum_quarter(chain, bits, mine, got, kept, *more, vec=()):
    rows, d = mine.shape[2:]
    arrays = [a[0] if isinstance(a, tuple) else a for a in more]

    def kernel(io, bits_ref, mine_ref, got_ref, *refs):
        *refs, out_ref = refs
        half = bits_ref[0]
        quarter = bits_ref[1] if kept else 1 - bits_ref[1]
        terms = [ref[a[1]] if isinstance(a, tuple) else ref[...] for a, ref in zip(more, refs)]
        out_ref[:rows] = plus(mine_ref[half, quarter], got_ref[half, quarter], *terms)
        if vec:
            out_ref[rows:] = refs[-1][...]

    args = (bits, mine, got, *arrays, *vec)
    return chain.call(
        kernel, "sum_quarter", args, [bf16(rows + (16 if vec else 0), d)], "s" + "v" * (len(args) - 1) + "-v",
        limit=8,
    )[0]


def sum_quarter_apart(chain, bits, mine, got, *more):
    rows, d = mine.shape[2:]
    arrays = [a[0] if isinstance(a, tuple) else a for a in more]

    def kernel(io, bits_ref, mine_ref, got_ref, *refs):
        *refs, upper_ref, lower_ref = refs
        half, quarter = bits_ref[0], bits_ref[1]
        terms = [ref[a[1]] if isinstance(a, tuple) else ref[...] for a, ref in zip(more, refs)]
        total = plus(mine_ref[half, quarter], got_ref[half, quarter], *terms)
        upper_ref[...] = total[: rows // 2]
        lower_ref[...] = total[rows // 2 :]

    args = (bits, mine, got, *arrays)
    return chain.call(
        kernel, "sum_quarter", args, [bf16(rows // 2, d)] * 2, "s" + "v" * (len(args) - 1) + "-vv", limit=8
    )


def side_by_side(chain, a, b, apart):
    rows, d = a.shape

    def kernel(io, a_ref, b_ref, *outs):
        first, second = outs if apart else (outs[0].at[:rows], outs[0].at[rows:])
        first[...] = a_ref[...]
        second[...] = b_ref[...]

    outs = [bf16(rows, d)] * 2 if apart else [bf16(2 * rows, d)]
    return chain.call(kernel, "side_by_side", (a, b), outs, "vv-" + "v" * len(outs), limit=8)


def sum_pairs(chain, *pairs):
    rows = [a.shape[0] for a, _ in pairs]

    def kernel(io, *refs):
        *refs, out_ref = refs
        start = 0
        for a_ref, b_ref in zip(refs[::2], refs[1::2]):
            out_ref[start : start + a_ref.shape[0]] = a_ref[...] + b_ref[...]
            start += a_ref.shape[0]

    args = [a for pair in pairs for a in pair]
    return chain.call(
        kernel, "sum_pairs", args, [bf16(sum(rows), args[0].shape[1])], "v" * len(args) + "-v", limit=8
    )[0]


def place_sums(chain, bits, quarters, rows, targets, outs, whole=(), vec=(), skip=0):
    d = quarters[0][0].shape[1]
    n = len(outs)
    arrays = []
    for a, *_ in quarters:
        if not any(a is b for b in arrays):
            arrays.append(a)
    which = [next(k for k, b in enumerate(arrays) if b is a) for a, *_ in quarters]

    def kernel(io, bits_ref, *refs):
        refs, (buf, sems) = refs[:-2], refs[-2:]
        ins = [refs[k] for k in which]
        refs = refs[len(arrays) + len(whole) :]
        out_refs, vec_refs = refs[:n], refs[n:]

        def each(step):
            for j, (_, _, half, quarter) in enumerate(quarters):
                if j < skip:
                    continue
                half = 1 - bits_ref[0] if half else bits_ref[0]
                quarter = 1 - bits_ref[1] if quarter else bits_ref[1]
                for at, (out, index, first) in enumerate(targets):
                    ref = out_refs[out]
                    ref = ref if index is None else ref.at[index]
                    ref = ref.at[first : first + rows]
                    copy = pltpu.make_async_copy(buf.at[j], ref, sems.at[j])
                    pl.when(2 * half + quarter == at)(functools.partial(step, copy))

        starts = [start for _, start, _, _ in quarters]
        for j, ref in enumerate(ins):
            if j >= skip:
                buf[j] = ref[starts[j] : starts[j] + rows].astype(F32)
        each(lambda copy: copy.start())
        if vec:
            a, b, c, e = (ref[x + rows : x + rows + 16].astype(F32) for ref, x in zip(ins, starts))
            total = jnp.where(bits_ref[5] == 0, (a + b) + (c + e), (a + c) + (b + e))
            for at, (length, ref) in enumerate(zip(vec, vec_refs)):
                ref[...] = total[at, :length]
        each(lambda copy: copy.wait())

    return chain.call(
        kernel, "place_sums", (bits, *arrays, *whole), [*outs, *(f32(length) for length in vec)],
        "s" + "v" * len(arrays) + "p" * len(whole) + "-" + "r" * n + "v" * len(vec), limit=8,
        aliases={1 + len(arrays) + j: j for j in range(len(whole))},
        scratch=[pltpu.VMEM((len(quarters), rows, d), F32), pltpu.SemaphoreType.DMA((len(quarters),))],
    )


def local(
    n_dp, n_tensor, tokens, node_counts, edge_counts, ln1_gain, ln1_bias, qkv_weight, out_weight,
    ln2_gain, ln2_bias, fc1_weight, fc1_bias, fc2_weight, out_grad,
):
    d = tokens.shape[1]
    shard = out_weight.shape[0]
    width = 2 * shard
    mols = tokens.shape[0] // LEN
    dp_at = lax.axis_index("dp")
    tensor_at = lax.axis_index("tensor")
    core = tensor_at % 2
    bit0 = dp_at % 2
    bit1 = (dp_at // 2) % 2
    bits = jnp.stack(
        [jnp.where(core == 0, bit0, bit1), jnp.where(core == 0, bit1, bit0), bit0, tensor_at * mols,
         (tensor_at ^ 2) * mols, core, bit1]
    ).astype(jnp.int32)
    chain = Chain()

    def swap_core(a):
        return lax.ppermute(a, "tensor", [(t, t ^ 1) for t in range(n_tensor)])

    def swap_y(a):
        return lax.ppermute(a, "tensor", [(t, t ^ 2) for t in range(n_tensor)])

    def swap_dp(a, mask0, mask1):
        pairs = [
            (p * n_tensor + t, (p ^ (mask1 if t % 2 else mask0)) * n_tensor + t)
            for p in range(n_dp)
            for t in range(n_tensor)
        ]
        return lax.ppermute(a, ("dp", "tensor"), pairs)

    swap_first = lambda a: swap_dp(a, 1, 2)
    swap_second = lambda a: swap_dp(a, 2, 1)
    far_masks = [1 << k for k in range(2, n_dp.bit_length() - 1)]

    w_got = swap_core(qkv_weight)
    x_got = swap_y(tokens)
    far_y = swap_y(pick(chain, bits, out_weight, fc1_weight, fc2_weight, fc1_bias))
    bias = jnp.pad(fc1_bias.reshape(1, -1), ((0, 15), (0, d - shard)))
    near, others = load(
        chain, out_weight, fc1_weight, fc2_weight, bias,
        (tokens, out_grad, ln1_gain, ln1_bias, ln2_gain, ln2_bias),
    )
    near = (near, swap_core(near))
    tokens, out_grad, ln1_gain, ln1_bias, ln2_gain, ln2_bias = others

    counts = (node_counts, edge_counts)
    norm1 = (ln1_gain, ln1_bias)
    a1_0, qt_0, kt_0, v_0, p_0, ot_0, packet, w_qkv = attention(
        chain, bits, 3, *counts, tokens, *norm1, (qkv_weight, w_got), out_grad
    )
    packet_got = swap_y(packet)
    far_y, short = hold(chain, far_y)
    far_x, far_z = swap_dp(short, 1, 1), swap_dp(short, 2, 2)
    far_z, pair = pair_up(chain, far_x, far_z)
    far_xz = swap_dp(far_z, 1, 1)
    a1_1, qt_1, kt_1, v_1, p_1, ot_1, o_1, wo, fc1, fc2 = attention(
        chain, bits, 4, *counts, x_got, *norm1, w_qkv, near=near
    )
    o_got = swap_y(o_1)
    spacer(chain)
    fars = (far_y, pair, far_xz)
    fars += tuple(swap_core(a) for a in fars)
    norm2 = (ln2_gain, ln2_bias)
    wo, fc1, fc2 = pack_far(chain, bits, (wo, fc1, fc2), fars)
    low, far_low = 3 * shard, 3 * shard // 4
    biases = ((near[0], low), (near[1], low), (fars[0], far_low), (fars[3], far_low))

    class Sum:
        def __init__(self, count, keep, got, apart, early):
            self.size = count * shard // 4
            self.apart, self.early = apart, early
            view = lambda a: a.reshape(2, 2, self.size, d)
            self.parts = (view(keep), view(got))

        def first(self):
            sent = sum_half(chain, bits, *self.parts, self.apart)
            got = [swap_first(a) for a in sent]
            self.on, self.kept = got if self.apart else ((got[0], 0), (got[0], 1))

        def second(self):
            self.got = swap_second(sum_quarter(chain, bits, *self.parts, False, self.on))

        def third(self, *vec):
            self.sum = sum_quarter(chain, bits, *self.parts, True, self.kept, self.got, vec=vec)
            self.got = swap_dp(self.sum, far_masks[0], far_masks[0])

        def third_apart(self):
            self.sums = sum_quarter_apart(chain, bits, *self.parts, self.kept, self.got)
            self.gots = [swap_dp(a, far_masks[0], far_masks[0]) for a in self.sums]
            self.halves = [None, None]

        def fourth_apart(self, at, *vec):
            self.sum, self.got = self.sums[at], self.gots[at]
            self.fourth(*vec)
            self.halves[at] = self.quarters

        def fourth(self, *vec):
            a = sum_pairs(chain, (self.sum, self.got), *vec)
            for mask in far_masks[1:]:
                a = sum_pairs(chain, (a, swap_dp(a, mask, mask)))
            b = swap_second(a)
            if self.early == 1:
                self.quarters = [(a, 0, 0, 0), (b, 0, 0, 1), (swap_first(a), 0, 1, 0), (swap_first(b), 0, 1, 1)]
            self.last = (a, b)

        def fifth(self):
            if self.early == 0:
                (a,) = side_by_side(chain, *self.last, False)
                b = swap_first(a)
                rows = a.shape[0] // 2
                self.quarters = [(a, 0, 0, 0), (a, rows, 0, 1), (b, 0, 1, 0), (b, rows, 1, 1)]
            if self.early == 2:
                a, b = side_by_side(chain, *self.last, True)
                self.quarters = [(a, 0, 0, 0), (b, 0, 0, 1), (swap_first(a), 0, 1, 0), (swap_first(b), 0, 1, 1)]

    h_1, a2_1, z_1, du_1, b1 = feed_far(chain, x_got, o_1, packet_got, *norm2, wo, fc1, fc2, biases)
    gh_1, dp_1 = backward(chain, (du_1, fc1, h_1, packet_got, ln2_gain, wo, p_1, qt_1, kt_1, v_1), False)
    h_0, a2_0, z_0, du_0, keep_r, send_r, bias_sums = feed_own(
        chain, tokens, packet, out_grad, o_got, *norm2, wo, fc1, b1, fc2, (z_1, du_1, a2_1, packet_got)
    )
    gh_0, dp_0, dh, sums = backward(chain, (du_0, fc1, h_0, out_grad, ln2_gain, wo, p_0, qt_0, kt_0, v_0), True)
    r = Sum(2, keep_r, swap_core(send_r), True, 1)
    r.first()
    a1s = (a1_0, a1_1)
    lefts = [(dp_0, dp_1, c * width) for c in range(3)] + [(ot_0, ot_1, 0)]
    rights = [a1s] * 3 + [(gh_0, gh_1)]
    got_q = swap_core(weight_grads(chain, "weight_grads", shard, 1, lefts, rights))
    q = Sum(4, weight_grads(chain, "weight_grads", shard, 0, lefts, rights), got_q, True, 2)
    r.second()
    q.first()
    r.third()
    q.second()
    da1_mine, da1_theirs = input_grads(chain, (dp_0, dp_1), w_qkv, (tokens, x_got), sums, bias_sums)
    da1_got = swap_y(da1_theirs)
    r.fourth()
    result = feed_result(chain, z_0, fc2, h_0)
    q.third()
    vec = vector_rows(chain, da1_theirs, da1_got)
    vec_got = swap_core(vec)
    r.fifth()
    halves = [(c, None, half * shard // 2) for c in range(2) for half in range(2)]
    grad_fc1, grad_fc2 = place_sums(chain, bits, r.quarters, r.size, halves, [f32(shard, d)] * 2)
    vec = vector_cores(chain, vec, vec_got, shard)
    vec_got = swap_dp(vec, far_masks[0], far_masks[0])
    q.fourth((vec, vec_got))
    grad_tokens = input_norm(chain, tokens, ln1_gain, da1_mine, da1_got, dh)
    q.fifth()
    each = [(0, 0, 0), (0, 1, 0), (0, 2, 0), (1, None, 0)]
    outs = [f32(3, shard, d), f32(shard, d)]
    grads = place_sums(chain, bits, q.quarters[:2], q.size, each, outs)
    grads = place_sums(chain, bits, q.quarters[:3], q.size, each, outs, grads, skip=2)
    grad_qkv, grad_out, gain1, bias1, gain2, bias2, grad_b = place_sums(
        chain, bits, q.quarters, q.size, each, outs, grads, (d, d, d, d, shard), 3
    )
    return (
        result, grad_tokens, gain1, bias1, grad_qkv, grad_out, gain2, bias2, grad_fc1, grad_b, grad_fc2,
    )


def solution(mesh):
    tokens = P(("dp", "tensor"), None)
    rows = P("tensor", None)
    qkv = P(None, "tensor", None)
    in_specs = (
        tokens, P("dp"), P("dp"), P(), P(), qkv, rows, P(), P(), rows, P("tensor"), rows, tokens,
    )
    out_specs = (tokens, tokens, P(), P(), qkv, rows, P(), P(), rows, P("tensor"), rows)
    step = functools.partial(local, mesh.shape["dp"], mesh.shape["tensor"])
    return jax.shard_map(step, mesh=mesh, in_specs=in_specs, out_specs=out_specs, check_vma=False)
```

```python
import functools

import jax
import jax.numpy as jnp
from jax import lax
from jax.experimental import pallas as pl
from jax.experimental.pallas import tpu as pltpu
from jax.sharding import PartitionSpec as P

HEAD_DIM = 24
LEN = 128
PAIR = 2 * HEAD_DIM
EPSILON = 1e-05
SCALE = HEAD_DIM ** (-0.5)
LOG2E = 1.4426950408889634
F32 = jnp.float32
BF16 = jnp.bfloat16
MIB = 1024 * 1024


def dot_nn(a, b):
    return lax.dot_general(a, b, (((1,), (0,)), ((), ())), preferred_element_type=F32)


def dot_nt(a, b):
    return lax.dot_general(a, b, (((1,), (1,)), ((), ())), preferred_element_type=F32)


def dot_tn(a, b):
    return lax.dot_general(a, b, (((0,), (0,)), ((), ())), preferred_element_type=F32)


def normalise(v):
    centered = v - jnp.mean(v, axis=-1, keepdims=True)
    r = lax.rsqrt(jnp.mean(centered * centered, axis=-1, keepdims=True) + EPSILON)
    return centered * r, r


def norm_back(da, gain, xh, r):
    e = da * gain
    return r * (
        e - jnp.mean(e, axis=-1, keepdims=True) - xh * jnp.mean(e * xh, axis=-1, keepdims=True)
    )


def pair_blocks(rows):
    rows = rows.astype(F32)
    none = jnp.zeros((HEAD_DIM, LEN), F32)
    left = jnp.concatenate([rows[:HEAD_DIM], none], axis=0)
    right = jnp.concatenate([none, rows[HEAD_DIM:]], axis=0)
    return jnp.concatenate([left, right], axis=1).astype(BF16)


def pair_window(i, width):
    low = min(PAIR * i // LEN * LEN, width - 2 * LEN)
    return low, PAIR * i - low


def placed(block, before):
    parts = []
    if before:
        parts.append(jnp.zeros((before, 2 * LEN), BF16))
    parts.append(block)
    after = 2 * LEN - PAIR - before
    if after:
        parts.append(jnp.zeros((after, 2 * LEN), BF16))
    return jnp.concatenate(parts, axis=0)


def diagonal(both):
    return jnp.concatenate([both[:HEAD_DIM, :LEN], both[HEAD_DIM:, LEN:]], axis=0)


STRIP = 256
COSTS = (0, 0, 100, 0, 0, 30, 30, 0, 0, 0, 0, 0, 100, 0, 0, 0, 200, 0, 60, 0, 0, 30, 0, 0, 0, 0, 0, 0, 0, 0, 0, 0, 0)


class IO:
    def __init__(self, reads, writes):
        self.reads, self.writes = reads, writes
        self.started = set()

    def wait(self, *args):
        for j in args:
            if j in self.reads:
                self.reads[j].wait()

    def flush(self, *outs):
        for j in outs:
            if j in self.writes:
                self.started.add(j)
                self.writes[j].start()

    def finish(self):
        self.flush(*(j for j in self.writes if j not in self.started))
        for copy in self.writes.values():
            copy.wait()


def pinned(a):
    return pltpu.with_memory_space_constraint(a, pltpu.HBM)


class Chain:
    def __init__(self):
        self.token, self.calls = None, 0

    def call(self, kernel, name, args, outs, kinds, scratch=(), limit=16, aliases={}):
        ins, out_kinds = kinds.split("-")
        cost = COSTS[min(self.calls, len(COSTS) - 1)]
        self.calls += 1
        assert len(ins) == len(args) and len(out_kinds) == len(outs)
        hbm = pl.BlockSpec(memory_space=pltpu.HBM)
        vmem = pl.BlockSpec(memory_space=pltpu.VMEM)
        smem = pl.BlockSpec(memory_space=pltpu.SMEM)
        spec = lambda kind: {"s": smem, "v": vmem}.get(kind, hbm)
        tokens = () if self.token is None else (self.token,)
        staged = [j for j, kind in enumerate(ins) if kind in "hcl"]
        written = [j for j, kind in enumerate(out_kinds) if kind == "w"]
        memory = lambda kind: pltpu.SMEM if kind == "c" else pltpu.VMEM
        buffers = [memory(ins[j])(args[j].shape, args[j].dtype) for j in staged]
        buffers += [pltpu.VMEM(outs[j].shape, outs[j].dtype) for j in written]
        n_in, n_out, n_buf = len(args) + len(tokens), len(outs), len(buffers)

        def body(*refs):
            arg_refs = list(refs[: len(args)])
            out_refs = list(refs[n_in : n_in + n_out])
            token_ref = refs[n_in + n_out]
            own = refs[n_in + n_out + 1 :]
            bufs, sems, extra = own[:n_buf], own[n_buf], own[n_buf + 1 :]
            reads, writes = {}, {}
            for at, j in enumerate(staged):
                reads[j] = pltpu.make_async_copy(arg_refs[j], bufs[at], sems.at[at])
                reads[j].start()
                arg_refs[j] = bufs[at]
            for at, j in enumerate(written, len(staged)):
                writes[j] = pltpu.make_async_copy(bufs[at], out_refs[j], sems.at[at])
                out_refs[j] = bufs[at]
            io = IO(reads, writes)
            io.wait(*(j for j in staged if ins[j] == "h"))
            token_ref[...] = jnp.zeros_like(token_ref)
            kernel(io, *arg_refs, *out_refs, *extra)
            io.finish()

        *results, self.token = pl.pallas_call(
            body,
            in_specs=[spec(kind) for kind in ins] + [vmem] * len(tokens),
            out_specs=[spec(kind) for kind in out_kinds] + [vmem],
            out_shape=[*outs, f32(8, 128)],
            input_output_aliases=aliases,
            scratch_shapes=[*buffers, pltpu.SemaphoreType.DMA((max(n_buf, 1),)), *scratch],
            compiler_params=pltpu.CompilerParams(vmem_limit_bytes=limit * MIB),
            cost_estimate=pl.CostEstimate(flops=cost * 10**8, bytes_accessed=10**8, transcendentals=0),
            name=name,
        )(*(pinned(a) if kind in "hclp" else a for a, kind in zip(args, ins)), *tokens)
        return results


def bf16(*shape):
    return jax.ShapeDtypeStruct(shape, BF16)


def f32(*shape):
    return jax.ShapeDtypeStruct(shape, F32)


def copies(sems, pairs):
    started = [pltpu.make_async_copy(a, b, sems.at[j]) for j, (a, b) in enumerate(pairs)]
    for copy in started:
        copy.start()
    return started


def finish(started):
    for copy in started:
        copy.wait()


def attention(chain, bits, place, nodes, edges, x, gain, bias, w, near=()):
    rows, d = x.shape
    apart = isinstance(w, tuple)
    width = 2 * w[0].shape[1] if apart else w.shape[1]
    shard = width // 2
    pairs = width // PAIR
    mols = rows // LEN

    def kernel(io, bits_ref, nodes_ref, edges_ref, x_ref, gain_ref, bias_ref, *refs):
        started = []
        if not apart:
            w_ref, near0, near1, *refs, wo_ref, fc1_ref, fc2_ref, sems = refs
            a1_ref, qt_ref, kt_ref, v_ref, p_ref, ot_ref, o_ref = refs
            pairs_w = []
            for at, ref in enumerate((near0, near1)):
                for c, out in enumerate((wo_ref, fc1_ref, fc2_ref)):
                    part = ref.at[c * shard : (c + 1) * shard]
                    pairs_w.append((part, out.at[at * shard : (at + 1) * shard]))
            started = copies(sems, pairs_w)
        else:
            own, got, *refs, w_ref, sems = refs
            a1_ref, qt_ref, kt_ref, v_ref, p_ref, ot_ref, o_ref = refs
            pairs_w = [(own, w_ref.at[:, :shard]), (got, w_ref.at[:, shard:])]
            near_w = copies(sems, pairs_w)
        xh, _ = normalise(x_ref[...].astype(F32))
        a1 = (xh * gain_ref[...][None, :] + bias_ref[...][None, :]).astype(BF16)
        a1_ref[...] = a1
        if apart:
            finish(near_w)
        qt = dot_nt(w_ref[0], a1).astype(BF16)
        keys = dot_nt(a1, w_ref[1]).astype(BF16)
        vt = dot_nt(w_ref[2], a1).astype(BF16)
        qt_ref[...] = qt
        every = [(m, i) for m in range(mols) for i in range(pairs)]
        lanes = lambda m: slice(LEN * m, LEN * (m + 1))
        rows_of = lambda i: slice(PAIR * i, PAIR * (i + 1))
        scores, probs = {}, {}
        for m, i in every:
            low, before = pair_window(i, width)
            rhs = placed(pair_blocks(qt[rows_of(i), lanes(m)]), before)
            scores[m, i] = dot_nn(keys[lanes(m), low : low + 2 * LEN], rhs)
        io.wait(1, 2)
        for m in range(mols):
            mol = bits_ref[place] + m
            count = 1 + nodes_ref[mol] + edges_ref[mol]
            valid = lax.broadcasted_iota(jnp.int32, (LEN, 2 * LEN), 0) < count
            for i in range(pairs):
                s = jnp.where(valid, scores[m, i], -1e30)
                e = jnp.exp2((s - jnp.max(s, axis=0, keepdims=True)) * (SCALE * LOG2E))
                p = (e * (1.0 / jnp.sum(e, axis=0, keepdims=True))).astype(BF16)
                p_ref[m, i] = p
                probs[m, i] = p
        for m, i in every:
            both = dot_nn(vt[rows_of(i), lanes(m)], probs[m, i])
            ot_ref[rows_of(i), lanes(m)] = diagonal(both).astype(BF16)
        o_ref[...] = ot_ref[...].T
        kt_ref[...] = dot_nt(w_ref[1], a1).astype(BF16)
        v_ref[...] = dot_nt(a1, w_ref[2]).astype(BF16)
        finish(started)

    outs = [
        bf16(rows, d), bf16(width, rows), bf16(width, rows), bf16(rows, width),
        bf16(mols, pairs, LEN, 2 * LEN), bf16(width, rows),
    ]
    args = (bits, nodes, edges, x, gain, bias)
    if not apart:
        return chain.call(
            kernel, "attention_forward", (*args, w, *near), [*outs, bf16(rows, width), bf16(2 * width, d), bf16(2 * width, d), bf16(2 * width, d)],
            "sccvvvvvv-vvvvvvvvvv", scratch=[pltpu.SemaphoreType.DMA((6,))],
        )
    return chain.call(
        kernel, "attention_forward", (*args, *w), [*outs, bf16(rows, width), bf16(3, width, d)],
        "sccvvvpr-vvvvvvvv", scratch=[pltpu.SemaphoreType.DMA((2,))],
    )


def pick(chain, bits, wo, fc1, fc2, bias):
    shard, d = wo.shape
    rows = 3 * shard // 4
    strips = d // STRIP

    def kernel(io, bits_ref, wo_ref, fc1_ref, fc2_ref, bias_ref, out_ref, sems):
        refs = (wo_ref, fc1_ref, fc2_ref)

        def part(quarter):
            pairs = []
            for c, first, at, n in quarter_rows(quarter, shard):
                for k in range(strips):
                    source = refs[c].at[first : first + n, k * STRIP : (k + 1) * STRIP]
                    pairs.append((source, out_ref.at[k * rows + at : k * rows + at + n]))
            started = copies(sems, pairs)
            io.wait(4)
            out_ref[strips * rows :] = jnp.concatenate(
                [jnp.broadcast_to(bias_ref[...].astype(F32)[None, :], (16, shard)), jnp.zeros((16, STRIP - shard), F32)],
                axis=1,
            ).astype(BF16)
            finish(started)

        which = 2 * bits_ref[2] + bits_ref[6]
        for at in range(4):
            pl.when(which == at)(functools.partial(part, at))

    return chain.call(
        kernel, "pick", (bits, wo, fc1, fc2, bias), [bf16(strips * rows + 16, STRIP)], "spppl-v", limit=4,
        scratch=[pltpu.SemaphoreType.DMA((2 * strips,))],
    )[0]


def quarter_rows(quarter, shard):
    size = 3 * shard // 4
    found, at = [], 0
    while at < size:
        which, first = divmod(quarter * size + at, shard)
        n = min(size - at, shard - first)
        found.append((which, first, at, n))
        at += n
    return found


def hold(chain, a, d):
    strips = d // STRIP
    rows = (a.shape[0] - 16) // strips

    def kernel(io, a_ref, out_ref, short_ref):
        for k in range(strips):
            strip = a_ref[k * rows : (k + 1) * rows]
            out_ref[:rows, k * STRIP : (k + 1) * STRIP] = strip
            short_ref[:, k * STRIP : (k + 1) * STRIP] = strip
        out_ref[rows:] = widened(a_ref[strips * rows :], d)

    return chain.call(kernel, "hold", (a,), [bf16(rows + 16, d), bf16(rows, d)], "v-vv", limit=4)


def widened(a, d):
    return jnp.concatenate([a, jnp.zeros((a.shape[0], d - a.shape[1]), a.dtype)], axis=1)


def pair_up(chain, a, b):
    def kernel(io, a_ref, b_ref, out_ref, both_ref):
        out_ref[...] = b_ref[...]
        both_ref[0] = a_ref[...]
        both_ref[1] = b_ref[...]

    return chain.call(kernel, "pair_up", (a, b), [bf16(*b.shape), bf16(2, *a.shape)], "vv-vv", limit=4)


def spacer(chain):
    def kernel(io):
        pass

    chain.call(kernel, "spacer", (), [], "-", limit=2)


def load(chain, out_weight, fc1_weight, fc2_weight, picked, others):
    shard, d = out_weight.shape
    n = len(others)

    def kernel(io, wo, fc1, fc2, picked_ref, *refs):
        others_in, (near_ref, *others_out, sems) = refs[:n], refs[n:]
        near_ref[3 * shard :] = widened(picked_ref[picked.shape[0] - 16 :], d)
        rows = lambda at: near_ref.at[at * shard : (at + 1) * shard]
        near = [(wo, rows(0)), (fc1, rows(1)), (fc2, rows(2))]
        finish(copies(sems, near + list(zip(others_in, others_out))))

    near, *others = chain.call(
        kernel, "load", (out_weight, fc1_weight, fc2_weight, picked, *others),
        [bf16(3 * shard + 16, d)] + [jax.ShapeDtypeStruct(a.shape, a.dtype) for a in others],
        "pppv" + "p" * n + "-v" + "v" * n, limit=4, scratch=[pltpu.SemaphoreType.DMA((3 + n,))],
    )
    return near, others


def feed_body(part, ob, dz, wo_ref, gain_ref, bias_ref, fc1_ref, b1, h_ref, a2_ref, z_ref, du_ref):
    h = part + dot_nn(ob, wo_ref[wo_ref.shape[0] // 2 :])
    h_ref[...] = h
    xh, _ = normalise(h)
    a2 = (xh * gain_ref[...][None, :] + bias_ref[...][None, :]).astype(BF16)
    a2_ref[...] = a2
    u = dot_nt(a2, fc1_ref[...]) + b1
    phi = 0.5 * (1.0 + lax.erf(u * (0.5**0.5)))
    slope = phi + u * (jnp.exp(-0.5 * u * u) * 0.3989422804014327)
    du_ref[...] = (dz * slope).astype(BF16)
    z_ref[...] = (u * phi).astype(BF16)


def pack_far(chain, bits, weights, fars):
    rows, d = weights[0].shape
    shard = rows // 4

    def kernel(io, bits_ref, wo_in, fc1_in, fc2_in, y0, pair0, xz0, y1, pair1, xz1, *outs):
        def placed_at(which):
            for at, (y, pair, xz) in enumerate(((y0, pair0, xz0), (y1, pair1, xz1))):
                for turn, ref in enumerate((y, pair.at[1], pair.at[0], xz)):
                    for c, first, start, n in quarter_rows(which ^ turn, shard):
                        row = (2 + at) * shard + first
                        outs[c][row : row + n] = ref[start : start + n]

        which = 2 * bits_ref[2] + bits_ref[6]
        for at in range(4):
            pl.when(which == at)(functools.partial(placed_at, at))

    return chain.call(
        kernel, "pack_far", (bits, *weights, *fars), [bf16(rows, d)] * 3, "s" + "v" * 9 + "-vvv", limit=4,
        aliases={1: 0, 2: 1, 3: 2},
    )


def feed_in(chain, xs, os, gs, wo, fc2, biases):
    rows, d = xs[0].shape
    columns = fc2.shape[0]
    shard = columns // 4

    def kernel(io, x0, x1, o0, o1, g0, g1, wo_ref, fc2_ref, *refs):
        b_refs, (h0, h1, dz0, dz1, b1_ref) = refs[:4], refs[4:]
        for x_ref, o_ref, h_ref in ((x0, o0, h0), (x1, o1, h1)):
            h_ref[...] = x_ref[...].astype(F32) + dot_nn(o_ref[...], wo_ref[: o_ref.shape[1]])
        for g_ref, dz_ref in ((g0, dz0), (g1, dz1)):
            dz_ref[...] = dot_nt(g_ref[...], fc2_ref[...])
        parts = [ref[row : row + 1, :shard].astype(F32) for ref, (_, row) in zip(b_refs, biases)]
        b1_ref[...] = jnp.concatenate(parts, axis=1)

    return chain.call(
        kernel, "feed_in", (*xs, *os, *gs, wo, fc2, *(a for a, _ in biases)),
        [f32(rows, d)] * 2 + [f32(rows, columns)] * 2 + [f32(1, columns)], "v" * 12 + "-vvvvv",
    )


def feed_far(chain, h, ob, dz, g, gain, bias, wo, fc1, b1):
    rows, d = h.shape
    columns = fc1.shape[0]
    width = columns // 2

    def kernel(io, part_ref, ob_ref, dz_ref, g_ref, gain_ref, bias_ref, wo_ref, fc1_ref, b1_ref,
               h_ref, du_ref, first_ref, second_ref, a2_ref, z_ref):
        feed_body(
            part_ref[...], ob_ref[...], dz_ref[...], wo_ref, gain_ref, bias_ref, fc1_ref, b1_ref[...], h_ref, a2_ref,
            z_ref, du_ref,
        )
        first_ref[...] = dot_tn(du_ref[:, :width], a2_ref[...])
        second_ref[...] = dot_tn(z_ref[:, :width], g_ref[...])

    return chain.call(
        kernel, "feed_far", (h, ob, dz, g, gain, bias, wo, fc1, b1),
        [f32(rows, d), bf16(rows, columns), f32(width, d), f32(width, d)], "v" * 9 + "-vvvv",
        scratch=[pltpu.VMEM((rows, d), BF16), pltpu.VMEM((rows, columns), BF16)],
    )


def feed_own(chain, h, ob, dz, g, gain, bias, wo, fc1, b1, far):
    rows, d = h.shape
    columns = fc1.shape[0]
    width = columns // 2
    shard = width // 2

    def kernel(io, part_ref, ob_ref, dz_ref, g_ref, gain_ref, bias_ref, wo_ref, fc1_ref, b1_ref, du1, first1, second1,
               h_ref, z_ref, du_ref, keep_ref, send_ref, sums_ref, a2_ref):
        feed_body(
            part_ref[...], ob_ref[...], dz_ref[...], wo_ref, gain_ref, bias_ref, fc1_ref, b1_ref[...], h_ref, a2_ref,
            z_ref, du_ref,
        )
        du = du_ref[:, :width]
        first = dot_tn(du, a2_ref[...]) + first1[...]
        second = dot_tn(z_ref[:, :width], g_ref[...]) + second1[...]
        for at, ref in enumerate((keep_ref, send_ref)):
            here = slice(at * shard, (at + 1) * shard)
            ref[0] = first[here].astype(BF16)
            ref[1] = second[here].astype(BF16)
        sums_ref[...] = jnp.sum(du.astype(F32), axis=0, keepdims=True) + jnp.sum(
            du1[:, :width].astype(F32), axis=0, keepdims=True
        )

    return chain.call(
        kernel, "feed_own", (h, ob, dz, g, gain, bias, wo, fc1, b1, *far),
        [f32(rows, d), bf16(rows, columns), bf16(rows, columns), bf16(2, shard, d), bf16(2, shard, d), f32(1, width)],
        "v" * 12 + "-vvvvvv", scratch=[pltpu.VMEM((rows, d), BF16)],
    )


def feed_result(chain, z, fc2, h):
    def kernel(io, z_ref, fc2_ref, h_ref, out_ref):
        out_ref[...] = (h_ref[...] + dot_nn(z_ref[...], fc2_ref[...])).astype(BF16)

    return chain.call(kernel, "feed_result", (z, fc2, h), [bf16(*h.shape)], "vvv-w", limit=8)[0]


def backward(chain, args, own):
    h, kt = args[2], args[8]
    rows, d = h.shape
    width = kt.shape[0]
    mols, pairs = rows // LEN, width // PAIR

    def kernel(io, du_ref, fc1_ref, h_ref, g_ref, gain_ref, wo_ref, p_ref, qt_ref, kt_ref, v_ref,
               gh_ref, dp_ref, dh_ref=None, sums_ref=None):
        da2 = dot_nn(du_ref[...], fc1_ref[...])
        xh, r = normalise(h_ref[...])
        dh = g_ref[:, :d].astype(F32) + norm_back(da2, gain_ref[...][None, :], xh, r)
        if own:
            dh_ref[...] = dh
            sums_ref[0:1] = jnp.sum(da2 * xh, axis=0, keepdims=True)
            sums_ref[1:2] = jnp.sum(da2, axis=0, keepdims=True)
            io.flush(2)
        gh = dh.astype(BF16)
        gh_ref[...] = gh
        dot = dot_nt(wo_ref[:width], gh).astype(BF16)
        every = [(m, i) for m in range(mols) for i in range(pairs)]
        lanes = lambda m: slice(LEN * m, LEN * (m + 1))
        rows_of = lambda i: slice(PAIR * i, PAIR * (i + 1))
        dps, dss, dos = {}, {}, {}
        for m, i in every:
            low, before = pair_window(i, width)
            dos[m, i] = pair_blocks(dot[rows_of(i), lanes(m)])
            dps[m, i] = dot_nn(v_ref[lanes(m), low : low + 2 * LEN], placed(dos[m, i], before))
        for m, i in every:
            dv = dot_nt(dos[m, i], p_ref[m, i])
            dp_ref[pl.ds(2 * width + PAIR * i, PAIR), lanes(m)] = dv.astype(BF16)
        for m, i in every:
            p = p_ref[m, i].astype(F32)
            t = dps[m, i] * p
            dss[m, i] = (t - p * jnp.sum(t, axis=0, keepdims=True)).astype(BF16)
        for m, i in every:
            dq = diagonal(dot_nn(kt_ref[rows_of(i), lanes(m)], dss[m, i])) * SCALE
            dp_ref[rows_of(i), lanes(m)] = dq.astype(BF16)
            dk = dot_nt(pair_blocks(qt_ref[rows_of(i), lanes(m)]), dss[m, i]) * SCALE
            dp_ref[pl.ds(width + PAIR * i, PAIR), lanes(m)] = dk.astype(BF16)

    outs = [bf16(rows, d), bf16(3 * width, rows)] + ([f32(rows, d), f32(8, d)] if own else [])
    return chain.call(
        kernel, "attention_backward", args, outs, "v" * 10 + ("-vvvv" if own else "-vv"),
    )


def weight_grads(chain, name, shard, at, lefts, rights):
    d = rights[0][0].shape[1]
    args, count = [], len(lefts)
    for (u0, u1, _), (v0, v1) in zip(lefts, rights):
        args += [u0, u1, v0, v1]

    def kernel(io, *refs):
        out_ref = refs[-1]
        for c in range(count):
            u0, u1, v0, v1 = refs[4 * c : 4 * c + 4]
            rows = slice(lefts[c][2] + at * shard, lefts[c][2] + (at + 1) * shard)
            left = jnp.concatenate([u0[rows], u1[rows]], axis=1)
            right = jnp.concatenate([v0[...], v1[...]], axis=0)
            out_ref[c] = dot_nn(left, right).astype(BF16)

    return chain.call(kernel, name, args, [bf16(count, shard, d)], "v" * len(args) + "-v")[0]


def input_grads(chain, dps, w, xs, sums, bias):
    rows, d = xs[0].shape

    def kernel(io, dp0, dp1, w_ref, x0, x1, sums_ref, bias_ref, mine_ref, theirs_ref):
        w = w_ref[...].reshape(dp0.shape[0], d)
        theirs = dot_tn(dp1[...], w)
        theirs_ref[:rows] = theirs.astype(BF16)
        mine = dot_tn(dp0[...], w)
        mine_ref[...] = mine
        xh0, _ = normalise(x0[...].astype(F32))
        xh1, _ = normalise(x1[...].astype(F32))
        bias = bias_ref[...]
        vec = [
            jnp.sum(mine * xh0, axis=0, keepdims=True) + jnp.sum(theirs * xh1, axis=0, keepdims=True),
            jnp.sum(mine, axis=0, keepdims=True) + jnp.sum(theirs, axis=0, keepdims=True),
            sums_ref[0:2],
            jnp.concatenate([bias, jnp.zeros((1, d - bias.shape[1]), F32)], axis=1),
            jnp.zeros((11, d), F32),
        ]
        theirs_ref[rows:] = jnp.concatenate(vec, axis=0).astype(BF16)

    return chain.call(
        kernel, "input_grads", (*dps, w, *xs, sums, bias), [f32(rows, d), bf16(rows + 16, d)], "vvvvvvv-vv"
    )


def input_norm(chain, x, gain, mine, got, dh):
    rows, d = x.shape

    def kernel(io, x_ref, gain_ref, mine_ref, got_ref, dh_ref, out_ref):
        xh, r = normalise(x_ref[...].astype(F32))
        da1 = mine_ref[...] + got_ref[:rows].astype(F32)
        out_ref[...] = (dh_ref[...] + norm_back(da1, gain_ref[...][None, :], xh, r)).astype(BF16)

    return chain.call(
        kernel, "input_norm", (x, gain, mine, got, dh), [bf16(rows, d)], "vvvvv-w", limit=8
    )[0]


def plus(*terms):
    total = terms[0].astype(F32)
    for term in terms[1:]:
        total = total + term.astype(F32)
    return total.astype(BF16)


def vector_rows(chain, mine, got):
    rows, d = mine.shape

    def kernel(io, mine_ref, got_ref, out_ref):
        a, b = mine_ref[rows - 16 :], got_ref[rows - 16 :]
        same = lax.broadcasted_iota(jnp.int32, (16, d), 0) < 4
        out_ref[...] = plus(a, jnp.where(same, b.astype(F32), 0.0))

    return chain.call(kernel, "vector_rows", (mine, got), [bf16(16, d)], "vv-v", limit=4)[0]


def vector_cores(chain, mine, got, shard):
    def kernel(io, mine_ref, got_ref, out_ref):
        a, b = mine_ref[...].astype(F32), got_ref[...].astype(F32)
        turned = jnp.concatenate([b[:, shard : 2 * shard], b[:, :shard], b[:, 2 * shard :]], axis=1)
        same = lax.broadcasted_iota(jnp.int32, a.shape, 0) < 4
        out_ref[...] = plus(a, jnp.where(same, b, turned))

    return chain.call(kernel, "vector_cores", (mine, got), [bf16(*mine.shape)], "vv-v", limit=4)[0]


def sum_half(chain, bits, mine, got, apart):
    def kernel(io, bits_ref, mine_ref, got_ref, *outs):
        half, quarter = 1 - bits_ref[0], bits_ref[1]
        on_ref, kept_ref = outs if apart else (outs[0].at[0], outs[0].at[1])
        on_ref[...] = mine_ref[half, 1 - quarter] + got_ref[half, 1 - quarter]
        kept_ref[...] = mine_ref[half, quarter] + got_ref[half, quarter]

    rows, d = mine.shape[2:]
    outs = [bf16(rows, d)] * 2 if apart else [bf16(2, rows, d)]
    return chain.call(kernel, "sum_half", (bits, mine, got), outs, "svv-" + "v" * len(outs), limit=8)


def sum_quarter(chain, bits, mine, got, kept, *more, vec=()):
    rows, d = mine.shape[2:]
    arrays = [a[0] if isinstance(a, tuple) else a for a in more]

    def kernel(io, bits_ref, mine_ref, got_ref, *refs):
        *refs, out_ref = refs
        half = bits_ref[0]
        quarter = bits_ref[1] if kept else 1 - bits_ref[1]
        terms = [ref[a[1]] if isinstance(a, tuple) else ref[...] for a, ref in zip(more, refs)]
        out_ref[:rows] = plus(mine_ref[half, quarter], got_ref[half, quarter], *terms)
        if vec:
            out_ref[rows:] = refs[-1][...]

    args = (bits, mine, got, *arrays, *vec)
    return chain.call(
        kernel, "sum_quarter", args, [bf16(rows + (16 if vec else 0), d)], "s" + "v" * (len(args) - 1) + "-v",
        limit=8,
    )[0]


def sum_quarter_apart(chain, bits, mine, got, *more):
    rows, d = mine.shape[2:]
    arrays = [a[0] if isinstance(a, tuple) else a for a in more]

    def kernel(io, bits_ref, mine_ref, got_ref, *refs):
        *refs, upper_ref, lower_ref = refs
        half, quarter = bits_ref[0], bits_ref[1]
        terms = [ref[a[1]] if isinstance(a, tuple) else ref[...] for a, ref in zip(more, refs)]
        total = plus(mine_ref[half, quarter], got_ref[half, quarter], *terms)
        upper_ref[...] = total[: rows // 2]
        lower_ref[...] = total[rows // 2 :]

    args = (bits, mine, got, *arrays)
    return chain.call(
        kernel, "sum_quarter", args, [bf16(rows // 2, d)] * 2, "s" + "v" * (len(args) - 1) + "-vv", limit=8
    )


def side_by_side(chain, a, b, apart):
    rows, d = a.shape

    def kernel(io, a_ref, b_ref, *outs):
        first, second = outs if apart else (outs[0].at[:rows], outs[0].at[rows:])
        first[...] = a_ref[...]
        second[...] = b_ref[...]

    outs = [bf16(rows, d)] * 2 if apart else [bf16(2 * rows, d)]
    return chain.call(kernel, "side_by_side", (a, b), outs, "vv-" + "v" * len(outs), limit=8)


def sum_pairs(chain, *pairs):
    rows = [a.shape[0] for a, _ in pairs]

    def kernel(io, *refs):
        *refs, out_ref = refs
        start = 0
        for a_ref, b_ref in zip(refs[::2], refs[1::2]):
            out_ref[start : start + a_ref.shape[0]] = a_ref[...] + b_ref[...]
            start += a_ref.shape[0]

    args = [a for pair in pairs for a in pair]
    return chain.call(
        kernel, "sum_pairs", args, [bf16(sum(rows), args[0].shape[1])], "v" * len(args) + "-v", limit=8
    )[0]


def place_sums(chain, bits, quarters, rows, targets, outs, whole=(), vec=(), skip=0):
    d = quarters[0][0].shape[1]
    n = len(outs)
    arrays = []
    for a, *_ in quarters:
        if not any(a is b for b in arrays):
            arrays.append(a)
    which = [next(k for k, b in enumerate(arrays) if b is a) for a, *_ in quarters]

    def kernel(io, bits_ref, *refs):
        refs, (buf, sems) = refs[:-2], refs[-2:]
        ins = [refs[k] for k in which]
        refs = refs[len(arrays) + len(whole) :]
        out_refs, vec_refs = refs[:n], refs[n:]

        def each(step):
            for j, (_, _, half, quarter) in enumerate(quarters):
                if j < skip:
                    continue
                half = 1 - bits_ref[0] if half else bits_ref[0]
                quarter = 1 - bits_ref[1] if quarter else bits_ref[1]
                for at, (out, index, first) in enumerate(targets):
                    ref = out_refs[out]
                    ref = ref if index is None else ref.at[index]
                    ref = ref.at[first : first + rows]
                    copy = pltpu.make_async_copy(buf.at[j], ref, sems.at[j])
                    pl.when(2 * half + quarter == at)(functools.partial(step, copy))

        starts = [start for _, start, _, _ in quarters]
        for j, ref in enumerate(ins):
            if j >= skip:
                buf[j] = ref[starts[j] : starts[j] + rows].astype(F32)
        each(lambda copy: copy.start())
        if vec:
            a, b, c, e = (ref[x + rows : x + rows + 16].astype(F32) for ref, x in zip(ins, starts))
            total = jnp.where(bits_ref[5] == 0, (a + b) + (c + e), (a + c) + (b + e))
            for at, (length, ref) in enumerate(zip(vec, vec_refs)):
                ref[...] = total[at, :length]
        each(lambda copy: copy.wait())

    return chain.call(
        kernel, "place_sums", (bits, *arrays, *whole), [*outs, *(f32(length) for length in vec)],
        "s" + "v" * len(arrays) + "p" * len(whole) + "-" + "r" * n + "v" * len(vec), limit=8,
        aliases={1 + len(arrays) + j: j for j in range(len(whole))},
        scratch=[pltpu.VMEM((len(quarters), rows, d), F32), pltpu.SemaphoreType.DMA((len(quarters),))],
    )


def local(
    n_dp, n_tensor, tokens, node_counts, edge_counts, ln1_gain, ln1_bias, qkv_weight, out_weight,
    ln2_gain, ln2_bias, fc1_weight, fc1_bias, fc2_weight, out_grad,
):
    d = tokens.shape[1]
    shard = out_weight.shape[0]
    width = 2 * shard
    mols = tokens.shape[0] // LEN
    dp_at = lax.axis_index("dp")
    tensor_at = lax.axis_index("tensor")
    core = tensor_at % 2
    bit0 = dp_at % 2
    bit1 = (dp_at // 2) % 2
    bits = jnp.stack(
        [jnp.where(core == 0, bit0, bit1), jnp.where(core == 0, bit1, bit0), bit0, tensor_at * mols,
         (tensor_at ^ 2) * mols, core, bit1]
    ).astype(jnp.int32)
    chain = Chain()

    def swap_core(a):
        return lax.ppermute(a, "tensor", [(t, t ^ 1) for t in range(n_tensor)])

    def swap_y(a):
        return lax.ppermute(a, "tensor", [(t, t ^ 2) for t in range(n_tensor)])

    def swap_dp(a, mask0, mask1):
        pairs = [
            (p * n_tensor + t, (p ^ (mask1 if t % 2 else mask0)) * n_tensor + t)
            for p in range(n_dp)
            for t in range(n_tensor)
        ]
        return lax.ppermute(a, ("dp", "tensor"), pairs)

    swap_first = lambda a: swap_dp(a, 1, 2)
    swap_second = lambda a: swap_dp(a, 2, 1)
    far_masks = [1 << k for k in range(2, n_dp.bit_length() - 1)]

    w_got = swap_core(qkv_weight)
    x_got, far_g = swap_y(tokens), swap_y(out_grad)
    picked = pick(chain, bits, out_weight, fc1_weight, fc2_weight, fc1_bias)
    far_y = swap_y(picked)
    near, others = load(
        chain, out_weight, fc1_weight, fc2_weight, picked,
        (tokens, out_grad, ln1_gain, ln1_bias, ln2_gain, ln2_bias),
    )
    near = (near, swap_core(near))
    tokens, out_grad, ln1_gain, ln1_bias, ln2_gain, ln2_bias = others

    counts = (node_counts, edge_counts)
    norm1 = (ln1_gain, ln1_bias)
    a1_0, qt_0, kt_0, v_0, p_0, ot_0, o_0, w_qkv = attention(
        chain, bits, 3, *counts, tokens, *norm1, (qkv_weight, w_got)
    )
    far_o = swap_y(o_0)
    far_y, short = hold(chain, far_y, d)
    far_x, far_z = swap_dp(short, 1, 1), swap_dp(short, 2, 2)
    far_z, pair = pair_up(chain, far_x, far_z)
    far_xz = swap_dp(far_z, 1, 1)
    a1_1, qt_1, kt_1, v_1, p_1, ot_1, o_1, wo, fc1, fc2 = attention(
        chain, bits, 4, *counts, x_got, *norm1, w_qkv, near=near
    )
    o_got = swap_y(o_1)
    spacer(chain)
    fars = (far_y, pair, far_xz)
    fars += tuple(swap_core(a) for a in fars)
    norm2 = (ln2_gain, ln2_bias)
    wo, fc1, fc2 = pack_far(chain, bits, (wo, fc1, fc2), fars)
    low, far_low = 3 * shard, 3 * shard // 4
    biases = ((near[0], low), (near[1], low), (fars[0], far_low), (fars[3], far_low))

    part_0, part_1, dz_0, dz_1, b1 = feed_in(
        chain, (tokens, x_got), (o_0, o_1), (out_grad, far_g), wo, fc2, biases
    )

    class Sum:
        def __init__(self, count, keep, got, apart, early):
            self.size = count * shard // 4
            self.apart, self.early = apart, early
            view = lambda a: a.reshape(2, 2, self.size, d)
            self.parts = (view(keep), view(got))

        def first(self):
            sent = sum_half(chain, bits, *self.parts, self.apart)
            got = [swap_first(a) for a in sent]
            self.on, self.kept = got if self.apart else ((got[0], 0), (got[0], 1))

        def second(self):
            self.got = swap_second(sum_quarter(chain, bits, *self.parts, False, self.on))

        def third(self, *vec):
            self.sum = sum_quarter(chain, bits, *self.parts, True, self.kept, self.got, vec=vec)
            self.got = swap_dp(self.sum, far_masks[0], far_masks[0])

        def third_apart(self):
            self.sums = sum_quarter_apart(chain, bits, *self.parts, self.kept, self.got)
            self.gots = [swap_dp(a, far_masks[0], far_masks[0]) for a in self.sums]
            self.halves = [None, None]

        def fourth_apart(self, at, *vec):
            self.sum, self.got = self.sums[at], self.gots[at]
            self.fourth(*vec)
            self.halves[at] = self.quarters

        def fourth(self, *vec):
            a = sum_pairs(chain, (self.sum, self.got), *vec)
            for mask in far_masks[1:]:
                a = sum_pairs(chain, (a, swap_dp(a, mask, mask)))
            b = swap_second(a)
            if self.early == 1:
                self.quarters = [(a, 0, 0, 0), (b, 0, 0, 1), (swap_first(a), 0, 1, 0), (swap_first(b), 0, 1, 1)]
            self.last = (a, b)

        def fifth(self):
            if self.early == 0:
                (a,) = side_by_side(chain, *self.last, False)
                b = swap_first(a)
                rows = a.shape[0] // 2
                self.quarters = [(a, 0, 0, 0), (a, rows, 0, 1), (b, 0, 1, 0), (b, rows, 1, 1)]
            if self.early == 2:
                a, b = side_by_side(chain, *self.last, True)
                self.quarters = [(a, 0, 0, 0), (b, 0, 0, 1), (swap_first(a), 0, 1, 0), (swap_first(b), 0, 1, 1)]

    h_1, du_1, *far_r = feed_far(chain, part_1, far_o, dz_1, far_g, *norm2, wo, fc1, b1)
    gh_1, dp_1 = backward(chain, (du_1, fc1, h_1, far_g, ln2_gain, wo, p_1, qt_1, kt_1, v_1), False)
    h_0, z_0, du_0, keep_r, send_r, bias_sums = feed_own(
        chain, part_0, o_got, dz_0, out_grad, *norm2, wo, fc1, b1, (du_1, *far_r)
    )
    gh_0, dp_0, dh, sums = backward(chain, (du_0, fc1, h_0, out_grad, ln2_gain, wo, p_0, qt_0, kt_0, v_0), True)
    r = Sum(2, keep_r, swap_core(send_r), True, 1)
    r.first()
    a1s = (a1_0, a1_1)
    lefts = [(dp_0, dp_1, c * width) for c in range(3)] + [(ot_0, ot_1, 0)]
    rights = [a1s] * 3 + [(gh_0, gh_1)]
    got_q = swap_core(weight_grads(chain, "weight_grads", shard, 1, lefts, rights))
    q = Sum(4, weight_grads(chain, "weight_grads", shard, 0, lefts, rights), got_q, True, 2)
    r.second()
    q.first()
    r.third()
    q.second()
    da1_mine, da1_theirs = input_grads(chain, (dp_0, dp_1), w_qkv, (tokens, x_got), sums, bias_sums)
    da1_got = swap_y(da1_theirs)
    r.fourth()
    result = feed_result(chain, z_0, fc2, h_0)
    q.third()
    vec = vector_rows(chain, da1_theirs, da1_got)
    vec_got = swap_core(vec)
    r.fifth()
    halves = [(c, None, half * shard // 2) for c in range(2) for half in range(2)]
    grad_fc1, grad_fc2 = place_sums(chain, bits, r.quarters, r.size, halves, [f32(shard, d)] * 2)
    vec = vector_cores(chain, vec, vec_got, shard)
    vec_got = swap_dp(vec, far_masks[0], far_masks[0])
    q.fourth((vec, vec_got))
    grad_tokens = input_norm(chain, tokens, ln1_gain, da1_mine, da1_got, dh)
    q.fifth()
    each = [(0, 0, 0), (0, 1, 0), (0, 2, 0), (1, None, 0)]
    outs = [f32(3, shard, d), f32(shard, d)]
    grads = place_sums(chain, bits, q.quarters[:2], q.size, each, outs)
    grads = place_sums(chain, bits, q.quarters[:3], q.size, each, outs, grads, skip=2)
    grad_qkv, grad_out, gain1, bias1, gain2, bias2, grad_b = place_sums(
        chain, bits, q.quarters, q.size, each, outs, grads, (d, d, d, d, shard), 3
    )
    return (
        result, grad_tokens, gain1, bias1, grad_qkv, grad_out, gain2, bias2, grad_fc1, grad_b, grad_fc2,
    )


def solution(mesh):
    tokens = P(("dp", "tensor"), None)
    rows = P("tensor", None)
    qkv = P(None, "tensor", None)
    in_specs = (
        tokens, P("dp"), P("dp"), P(), P(), qkv, rows, P(), P(), rows, P("tensor"), rows, tokens,
    )
    out_specs = (tokens, tokens, P(), P(), qkv, rows, P(), P(), rows, P("tensor"), rows)
    step = functools.partial(local, mesh.shape["dp"], mesh.shape["tensor"])
    return jax.shard_map(step, mesh=mesh, in_specs=in_specs, out_specs=out_specs, check_vma=False)
```

```python
import functools

import jax
import jax.numpy as jnp
from jax import lax
from jax.experimental import pallas as pl
from jax.experimental.pallas import tpu as pltpu
from jax.sharding import PartitionSpec as P

HEAD_DIM = 24
LEN = 128
PAIR = 2 * HEAD_DIM
EPSILON = 1e-05
SCALE = HEAD_DIM ** (-0.5)
LOG2E = 1.4426950408889634
F32 = jnp.float32
BF16 = jnp.bfloat16
MIB = 1024 * 1024


def dot_nn(a, b):
    return lax.dot_general(a, b, (((1,), (0,)), ((), ())), preferred_element_type=F32)


def dot_nt(a, b):
    return lax.dot_general(a, b, (((1,), (1,)), ((), ())), preferred_element_type=F32)


def dot_tn(a, b):
    return lax.dot_general(a, b, (((0,), (0,)), ((), ())), preferred_element_type=F32)


def normalise(v):
    centered = v - jnp.mean(v, axis=-1, keepdims=True)
    r = lax.rsqrt(jnp.mean(centered * centered, axis=-1, keepdims=True) + EPSILON)
    return centered * r, r


def norm_back(da, gain, xh, r):
    e = da * gain
    return r * (
        e - jnp.mean(e, axis=-1, keepdims=True) - xh * jnp.mean(e * xh, axis=-1, keepdims=True)
    )


def pair_blocks(rows):
    rows = rows.astype(F32)
    none = jnp.zeros((HEAD_DIM, LEN), F32)
    left = jnp.concatenate([rows[:HEAD_DIM], none], axis=0)
    right = jnp.concatenate([none, rows[HEAD_DIM:]], axis=0)
    return jnp.concatenate([left, right], axis=1).astype(BF16)


def pair_window(i, width):
    low = min(PAIR * i // LEN * LEN, width - 2 * LEN)
    return low, PAIR * i - low


def placed(block, before):
    parts = []
    if before:
        parts.append(jnp.zeros((before, 2 * LEN), BF16))
    parts.append(block)
    after = 2 * LEN - PAIR - before
    if after:
        parts.append(jnp.zeros((after, 2 * LEN), BF16))
    return jnp.concatenate(parts, axis=0)


def diagonal(both):
    return jnp.concatenate([both[:HEAD_DIM, :LEN], both[HEAD_DIM:, LEN:]], axis=0)


STRIP = 256
COSTS = (0, 0, 100, 0, 0, 30, 30, 0, 0, 0, 0, 0, 100, 0, 0, 0, 200, 0, 60, 0, 0, 30, 0, 0, 0, 0, 0, 0, 0, 0, 0, 0)


class IO:
    def __init__(self, reads, writes):
        self.reads, self.writes = reads, writes
        self.started = set()

    def wait(self, *args):
        for j in args:
            if j in self.reads:
                self.reads[j].wait()

    def flush(self, *outs):
        for j in outs:
            if j in self.writes:
                self.started.add(j)
                self.writes[j].start()

    def finish(self):
        self.flush(*(j for j in self.writes if j not in self.started))
        for copy in self.writes.values():
            copy.wait()


def pinned(a):
    return pltpu.with_memory_space_constraint(a, pltpu.HBM)


class Chain:
    def __init__(self):
        self.token, self.calls = None, 0

    def call(self, kernel, name, args, outs, kinds, scratch=(), limit=16, aliases={}):
        ins, out_kinds = kinds.split("-")
        cost = COSTS[min(self.calls, len(COSTS) - 1)]
        self.calls += 1
        assert len(ins) == len(args) and len(out_kinds) == len(outs)
        hbm = pl.BlockSpec(memory_space=pltpu.HBM)
        vmem = pl.BlockSpec(memory_space=pltpu.VMEM)
        smem = pl.BlockSpec(memory_space=pltpu.SMEM)
        spec = lambda kind: {"s": smem, "v": vmem}.get(kind, hbm)
        tokens = () if self.token is None else (self.token,)
        staged = [j for j, kind in enumerate(ins) if kind in "hcl"]
        written = [j for j, kind in enumerate(out_kinds) if kind == "w"]
        memory = lambda kind: pltpu.SMEM if kind == "c" else pltpu.VMEM
        buffers = [memory(ins[j])(args[j].shape, args[j].dtype) for j in staged]
        buffers += [pltpu.VMEM(outs[j].shape, outs[j].dtype) for j in written]
        n_in, n_out, n_buf = len(args) + len(tokens), len(outs), len(buffers)

        def body(*refs):
            arg_refs = list(refs[: len(args)])
            out_refs = list(refs[n_in : n_in + n_out])
            token_ref = refs[n_in + n_out]
            own = refs[n_in + n_out + 1 :]
            bufs, sems, extra = own[:n_buf], own[n_buf], own[n_buf + 1 :]
            reads, writes = {}, {}
            for at, j in enumerate(staged):
                reads[j] = pltpu.make_async_copy(arg_refs[j], bufs[at], sems.at[at])
                reads[j].start()
                arg_refs[j] = bufs[at]
            for at, j in enumerate(written, len(staged)):
                writes[j] = pltpu.make_async_copy(bufs[at], out_refs[j], sems.at[at])
                out_refs[j] = bufs[at]
            io = IO(reads, writes)
            io.wait(*(j for j in staged if ins[j] == "h"))
            token_ref[...] = jnp.zeros_like(token_ref)
            kernel(io, *arg_refs, *out_refs, *extra)
            io.finish()

        *results, self.token = pl.pallas_call(
            body,
            in_specs=[spec(kind) for kind in ins] + [vmem] * len(tokens),
            out_specs=[spec(kind) for kind in out_kinds] + [vmem],
            out_shape=[*outs, f32(8, 128)],
            input_output_aliases=aliases,
            scratch_shapes=[*buffers, pltpu.SemaphoreType.DMA((max(n_buf, 1),)), *scratch],
            compiler_params=pltpu.CompilerParams(vmem_limit_bytes=limit * MIB),
            cost_estimate=pl.CostEstimate(flops=cost * 10**8, bytes_accessed=10**8, transcendentals=0),
            name=name,
        )(*(pinned(a) if kind in "hclp" else a for a, kind in zip(args, ins)), *tokens)
        return results


def bf16(*shape):
    return jax.ShapeDtypeStruct(shape, BF16)


def f32(*shape):
    return jax.ShapeDtypeStruct(shape, F32)


def copies(sems, pairs):
    started = [pltpu.make_async_copy(a, b, sems.at[j]) for j, (a, b) in enumerate(pairs)]
    for copy in started:
        copy.start()
    return started


def finish(started):
    for copy in started:
        copy.wait()


def attention(chain, bits, place, nodes, edges, x, gain, bias, w, near=()):
    rows, d = x.shape
    apart = isinstance(w, tuple)
    width = 2 * w[0].shape[1] if apart else w.shape[1]
    shard = width // 2
    pairs = width // PAIR
    mols = rows // LEN

    def kernel(io, bits_ref, nodes_ref, edges_ref, x_ref, gain_ref, bias_ref, *refs):
        started = []
        if not apart:
            w_ref, near0, near1, *refs, wo_ref, fc1_ref, fc2_ref, sems = refs
            a1_ref, qt_ref, kt_ref, v_ref, p_ref, ot_ref, o_ref = refs
            pairs_w = []
            for at, ref in enumerate((near0, near1)):
                for c, out in enumerate((wo_ref, fc1_ref, fc2_ref)):
                    part = ref.at[c * shard : (c + 1) * shard]
                    pairs_w.append((part, out.at[at * shard : (at + 1) * shard]))
            started = copies(sems, pairs_w)
        else:
            own, got, *refs, w_ref, sems = refs
            a1_ref, qt_ref, kt_ref, v_ref, p_ref, ot_ref, o_ref = refs
            pairs_w = [(own, w_ref.at[:, :shard]), (got, w_ref.at[:, shard:])]
            near_w = copies(sems, pairs_w)
        xh, _ = normalise(x_ref[...].astype(F32))
        a1 = (xh * gain_ref[...][None, :] + bias_ref[...][None, :]).astype(BF16)
        a1_ref[...] = a1
        if apart:
            finish(near_w)
        qt = dot_nt(w_ref[0], a1).astype(BF16)
        keys = dot_nt(a1, w_ref[1]).astype(BF16)
        vt = dot_nt(w_ref[2], a1).astype(BF16)
        qt_ref[...] = qt
        every = [(m, i) for m in range(mols) for i in range(pairs)]
        lanes = lambda m: slice(LEN * m, LEN * (m + 1))
        rows_of = lambda i: slice(PAIR * i, PAIR * (i + 1))
        scores, probs = {}, {}
        for m, i in every:
            low, before = pair_window(i, width)
            rhs = placed(pair_blocks(qt[rows_of(i), lanes(m)]), before)
            scores[m, i] = dot_nn(keys[lanes(m), low : low + 2 * LEN], rhs)
        io.wait(1, 2)
        for m in range(mols):
            mol = bits_ref[place] + m
            count = 1 + nodes_ref[mol] + edges_ref[mol]
            valid = lax.broadcasted_iota(jnp.int32, (LEN, 2 * LEN), 0) < count
            for i in range(pairs):
                s = jnp.where(valid, scores[m, i], -1e30)
                e = jnp.exp2((s - jnp.max(s, axis=0, keepdims=True)) * (SCALE * LOG2E))
                p = (e * (1.0 / jnp.sum(e, axis=0, keepdims=True))).astype(BF16)
                p_ref[m, i] = p
                probs[m, i] = p
        for m, i in every:
            both = dot_nn(vt[rows_of(i), lanes(m)], probs[m, i])
            ot_ref[rows_of(i), lanes(m)] = diagonal(both).astype(BF16)
        o_ref[...] = ot_ref[...].T
        kt_ref[...] = dot_nt(w_ref[1], a1).astype(BF16)
        v_ref[...] = dot_nt(a1, w_ref[2]).astype(BF16)
        finish(started)

    outs = [
        bf16(rows, d), bf16(width, rows), bf16(width, rows), bf16(rows, width),
        bf16(mols, pairs, LEN, 2 * LEN), bf16(width, rows),
    ]
    args = (bits, nodes, edges, x, gain, bias)
    if not apart:
        return chain.call(
            kernel, "attention_forward", (*args, w, *near), [*outs, bf16(rows, width), bf16(2 * width, d), bf16(2 * width, d), bf16(2 * width, d)],
            "sccvvvvvv-vvvvvvvvvv", scratch=[pltpu.SemaphoreType.DMA((6,))],
        )
    return chain.call(
        kernel, "attention_forward", (*args, *w), [*outs, bf16(rows, width), bf16(3, width, d)],
        "sccvvvpr-vvvvvvvv", scratch=[pltpu.SemaphoreType.DMA((2,))],
    )


def pick(chain, bits, wo, fc1, fc2, bias):
    shard, d = wo.shape
    rows = 3 * shard // 4
    strips = d // STRIP

    def kernel(io, bits_ref, wo_ref, fc1_ref, fc2_ref, bias_ref, out_ref, sems):
        refs = (wo_ref, fc1_ref, fc2_ref)

        def part(quarter):
            pairs = []
            for c, first, at, n in quarter_rows(quarter, shard):
                for k in range(strips):
                    source = refs[c].at[first : first + n, k * STRIP : (k + 1) * STRIP]
                    pairs.append((source, out_ref.at[k * rows + at : k * rows + at + n]))
            started = copies(sems, pairs)
            io.wait(4)
            out_ref[strips * rows :] = jnp.concatenate(
                [jnp.broadcast_to(bias_ref[...].astype(F32)[None, :], (16, shard)), jnp.zeros((16, STRIP - shard), F32)],
                axis=1,
            ).astype(BF16)
            finish(started)

        which = 2 * bits_ref[2] + bits_ref[6]
        for at in range(4):
            pl.when(which == at)(functools.partial(part, at))

    return chain.call(
        kernel, "pick", (bits, wo, fc1, fc2, bias), [bf16(strips * rows + 16, STRIP)], "spppl-v", limit=4,
        scratch=[pltpu.SemaphoreType.DMA((2 * strips,))],
    )[0]


def quarter_rows(quarter, shard):
    size = 3 * shard // 4
    found, at = [], 0
    while at < size:
        which, first = divmod(quarter * size + at, shard)
        n = min(size - at, shard - first)
        found.append((which, first, at, n))
        at += n
    return found


def hold(chain, a, d):
    strips = d // STRIP
    rows = (a.shape[0] - 16) // strips

    def kernel(io, a_ref, out_ref, short_ref):
        for k in range(strips):
            strip = a_ref[k * rows : (k + 1) * rows]
            out_ref[:rows, k * STRIP : (k + 1) * STRIP] = strip
            short_ref[:, k * STRIP : (k + 1) * STRIP] = strip
        out_ref[rows:] = widened(a_ref[strips * rows :], d)

    return chain.call(kernel, "hold", (a,), [bf16(rows + 16, d), bf16(rows, d)], "v-vv", limit=4)


def widened(a, d):
    return jnp.concatenate([a, jnp.zeros((a.shape[0], d - a.shape[1]), a.dtype)], axis=1)


def pair_up(chain, a, b):
    def kernel(io, a_ref, b_ref, out_ref, both_ref):
        out_ref[...] = b_ref[...]
        both_ref[0] = a_ref[...]
        both_ref[1] = b_ref[...]

    return chain.call(kernel, "pair_up", (a, b), [bf16(*b.shape), bf16(2, *a.shape)], "vv-vv", limit=4)


def spacer(chain, *after):
    def kernel(io, *refs):
        pass

    chain.call(kernel, "spacer", after, [], "r" * len(after) + "-", limit=2)


def load(chain, out_weight, fc1_weight, fc2_weight, picked, others):
    shard, d = out_weight.shape
    n = len(others)

    def kernel(io, wo, fc1, fc2, picked_ref, *refs):
        others_in, (near_ref, *others_out, sems) = refs[:n], refs[n:]
        near_ref[3 * shard :] = widened(picked_ref[picked.shape[0] - 16 :], d)
        rows = lambda at: near_ref.at[at * shard : (at + 1) * shard]
        near = [(wo, rows(0)), (fc1, rows(1)), (fc2, rows(2))]
        finish(copies(sems, near + list(zip(others_in, others_out))))

    near, *others = chain.call(
        kernel, "load", (out_weight, fc1_weight, fc2_weight, picked, *others),
        [bf16(3 * shard + 16, d)] + [jax.ShapeDtypeStruct(a.shape, a.dtype) for a in others],
        "pppv" + "p" * n + "-v" + "v" * n, limit=4, scratch=[pltpu.SemaphoreType.DMA((3 + n,))],
    )
    return near, others


def feed_body(part, ob, dz, wo_ref, gain_ref, bias_ref, fc1_ref, b1, h_ref, a2_ref, z_ref, du_ref):
    h = part + dot_nn(ob, wo_ref[wo_ref.shape[0] // 2 :])
    h_ref[...] = h
    xh, _ = normalise(h)
    a2 = (xh * gain_ref[...][None, :] + bias_ref[...][None, :]).astype(BF16)
    a2_ref[...] = a2
    u = dot_nt(a2, fc1_ref[...]) + b1
    phi = 0.5 * (1.0 + lax.erf(u * (0.5**0.5)))
    slope = phi + u * (jnp.exp(-0.5 * u * u) * 0.3989422804014327)
    du_ref[...] = (dz * slope).astype(BF16)
    z_ref[...] = (u * phi).astype(BF16)


def pack_far(chain, bits, weights, fars):
    rows, d = weights[0].shape
    shard = rows // 4

    def kernel(io, bits_ref, wo_in, fc1_in, fc2_in, y0, pair0, xz0, y1, pair1, xz1, *outs):
        def placed_at(which):
            for at, (y, pair, xz) in enumerate(((y0, pair0, xz0), (y1, pair1, xz1))):
                for turn, ref in enumerate((y, pair.at[1], pair.at[0], xz)):
                    for c, first, start, n in quarter_rows(which ^ turn, shard):
                        row = (2 + at) * shard + first
                        outs[c][row : row + n] = ref[start : start + n]

        which = 2 * bits_ref[2] + bits_ref[6]
        for at in range(4):
            pl.when(which == at)(functools.partial(placed_at, at))

    return chain.call(
        kernel, "pack_far", (bits, *weights, *fars), [bf16(rows, d)] * 3, "s" + "v" * 9 + "-vvv", limit=4,
        aliases={1: 0, 2: 1, 3: 2},
    )


def feed_in(chain, xs, os, gs, wo, fc2, biases):
    rows, d = xs[0].shape
    columns = fc2.shape[0]
    shard = columns // 4

    def kernel(io, x0, x1, o0, o1, g0, g1, wo_ref, fc2_ref, *refs):
        b_refs, (h0, h1, dz0, dz1, b1_ref) = refs[:4], refs[4:]
        for x_ref, o_ref, h_ref in ((x0, o0, h0), (x1, o1, h1)):
            h_ref[...] = x_ref[...].astype(F32) + dot_nn(o_ref[...], wo_ref[: o_ref.shape[1]])
        for g_ref, dz_ref in ((g0, dz0), (g1, dz1)):
            dz_ref[...] = dot_nt(g_ref[...], fc2_ref[...])
        parts = [ref[row : row + 1, :shard].astype(F32) for ref, (_, row) in zip(b_refs, biases)]
        b1_ref[...] = jnp.concatenate(parts, axis=1)

    return chain.call(
        kernel, "feed_in", (*xs, *os, *gs, wo, fc2, *(a for a, _ in biases)),
        [f32(rows, d)] * 2 + [f32(rows, columns)] * 2 + [f32(1, columns)], "v" * 12 + "-vvvvv",
    )


def feed_far(chain, h, ob, dz, g, gain, bias, wo, fc1, b1):
    rows, d = h.shape
    columns = fc1.shape[0]
    width = columns // 2

    def kernel(io, part_ref, ob_ref, dz_ref, g_ref, gain_ref, bias_ref, wo_ref, fc1_ref, b1_ref,
               h_ref, du_ref, first_ref, second_ref, a2_ref, z_ref):
        feed_body(
            part_ref[...], ob_ref[...], dz_ref[...], wo_ref, gain_ref, bias_ref, fc1_ref, b1_ref[...], h_ref, a2_ref,
            z_ref, du_ref,
        )
        first_ref[...] = dot_tn(du_ref[:, :width], a2_ref[...])
        second_ref[...] = dot_tn(z_ref[:, :width], g_ref[...])

    return chain.call(
        kernel, "feed_far", (h, ob, dz, g, gain, bias, wo, fc1, b1),
        [f32(rows, d), bf16(rows, columns), f32(width, d), f32(width, d)], "v" * 9 + "-vvvv",
        scratch=[pltpu.VMEM((rows, d), BF16), pltpu.VMEM((rows, columns), BF16)],
    )


def feed_own(chain, h, ob, dz, g, gain, bias, wo, fc1, b1, far):
    rows, d = h.shape
    columns = fc1.shape[0]
    width = columns // 2
    shard = width // 2

    def kernel(io, part_ref, ob_ref, dz_ref, g_ref, gain_ref, bias_ref, wo_ref, fc1_ref, b1_ref, du1, first1, second1,
               h_ref, z_ref, du_ref, keep_ref, send_ref, sums_ref, a2_ref):
        feed_body(
            part_ref[...], ob_ref[...], dz_ref[...], wo_ref, gain_ref, bias_ref, fc1_ref, b1_ref[...], h_ref, a2_ref,
            z_ref, du_ref,
        )
        du = du_ref[:, :width]
        first = dot_tn(du, a2_ref[...]) + first1[...]
        second = dot_tn(z_ref[:, :width], g_ref[...]) + second1[...]
        for at, ref in enumerate((keep_ref, send_ref)):
            here = slice(at * shard, (at + 1) * shard)
            ref[0] = first[here].astype(BF16)
            ref[1] = second[here].astype(BF16)
        sums_ref[...] = jnp.sum(du.astype(F32), axis=0, keepdims=True) + jnp.sum(
            du1[:, :width].astype(F32), axis=0, keepdims=True
        )

    return chain.call(
        kernel, "feed_own", (h, ob, dz, g, gain, bias, wo, fc1, b1, *far),
        [f32(rows, d), bf16(rows, columns), bf16(rows, columns), bf16(2, shard, d), bf16(2, shard, d), f32(1, width)],
        "v" * 12 + "-vvvvvv", scratch=[pltpu.VMEM((rows, d), BF16)],
    )


def feed_result(chain, z, fc2, h):
    def kernel(io, z_ref, fc2_ref, h_ref, out_ref):
        out_ref[...] = (h_ref[...] + dot_nn(z_ref[...], fc2_ref[...])).astype(BF16)

    return chain.call(kernel, "feed_result", (z, fc2, h), [bf16(*h.shape)], "vvv-w", limit=8)[0]


def backward(chain, args, own):
    h, kt = args[2], args[8]
    rows, d = h.shape
    width = kt.shape[0]
    mols, pairs = rows // LEN, width // PAIR

    def kernel(io, du_ref, fc1_ref, h_ref, g_ref, gain_ref, wo_ref, p_ref, qt_ref, kt_ref, v_ref,
               gh_ref, dp_ref, dh_ref=None, sums_ref=None):
        da2 = dot_nn(du_ref[...], fc1_ref[...])
        xh, r = normalise(h_ref[...])
        dh = g_ref[:, :d].astype(F32) + norm_back(da2, gain_ref[...][None, :], xh, r)
        if own:
            dh_ref[...] = dh
            sums_ref[0:1] = jnp.sum(da2 * xh, axis=0, keepdims=True)
            sums_ref[1:2] = jnp.sum(da2, axis=0, keepdims=True)
            io.flush(2)
        gh = dh.astype(BF16)
        gh_ref[...] = gh
        dot = dot_nt(wo_ref[:width], gh).astype(BF16)
        every = [(m, i) for m in range(mols) for i in range(pairs)]
        lanes = lambda m: slice(LEN * m, LEN * (m + 1))
        rows_of = lambda i: slice(PAIR * i, PAIR * (i + 1))
        dps, dss, dos = {}, {}, {}
        for m, i in every:
            low, before = pair_window(i, width)
            dos[m, i] = pair_blocks(dot[rows_of(i), lanes(m)])
            dps[m, i] = dot_nn(v_ref[lanes(m), low : low + 2 * LEN], placed(dos[m, i], before))
        for m, i in every:
            dv = dot_nt(dos[m, i], p_ref[m, i])
            dp_ref[pl.ds(2 * width + PAIR * i, PAIR), lanes(m)] = dv.astype(BF16)
        for m, i in every:
            p = p_ref[m, i].astype(F32)
            t = dps[m, i] * p
            dss[m, i] = (t - p * jnp.sum(t, axis=0, keepdims=True)).astype(BF16)
        for m, i in every:
            dq = diagonal(dot_nn(kt_ref[rows_of(i), lanes(m)], dss[m, i])) * SCALE
            dp_ref[rows_of(i), lanes(m)] = dq.astype(BF16)
            dk = dot_nt(pair_blocks(qt_ref[rows_of(i), lanes(m)]), dss[m, i]) * SCALE
            dp_ref[pl.ds(width + PAIR * i, PAIR), lanes(m)] = dk.astype(BF16)

    outs = [bf16(rows, d), bf16(3 * width, rows)] + ([f32(rows, d), f32(8, d)] if own else [])
    return chain.call(
        kernel, "attention_backward", args, outs, "v" * 10 + ("-vvvv" if own else "-vv"),
    )


def weight_grads(chain, name, shard, at, lefts, rights):
    d = rights[0][0].shape[1]
    args, count = [], len(lefts)
    for (u0, u1, _), (v0, v1) in zip(lefts, rights):
        args += [u0, u1, v0, v1]

    def kernel(io, *refs):
        out_ref = refs[-1]
        for c in range(count):
            u0, u1, v0, v1 = refs[4 * c : 4 * c + 4]
            rows = slice(lefts[c][2] + at * shard, lefts[c][2] + (at + 1) * shard)
            left = jnp.concatenate([u0[rows], u1[rows]], axis=1)
            right = jnp.concatenate([v0[...], v1[...]], axis=0)
            out_ref[c] = dot_nn(left, right).astype(BF16)

    return chain.call(kernel, name, args, [bf16(count, shard, d)], "v" * len(args) + "-v")[0]


def input_grads(chain, dps, w, xs, sums, bias):
    rows, d = xs[0].shape

    def kernel(io, dp0, dp1, w_ref, x0, x1, sums_ref, bias_ref, mine_ref, theirs_ref):
        w = w_ref[...].reshape(dp0.shape[0], d)
        theirs = dot_tn(dp1[...], w)
        theirs_ref[:rows] = theirs.astype(BF16)
        mine = dot_tn(dp0[...], w)
        mine_ref[...] = mine
        xh0, _ = normalise(x0[...].astype(F32))
        xh1, _ = normalise(x1[...].astype(F32))
        bias = bias_ref[...]
        vec = [
            jnp.sum(mine * xh0, axis=0, keepdims=True) + jnp.sum(theirs * xh1, axis=0, keepdims=True),
            jnp.sum(mine, axis=0, keepdims=True) + jnp.sum(theirs, axis=0, keepdims=True),
            sums_ref[0:2],
            jnp.concatenate([bias, jnp.zeros((1, d - bias.shape[1]), F32)], axis=1),
            jnp.zeros((11, d), F32),
        ]
        theirs_ref[rows:] = jnp.concatenate(vec, axis=0).astype(BF16)

    return chain.call(
        kernel, "input_grads", (*dps, w, *xs, sums, bias), [f32(rows, d), bf16(rows + 16, d)], "vvvvvvv-vv"
    )


def input_norm(chain, x, gain, mine, got, dh):
    rows, d = x.shape

    def kernel(io, x_ref, gain_ref, mine_ref, got_ref, dh_ref, out_ref):
        xh, r = normalise(x_ref[...].astype(F32))
        da1 = mine_ref[...] + got_ref[:rows].astype(F32)
        out_ref[...] = (dh_ref[...] + norm_back(da1, gain_ref[...][None, :], xh, r)).astype(BF16)

    return chain.call(
        kernel, "input_norm", (x, gain, mine, got, dh), [bf16(rows, d)], "vvvvv-w", limit=8
    )[0]


def plus(*terms):
    total = terms[0].astype(F32)
    for term in terms[1:]:
        total = total + term.astype(F32)
    return total.astype(BF16)


def vector_rows(chain, mine, got):
    rows, d = mine.shape

    def kernel(io, mine_ref, got_ref, out_ref):
        a, b = mine_ref[rows - 16 :], got_ref[rows - 16 :]
        same = lax.broadcasted_iota(jnp.int32, (16, d), 0) < 4
        out_ref[...] = plus(a, jnp.where(same, b.astype(F32), 0.0))

    return chain.call(kernel, "vector_rows", (mine, got), [bf16(16, d)], "vv-v", limit=4)[0]


def vector_cores(chain, mine, got, shard):
    def kernel(io, mine_ref, got_ref, out_ref):
        a, b = mine_ref[...].astype(F32), got_ref[...].astype(F32)
        turned = jnp.concatenate([b[:, shard : 2 * shard], b[:, :shard], b[:, 2 * shard :]], axis=1)
        same = lax.broadcasted_iota(jnp.int32, a.shape, 0) < 4
        out_ref[...] = plus(a, jnp.where(same, b, turned))

    return chain.call(kernel, "vector_cores", (mine, got), [bf16(*mine.shape)], "vv-v", limit=4)[0]


def sum_half(chain, bits, mine, got, apart):
    def kernel(io, bits_ref, mine_ref, got_ref, *outs):
        half, quarter = 1 - bits_ref[0], bits_ref[1]
        on_ref, kept_ref = outs if apart else (outs[0].at[0], outs[0].at[1])
        on_ref[...] = mine_ref[half, 1 - quarter] + got_ref[half, 1 - quarter]
        kept_ref[...] = mine_ref[half, quarter] + got_ref[half, quarter]

    rows, d = mine.shape[2:]
    outs = [bf16(rows, d)] * 2 if apart else [bf16(2, rows, d)]
    return chain.call(kernel, "sum_half", (bits, mine, got), outs, "svv-" + "v" * len(outs), limit=8)


def sum_quarter(chain, bits, mine, got, kept, *more, vec=()):
    rows, d = mine.shape[2:]
    arrays = [a[0] if isinstance(a, tuple) else a for a in more]

    def kernel(io, bits_ref, mine_ref, got_ref, *refs):
        *refs, out_ref = refs
        half = bits_ref[0]
        quarter = bits_ref[1] if kept else 1 - bits_ref[1]
        terms = [ref[a[1]] if isinstance(a, tuple) else ref[...] for a, ref in zip(more, refs)]
        out_ref[:rows] = plus(mine_ref[half, quarter], got_ref[half, quarter], *terms)
        if vec:
            out_ref[rows:] = refs[-1][...]

    args = (bits, mine, got, *arrays, *vec)
    return chain.call(
        kernel, "sum_quarter", args, [bf16(rows + (16 if vec else 0), d)], "s" + "v" * (len(args) - 1) + "-v",
        limit=8,
    )[0]


def sum_quarter_apart(chain, bits, mine, got, *more):
    rows, d = mine.shape[2:]
    arrays = [a[0] if isinstance(a, tuple) else a for a in more]

    def kernel(io, bits_ref, mine_ref, got_ref, *refs):
        *refs, upper_ref, lower_ref = refs
        half, quarter = bits_ref[0], bits_ref[1]
        terms = [ref[a[1]] if isinstance(a, tuple) else ref[...] for a, ref in zip(more, refs)]
        total = plus(mine_ref[half, quarter], got_ref[half, quarter], *terms)
        upper_ref[...] = total[: rows // 2]
        lower_ref[...] = total[rows // 2 :]

    args = (bits, mine, got, *arrays)
    return chain.call(
        kernel, "sum_quarter", args, [bf16(rows // 2, d)] * 2, "s" + "v" * (len(args) - 1) + "-vv", limit=8
    )


def side_by_side(chain, a, b, apart):
    rows, d = a.shape

    def kernel(io, a_ref, b_ref, *outs):
        first, second = outs if apart else (outs[0].at[:rows], outs[0].at[rows:])
        first[...] = a_ref[...]
        second[...] = b_ref[...]

    outs = [bf16(rows, d)] * 2 if apart else [bf16(2 * rows, d)]
    return chain.call(kernel, "side_by_side", (a, b), outs, "vv-" + "v" * len(outs), limit=8)


def sum_pairs(chain, *pairs):
    rows = [a.shape[0] for a, _ in pairs]

    def kernel(io, *refs):
        *refs, out_ref = refs
        start = 0
        for a_ref, b_ref in zip(refs[::2], refs[1::2]):
            out_ref[start : start + a_ref.shape[0]] = a_ref[...] + b_ref[...]
            start += a_ref.shape[0]

    args = [a for pair in pairs for a in pair]
    return chain.call(
        kernel, "sum_pairs", args, [bf16(sum(rows), args[0].shape[1])], "v" * len(args) + "-v", limit=8
    )[0]


def place_sums(chain, bits, quarters, rows, targets, outs, whole=(), vec=(), skip=0):
    d = quarters[0][0].shape[1]
    n = len(outs)
    arrays = []
    for a, *_ in quarters:
        if not any(a is b for b in arrays):
            arrays.append(a)
    which = [next(k for k, b in enumerate(arrays) if b is a) for a, *_ in quarters]

    def kernel(io, bits_ref, *refs):
        refs, (buf, sems) = refs[:-2], refs[-2:]
        ins = [refs[k] for k in which]
        refs = refs[len(arrays) + len(whole) :]
        out_refs, vec_refs = refs[:n], refs[n:]

        def each(step):
            for j, (_, _, half, quarter) in enumerate(quarters):
                if j < skip:
                    continue
                half = 1 - bits_ref[0] if half else bits_ref[0]
                quarter = 1 - bits_ref[1] if quarter else bits_ref[1]
                for at, (out, index, first) in enumerate(targets):
                    ref = out_refs[out]
                    ref = ref if index is None else ref.at[index]
                    ref = ref.at[first : first + rows]
                    copy = pltpu.make_async_copy(buf.at[j], ref, sems.at[j])
                    pl.when(2 * half + quarter == at)(functools.partial(step, copy))

        starts = [start for _, start, _, _ in quarters]
        for j, ref in enumerate(ins):
            if j >= skip:
                buf[j] = ref[starts[j] : starts[j] + rows].astype(F32)
        each(lambda copy: copy.start())
        if vec:
            a, b, c, e = (ref[x + rows : x + rows + 16].astype(F32) for ref, x in zip(ins, starts))
            total = jnp.where(bits_ref[5] == 0, (a + b) + (c + e), (a + c) + (b + e))
            for at, (length, ref) in enumerate(zip(vec, vec_refs)):
                ref[...] = total[at, :length]
        each(lambda copy: copy.wait())

    return chain.call(
        kernel, "place_sums", (bits, *arrays, *whole), [*outs, *(f32(length) for length in vec)],
        "s" + "v" * len(arrays) + "p" * len(whole) + "-" + "r" * n + "v" * len(vec), limit=8,
        aliases={1 + len(arrays) + j: j for j in range(len(whole))},
        scratch=[pltpu.VMEM((len(quarters), rows, d), F32), pltpu.SemaphoreType.DMA((len(quarters),))],
    )


def local(
    n_dp, n_tensor, tokens, node_counts, edge_counts, ln1_gain, ln1_bias, qkv_weight, out_weight,
    ln2_gain, ln2_bias, fc1_weight, fc1_bias, fc2_weight, out_grad,
):
    d = tokens.shape[1]
    shard = out_weight.shape[0]
    width = 2 * shard
    mols = tokens.shape[0] // LEN
    dp_at = lax.axis_index("dp")
    tensor_at = lax.axis_index("tensor")
    core = tensor_at % 2
    bit0 = dp_at % 2
    bit1 = (dp_at // 2) % 2
    bits = jnp.stack(
        [jnp.where(core == 0, bit0, bit1), jnp.where(core == 0, bit1, bit0), bit0, tensor_at * mols,
         (tensor_at ^ 2) * mols, core, bit1]
    ).astype(jnp.int32)
    chain = Chain()

    def swap_core(a):
        return lax.ppermute(a, "tensor", [(t, t ^ 1) for t in range(n_tensor)])

    def swap_y(a):
        return lax.ppermute(a, "tensor", [(t, t ^ 2) for t in range(n_tensor)])

    def swap_dp(a, mask0, mask1):
        pairs = [
            (p * n_tensor + t, (p ^ (mask1 if t % 2 else mask0)) * n_tensor + t)
            for p in range(n_dp)
            for t in range(n_tensor)
        ]
        return lax.ppermute(a, ("dp", "tensor"), pairs)

    swap_first = lambda a: swap_dp(a, 1, 2)
    swap_second = lambda a: swap_dp(a, 2, 1)
    far_masks = [1 << k for k in range(2, n_dp.bit_length() - 1)]

    w_got = swap_core(qkv_weight)
    x_got, far_g = swap_y(tokens), swap_y(out_grad)
    picked = pick(chain, bits, out_weight, fc1_weight, fc2_weight, fc1_bias)
    far_y = swap_y(picked)
    near, others = load(
        chain, out_weight, fc1_weight, fc2_weight, picked,
        (tokens, out_grad, ln1_gain, ln1_bias, ln2_gain, ln2_bias),
    )
    near = (near, swap_core(near))
    tokens, out_grad, ln1_gain, ln1_bias, ln2_gain, ln2_bias = others

    counts = (node_counts, edge_counts)
    norm1 = (ln1_gain, ln1_bias)
    a1_0, qt_0, kt_0, v_0, p_0, ot_0, o_0, w_qkv = attention(
        chain, bits, 3, *counts, tokens, *norm1, (qkv_weight, w_got)
    )
    far_o = swap_y(o_0)
    far_y, short = hold(chain, far_y, d)
    far_x, far_z = swap_dp(short, 1, 1), swap_dp(short, 2, 2)
    far_z, pair = pair_up(chain, far_x, far_z)
    far_xz = swap_dp(far_z, 1, 1)
    a1_1, qt_1, kt_1, v_1, p_1, ot_1, o_1, wo, fc1, fc2 = attention(
        chain, bits, 4, *counts, x_got, *norm1, w_qkv, near=near
    )
    o_got = swap_y(o_1)
    spacer(chain)
    fars = (far_y, pair, far_xz)
    fars += tuple(swap_core(a) for a in fars)
    norm2 = (ln2_gain, ln2_bias)
    wo, fc1, fc2 = pack_far(chain, bits, (wo, fc1, fc2), fars)
    low, far_low = 3 * shard, 3 * shard // 4
    biases = ((near[0], low), (near[1], low), (fars[0], far_low), (fars[3], far_low))

    part_0, part_1, dz_0, dz_1, b1 = feed_in(
        chain, (tokens, x_got), (o_0, o_1), (out_grad, far_g), wo, fc2, biases
    )

    class Sum:
        def __init__(self, count, keep, got, apart, early):
            self.size = count * shard // 4
            self.apart, self.early = apart, early
            view = lambda a: a.reshape(2, 2, self.size, d)
            self.parts = (view(keep), view(got))

        def first(self):
            sent = sum_half(chain, bits, *self.parts, self.apart)
            got = [swap_first(a) for a in sent]
            self.on, self.kept = got if self.apart else ((got[0], 0), (got[0], 1))

        def second(self):
            self.got = swap_second(sum_quarter(chain, bits, *self.parts, False, self.on))

        def third(self, *vec):
            self.sum = sum_quarter(chain, bits, *self.parts, True, self.kept, self.got, vec=vec)
            self.got = swap_dp(self.sum, far_masks[0], far_masks[0])

        def third_apart(self):
            self.sums = sum_quarter_apart(chain, bits, *self.parts, self.kept, self.got)
            self.gots = [swap_dp(a, far_masks[0], far_masks[0]) for a in self.sums]
            self.halves = [None, None]

        def fourth_apart(self, at, *vec):
            self.sum, self.got = self.sums[at], self.gots[at]
            self.fourth(*vec)
            self.halves[at] = self.quarters

        def fourth(self, *vec):
            a = sum_pairs(chain, (self.sum, self.got), *vec)
            for mask in far_masks[1:]:
                a = sum_pairs(chain, (a, swap_dp(a, mask, mask)))
            b = swap_second(a)
            if self.early == 1:
                self.quarters = [(a, 0, 0, 0), (b, 0, 0, 1), (swap_first(a), 0, 1, 0), (swap_first(b), 0, 1, 1)]
            self.last = (a, b)

        def fifth(self):
            if self.early == 0:
                (a,) = side_by_side(chain, *self.last, False)
                b = swap_first(a)
                rows = a.shape[0] // 2
                self.quarters = [(a, 0, 0, 0), (a, rows, 0, 1), (b, 0, 1, 0), (b, rows, 1, 1)]
            if self.early == 3:
                a, b = self.last
                sent = lax.optimization_barrier((a, chain.token))[0]
                self.quarters = [(a, 0, 0, 0), (b, 0, 0, 1), (swap_first(sent), 0, 1, 0), (swap_first(b), 0, 1, 1)]
            if self.early == 2:
                a, b = side_by_side(chain, *self.last, True)
                self.quarters = [(a, 0, 0, 0), (b, 0, 0, 1), (swap_first(a), 0, 1, 0), (swap_first(b), 0, 1, 1)]

    h_1, du_1, *far_r = feed_far(chain, part_1, far_o, dz_1, far_g, *norm2, wo, fc1, b1)
    gh_1, dp_1 = backward(chain, (du_1, fc1, h_1, far_g, ln2_gain, wo, p_1, qt_1, kt_1, v_1), False)
    h_0, z_0, du_0, keep_r, send_r, bias_sums = feed_own(
        chain, part_0, o_got, dz_0, out_grad, *norm2, wo, fc1, b1, (du_1, *far_r)
    )
    gh_0, dp_0, dh, sums = backward(chain, (du_0, fc1, h_0, out_grad, ln2_gain, wo, p_0, qt_0, kt_0, v_0), True)
    r = Sum(2, keep_r, swap_core(send_r), True, 1)
    r.first()
    a1s = (a1_0, a1_1)
    lefts = [(dp_0, dp_1, c * width) for c in range(3)] + [(ot_0, ot_1, 0)]
    rights = [a1s] * 3 + [(gh_0, gh_1)]
    got_q = swap_core(weight_grads(chain, "weight_grads", shard, 1, lefts, rights))
    q = Sum(4, weight_grads(chain, "weight_grads", shard, 0, lefts, rights), got_q, True, 3)
    r.second()
    q.first()
    r.third()
    q.second()
    da1_mine, da1_theirs = input_grads(chain, (dp_0, dp_1), w_qkv, (tokens, x_got), sums, bias_sums)
    da1_got = swap_y(da1_theirs)
    r.fourth()
    q.third()
    vec = vector_rows(chain, da1_theirs, da1_got)
    vec_got = swap_core(vec)
    r.fifth()
    halves = [(c, None, half * shard // 2) for c in range(2) for half in range(2)]
    grad_fc1, grad_fc2 = place_sums(chain, bits, r.quarters, r.size, halves, [f32(shard, d)] * 2)
    vec = vector_cores(chain, vec, vec_got, shard)
    vec_got = swap_dp(vec, far_masks[0], far_masks[0])
    q.fourth((vec, vec_got))
    result = feed_result(chain, z_0, fc2, h_0)
    grad_tokens = input_norm(chain, tokens, ln1_gain, da1_mine, da1_got, dh)
    q.fifth()
    each = [(0, 0, 0), (0, 1, 0), (0, 2, 0), (1, None, 0)]
    outs = [f32(3, shard, d), f32(shard, d)]
    grads = place_sums(chain, bits, q.quarters[:3], q.size, each, outs)
    grad_qkv, grad_out, gain1, bias1, gain2, bias2, grad_b = place_sums(
        chain, bits, q.quarters, q.size, each, outs, grads, (d, d, d, d, shard), 3
    )
    return (
        result, grad_tokens, gain1, bias1, grad_qkv, grad_out, gain2, bias2, grad_fc1, grad_b, grad_fc2,
    )


def solution(mesh):
    tokens = P(("dp", "tensor"), None)
    rows = P("tensor", None)
    qkv = P(None, "tensor", None)
    in_specs = (
        tokens, P("dp"), P("dp"), P(), P(), qkv, rows, P(), P(), rows, P("tensor"), rows, tokens,
    )
    out_specs = (tokens, tokens, P(), P(), qkv, rows, P(), P(), rows, P("tensor"), rows)
    step = functools.partial(local, mesh.shape["dp"], mesh.shape["tensor"])
    return jax.shard_map(step, mesh=mesh, in_specs=in_specs, out_specs=out_specs, check_vma=False)
```

```python
import functools

import jax
import jax.numpy as jnp
from jax import lax
from jax.experimental import pallas as pl
from jax.experimental.pallas import tpu as pltpu
from jax.sharding import PartitionSpec as P

HEAD_DIM = 24
LEN = 128
PAIR = 2 * HEAD_DIM
EPSILON = 1e-05
SCALE = HEAD_DIM ** (-0.5)
LOG2E = 1.4426950408889634
F32 = jnp.float32
BF16 = jnp.bfloat16
MIB = 1024 * 1024


def dot_nn(a, b):
    return lax.dot_general(a, b, (((1,), (0,)), ((), ())), preferred_element_type=F32)


def dot_nt(a, b):
    return lax.dot_general(a, b, (((1,), (1,)), ((), ())), preferred_element_type=F32)


def dot_tn(a, b):
    return lax.dot_general(a, b, (((0,), (0,)), ((), ())), preferred_element_type=F32)


def normalise(v):
    centered = v - jnp.mean(v, axis=-1, keepdims=True)
    r = lax.rsqrt(jnp.mean(centered * centered, axis=-1, keepdims=True) + EPSILON)
    return centered * r, r


def norm_back(da, gain, xh, r):
    e = da * gain
    return r * (
        e - jnp.mean(e, axis=-1, keepdims=True) - xh * jnp.mean(e * xh, axis=-1, keepdims=True)
    )


def pair_blocks(rows):
    rows = rows.astype(F32)
    none = jnp.zeros((HEAD_DIM, LEN), F32)
    left = jnp.concatenate([rows[:HEAD_DIM], none], axis=0)
    right = jnp.concatenate([none, rows[HEAD_DIM:]], axis=0)
    return jnp.concatenate([left, right], axis=1).astype(BF16)


def pair_window(i, width):
    low = min(PAIR * i // LEN * LEN, width - 2 * LEN)
    return low, PAIR * i - low


def placed(block, before):
    parts = []
    if before:
        parts.append(jnp.zeros((before, 2 * LEN), BF16))
    parts.append(block)
    after = 2 * LEN - PAIR - before
    if after:
        parts.append(jnp.zeros((after, 2 * LEN), BF16))
    return jnp.concatenate(parts, axis=0)


def diagonal(both):
    return jnp.concatenate([both[:HEAD_DIM, :LEN], both[HEAD_DIM:, LEN:]], axis=0)


STRIP = 256
COSTS = (0, 0, 100, 0, 0, 30, 30, 0, 0, 0, 0, 0, 100, 0, 0, 0, 200, 0, 60, 0, 0, 30, 0, 0, 0, 0, 0, 0, 0, 0, 0, 0)


class IO:
    def __init__(self, reads, writes):
        self.reads, self.writes = reads, writes
        self.started = set()

    def wait(self, *args):
        for j in args:
            if j in self.reads:
                self.reads[j].wait()

    def flush(self, *outs):
        for j in outs:
            if j in self.writes:
                self.started.add(j)
                self.writes[j].start()

    def finish(self):
        self.flush(*(j for j in self.writes if j not in self.started))
        for copy in self.writes.values():
            copy.wait()


def pinned(a):
    return pltpu.with_memory_space_constraint(a, pltpu.HBM)


class Chain:
    def __init__(self):
        self.token, self.calls = None, 0

    def call(self, kernel, name, args, outs, kinds, scratch=(), limit=16, aliases={}, last=False):
        ins, out_kinds = kinds.split("-")
        cost = COSTS[min(self.calls, len(COSTS) - 1)]
        self.calls += 1
        assert len(ins) == len(args) and len(out_kinds) == len(outs)
        hbm = pl.BlockSpec(memory_space=pltpu.HBM)
        vmem = pl.BlockSpec(memory_space=pltpu.VMEM)
        smem = pl.BlockSpec(memory_space=pltpu.SMEM)
        spec = lambda kind: {"s": smem, "v": vmem}.get(kind, hbm)
        tokens = () if self.token is None else (self.token,)
        staged = [j for j, kind in enumerate(ins) if kind in "hcl"]
        written = [j for j, kind in enumerate(out_kinds) if kind == "w"]
        memory = lambda kind: pltpu.SMEM if kind == "c" else pltpu.VMEM
        buffers = [memory(ins[j])(args[j].shape, args[j].dtype) for j in staged]
        buffers += [pltpu.VMEM(outs[j].shape, outs[j].dtype) for j in written]
        n_in, n_out, n_buf, n_tokens = len(args) + len(tokens), len(outs), len(buffers), 0 if last else 1

        def body(*refs):
            arg_refs = list(refs[: len(args)])
            out_refs = list(refs[n_in : n_in + n_out])
            tokens_out, own = refs[n_in + n_out :][:n_tokens], refs[n_in + n_out + n_tokens :]
            bufs, sems, extra = own[:n_buf], own[n_buf], own[n_buf + 1 :]
            reads, writes = {}, {}
            for at, j in enumerate(staged):
                reads[j] = pltpu.make_async_copy(arg_refs[j], bufs[at], sems.at[at])
                reads[j].start()
                arg_refs[j] = bufs[at]
            for at, j in enumerate(written, len(staged)):
                writes[j] = pltpu.make_async_copy(bufs[at], out_refs[j], sems.at[at])
                out_refs[j] = bufs[at]
            io = IO(reads, writes)
            io.wait(*(j for j in staged if ins[j] == "h"))
            for token_ref in tokens_out:
                token_ref[...] = jnp.zeros_like(token_ref)
            kernel(io, *arg_refs, *out_refs, *extra)
            io.finish()

        results = pl.pallas_call(
            body,
            in_specs=[spec(kind) for kind in ins] + [vmem] * len(tokens),
            out_specs=[spec(kind) for kind in out_kinds] + [vmem] * n_tokens,
            out_shape=[*outs, *[f32(8, 128)] * n_tokens],
            input_output_aliases=aliases,
            scratch_shapes=[*buffers, pltpu.SemaphoreType.DMA((max(n_buf, 1),)), *scratch],
            compiler_params=pltpu.CompilerParams(vmem_limit_bytes=limit * MIB),
            cost_estimate=pl.CostEstimate(flops=cost * 10**8, bytes_accessed=10**8, transcendentals=0),
            name=name,
        )(*(pinned(a) if kind in "hclp" else a for a, kind in zip(args, ins)), *tokens)
        self.token = None if last else results[-1]
        return results[: len(outs)]


def bf16(*shape):
    return jax.ShapeDtypeStruct(shape, BF16)


def f32(*shape):
    return jax.ShapeDtypeStruct(shape, F32)


def copies(sems, pairs):
    started = [pltpu.make_async_copy(a, b, sems.at[j]) for j, (a, b) in enumerate(pairs)]
    for copy in started:
        copy.start()
    return started


def finish(started):
    for copy in started:
        copy.wait()


def attention(chain, bits, place, nodes, edges, x, gain, bias, w, near=()):
    rows, d = x.shape
    apart = isinstance(w, tuple)
    width = 2 * w[0].shape[1] if apart else w.shape[1]
    shard = width // 2
    pairs = width // PAIR
    mols = rows // LEN

    def kernel(io, bits_ref, nodes_ref, edges_ref, x_ref, gain_ref, bias_ref, *refs):
        started = []
        if not apart:
            w_ref, near0, near1, *refs, wo_ref, fc1_ref, fc2_ref, sems = refs
            a1_ref, qt_ref, kt_ref, v_ref, p_ref, ot_ref, o_ref = refs
            pairs_w = []
            for at, ref in enumerate((near0, near1)):
                for c, out in enumerate((wo_ref, fc1_ref, fc2_ref)):
                    part = ref.at[c * shard : (c + 1) * shard]
                    pairs_w.append((part, out.at[at * shard : (at + 1) * shard]))
            started = copies(sems, pairs_w)
        else:
            own, got, *refs, w_ref, sems = refs
            a1_ref, qt_ref, kt_ref, v_ref, p_ref, ot_ref, o_ref = refs
            pairs_w = [(own, w_ref.at[:, :shard]), (got, w_ref.at[:, shard:])]
            near_w = copies(sems, pairs_w)
        xh, _ = normalise(x_ref[...].astype(F32))
        a1 = (xh * gain_ref[...][None, :] + bias_ref[...][None, :]).astype(BF16)
        a1_ref[...] = a1
        if apart:
            finish(near_w)
        qt = dot_nt(w_ref[0], a1).astype(BF16)
        keys = dot_nt(a1, w_ref[1]).astype(BF16)
        vt = dot_nt(w_ref[2], a1).astype(BF16)
        qt_ref[...] = qt
        every = [(m, i) for m in range(mols) for i in range(pairs)]
        lanes = lambda m: slice(LEN * m, LEN * (m + 1))
        rows_of = lambda i: slice(PAIR * i, PAIR * (i + 1))
        scores, probs = {}, {}
        for m, i in every:
            low, before = pair_window(i, width)
            rhs = placed(pair_blocks(qt[rows_of(i), lanes(m)]), before)
            scores[m, i] = dot_nn(keys[lanes(m), low : low + 2 * LEN], rhs)
        io.wait(1, 2)
        for m in range(mols):
            mol = bits_ref[place] + m
            count = 1 + nodes_ref[mol] + edges_ref[mol]
            valid = lax.broadcasted_iota(jnp.int32, (LEN, 2 * LEN), 0) < count
            for i in range(pairs):
                s = jnp.where(valid, scores[m, i], -1e30)
                e = jnp.exp2((s - jnp.max(s, axis=0, keepdims=True)) * (SCALE * LOG2E))
                p = (e * (1.0 / jnp.sum(e, axis=0, keepdims=True))).astype(BF16)
                p_ref[m, i] = p
                probs[m, i] = p
        for m, i in every:
            both = dot_nn(vt[rows_of(i), lanes(m)], probs[m, i])
            ot_ref[rows_of(i), lanes(m)] = diagonal(both).astype(BF16)
        o_ref[...] = ot_ref[...].T
        kt_ref[...] = dot_nt(w_ref[1], a1).astype(BF16)
        v_ref[...] = dot_nt(a1, w_ref[2]).astype(BF16)
        finish(started)

    outs = [
        bf16(rows, d), bf16(width, rows), bf16(width, rows), bf16(rows, width),
        bf16(mols, pairs, LEN, 2 * LEN), bf16(width, rows),
    ]
    args = (bits, nodes, edges, x, gain, bias)
    if not apart:
        return chain.call(
            kernel, "attention_forward", (*args, w, *near), [*outs, bf16(rows, width), bf16(2 * width, d), bf16(2 * width, d), bf16(2 * width, d)],
            "sccvvvvvv-vvvvvvvvvv", scratch=[pltpu.SemaphoreType.DMA((6,))],
        )
    return chain.call(
        kernel, "attention_forward", (*args, *w), [*outs, bf16(rows, width), bf16(3, width, d)],
        "sccvvvpr-vvvvvvvv", scratch=[pltpu.SemaphoreType.DMA((2,))],
    )


def pick(chain, bits, wo, fc1, fc2, bias):
    shard, d = wo.shape
    rows = 3 * shard // 4
    strips = d // STRIP

    def kernel(io, bits_ref, wo_ref, fc1_ref, fc2_ref, bias_ref, out_ref, sems):
        refs = (wo_ref, fc1_ref, fc2_ref)

        def part(quarter):
            pairs = []
            for c, first, at, n in quarter_rows(quarter, shard):
                for k in range(strips):
                    source = refs[c].at[first : first + n, k * STRIP : (k + 1) * STRIP]
                    pairs.append((source, out_ref.at[k * rows + at : k * rows + at + n]))
            started = copies(sems, pairs)
            io.wait(4)
            out_ref[strips * rows :] = jnp.concatenate(
                [jnp.broadcast_to(bias_ref[...].astype(F32)[None, :], (16, shard)), jnp.zeros((16, STRIP - shard), F32)],
                axis=1,
            ).astype(BF16)
            finish(started)

        which = 2 * bits_ref[2] + bits_ref[6]
        for at in range(4):
            pl.when(which == at)(functools.partial(part, at))

    return chain.call(
        kernel, "pick", (bits, wo, fc1, fc2, bias), [bf16(strips * rows + 16, STRIP)], "spppl-v", limit=4,
        scratch=[pltpu.SemaphoreType.DMA((2 * strips,))],
    )[0]


def quarter_rows(quarter, shard):
    size = 3 * shard // 4
    found, at = [], 0
    while at < size:
        which, first = divmod(quarter * size + at, shard)
        n = min(size - at, shard - first)
        found.append((which, first, at, n))
        at += n
    return found


def hold(chain, a, d):
    strips = d // STRIP
    rows = (a.shape[0] - 16) // strips

    def kernel(io, a_ref, out_ref, short_ref):
        for k in range(strips):
            strip = a_ref[k * rows : (k + 1) * rows]
            out_ref[:rows, k * STRIP : (k + 1) * STRIP] = strip
            short_ref[:, k * STRIP : (k + 1) * STRIP] = strip
        out_ref[rows:] = widened(a_ref[strips * rows :], d)

    return chain.call(kernel, "hold", (a,), [bf16(rows + 16, d), bf16(rows, d)], "v-vv", limit=4)


def widened(a, d):
    return jnp.concatenate([a, jnp.zeros((a.shape[0], d - a.shape[1]), a.dtype)], axis=1)


def pair_up(chain, a, b):
    def kernel(io, a_ref, b_ref, out_ref, both_ref):
        out_ref[...] = b_ref[...]
        both_ref[0] = a_ref[...]
        both_ref[1] = b_ref[...]

    return chain.call(kernel, "pair_up", (a, b), [bf16(*b.shape), bf16(2, *a.shape)], "vv-vv", limit=4)


def spacer(chain, *after):
    def kernel(io, *refs):
        pass

    chain.call(kernel, "spacer", after, [], "r" * len(after) + "-", limit=2)


def load(chain, out_weight, fc1_weight, fc2_weight, picked, others):
    shard, d = out_weight.shape
    n = len(others)

    def kernel(io, wo, fc1, fc2, picked_ref, *refs):
        others_in, (near_ref, *others_out, sems) = refs[:n], refs[n:]
        near_ref[3 * shard :] = widened(picked_ref[picked.shape[0] - 16 :], d)
        rows = lambda at: near_ref.at[at * shard : (at + 1) * shard]
        near = [(wo, rows(0)), (fc1, rows(1)), (fc2, rows(2))]
        finish(copies(sems, near + list(zip(others_in, others_out))))

    near, *others = chain.call(
        kernel, "load", (out_weight, fc1_weight, fc2_weight, picked, *others),
        [bf16(3 * shard + 16, d)] + [jax.ShapeDtypeStruct(a.shape, a.dtype) for a in others],
        "pppv" + "p" * n + "-v" + "v" * n, limit=4, scratch=[pltpu.SemaphoreType.DMA((3 + n,))],
    )
    return near, others


def feed_body(part, ob, dz, wo_ref, gain_ref, bias_ref, fc1_ref, b1, h_ref, a2_ref, z_ref, du_ref):
    h = part + dot_nn(ob, wo_ref[wo_ref.shape[0] // 2 :])
    h_ref[...] = h
    xh, _ = normalise(h)
    a2 = (xh * gain_ref[...][None, :] + bias_ref[...][None, :]).astype(BF16)
    a2_ref[...] = a2
    u = dot_nt(a2, fc1_ref[...]) + b1
    phi = 0.5 * (1.0 + lax.erf(u * (0.5**0.5)))
    slope = phi + u * (jnp.exp(-0.5 * u * u) * 0.3989422804014327)
    du_ref[...] = (dz * slope).astype(BF16)
    z_ref[...] = (u * phi).astype(BF16)


def pack_far(chain, bits, weights, fars):
    rows, d = weights[0].shape
    shard = rows // 4

    def kernel(io, bits_ref, wo_in, fc1_in, fc2_in, y0, pair0, xz0, y1, pair1, xz1, *outs):
        def placed_at(which):
            for at, (y, pair, xz) in enumerate(((y0, pair0, xz0), (y1, pair1, xz1))):
                for turn, ref in enumerate((y, pair.at[1], pair.at[0], xz)):
                    for c, first, start, n in quarter_rows(which ^ turn, shard):
                        row = (2 + at) * shard + first
                        outs[c][row : row + n] = ref[start : start + n]

        which = 2 * bits_ref[2] + bits_ref[6]
        for at in range(4):
            pl.when(which == at)(functools.partial(placed_at, at))

    return chain.call(
        kernel, "pack_far", (bits, *weights, *fars), [bf16(rows, d)] * 3, "s" + "v" * 9 + "-vvv", limit=4,
        aliases={1: 0, 2: 1, 3: 2},
    )


def feed_in(chain, xs, os, gs, wo, fc2, biases):
    rows, d = xs[0].shape
    columns = fc2.shape[0]
    shard = columns // 4

    def kernel(io, x0, x1, o0, o1, g0, g1, wo_ref, fc2_ref, *refs):
        b_refs, (h0, h1, dz0, dz1, b1_ref) = refs[:4], refs[4:]
        for x_ref, o_ref, h_ref in ((x0, o0, h0), (x1, o1, h1)):
            h_ref[...] = x_ref[...].astype(F32) + dot_nn(o_ref[...], wo_ref[: o_ref.shape[1]])
        for g_ref, dz_ref in ((g0, dz0), (g1, dz1)):
            dz_ref[...] = dot_nt(g_ref[...], fc2_ref[...])
        parts = [ref[row : row + 1, :shard].astype(F32) for ref, (_, row) in zip(b_refs, biases)]
        b1_ref[...] = jnp.concatenate(parts, axis=1)

    return chain.call(
        kernel, "feed_in", (*xs, *os, *gs, wo, fc2, *(a for a, _ in biases)),
        [f32(rows, d)] * 2 + [f32(rows, columns)] * 2 + [f32(1, columns)], "v" * 12 + "-vvvvv",
    )


def feed_far(chain, h, ob, dz, g, gain, bias, wo, fc1, b1):
    rows, d = h.shape
    columns = fc1.shape[0]
    width = columns // 2

    def kernel(io, part_ref, ob_ref, dz_ref, g_ref, gain_ref, bias_ref, wo_ref, fc1_ref, b1_ref,
               h_ref, du_ref, first_ref, second_ref, a2_ref, z_ref):
        feed_body(
            part_ref[...], ob_ref[...], dz_ref[...], wo_ref, gain_ref, bias_ref, fc1_ref, b1_ref[...], h_ref, a2_ref,
            z_ref, du_ref,
        )
        first_ref[...] = dot_tn(du_ref[:, :width], a2_ref[...])
        second_ref[...] = dot_tn(z_ref[:, :width], g_ref[...])

    return chain.call(
        kernel, "feed_far", (h, ob, dz, g, gain, bias, wo, fc1, b1),
        [f32(rows, d), bf16(rows, columns), f32(width, d), f32(width, d)], "v" * 9 + "-vvvv",
        scratch=[pltpu.VMEM((rows, d), BF16), pltpu.VMEM((rows, columns), BF16)],
    )


def feed_own(chain, h, ob, dz, g, gain, bias, wo, fc1, b1, far):
    rows, d = h.shape
    columns = fc1.shape[0]
    width = columns // 2
    shard = width // 2

    def kernel(io, part_ref, ob_ref, dz_ref, g_ref, gain_ref, bias_ref, wo_ref, fc1_ref, b1_ref, du1, first1, second1,
               h_ref, z_ref, du_ref, keep_ref, send_ref, sums_ref, a2_ref):
        feed_body(
            part_ref[...], ob_ref[...], dz_ref[...], wo_ref, gain_ref, bias_ref, fc1_ref, b1_ref[...], h_ref, a2_ref,
            z_ref, du_ref,
        )
        du = du_ref[:, :width]
        first = dot_tn(du, a2_ref[...]) + first1[...]
        second = dot_tn(z_ref[:, :width], g_ref[...]) + second1[...]
        for at, ref in enumerate((keep_ref, send_ref)):
            here = slice(at * shard, (at + 1) * shard)
            ref[0] = first[here].astype(BF16)
            ref[1] = second[here].astype(BF16)
        sums_ref[...] = jnp.sum(du.astype(F32), axis=0, keepdims=True) + jnp.sum(
            du1[:, :width].astype(F32), axis=0, keepdims=True
        )

    return chain.call(
        kernel, "feed_own", (h, ob, dz, g, gain, bias, wo, fc1, b1, *far),
        [f32(rows, d), bf16(rows, columns), bf16(rows, columns), bf16(2, shard, d), bf16(2, shard, d), f32(1, width)],
        "v" * 12 + "-vvvvvv", scratch=[pltpu.VMEM((rows, d), BF16)],
    )


def feed_result(chain, z, fc2, h):
    def kernel(io, z_ref, fc2_ref, h_ref, out_ref):
        out_ref[...] = (h_ref[...] + dot_nn(z_ref[...], fc2_ref[...])).astype(BF16)

    return chain.call(kernel, "feed_result", (z, fc2, h), [bf16(*h.shape)], "vvv-w", limit=8)[0]


def backward(chain, args, own):
    h, kt = args[2], args[8]
    rows, d = h.shape
    width = kt.shape[0]
    mols, pairs = rows // LEN, width // PAIR

    def kernel(io, du_ref, fc1_ref, h_ref, g_ref, gain_ref, wo_ref, p_ref, qt_ref, kt_ref, v_ref,
               gh_ref, dp_ref, dh_ref=None, sums_ref=None):
        da2 = dot_nn(du_ref[...], fc1_ref[...])
        xh, r = normalise(h_ref[...])
        dh = g_ref[:, :d].astype(F32) + norm_back(da2, gain_ref[...][None, :], xh, r)
        if own:
            dh_ref[...] = dh
            sums_ref[0:1] = jnp.sum(da2 * xh, axis=0, keepdims=True)
            sums_ref[1:2] = jnp.sum(da2, axis=0, keepdims=True)
            io.flush(2)
        gh = dh.astype(BF16)
        gh_ref[...] = gh
        dot = dot_nt(wo_ref[:width], gh).astype(BF16)
        every = [(m, i) for m in range(mols) for i in range(pairs)]
        lanes = lambda m: slice(LEN * m, LEN * (m + 1))
        rows_of = lambda i: slice(PAIR * i, PAIR * (i + 1))
        dps, dss, dos = {}, {}, {}
        for m, i in every:
            low, before = pair_window(i, width)
            dos[m, i] = pair_blocks(dot[rows_of(i), lanes(m)])
            dps[m, i] = dot_nn(v_ref[lanes(m), low : low + 2 * LEN], placed(dos[m, i], before))
        for m, i in every:
            dv = dot_nt(dos[m, i], p_ref[m, i])
            dp_ref[pl.ds(2 * width + PAIR * i, PAIR), lanes(m)] = dv.astype(BF16)
        for m, i in every:
            p = p_ref[m, i].astype(F32)
            t = dps[m, i] * p
            dss[m, i] = (t - p * jnp.sum(t, axis=0, keepdims=True)).astype(BF16)
        for m, i in every:
            dq = diagonal(dot_nn(kt_ref[rows_of(i), lanes(m)], dss[m, i])) * SCALE
            dp_ref[rows_of(i), lanes(m)] = dq.astype(BF16)
            dk = dot_nt(pair_blocks(qt_ref[rows_of(i), lanes(m)]), dss[m, i]) * SCALE
            dp_ref[pl.ds(width + PAIR * i, PAIR), lanes(m)] = dk.astype(BF16)

    outs = [bf16(rows, d), bf16(3 * width, rows)] + ([f32(rows, d), f32(8, d)] if own else [])
    return chain.call(
        kernel, "attention_backward", args, outs, "v" * 10 + ("-vvvv" if own else "-vv"),
    )


def weight_grads(chain, name, shard, at, lefts, rights):
    d = rights[0][0].shape[1]
    args, count = [], len(lefts)
    for (u0, u1, _), (v0, v1) in zip(lefts, rights):
        args += [u0, u1, v0, v1]

    def kernel(io, *refs):
        out_ref = refs[-1]
        for c in range(count):
            u0, u1, v0, v1 = refs[4 * c : 4 * c + 4]
            rows = slice(lefts[c][2] + at * shard, lefts[c][2] + (at + 1) * shard)
            left = jnp.concatenate([u0[rows], u1[rows]], axis=1)
            right = jnp.concatenate([v0[...], v1[...]], axis=0)
            out_ref[c] = dot_nn(left, right).astype(BF16)

    return chain.call(kernel, name, args, [bf16(count, shard, d)], "v" * len(args) + "-v")[0]


def input_grads(chain, dps, w, xs, sums, bias):
    rows, d = xs[0].shape

    def kernel(io, dp0, dp1, w_ref, x0, x1, sums_ref, bias_ref, mine_ref, theirs_ref):
        w = w_ref[...].reshape(dp0.shape[0], d)
        theirs = dot_tn(dp1[...], w)
        theirs_ref[:rows] = theirs.astype(BF16)
        mine = dot_tn(dp0[...], w)
        mine_ref[...] = mine
        xh0, _ = normalise(x0[...].astype(F32))
        xh1, _ = normalise(x1[...].astype(F32))
        bias = bias_ref[...]
        vec = [
            jnp.sum(mine * xh0, axis=0, keepdims=True) + jnp.sum(theirs * xh1, axis=0, keepdims=True),
            jnp.sum(mine, axis=0, keepdims=True) + jnp.sum(theirs, axis=0, keepdims=True),
            sums_ref[0:2],
            jnp.concatenate([bias, jnp.zeros((1, d - bias.shape[1]), F32)], axis=1),
            jnp.zeros((11, d), F32),
        ]
        theirs_ref[rows:] = jnp.concatenate(vec, axis=0).astype(BF16)

    return chain.call(
        kernel, "input_grads", (*dps, w, *xs, sums, bias), [f32(rows, d), bf16(rows + 16, d)], "vvvvvvv-vv"
    )


def input_norm(chain, x, gain, mine, got, dh):
    rows, d = x.shape

    def kernel(io, x_ref, gain_ref, mine_ref, got_ref, dh_ref, out_ref):
        xh, r = normalise(x_ref[...].astype(F32))
        da1 = mine_ref[...] + got_ref[:rows].astype(F32)
        out_ref[...] = (dh_ref[...] + norm_back(da1, gain_ref[...][None, :], xh, r)).astype(BF16)

    return chain.call(
        kernel, "input_norm", (x, gain, mine, got, dh), [bf16(rows, d)], "vvvvv-w", limit=8
    )[0]


def plus(*terms):
    total = terms[0].astype(F32)
    for term in terms[1:]:
        total = total + term.astype(F32)
    return total.astype(BF16)


def vector_rows(chain, mine, got):
    rows, d = mine.shape

    def kernel(io, mine_ref, got_ref, out_ref):
        a, b = mine_ref[rows - 16 :], got_ref[rows - 16 :]
        same = lax.broadcasted_iota(jnp.int32, (16, d), 0) < 4
        out_ref[...] = plus(a, jnp.where(same, b.astype(F32), 0.0))

    return chain.call(kernel, "vector_rows", (mine, got), [bf16(16, d)], "vv-v", limit=4)[0]


def vector_cores(chain, mine, got, shard):
    def kernel(io, mine_ref, got_ref, out_ref):
        a, b = mine_ref[...].astype(F32), got_ref[...].astype(F32)
        turned = jnp.concatenate([b[:, shard : 2 * shard], b[:, :shard], b[:, 2 * shard :]], axis=1)
        same = lax.broadcasted_iota(jnp.int32, a.shape, 0) < 4
        out_ref[...] = plus(a, jnp.where(same, b, turned))

    return chain.call(kernel, "vector_cores", (mine, got), [bf16(*mine.shape)], "vv-v", limit=4)[0]


def sum_half(chain, bits, mine, got, apart):
    def kernel(io, bits_ref, mine_ref, got_ref, *outs):
        half, quarter = 1 - bits_ref[0], bits_ref[1]
        on_ref, kept_ref = outs if apart else (outs[0].at[0], outs[0].at[1])
        on_ref[...] = mine_ref[half, 1 - quarter] + got_ref[half, 1 - quarter]
        kept_ref[...] = mine_ref[half, quarter] + got_ref[half, quarter]

    rows, d = mine.shape[2:]
    outs = [bf16(rows, d)] * 2 if apart else [bf16(2, rows, d)]
    return chain.call(kernel, "sum_half", (bits, mine, got), outs, "svv-" + "v" * len(outs), limit=8)


def sum_quarter(chain, bits, mine, got, kept, *more, vec=()):
    rows, d = mine.shape[2:]
    arrays = [a[0] if isinstance(a, tuple) else a for a in more]

    def kernel(io, bits_ref, mine_ref, got_ref, *refs):
        *refs, out_ref = refs
        half = bits_ref[0]
        quarter = bits_ref[1] if kept else 1 - bits_ref[1]
        terms = [ref[a[1]] if isinstance(a, tuple) else ref[...] for a, ref in zip(more, refs)]
        out_ref[:rows] = plus(mine_ref[half, quarter], got_ref[half, quarter], *terms)
        if vec:
            out_ref[rows:] = refs[-1][...]

    args = (bits, mine, got, *arrays, *vec)
    return chain.call(
        kernel, "sum_quarter", args, [bf16(rows + (16 if vec else 0), d)], "s" + "v" * (len(args) - 1) + "-v",
        limit=8,
    )[0]


def sum_quarter_apart(chain, bits, mine, got, *more):
    rows, d = mine.shape[2:]
    arrays = [a[0] if isinstance(a, tuple) else a for a in more]

    def kernel(io, bits_ref, mine_ref, got_ref, *refs):
        *refs, upper_ref, lower_ref = refs
        half, quarter = bits_ref[0], bits_ref[1]
        terms = [ref[a[1]] if isinstance(a, tuple) else ref[...] for a, ref in zip(more, refs)]
        total = plus(mine_ref[half, quarter], got_ref[half, quarter], *terms)
        upper_ref[...] = total[: rows // 2]
        lower_ref[...] = total[rows // 2 :]

    args = (bits, mine, got, *arrays)
    return chain.call(
        kernel, "sum_quarter", args, [bf16(rows // 2, d)] * 2, "s" + "v" * (len(args) - 1) + "-vv", limit=8
    )


def side_by_side(chain, a, b, apart):
    rows, d = a.shape

    def kernel(io, a_ref, b_ref, *outs):
        first, second = outs if apart else (outs[0].at[:rows], outs[0].at[rows:])
        first[...] = a_ref[...]
        second[...] = b_ref[...]

    outs = [bf16(rows, d)] * 2 if apart else [bf16(2 * rows, d)]
    return chain.call(kernel, "side_by_side", (a, b), outs, "vv-" + "v" * len(outs), limit=8)


def sum_pairs(chain, *pairs):
    rows = [a.shape[0] for a, _ in pairs]

    def kernel(io, *refs):
        *refs, out_ref = refs
        start = 0
        for a_ref, b_ref in zip(refs[::2], refs[1::2]):
            out_ref[start : start + a_ref.shape[0]] = a_ref[...] + b_ref[...]
            start += a_ref.shape[0]

    args = [a for pair in pairs for a in pair]
    return chain.call(
        kernel, "sum_pairs", args, [bf16(sum(rows), args[0].shape[1])], "v" * len(args) + "-v", limit=8
    )[0]


def place_sums(chain, bits, quarters, rows, targets, outs, whole=(), vec=(), skip=0):
    d = quarters[0][0].shape[1]
    n = len(outs)
    arrays = []
    for a, *_ in quarters:
        if not any(a is b for b in arrays):
            arrays.append(a)
    which = [next(k for k, b in enumerate(arrays) if b is a) for a, *_ in quarters]

    def kernel(io, bits_ref, *refs):
        refs, (buf, sems) = refs[:-2], refs[-2:]
        ins = [refs[k] for k in which]
        refs = refs[len(arrays) + len(whole) :]
        out_refs, vec_refs = refs[:n], refs[n:]

        def each(step):
            for j, (_, _, half, quarter) in enumerate(quarters):
                if j < skip:
                    continue
                half = 1 - bits_ref[0] if half else bits_ref[0]
                quarter = 1 - bits_ref[1] if quarter else bits_ref[1]
                for at, (out, index, first) in enumerate(targets):
                    ref = out_refs[out]
                    ref = ref if index is None else ref.at[index]
                    ref = ref.at[first : first + rows]
                    copy = pltpu.make_async_copy(buf.at[j], ref, sems.at[j])
                    pl.when(2 * half + quarter == at)(functools.partial(step, copy))

        starts = [start for _, start, _, _ in quarters]
        for j, ref in enumerate(ins):
            if j >= skip:
                buf[j] = ref[starts[j] : starts[j] + rows].astype(F32)
        each(lambda copy: copy.start())
        if vec:
            a, b, c, e = (ref[x + rows : x + rows + 16].astype(F32) for ref, x in zip(ins, starts))
            total = jnp.where(bits_ref[5] == 0, (a + b) + (c + e), (a + c) + (b + e))
            for at, (length, ref) in enumerate(zip(vec, vec_refs)):
                ref[...] = total[at, :length]
            io.flush(*range(n, n + len(vec)))
        each(lambda copy: copy.wait())

    return chain.call(
        kernel, "place_sums", (bits, *arrays, *whole), [*outs, *(f32(length) for length in vec)],
        "s" + "v" * len(arrays) + "p" * len(whole) + "-" + "r" * n + "w" * len(vec), limit=8, last=bool(vec),
        aliases={1 + len(arrays) + j: j for j in range(len(whole))},
        scratch=[pltpu.VMEM((len(quarters), rows, d), F32), pltpu.SemaphoreType.DMA((len(quarters),))],
    )


def local(
    n_dp, n_tensor, tokens, node_counts, edge_counts, ln1_gain, ln1_bias, qkv_weight, out_weight,
    ln2_gain, ln2_bias, fc1_weight, fc1_bias, fc2_weight, out_grad,
):
    d = tokens.shape[1]
    shard = out_weight.shape[0]
    width = 2 * shard
    mols = tokens.shape[0] // LEN
    dp_at = lax.axis_index("dp")
    tensor_at = lax.axis_index("tensor")
    core = tensor_at % 2
    bit0 = dp_at % 2
    bit1 = (dp_at // 2) % 2
    bits = jnp.stack(
        [jnp.where(core == 0, bit0, bit1), jnp.where(core == 0, bit1, bit0), bit0, tensor_at * mols,
         (tensor_at ^ 2) * mols, core, bit1]
    ).astype(jnp.int32)
    chain = Chain()

    def swap_core(a):
        return lax.ppermute(a, "tensor", [(t, t ^ 1) for t in range(n_tensor)])

    def swap_y(a):
        return lax.ppermute(a, "tensor", [(t, t ^ 2) for t in range(n_tensor)])

    def swap_dp(a, mask0, mask1):
        pairs = [
            (p * n_tensor + t, (p ^ (mask1 if t % 2 else mask0)) * n_tensor + t)
            for p in range(n_dp)
            for t in range(n_tensor)
        ]
        return lax.ppermute(a, ("dp", "tensor"), pairs)

    swap_first = lambda a: swap_dp(a, 1, 2)
    swap_second = lambda a: swap_dp(a, 2, 1)
    far_masks = [1 << k for k in range(2, n_dp.bit_length() - 1)]

    w_got = swap_core(qkv_weight)
    x_got, far_g = swap_y(tokens), swap_y(out_grad)
    picked = pick(chain, bits, out_weight, fc1_weight, fc2_weight, fc1_bias)
    far_y = swap_y(picked)
    near, others = load(
        chain, out_weight, fc1_weight, fc2_weight, picked,
        (tokens, out_grad, ln1_gain, ln1_bias, ln2_gain, ln2_bias),
    )
    near = (near, swap_core(near))
    tokens, out_grad, ln1_gain, ln1_bias, ln2_gain, ln2_bias = others

    counts = (node_counts, edge_counts)
    norm1 = (ln1_gain, ln1_bias)
    a1_0, qt_0, kt_0, v_0, p_0, ot_0, o_0, w_qkv = attention(
        chain, bits, 3, *counts, tokens, *norm1, (qkv_weight, w_got)
    )
    far_o = swap_y(o_0)
    far_y, short = hold(chain, far_y, d)
    far_x, far_z = swap_dp(short, 1, 1), swap_dp(short, 2, 2)
    far_z, pair = pair_up(chain, far_x, far_z)
    far_xz = swap_dp(far_z, 1, 1)
    a1_1, qt_1, kt_1, v_1, p_1, ot_1, o_1, wo, fc1, fc2 = attention(
        chain, bits, 4, *counts, x_got, *norm1, w_qkv, near=near
    )
    o_got = swap_y(o_1)
    spacer(chain)
    fars = (far_y, pair, far_xz)
    fars += tuple(swap_core(a) for a in fars)
    norm2 = (ln2_gain, ln2_bias)
    wo, fc1, fc2 = pack_far(chain, bits, (wo, fc1, fc2), fars)
    low, far_low = 3 * shard, 3 * shard // 4
    biases = ((near[0], low), (near[1], low), (fars[0], far_low), (fars[3], far_low))

    part_0, part_1, dz_0, dz_1, b1 = feed_in(
        chain, (tokens, x_got), (o_0, o_1), (out_grad, far_g), wo, fc2, biases
    )

    class Sum:
        def __init__(self, count, keep, got, apart, early):
            self.size = count * shard // 4
            self.apart, self.early = apart, early
            view = lambda a: a.reshape(2, 2, self.size, d)
            self.parts = (view(keep), view(got))

        def first(self):
            sent = sum_half(chain, bits, *self.parts, self.apart)
            got = [swap_first(a) for a in sent]
            self.on, self.kept = got if self.apart else ((got[0], 0), (got[0], 1))

        def second(self):
            self.got = swap_second(sum_quarter(chain, bits, *self.parts, False, self.on))

        def third(self, *vec):
            self.sum = sum_quarter(chain, bits, *self.parts, True, self.kept, self.got, vec=vec)
            self.got = swap_dp(self.sum, far_masks[0], far_masks[0])

        def third_apart(self):
            self.sums = sum_quarter_apart(chain, bits, *self.parts, self.kept, self.got)
            self.gots = [swap_dp(a, far_masks[0], far_masks[0]) for a in self.sums]
            self.halves = [None, None]

        def fourth_apart(self, at, *vec):
            self.sum, self.got = self.sums[at], self.gots[at]
            self.fourth(*vec)
            self.halves[at] = self.quarters

        def fourth(self, *vec):
            a = sum_pairs(chain, (self.sum, self.got), *vec)
            for mask in far_masks[1:]:
                a = sum_pairs(chain, (a, swap_dp(a, mask, mask)))
            b = swap_second(a)
            if self.early == 1:
                self.quarters = [(a, 0, 0, 0), (b, 0, 0, 1), (swap_first(a), 0, 1, 0), (swap_first(b), 0, 1, 1)]
            self.last = (a, b)

        def fifth(self):
            if self.early == 0:
                (a,) = side_by_side(chain, *self.last, False)
                b = swap_first(a)
                rows = a.shape[0] // 2
                self.quarters = [(a, 0, 0, 0), (a, rows, 0, 1), (b, 0, 1, 0), (b, rows, 1, 1)]
            if self.early == 3:
                a, b = self.last
                sent = lax.optimization_barrier((a, chain.token))[0]
                self.quarters = [(a, 0, 0, 0), (b, 0, 0, 1), (swap_first(sent), 0, 1, 0), (swap_first(b), 0, 1, 1)]
            if self.early == 2:
                a, b = side_by_side(chain, *self.last, True)
                self.quarters = [(a, 0, 0, 0), (b, 0, 0, 1), (swap_first(a), 0, 1, 0), (swap_first(b), 0, 1, 1)]

    h_1, du_1, *far_r = feed_far(chain, part_1, far_o, dz_1, far_g, *norm2, wo, fc1, b1)
    gh_1, dp_1 = backward(chain, (du_1, fc1, h_1, far_g, ln2_gain, wo, p_1, qt_1, kt_1, v_1), False)
    h_0, z_0, du_0, keep_r, send_r, bias_sums = feed_own(
        chain, part_0, o_got, dz_0, out_grad, *norm2, wo, fc1, b1, (du_1, *far_r)
    )
    gh_0, dp_0, dh, sums = backward(chain, (du_0, fc1, h_0, out_grad, ln2_gain, wo, p_0, qt_0, kt_0, v_0), True)
    r = Sum(2, keep_r, swap_core(send_r), True, 1)
    r.first()
    a1s = (a1_0, a1_1)
    lefts = [(dp_0, dp_1, c * width) for c in range(3)] + [(ot_0, ot_1, 0)]
    rights = [a1s] * 3 + [(gh_0, gh_1)]
    got_q = swap_core(weight_grads(chain, "weight_grads", shard, 1, lefts, rights))
    q = Sum(4, weight_grads(chain, "weight_grads", shard, 0, lefts, rights), got_q, True, 3)
    r.second()
    q.first()
    r.third()
    q.second()
    da1_mine, da1_theirs = input_grads(chain, (dp_0, dp_1), w_qkv, (tokens, x_got), sums, bias_sums)
    da1_got = swap_y(da1_theirs)
    r.fourth()
    q.third()
    vec = vector_rows(chain, da1_theirs, da1_got)
    vec_got = swap_core(vec)
    r.fifth()
    halves = [(c, None, half * shard // 2) for c in range(2) for half in range(2)]
    grad_fc1, grad_fc2 = place_sums(chain, bits, r.quarters, r.size, halves, [f32(shard, d)] * 2)
    vec = vector_cores(chain, vec, vec_got, shard)
    vec_got = swap_dp(vec, far_masks[0], far_masks[0])
    q.fourth((vec, vec_got))
    result = feed_result(chain, z_0, fc2, h_0)
    grad_tokens = input_norm(chain, tokens, ln1_gain, da1_mine, da1_got, dh)
    q.fifth()
    each = [(0, 0, 0), (0, 1, 0), (0, 2, 0), (1, None, 0)]
    outs = [f32(3, shard, d), f32(shard, d)]
    grads = place_sums(chain, bits, q.quarters[:3], q.size, each, outs)
    grad_qkv, grad_out, gain1, bias1, gain2, bias2, grad_b = place_sums(
        chain, bits, q.quarters, q.size, each, outs, grads, (d, d, d, d, shard), 3
    )
    return (
        result, grad_tokens, gain1, bias1, grad_qkv, grad_out, gain2, bias2, grad_fc1, grad_b, grad_fc2,
    )


def solution(mesh):
    tokens = P(("dp", "tensor"), None)
    rows = P("tensor", None)
    qkv = P(None, "tensor", None)
    in_specs = (
        tokens, P("dp"), P("dp"), P(), P(), qkv, rows, P(), P(), rows, P("tensor"), rows, tokens,
    )
    out_specs = (tokens, tokens, P(), P(), qkv, rows, P(), P(), rows, P("tensor"), rows)
    step = functools.partial(local, mesh.shape["dp"], mesh.shape["tensor"])
    return jax.shard_map(step, mesh=mesh, in_specs=in_specs, out_specs=out_specs, check_vma=False)
```

```python
import functools

import jax
import jax.numpy as jnp
from jax import lax
from jax.experimental import pallas as pl
from jax.experimental.pallas import tpu as pltpu
from jax.sharding import PartitionSpec as P

HEAD_DIM = 24
LEN = 128
PAIR = 2 * HEAD_DIM
EPSILON = 1e-05
SCALE = HEAD_DIM ** (-0.5)
LOG2E = 1.4426950408889634
F32 = jnp.float32
BF16 = jnp.bfloat16
MIB = 1024 * 1024


def dot_nn(a, b):
    return lax.dot_general(a, b, (((1,), (0,)), ((), ())), preferred_element_type=F32)


def dot_nt(a, b):
    return lax.dot_general(a, b, (((1,), (1,)), ((), ())), preferred_element_type=F32)


def dot_tn(a, b):
    return lax.dot_general(a, b, (((0,), (0,)), ((), ())), preferred_element_type=F32)


def normalise(v):
    centered = v - jnp.mean(v, axis=-1, keepdims=True)
    r = lax.rsqrt(jnp.mean(centered * centered, axis=-1, keepdims=True) + EPSILON)
    return centered * r, r


def norm_back(da, gain, xh, r):
    e = da * gain
    return r * (
        e - jnp.mean(e, axis=-1, keepdims=True) - xh * jnp.mean(e * xh, axis=-1, keepdims=True)
    )


def pair_blocks(rows):
    rows = rows.astype(F32)
    none = jnp.zeros((HEAD_DIM, LEN), F32)
    left = jnp.concatenate([rows[:HEAD_DIM], none], axis=0)
    right = jnp.concatenate([none, rows[HEAD_DIM:]], axis=0)
    return jnp.concatenate([left, right], axis=1).astype(BF16)


def pair_window(i, width):
    low = min(PAIR * i // LEN * LEN, width - 2 * LEN)
    return low, PAIR * i - low


def placed(block, before):
    parts = []
    if before:
        parts.append(jnp.zeros((before, 2 * LEN), BF16))
    parts.append(block)
    after = 2 * LEN - PAIR - before
    if after:
        parts.append(jnp.zeros((after, 2 * LEN), BF16))
    return jnp.concatenate(parts, axis=0)


def diagonal(both):
    return jnp.concatenate([both[:HEAD_DIM, :LEN], both[HEAD_DIM:, LEN:]], axis=0)


STRIP = 256
COSTS = (0, 0, 100, 0, 0, 30, 30, 0, 0, 0, 0, 0, 100, 0, 0, 0, 200, 0, 30, 0, 0, 30, 0, 0, 0, 0, 0, 0, 0, 0, 0, 0)


class IO:
    def __init__(self, reads, writes):
        self.reads, self.writes = reads, writes
        self.started = set()

    def wait(self, *args):
        for j in args:
            if j in self.reads:
                self.reads[j].wait()

    def flush(self, *outs):
        for j in outs:
            if j in self.writes:
                self.started.add(j)
                self.writes[j].start()

    def finish(self):
        self.flush(*(j for j in self.writes if j not in self.started))
        for copy in self.writes.values():
            copy.wait()


def pinned(a):
    return pltpu.with_memory_space_constraint(a, pltpu.HBM)


class Chain:
    def __init__(self):
        self.token, self.calls = None, 0

    def call(self, kernel, name, args, outs, kinds, scratch=(), limit=16, aliases={}, last=False):
        ins, out_kinds = kinds.split("-")
        cost = COSTS[min(self.calls, len(COSTS) - 1)]
        self.calls += 1
        assert len(ins) == len(args) and len(out_kinds) == len(outs)
        hbm = pl.BlockSpec(memory_space=pltpu.HBM)
        vmem = pl.BlockSpec(memory_space=pltpu.VMEM)
        smem = pl.BlockSpec(memory_space=pltpu.SMEM)
        spec = lambda kind: {"s": smem, "v": vmem}.get(kind, hbm)
        tokens = () if self.token is None else (self.token,)
        staged = [j for j, kind in enumerate(ins) if kind in "hcl"]
        written = [j for j, kind in enumerate(out_kinds) if kind == "w"]
        memory = lambda kind: pltpu.SMEM if kind == "c" else pltpu.VMEM
        buffers = [memory(ins[j])(args[j].shape, args[j].dtype) for j in staged]
        buffers += [pltpu.VMEM(outs[j].shape, outs[j].dtype) for j in written]
        n_in, n_out, n_buf, n_tokens = len(args) + len(tokens), len(outs), len(buffers), 0 if last else 1

        def body(*refs):
            arg_refs = list(refs[: len(args)])
            out_refs = list(refs[n_in : n_in + n_out])
            tokens_out, own = refs[n_in + n_out :][:n_tokens], refs[n_in + n_out + n_tokens :]
            bufs, sems, extra = own[:n_buf], own[n_buf], own[n_buf + 1 :]
            reads, writes = {}, {}
            for at, j in enumerate(staged):
                reads[j] = pltpu.make_async_copy(arg_refs[j], bufs[at], sems.at[at])
                reads[j].start()
                arg_refs[j] = bufs[at]
            for at, j in enumerate(written, len(staged)):
                writes[j] = pltpu.make_async_copy(bufs[at], out_refs[j], sems.at[at])
                out_refs[j] = bufs[at]
            io = IO(reads, writes)
            io.wait(*(j for j in staged if ins[j] == "h"))
            for token_ref in tokens_out:
                token_ref[...] = jnp.zeros_like(token_ref)
            kernel(io, *arg_refs, *out_refs, *extra)
            io.finish()

        results = pl.pallas_call(
            body,
            in_specs=[spec(kind) for kind in ins] + [vmem] * len(tokens),
            out_specs=[spec(kind) for kind in out_kinds] + [vmem] * n_tokens,
            out_shape=[*outs, *[f32(8, 128)] * n_tokens],
            input_output_aliases=aliases,
            scratch_shapes=[*buffers, pltpu.SemaphoreType.DMA((max(n_buf, 1),)), *scratch],
            compiler_params=pltpu.CompilerParams(vmem_limit_bytes=limit * MIB),
            cost_estimate=pl.CostEstimate(flops=cost * 10**8, bytes_accessed=10**8, transcendentals=0),
            name=name,
        )(*(pinned(a) if kind in "hclp" else a for a, kind in zip(args, ins)), *tokens)
        self.token = None if last else results[-1]
        return results[: len(outs)]


def bf16(*shape):
    return jax.ShapeDtypeStruct(shape, BF16)


def f32(*shape):
    return jax.ShapeDtypeStruct(shape, F32)


def copies(sems, pairs):
    started = [pltpu.make_async_copy(a, b, sems.at[j]) for j, (a, b) in enumerate(pairs)]
    for copy in started:
        copy.start()
    return started


def finish(started):
    for copy in started:
        copy.wait()


def attention(chain, bits, place, nodes, edges, x, gain, bias, w, near=()):
    rows, d = x.shape
    apart = isinstance(w, tuple)
    width = 2 * w[0].shape[1] if apart else w.shape[1]
    shard = width // 2
    pairs = width // PAIR
    mols = rows // LEN

    def kernel(io, bits_ref, nodes_ref, edges_ref, x_ref, gain_ref, bias_ref, *refs):
        started = []
        if not apart:
            w_ref, near0, near1, *refs, wo_ref, fc1_ref, fc2_ref, sems = refs
            a1_ref, qt_ref, kt_ref, v_ref, p_ref, ot_ref, o_ref = refs
            pairs_w = []
            for at, ref in enumerate((near0, near1)):
                for c, out in enumerate((wo_ref, fc1_ref, fc2_ref)):
                    part = ref.at[c * shard : (c + 1) * shard]
                    pairs_w.append((part, out.at[at * shard : (at + 1) * shard]))
            started = copies(sems, pairs_w)
        else:
            own, got, *refs, w_ref, sems = refs
            a1_ref, qt_ref, kt_ref, v_ref, p_ref, ot_ref, o_ref = refs
            pairs_w = [(own, w_ref.at[:, :shard]), (got, w_ref.at[:, shard:])]
            near_w = copies(sems, pairs_w)
        xh, _ = normalise(x_ref[...].astype(F32))
        a1 = (xh * gain_ref[...][None, :] + bias_ref[...][None, :]).astype(BF16)
        a1_ref[...] = a1
        if apart:
            finish(near_w)
        qt = dot_nt(w_ref[0], a1).astype(BF16)
        keys = dot_nt(a1, w_ref[1]).astype(BF16)
        vt = dot_nt(w_ref[2], a1).astype(BF16)
        qt_ref[...] = qt
        every = [(m, i) for m in range(mols) for i in range(pairs)]
        lanes = lambda m: slice(LEN * m, LEN * (m + 1))
        rows_of = lambda i: slice(PAIR * i, PAIR * (i + 1))
        scores, probs = {}, {}
        for m, i in every:
            low, before = pair_window(i, width)
            rhs = placed(pair_blocks(qt[rows_of(i), lanes(m)]), before)
            scores[m, i] = dot_nn(keys[lanes(m), low : low + 2 * LEN], rhs)
        io.wait(1, 2)
        for m in range(mols):
            mol = bits_ref[place] + m
            count = 1 + nodes_ref[mol] + edges_ref[mol]
            valid = lax.broadcasted_iota(jnp.int32, (LEN, 2 * LEN), 0) < count
            for i in range(pairs):
                s = jnp.where(valid, scores[m, i], -1e30)
                e = jnp.exp2((s - jnp.max(s, axis=0, keepdims=True)) * (SCALE * LOG2E))
                p = (e * (1.0 / jnp.sum(e, axis=0, keepdims=True))).astype(BF16)
                p_ref[m, i] = p
                probs[m, i] = p
        for m, i in every:
            both = dot_nn(vt[rows_of(i), lanes(m)], probs[m, i])
            ot_ref[rows_of(i), lanes(m)] = diagonal(both).astype(BF16)
        o_ref[...] = ot_ref[...].T
        kt_ref[...] = dot_nt(w_ref[1], a1).astype(BF16)
        v_ref[...] = dot_nt(a1, w_ref[2]).astype(BF16)
        finish(started)

    outs = [
        bf16(rows, d), bf16(width, rows), bf16(width, rows), bf16(rows, width),
        bf16(mols, pairs, LEN, 2 * LEN), bf16(width, rows),
    ]
    args = (bits, nodes, edges, x, gain, bias)
    if not apart:
        return chain.call(
            kernel, "attention_forward", (*args, w, *near), [*outs, bf16(rows, width), bf16(2 * width, d), bf16(2 * width, d), bf16(2 * width, d)],
            "sccvvvvvv-vvvvvvvvvv", scratch=[pltpu.SemaphoreType.DMA((6,))],
        )
    return chain.call(
        kernel, "attention_forward", (*args, *w), [*outs, bf16(rows, width), bf16(3, width, d)],
        "sccvvvpr-vvvvvvvv", scratch=[pltpu.SemaphoreType.DMA((2,))],
    )


def pick(chain, bits, wo, fc1, fc2, bias):
    shard, d = wo.shape
    rows = 3 * shard // 4
    strips = d // STRIP

    def kernel(io, bits_ref, wo_ref, fc1_ref, fc2_ref, bias_ref, out_ref, sems):
        refs = (wo_ref, fc1_ref, fc2_ref)

        def part(quarter):
            pairs = []
            for c, first, at, n in quarter_rows(quarter, shard):
                for k in range(strips):
                    source = refs[c].at[first : first + n, k * STRIP : (k + 1) * STRIP]
                    pairs.append((source, out_ref.at[k * rows + at : k * rows + at + n]))
            started = copies(sems, pairs)
            io.wait(4)
            out_ref[strips * rows :] = jnp.concatenate(
                [jnp.broadcast_to(bias_ref[...].astype(F32)[None, :], (16, shard)), jnp.zeros((16, STRIP - shard), F32)],
                axis=1,
            ).astype(BF16)
            finish(started)

        which = 2 * bits_ref[2] + bits_ref[6]
        for at in range(4):
            pl.when(which == at)(functools.partial(part, at))

    return chain.call(
        kernel, "pick", (bits, wo, fc1, fc2, bias), [bf16(strips * rows + 16, STRIP)], "spppl-v", limit=4,
        scratch=[pltpu.SemaphoreType.DMA((2 * strips,))],
    )[0]


def quarter_rows(quarter, shard):
    size = 3 * shard // 4
    found, at = [], 0
    while at < size:
        which, first = divmod(quarter * size + at, shard)
        n = min(size - at, shard - first)
        found.append((which, first, at, n))
        at += n
    return found


def hold(chain, a, d):
    strips = d // STRIP
    rows = (a.shape[0] - 16) // strips

    def kernel(io, a_ref, out_ref, short_ref):
        for k in range(strips):
            strip = a_ref[k * rows : (k + 1) * rows]
            out_ref[:rows, k * STRIP : (k + 1) * STRIP] = strip
            short_ref[:, k * STRIP : (k + 1) * STRIP] = strip
        out_ref[rows:] = widened(a_ref[strips * rows :], d)

    return chain.call(kernel, "hold", (a,), [bf16(rows + 16, d), bf16(rows, d)], "v-vv", limit=4)


def widened(a, d):
    return jnp.concatenate([a, jnp.zeros((a.shape[0], d - a.shape[1]), a.dtype)], axis=1)


def pair_up(chain, a, b):
    def kernel(io, a_ref, b_ref, out_ref, both_ref):
        out_ref[...] = b_ref[...]
        both_ref[0] = a_ref[...]
        both_ref[1] = b_ref[...]

    return chain.call(kernel, "pair_up", (a, b), [bf16(*b.shape), bf16(2, *a.shape)], "vv-vv", limit=4)


def spacer(chain, *after):
    def kernel(io, *refs):
        pass

    chain.call(kernel, "spacer", after, [], "r" * len(after) + "-", limit=2)


def load(chain, out_weight, fc1_weight, fc2_weight, picked, others):
    shard, d = out_weight.shape
    n = len(others)

    def kernel(io, wo, fc1, fc2, picked_ref, *refs):
        others_in, (near_ref, *others_out, sems) = refs[:n], refs[n:]
        near_ref[3 * shard :] = widened(picked_ref[picked.shape[0] - 16 :], d)
        rows = lambda at: near_ref.at[at * shard : (at + 1) * shard]
        near = [(wo, rows(0)), (fc1, rows(1)), (fc2, rows(2))]
        finish(copies(sems, near + list(zip(others_in, others_out))))

    near, *others = chain.call(
        kernel, "load", (out_weight, fc1_weight, fc2_weight, picked, *others),
        [bf16(3 * shard + 16, d)] + [jax.ShapeDtypeStruct(a.shape, a.dtype) for a in others],
        "pppv" + "p" * n + "-v" + "v" * n, limit=4, scratch=[pltpu.SemaphoreType.DMA((3 + n,))],
    )
    return near, others


def feed_body(part, ob, dz, wo_ref, gain_ref, bias_ref, fc1_ref, b1, h_ref, a2_ref, z_ref, du_ref):
    h = part + dot_nn(ob, wo_ref[wo_ref.shape[0] // 2 :])
    h_ref[...] = h
    xh, _ = normalise(h)
    a2 = (xh * gain_ref[...][None, :] + bias_ref[...][None, :]).astype(BF16)
    a2_ref[...] = a2
    u = dot_nt(a2, fc1_ref[...]) + b1
    phi = 0.5 * (1.0 + lax.erf(u * (0.5**0.5)))
    slope = phi + u * (jnp.exp(-0.5 * u * u) * 0.3989422804014327)
    du_ref[...] = (dz * slope).astype(BF16)
    z_ref[...] = (u * phi).astype(BF16)


def pack_far(chain, bits, weights, fars):
    rows, d = weights[0].shape
    shard = rows // 4

    def kernel(io, bits_ref, wo_in, fc1_in, fc2_in, y0, pair0, xz0, y1, pair1, xz1, *outs):
        def placed_at(which):
            for at, (y, pair, xz) in enumerate(((y0, pair0, xz0), (y1, pair1, xz1))):
                for turn, ref in enumerate((y, pair.at[1], pair.at[0], xz)):
                    for c, first, start, n in quarter_rows(which ^ turn, shard):
                        row = (2 + at) * shard + first
                        outs[c][row : row + n] = ref[start : start + n]

        which = 2 * bits_ref[2] + bits_ref[6]
        for at in range(4):
            pl.when(which == at)(functools.partial(placed_at, at))

    return chain.call(
        kernel, "pack_far", (bits, *weights, *fars), [bf16(rows, d)] * 3, "s" + "v" * 9 + "-vvv", limit=4,
        aliases={1: 0, 2: 1, 3: 2},
    )


def feed_in(chain, xs, os, gs, wo, fc2, biases):
    rows, d = xs[0].shape
    columns = fc2.shape[0]
    shard = columns // 4

    def kernel(io, x0, x1, o0, o1, g0, g1, wo_ref, fc2_ref, *refs):
        b_refs, (h0, h1, dz0, dz1, b1_ref) = refs[:4], refs[4:]
        for x_ref, o_ref, h_ref in ((x0, o0, h0), (x1, o1, h1)):
            h_ref[...] = x_ref[...].astype(F32) + dot_nn(o_ref[...], wo_ref[: o_ref.shape[1]])
        for g_ref, dz_ref in ((g0, dz0), (g1, dz1)):
            dz_ref[...] = dot_nt(g_ref[...], fc2_ref[...])
        parts = [ref[row : row + 1, :shard].astype(F32) for ref, (_, row) in zip(b_refs, biases)]
        b1_ref[...] = jnp.concatenate(parts, axis=1)

    return chain.call(
        kernel, "feed_in", (*xs, *os, *gs, wo, fc2, *(a for a, _ in biases)),
        [f32(rows, d)] * 2 + [f32(rows, columns)] * 2 + [f32(1, columns)], "v" * 12 + "-vvvvv",
    )


def feed_far(chain, h, ob, dz, g, gain, bias, wo, fc1, b1):
    rows, d = h.shape
    columns = fc1.shape[0]
    width = columns // 2

    def kernel(io, part_ref, ob_ref, dz_ref, g_ref, gain_ref, bias_ref, wo_ref, fc1_ref, b1_ref,
               h_ref, du_ref, first_ref, second_ref, a2_ref, z_ref):
        feed_body(
            part_ref[...], ob_ref[...], dz_ref[...], wo_ref, gain_ref, bias_ref, fc1_ref, b1_ref[...], h_ref, a2_ref,
            z_ref, du_ref,
        )
        first_ref[...] = dot_tn(du_ref[:, :width], a2_ref[...])
        second_ref[...] = dot_tn(z_ref[:, :width], g_ref[...])

    return chain.call(
        kernel, "feed_far", (h, ob, dz, g, gain, bias, wo, fc1, b1),
        [f32(rows, d), bf16(rows, columns), f32(width, d), f32(width, d)], "v" * 9 + "-vvvv",
        scratch=[pltpu.VMEM((rows, d), BF16), pltpu.VMEM((rows, columns), BF16)],
    )


def feed_own(chain, h, ob, dz, g, gain, bias, wo, fc1, b1, far):
    rows, d = h.shape
    columns = fc1.shape[0]
    width = columns // 2
    shard = width // 2

    def kernel(io, part_ref, ob_ref, dz_ref, g_ref, gain_ref, bias_ref, wo_ref, fc1_ref, b1_ref, du1, first1, second1,
               h_ref, z_ref, du_ref, keep_ref, send_ref, sums_ref, a2_ref):
        feed_body(
            part_ref[...], ob_ref[...], dz_ref[...], wo_ref, gain_ref, bias_ref, fc1_ref, b1_ref[...], h_ref, a2_ref,
            z_ref, du_ref,
        )
        du = du_ref[:, :width]
        first = dot_tn(du, a2_ref[...]) + first1[...]
        second = dot_tn(z_ref[:, :width], g_ref[...]) + second1[...]
        for at, ref in enumerate((keep_ref, send_ref)):
            here = slice(at * shard, (at + 1) * shard)
            ref[0] = first[here].astype(BF16)
            ref[1] = second[here].astype(BF16)
        sums_ref[...] = jnp.sum(du.astype(F32), axis=0, keepdims=True) + jnp.sum(
            du1[:, :width].astype(F32), axis=0, keepdims=True
        )

    return chain.call(
        kernel, "feed_own", (h, ob, dz, g, gain, bias, wo, fc1, b1, *far),
        [f32(rows, d), bf16(rows, columns), bf16(rows, columns), bf16(2, shard, d), bf16(2, shard, d), f32(1, width)],
        "v" * 12 + "-vvvvvv", scratch=[pltpu.VMEM((rows, d), BF16)],
    )


def feed_result(chain, z, fc2, h):
    def kernel(io, z_ref, fc2_ref, h_ref, out_ref):
        out_ref[...] = (h_ref[...] + dot_nn(z_ref[...], fc2_ref[...])).astype(BF16)

    return chain.call(kernel, "feed_result", (z, fc2, h), [bf16(*h.shape)], "vvv-w", limit=8)[0]


def backward(chain, args, own):
    h, kt = args[2], args[8]
    rows, d = h.shape
    width = kt.shape[0]
    mols, pairs = rows // LEN, width // PAIR

    def kernel(io, du_ref, fc1_ref, h_ref, g_ref, gain_ref, wo_ref, p_ref, qt_ref, kt_ref, v_ref,
               gh_ref, dp_ref, dh_ref=None, sums_ref=None):
        da2 = dot_nn(du_ref[...], fc1_ref[...])
        xh, r = normalise(h_ref[...])
        dh = g_ref[:, :d].astype(F32) + norm_back(da2, gain_ref[...][None, :], xh, r)
        if own:
            dh_ref[...] = dh
            sums_ref[0:1] = jnp.sum(da2 * xh, axis=0, keepdims=True)
            sums_ref[1:2] = jnp.sum(da2, axis=0, keepdims=True)
            io.flush(2)
        gh = dh.astype(BF16)
        gh_ref[...] = gh
        dot = dot_nt(wo_ref[:width], gh).astype(BF16)
        every = [(m, i) for m in range(mols) for i in range(pairs)]
        lanes = lambda m: slice(LEN * m, LEN * (m + 1))
        rows_of = lambda i: slice(PAIR * i, PAIR * (i + 1))
        dps, dss, dos = {}, {}, {}
        for m, i in every:
            low, before = pair_window(i, width)
            dos[m, i] = pair_blocks(dot[rows_of(i), lanes(m)])
            dps[m, i] = dot_nn(v_ref[lanes(m), low : low + 2 * LEN], placed(dos[m, i], before))
        for m, i in every:
            dv = dot_nt(dos[m, i], p_ref[m, i])
            dp_ref[pl.ds(2 * width + PAIR * i, PAIR), lanes(m)] = dv.astype(BF16)
        for m, i in every:
            p = p_ref[m, i].astype(F32)
            t = dps[m, i] * p
            dss[m, i] = (t - p * jnp.sum(t, axis=0, keepdims=True)).astype(BF16)
        for m, i in every:
            dq = diagonal(dot_nn(kt_ref[rows_of(i), lanes(m)], dss[m, i])) * SCALE
            dp_ref[rows_of(i), lanes(m)] = dq.astype(BF16)
            dk = dot_nt(pair_blocks(qt_ref[rows_of(i), lanes(m)]), dss[m, i]) * SCALE
            dp_ref[pl.ds(width + PAIR * i, PAIR), lanes(m)] = dk.astype(BF16)

    outs = [bf16(rows, d), bf16(3 * width, rows)] + ([f32(rows, d), f32(8, d)] if own else [])
    return chain.call(
        kernel, "attention_backward", args, outs, "v" * 10 + ("-vvvv" if own else "-vv"),
    )


def weight_grads(chain, name, shard, at, lefts, rights):
    d = rights[0][0].shape[1]
    args, count = [], len(lefts)
    for (u0, u1, _), (v0, v1) in zip(lefts, rights):
        args += [u0, u1, v0, v1]

    def kernel(io, *refs):
        out_ref = refs[-1]
        for c in range(count):
            u0, u1, v0, v1 = refs[4 * c : 4 * c + 4]
            rows = slice(lefts[c][2] + at * shard, lefts[c][2] + (at + 1) * shard)
            left = jnp.concatenate([u0[rows], u1[rows]], axis=1)
            right = jnp.concatenate([v0[...], v1[...]], axis=0)
            out_ref[c] = dot_nn(left, right).astype(BF16)

    return chain.call(kernel, name, args, [bf16(count, shard, d)], "v" * len(args) + "-v")[0]


def input_grads(chain, dps, w, xs, sums, bias):
    rows, d = xs[0].shape

    def kernel(io, dp0, dp1, w_ref, x0, x1, sums_ref, bias_ref, mine_ref, theirs_ref):
        w = w_ref[...].reshape(dp0.shape[0], d)
        theirs = dot_tn(dp1[...], w)
        theirs_ref[:rows] = theirs.astype(BF16)
        mine = dot_tn(dp0[...], w)
        mine_ref[...] = mine
        xh0, _ = normalise(x0[...].astype(F32))
        xh1, _ = normalise(x1[...].astype(F32))
        bias = bias_ref[...]
        vec = [
            jnp.sum(mine * xh0, axis=0, keepdims=True) + jnp.sum(theirs * xh1, axis=0, keepdims=True),
            jnp.sum(mine, axis=0, keepdims=True) + jnp.sum(theirs, axis=0, keepdims=True),
            sums_ref[0:2],
            jnp.concatenate([bias, jnp.zeros((1, d - bias.shape[1]), F32)], axis=1),
            jnp.zeros((11, d), F32),
        ]
        theirs_ref[rows:] = jnp.concatenate(vec, axis=0).astype(BF16)

    return chain.call(
        kernel, "input_grads", (*dps, w, *xs, sums, bias), [f32(rows, d), bf16(rows + 16, d)], "vvvvvvv-vv"
    )


def input_norm(chain, x, gain, mine, got, dh):
    rows, d = x.shape

    def kernel(io, x_ref, gain_ref, mine_ref, got_ref, dh_ref, out_ref):
        xh, r = normalise(x_ref[...].astype(F32))
        da1 = mine_ref[...] + got_ref[:rows].astype(F32)
        out_ref[...] = (dh_ref[...] + norm_back(da1, gain_ref[...][None, :], xh, r)).astype(BF16)

    return chain.call(
        kernel, "input_norm", (x, gain, mine, got, dh), [bf16(rows, d)], "vvvvv-w", limit=8
    )[0]


def plus(*terms):
    total = terms[0].astype(F32)
    for term in terms[1:]:
        total = total + term.astype(F32)
    return total.astype(BF16)


def vector_rows(chain, mine, got):
    rows, d = mine.shape

    def kernel(io, mine_ref, got_ref, out_ref):
        a, b = mine_ref[rows - 16 :], got_ref[rows - 16 :]
        same = lax.broadcasted_iota(jnp.int32, (16, d), 0) < 4
        out_ref[...] = plus(a, jnp.where(same, b.astype(F32), 0.0))

    return chain.call(kernel, "vector_rows", (mine, got), [bf16(16, d)], "vv-v", limit=4)[0]


def vector_cores(chain, mine, got, shard):
    def kernel(io, mine_ref, got_ref, out_ref):
        a, b = mine_ref[...].astype(F32), got_ref[...].astype(F32)
        turned = jnp.concatenate([b[:, shard : 2 * shard], b[:, :shard], b[:, 2 * shard :]], axis=1)
        same = lax.broadcasted_iota(jnp.int32, a.shape, 0) < 4
        out_ref[...] = plus(a, jnp.where(same, b, turned))

    return chain.call(kernel, "vector_cores", (mine, got), [bf16(*mine.shape)], "vv-v", limit=4)[0]


def sum_half(chain, bits, mine, got, apart):
    def kernel(io, bits_ref, mine_ref, got_ref, *outs):
        half, quarter = 1 - bits_ref[0], bits_ref[1]
        on_ref, kept_ref = outs if apart else (outs[0].at[0], outs[0].at[1])
        on_ref[...] = mine_ref[half, 1 - quarter] + got_ref[half, 1 - quarter]
        kept_ref[...] = mine_ref[half, quarter] + got_ref[half, quarter]

    rows, d = mine.shape[2:]
    outs = [bf16(rows, d)] * 2 if apart else [bf16(2, rows, d)]
    return chain.call(kernel, "sum_half", (bits, mine, got), outs, "svv-" + "v" * len(outs), limit=8)


def sum_quarter(chain, bits, mine, got, kept, *more, vec=()):
    rows, d = mine.shape[2:]
    arrays = [a[0] if isinstance(a, tuple) else a for a in more]

    def kernel(io, bits_ref, mine_ref, got_ref, *refs):
        *refs, out_ref = refs
        half = bits_ref[0]
        quarter = bits_ref[1] if kept else 1 - bits_ref[1]
        terms = [ref[a[1]] if isinstance(a, tuple) else ref[...] for a, ref in zip(more, refs)]
        out_ref[:rows] = plus(mine_ref[half, quarter], got_ref[half, quarter], *terms)
        if vec:
            out_ref[rows:] = refs[-1][...]

    args = (bits, mine, got, *arrays, *vec)
    return chain.call(
        kernel, "sum_quarter", args, [bf16(rows + (16 if vec else 0), d)], "s" + "v" * (len(args) - 1) + "-v",
        limit=8,
    )[0]


def sum_quarter_apart(chain, bits, mine, got, *more):
    rows, d = mine.shape[2:]
    arrays = [a[0] if isinstance(a, tuple) else a for a in more]

    def kernel(io, bits_ref, mine_ref, got_ref, *refs):
        *refs, upper_ref, lower_ref = refs
        half, quarter = bits_ref[0], bits_ref[1]
        terms = [ref[a[1]] if isinstance(a, tuple) else ref[...] for a, ref in zip(more, refs)]
        total = plus(mine_ref[half, quarter], got_ref[half, quarter], *terms)
        upper_ref[...] = total[: rows // 2]
        lower_ref[...] = total[rows // 2 :]

    args = (bits, mine, got, *arrays)
    return chain.call(
        kernel, "sum_quarter", args, [bf16(rows // 2, d)] * 2, "s" + "v" * (len(args) - 1) + "-vv", limit=8
    )


def side_by_side(chain, a, b, apart):
    rows, d = a.shape

    def kernel(io, a_ref, b_ref, *outs):
        first, second = outs if apart else (outs[0].at[:rows], outs[0].at[rows:])
        first[...] = a_ref[...]
        second[...] = b_ref[...]

    outs = [bf16(rows, d)] * 2 if apart else [bf16(2 * rows, d)]
    return chain.call(kernel, "side_by_side", (a, b), outs, "vv-" + "v" * len(outs), limit=8)


def sum_pairs(chain, *pairs):
    rows = [a.shape[0] for a, _ in pairs]

    def kernel(io, *refs):
        *refs, out_ref = refs
        start = 0
        for a_ref, b_ref in zip(refs[::2], refs[1::2]):
            out_ref[start : start + a_ref.shape[0]] = a_ref[...] + b_ref[...]
            start += a_ref.shape[0]

    args = [a for pair in pairs for a in pair]
    return chain.call(
        kernel, "sum_pairs", args, [bf16(sum(rows), args[0].shape[1])], "v" * len(args) + "-v", limit=8
    )[0]


def place_sums(chain, bits, quarters, rows, targets, outs, whole=(), vec=(), skip=0):
    d = quarters[0][0].shape[1]
    n = len(outs)
    arrays = []
    for a, *_ in quarters:
        if not any(a is b for b in arrays):
            arrays.append(a)
    which = [next(k for k, b in enumerate(arrays) if b is a) for a, *_ in quarters]

    def kernel(io, bits_ref, *refs):
        refs, (buf, sems) = refs[:-2], refs[-2:]
        ins = [refs[k] for k in which]
        refs = refs[len(arrays) + len(whole) :]
        out_refs, vec_refs = refs[:n], refs[n:]

        def each(step):
            for j, (_, _, half, quarter) in enumerate(quarters):
                if j < skip:
                    continue
                half = 1 - bits_ref[0] if half else bits_ref[0]
                quarter = 1 - bits_ref[1] if quarter else bits_ref[1]
                for at, (out, index, first) in enumerate(targets):
                    ref = out_refs[out]
                    ref = ref if index is None else ref.at[index]
                    ref = ref.at[first : first + rows]
                    copy = pltpu.make_async_copy(buf.at[j], ref, sems.at[j])
                    pl.when(2 * half + quarter == at)(functools.partial(step, copy))

        starts = [start for _, start, _, _ in quarters]
        for j, ref in enumerate(ins):
            if j >= skip:
                buf[j] = ref[starts[j] : starts[j] + rows].astype(F32)
        each(lambda copy: copy.start())
        if vec:
            a, b, c, e = (ref[x + rows : x + rows + 16].astype(F32) for ref, x in zip(ins, starts))
            total = jnp.where(bits_ref[5] == 0, (a + b) + (c + e), (a + c) + (b + e))
            for at, (length, ref) in enumerate(zip(vec, vec_refs)):
                ref[...] = total[at, :length]
            io.flush(*range(n, n + len(vec)))
        each(lambda copy: copy.wait())

    return chain.call(
        kernel, "place_sums", (bits, *arrays, *whole), [*outs, *(f32(length) for length in vec)],
        "s" + "v" * len(arrays) + "p" * len(whole) + "-" + "r" * n + "w" * len(vec), limit=8, last=bool(vec),
        aliases={1 + len(arrays) + j: j for j in range(len(whole))},
        scratch=[pltpu.VMEM((len(quarters), rows, d), F32), pltpu.SemaphoreType.DMA((len(quarters),))],
    )


def local(
    n_dp, n_tensor, tokens, node_counts, edge_counts, ln1_gain, ln1_bias, qkv_weight, out_weight,
    ln2_gain, ln2_bias, fc1_weight, fc1_bias, fc2_weight, out_grad,
):
    d = tokens.shape[1]
    shard = out_weight.shape[0]
    width = 2 * shard
    mols = tokens.shape[0] // LEN
    dp_at = lax.axis_index("dp")
    tensor_at = lax.axis_index("tensor")
    core = tensor_at % 2
    bit0 = dp_at % 2
    bit1 = (dp_at // 2) % 2
    bits = jnp.stack(
        [jnp.where(core == 0, bit0, bit1), jnp.where(core == 0, bit1, bit0), bit0, tensor_at * mols,
         (tensor_at ^ 2) * mols, core, bit1]
    ).astype(jnp.int32)
    chain = Chain()

    def swap_core(a):
        return lax.ppermute(a, "tensor", [(t, t ^ 1) for t in range(n_tensor)])

    def swap_y(a):
        return lax.ppermute(a, "tensor", [(t, t ^ 2) for t in range(n_tensor)])

    def swap_dp(a, mask0, mask1):
        pairs = [
            (p * n_tensor + t, (p ^ (mask1 if t % 2 else mask0)) * n_tensor + t)
            for p in range(n_dp)
            for t in range(n_tensor)
        ]
        return lax.ppermute(a, ("dp", "tensor"), pairs)

    swap_first = lambda a: swap_dp(a, 1, 2)
    swap_second = lambda a: swap_dp(a, 2, 1)
    far_masks = [1 << k for k in range(2, n_dp.bit_length() - 1)]

    w_got = swap_core(qkv_weight)
    x_got, far_g = swap_y(tokens), swap_y(out_grad)
    picked = pick(chain, bits, out_weight, fc1_weight, fc2_weight, fc1_bias)
    far_y = swap_y(picked)
    near, others = load(
        chain, out_weight, fc1_weight, fc2_weight, picked,
        (tokens, out_grad, ln1_gain, ln1_bias, ln2_gain, ln2_bias),
    )
    near = (near, swap_core(near))
    tokens, out_grad, ln1_gain, ln1_bias, ln2_gain, ln2_bias = others

    counts = (node_counts, edge_counts)
    norm1 = (ln1_gain, ln1_bias)
    a1_0, qt_0, kt_0, v_0, p_0, ot_0, o_0, w_qkv = attention(
        chain, bits, 3, *counts, tokens, *norm1, (qkv_weight, w_got)
    )
    far_o = swap_y(o_0)
    far_y, short = hold(chain, far_y, d)
    far_x, far_z = swap_dp(short, 1, 1), swap_dp(short, 2, 2)
    far_z, pair = pair_up(chain, far_x, far_z)
    far_xz = swap_dp(far_z, 1, 1)
    a1_1, qt_1, kt_1, v_1, p_1, ot_1, o_1, wo, fc1, fc2 = attention(
        chain, bits, 4, *counts, x_got, *norm1, w_qkv, near=near
    )
    o_got = swap_y(o_1)
    spacer(chain)
    fars = (far_y, pair, far_xz)
    fars += tuple(swap_core(a) for a in fars)
    norm2 = (ln2_gain, ln2_bias)
    wo, fc1, fc2 = pack_far(chain, bits, (wo, fc1, fc2), fars)
    low, far_low = 3 * shard, 3 * shard // 4
    biases = ((near[0], low), (near[1], low), (fars[0], far_low), (fars[3], far_low))

    part_0, part_1, dz_0, dz_1, b1 = feed_in(
        chain, (tokens, x_got), (o_0, o_1), (out_grad, far_g), wo, fc2, biases
    )

    class Sum:
        def __init__(self, count, keep, got, apart, early):
            self.size = count * shard // 4
            self.apart, self.early = apart, early
            view = lambda a: a.reshape(2, 2, self.size, d)
            self.parts = (view(keep), view(got))

        def first(self):
            sent = sum_half(chain, bits, *self.parts, self.apart)
            got = [swap_first(a) for a in sent]
            self.on, self.kept = got if self.apart else ((got[0], 0), (got[0], 1))

        def second(self):
            self.got = swap_second(sum_quarter(chain, bits, *self.parts, False, self.on))

        def third(self, *vec):
            self.sum = sum_quarter(chain, bits, *self.parts, True, self.kept, self.got, vec=vec)
            self.got = swap_dp(self.sum, far_masks[0], far_masks[0])

        def third_apart(self):
            self.sums = sum_quarter_apart(chain, bits, *self.parts, self.kept, self.got)
            self.gots = [swap_dp(a, far_masks[0], far_masks[0]) for a in self.sums]
            self.halves = [None, None]

        def fourth_apart(self, at, *vec):
            self.sum, self.got = self.sums[at], self.gots[at]
            self.fourth(*vec)
            self.halves[at] = self.quarters

        def fourth(self, *vec):
            a = sum_pairs(chain, (self.sum, self.got), *vec)
            for mask in far_masks[1:]:
                a = sum_pairs(chain, (a, swap_dp(a, mask, mask)))
            b = swap_second(a)
            if self.early == 1:
                self.quarters = [(a, 0, 0, 0), (b, 0, 0, 1), (swap_first(a), 0, 1, 0), (swap_first(b), 0, 1, 1)]
            self.last = (a, b)

        def fifth(self):
            if self.early == 0:
                (a,) = side_by_side(chain, *self.last, False)
                b = swap_first(a)
                rows = a.shape[0] // 2
                self.quarters = [(a, 0, 0, 0), (a, rows, 0, 1), (b, 0, 1, 0), (b, rows, 1, 1)]
            if self.early == 3:
                a, b = self.last
                sent = lax.optimization_barrier((a, chain.token))[0]
                self.quarters = [(a, 0, 0, 0), (b, 0, 0, 1), (swap_first(sent), 0, 1, 0), (swap_first(b), 0, 1, 1)]
            if self.early == 2:
                a, b = side_by_side(chain, *self.last, True)
                self.quarters = [(a, 0, 0, 0), (b, 0, 0, 1), (swap_first(a), 0, 1, 0), (swap_first(b), 0, 1, 1)]

    h_1, du_1, *far_r = feed_far(chain, part_1, far_o, dz_1, far_g, *norm2, wo, fc1, b1)
    gh_1, dp_1 = backward(chain, (du_1, fc1, h_1, far_g, ln2_gain, wo, p_1, qt_1, kt_1, v_1), False)
    h_0, z_0, du_0, keep_r, send_r, bias_sums = feed_own(
        chain, part_0, o_got, dz_0, out_grad, *norm2, wo, fc1, b1, (du_1, *far_r)
    )
    gh_0, dp_0, dh, sums = backward(chain, (du_0, fc1, h_0, out_grad, ln2_gain, wo, p_0, qt_0, kt_0, v_0), True)
    r = Sum(2, keep_r, swap_core(send_r), True, 1)
    r.first()
    a1s = (a1_0, a1_1)
    lefts = [(dp_0, dp_1, c * width) for c in range(3)] + [(ot_0, ot_1, 0)]
    rights = [a1s] * 3 + [(gh_0, gh_1)]
    got_q = swap_core(weight_grads(chain, "weight_grads", shard, 1, lefts, rights))
    q = Sum(4, weight_grads(chain, "weight_grads", shard, 0, lefts, rights), got_q, True, 3)
    r.second()
    q.first()
    r.third()
    q.second()
    da1_mine, da1_theirs = input_grads(chain, (dp_0, dp_1), w_qkv, (tokens, x_got), sums, bias_sums)
    da1_got = swap_y(da1_theirs)
    r.fourth()
    q.third()
    vec = vector_rows(chain, da1_theirs, da1_got)
    vec_got = swap_core(vec)
    r.fifth()
    halves = [(c, None, half * shard // 2) for c in range(2) for half in range(2)]
    grad_fc1, grad_fc2 = place_sums(chain, bits, r.quarters, r.size, halves, [f32(shard, d)] * 2)
    vec = vector_cores(chain, vec, vec_got, shard)
    vec_got = swap_dp(vec, far_masks[0], far_masks[0])
    q.fourth((vec, vec_got))
    grad_tokens = input_norm(chain, tokens, ln1_gain, da1_mine, da1_got, dh)
    result = feed_result(chain, z_0, fc2, h_0)
    q.fifth()
    each = [(0, 0, 0), (0, 1, 0), (0, 2, 0), (1, None, 0)]
    outs = [f32(3, shard, d), f32(shard, d)]
    grads = place_sums(chain, bits, q.quarters[:3], q.size, each, outs)
    grad_qkv, grad_out, gain1, bias1, gain2, bias2, grad_b = place_sums(
        chain, bits, q.quarters, q.size, each, outs, grads, (d, d, d, d, shard), 3
    )
    return (
        result, grad_tokens, gain1, bias1, grad_qkv, grad_out, gain2, bias2, grad_fc1, grad_b, grad_fc2,
    )


def solution(mesh):
    tokens = P(("dp", "tensor"), None)
    rows = P("tensor", None)
    qkv = P(None, "tensor", None)
    in_specs = (
        tokens, P("dp"), P("dp"), P(), P(), qkv, rows, P(), P(), rows, P("tensor"), rows, tokens,
    )
    out_specs = (tokens, tokens, P(), P(), qkv, rows, P(), P(), rows, P("tensor"), rows)
    step = functools.partial(local, mesh.shape["dp"], mesh.shape["tensor"])
    return jax.shard_map(step, mesh=mesh, in_specs=in_specs, out_specs=out_specs, check_vma=False)
```

```python
import functools

import jax
import jax.numpy as jnp
from jax import lax
from jax.experimental import pallas as pl
from jax.experimental.pallas import tpu as pltpu
from jax.sharding import PartitionSpec as P

HEAD_DIM = 24
LEN = 128
PAIR = 2 * HEAD_DIM
EPSILON = 1e-05
SCALE = HEAD_DIM ** (-0.5)
LOG2E = 1.4426950408889634
F32 = jnp.float32
BF16 = jnp.bfloat16
MIB = 1024 * 1024


def dot_nn(a, b):
    return lax.dot_general(a, b, (((1,), (0,)), ((), ())), preferred_element_type=F32)


def dot_nt(a, b):
    return lax.dot_general(a, b, (((1,), (1,)), ((), ())), preferred_element_type=F32)


def dot_tn(a, b):
    return lax.dot_general(a, b, (((0,), (0,)), ((), ())), preferred_element_type=F32)


def normalise(v):
    centered = v - jnp.mean(v, axis=-1, keepdims=True)
    r = lax.rsqrt(jnp.mean(centered * centered, axis=-1, keepdims=True) + EPSILON)
    return centered * r, r


def norm_back(da, gain, xh, r):
    e = da * gain
    return r * (
        e - jnp.mean(e, axis=-1, keepdims=True) - xh * jnp.mean(e * xh, axis=-1, keepdims=True)
    )


def pair_blocks(rows):
    rows = rows.astype(F32)
    none = jnp.zeros((HEAD_DIM, LEN), F32)
    left = jnp.concatenate([rows[:HEAD_DIM], none], axis=0)
    right = jnp.concatenate([none, rows[HEAD_DIM:]], axis=0)
    return jnp.concatenate([left, right], axis=1).astype(BF16)


def pair_window(i, width):
    low = min(PAIR * i // LEN * LEN, width - 2 * LEN)
    return low, PAIR * i - low


def placed(block, before):
    parts = []
    if before:
        parts.append(jnp.zeros((before, 2 * LEN), BF16))
    parts.append(block)
    after = 2 * LEN - PAIR - before
    if after:
        parts.append(jnp.zeros((after, 2 * LEN), BF16))
    return jnp.concatenate(parts, axis=0)


def diagonal(both):
    return jnp.concatenate([both[:HEAD_DIM, :LEN], both[HEAD_DIM:, LEN:]], axis=0)


STRIP = 256
COSTS = (0, 0, 100, 0, 0, 30, 30, 0, 0, 0, 0, 0, 100, 0, 0, 0, 200, 0, 30, 0, 0, 30, 0, 0, 0, 0, 0, 0, 0, 0, 60, 0)


class IO:
    def __init__(self, reads, writes):
        self.reads, self.writes = reads, writes
        self.started = set()

    def wait(self, *args):
        for j in args:
            if j in self.reads:
                self.reads[j].wait()

    def flush(self, *outs):
        for j in outs:
            if j in self.writes:
                self.started.add(j)
                self.writes[j].start()

    def finish(self):
        self.flush(*(j for j in self.writes if j not in self.started))
        for copy in self.writes.values():
            copy.wait()


def pinned(a):
    return pltpu.with_memory_space_constraint(a, pltpu.HBM)


class Chain:
    def __init__(self):
        self.token, self.calls = None, 0

    def call(self, kernel, name, args, outs, kinds, scratch=(), limit=16, aliases={}, last=False):
        ins, out_kinds = kinds.split("-")
        cost = COSTS[min(self.calls, len(COSTS) - 1)]
        self.calls += 1
        assert len(ins) == len(args) and len(out_kinds) == len(outs)
        hbm = pl.BlockSpec(memory_space=pltpu.HBM)
        vmem = pl.BlockSpec(memory_space=pltpu.VMEM)
        smem = pl.BlockSpec(memory_space=pltpu.SMEM)
        spec = lambda kind: {"s": smem, "v": vmem}.get(kind, hbm)
        tokens = () if self.token is None else (self.token,)
        staged = [j for j, kind in enumerate(ins) if kind in "hcl"]
        written = [j for j, kind in enumerate(out_kinds) if kind == "w"]
        memory = lambda kind: pltpu.SMEM if kind == "c" else pltpu.VMEM
        buffers = [memory(ins[j])(args[j].shape, args[j].dtype) for j in staged]
        buffers += [pltpu.VMEM(outs[j].shape, outs[j].dtype) for j in written]
        n_in, n_out, n_buf, n_tokens = len(args) + len(tokens), len(outs), len(buffers), 0 if last else 1

        def body(*refs):
            arg_refs = list(refs[: len(args)])
            out_refs = list(refs[n_in : n_in + n_out])
            tokens_out, own = refs[n_in + n_out :][:n_tokens], refs[n_in + n_out + n_tokens :]
            bufs, sems, extra = own[:n_buf], own[n_buf], own[n_buf + 1 :]
            reads, writes = {}, {}
            for at, j in enumerate(staged):
                reads[j] = pltpu.make_async_copy(arg_refs[j], bufs[at], sems.at[at])
                reads[j].start()
                arg_refs[j] = bufs[at]
            for at, j in enumerate(written, len(staged)):
                writes[j] = pltpu.make_async_copy(bufs[at], out_refs[j], sems.at[at])
                out_refs[j] = bufs[at]
            io = IO(reads, writes)
            io.wait(*(j for j in staged if ins[j] == "h"))
            for token_ref in tokens_out:
                token_ref[...] = jnp.zeros_like(token_ref)
            kernel(io, *arg_refs, *out_refs, *extra)
            io.finish()

        results = pl.pallas_call(
            body,
            in_specs=[spec(kind) for kind in ins] + [vmem] * len(tokens),
            out_specs=[spec(kind) for kind in out_kinds] + [vmem] * n_tokens,
            out_shape=[*outs, *[f32(8, 128)] * n_tokens],
            input_output_aliases=aliases,
            scratch_shapes=[*buffers, pltpu.SemaphoreType.DMA((max(n_buf, 1),)), *scratch],
            compiler_params=pltpu.CompilerParams(vmem_limit_bytes=limit * MIB),
            cost_estimate=pl.CostEstimate(flops=cost * 10**8, bytes_accessed=10**8, transcendentals=0),
            name=name,
        )(*(pinned(a) if kind in "hclp" else a for a, kind in zip(args, ins)), *tokens)
        self.token = None if last else results[-1]
        return results[: len(outs)]


def bf16(*shape):
    return jax.ShapeDtypeStruct(shape, BF16)


def f32(*shape):
    return jax.ShapeDtypeStruct(shape, F32)


def copies(sems, pairs):
    started = [pltpu.make_async_copy(a, b, sems.at[j]) for j, (a, b) in enumerate(pairs)]
    for copy in started:
        copy.start()
    return started


def finish(started):
    for copy in started:
        copy.wait()


def attention(chain, bits, place, nodes, edges, x, gain, bias, w, near=()):
    rows, d = x.shape
    apart = isinstance(w, tuple)
    width = 2 * w[0].shape[1] if apart else w.shape[1]
    shard = width // 2
    pairs = width // PAIR
    mols = rows // LEN

    def kernel(io, bits_ref, nodes_ref, edges_ref, x_ref, gain_ref, bias_ref, *refs):
        started = []
        if not apart:
            w_ref, near0, near1, *refs, wo_ref, fc1_ref, fc2_ref, sems = refs
            a1_ref, qt_ref, kt_ref, v_ref, p_ref, ot_ref, o_ref = refs
            pairs_w = []
            for at, ref in enumerate((near0, near1)):
                for c, out in enumerate((wo_ref, fc1_ref, fc2_ref)):
                    part = ref.at[c * shard : (c + 1) * shard]
                    pairs_w.append((part, out.at[at * shard : (at + 1) * shard]))
            started = copies(sems, pairs_w)
        else:
            own, got, *refs, w_ref, sems = refs
            a1_ref, qt_ref, kt_ref, v_ref, p_ref, ot_ref, o_ref = refs
            pairs_w = [(own, w_ref.at[:, :shard]), (got, w_ref.at[:, shard:])]
            near_w = copies(sems, pairs_w)
        xh, _ = normalise(x_ref[...].astype(F32))
        a1 = (xh * gain_ref[...][None, :] + bias_ref[...][None, :]).astype(BF16)
        a1_ref[...] = a1
        if apart:
            finish(near_w)
        qt = dot_nt(w_ref[0], a1).astype(BF16)
        keys = dot_nt(a1, w_ref[1]).astype(BF16)
        vt = dot_nt(w_ref[2], a1).astype(BF16)
        qt_ref[...] = qt
        every = [(m, i) for m in range(mols) for i in range(pairs)]
        lanes = lambda m: slice(LEN * m, LEN * (m + 1))
        rows_of = lambda i: slice(PAIR * i, PAIR * (i + 1))
        scores, probs = {}, {}
        for m, i in every:
            low, before = pair_window(i, width)
            rhs = placed(pair_blocks(qt[rows_of(i), lanes(m)]), before)
            scores[m, i] = dot_nn(keys[lanes(m), low : low + 2 * LEN], rhs)
        io.wait(1, 2)
        for m in range(mols):
            mol = bits_ref[place] + m
            count = 1 + nodes_ref[mol] + edges_ref[mol]
            valid = lax.broadcasted_iota(jnp.int32, (LEN, 2 * LEN), 0) < count
            for i in range(pairs):
                s = jnp.where(valid, scores[m, i], -1e30)
                e = jnp.exp2((s - jnp.max(s, axis=0, keepdims=True)) * (SCALE * LOG2E))
                p = (e * (1.0 / jnp.sum(e, axis=0, keepdims=True))).astype(BF16)
                p_ref[m, i] = p
                probs[m, i] = p
        for m, i in every:
            both = dot_nn(vt[rows_of(i), lanes(m)], probs[m, i])
            ot_ref[rows_of(i), lanes(m)] = diagonal(both).astype(BF16)
        o_ref[...] = ot_ref[...].T
        kt_ref[...] = dot_nt(w_ref[1], a1).astype(BF16)
        v_ref[...] = dot_nt(a1, w_ref[2]).astype(BF16)
        finish(started)

    outs = [
        bf16(rows, d), bf16(width, rows), bf16(width, rows), bf16(rows, width),
        bf16(mols, pairs, LEN, 2 * LEN), bf16(width, rows),
    ]
    args = (bits, nodes, edges, x, gain, bias)
    if not apart:
        return chain.call(
            kernel, "attention_forward", (*args, w, *near), [*outs, bf16(rows, width), bf16(2 * width, d), bf16(2 * width, d), bf16(2 * width, d)],
            "sccvvvvvv-vvvvvvvvvv", scratch=[pltpu.SemaphoreType.DMA((6,))],
        )
    return chain.call(
        kernel, "attention_forward", (*args, *w), [*outs, bf16(rows, width), bf16(3, width, d)],
        "sccvvvpr-vvvvvvvv", scratch=[pltpu.SemaphoreType.DMA((2,))],
    )


def pick(chain, bits, wo, fc1, fc2, bias):
    shard, d = wo.shape
    rows = 3 * shard // 4
    strips = d // STRIP

    def kernel(io, bits_ref, wo_ref, fc1_ref, fc2_ref, bias_ref, out_ref, sems):
        refs = (wo_ref, fc1_ref, fc2_ref)

        def part(quarter):
            pairs = []
            for c, first, at, n in quarter_rows(quarter, shard):
                for k in range(strips):
                    source = refs[c].at[first : first + n, k * STRIP : (k + 1) * STRIP]
                    pairs.append((source, out_ref.at[k * rows + at : k * rows + at + n]))
            started = copies(sems, pairs)
            io.wait(4)
            out_ref[strips * rows :] = jnp.concatenate(
                [jnp.broadcast_to(bias_ref[...].astype(F32)[None, :], (16, shard)), jnp.zeros((16, STRIP - shard), F32)],
                axis=1,
            ).astype(BF16)
            finish(started)

        which = 2 * bits_ref[2] + bits_ref[6]
        for at in range(4):
            pl.when(which == at)(functools.partial(part, at))

    return chain.call(
        kernel, "pick", (bits, wo, fc1, fc2, bias), [bf16(strips * rows + 16, STRIP)], "spppl-v", limit=4,
        scratch=[pltpu.SemaphoreType.DMA((2 * strips,))],
    )[0]


def quarter_rows(quarter, shard):
    size = 3 * shard // 4
    found, at = [], 0
    while at < size:
        which, first = divmod(quarter * size + at, shard)
        n = min(size - at, shard - first)
        found.append((which, first, at, n))
        at += n
    return found


def hold(chain, a, d):
    strips = d // STRIP
    rows = (a.shape[0] - 16) // strips

    def kernel(io, a_ref, out_ref, short_ref):
        for k in range(strips):
            strip = a_ref[k * rows : (k + 1) * rows]
            out_ref[:rows, k * STRIP : (k + 1) * STRIP] = strip
            short_ref[:, k * STRIP : (k + 1) * STRIP] = strip
        out_ref[rows:] = widened(a_ref[strips * rows :], d)

    return chain.call(kernel, "hold", (a,), [bf16(rows + 16, d), bf16(rows, d)], "v-vv", limit=4)


def widened(a, d):
    return jnp.concatenate([a, jnp.zeros((a.shape[0], d - a.shape[1]), a.dtype)], axis=1)


def pair_up(chain, a, b):
    def kernel(io, a_ref, b_ref, out_ref, both_ref):
        out_ref[...] = b_ref[...]
        both_ref[0] = a_ref[...]
        both_ref[1] = b_ref[...]

    return chain.call(kernel, "pair_up", (a, b), [bf16(*b.shape), bf16(2, *a.shape)], "vv-vv", limit=4)


def spacer(chain, *after):
    def kernel(io, *refs):
        pass

    chain.call(kernel, "spacer", after, [], "r" * len(after) + "-", limit=2)


def load(chain, out_weight, fc1_weight, fc2_weight, picked, others):
    shard, d = out_weight.shape
    n = len(others)

    def kernel(io, wo, fc1, fc2, picked_ref, *refs):
        others_in, (near_ref, *others_out, sems) = refs[:n], refs[n:]
        near_ref[3 * shard :] = widened(picked_ref[picked.shape[0] - 16 :], d)
        rows = lambda at: near_ref.at[at * shard : (at + 1) * shard]
        near = [(wo, rows(0)), (fc1, rows(1)), (fc2, rows(2))]
        finish(copies(sems, near + list(zip(others_in, others_out))))

    near, *others = chain.call(
        kernel, "load", (out_weight, fc1_weight, fc2_weight, picked, *others),
        [bf16(3 * shard + 16, d)] + [jax.ShapeDtypeStruct(a.shape, a.dtype) for a in others],
        "pppv" + "p" * n + "-v" + "v" * n, limit=4, scratch=[pltpu.SemaphoreType.DMA((3 + n,))],
    )
    return near, others


def feed_body(part, ob, dz, wo_ref, gain_ref, bias_ref, fc1_ref, b1, h_ref, a2_ref, z_ref, du_ref):
    h = part + dot_nn(ob, wo_ref[wo_ref.shape[0] // 2 :])
    h_ref[...] = h
    xh, _ = normalise(h)
    a2 = (xh * gain_ref[...][None, :] + bias_ref[...][None, :]).astype(BF16)
    a2_ref[...] = a2
    u = dot_nt(a2, fc1_ref[...]) + b1
    phi = 0.5 * (1.0 + lax.erf(u * (0.5**0.5)))
    slope = phi + u * (jnp.exp(-0.5 * u * u) * 0.3989422804014327)
    du_ref[...] = (dz * slope).astype(BF16)
    z_ref[...] = (u * phi).astype(BF16)


def pack_far(chain, bits, weights, fars):
    rows, d = weights[0].shape
    shard = rows // 4

    def kernel(io, bits_ref, wo_in, fc1_in, fc2_in, y0, pair0, xz0, y1, pair1, xz1, *outs):
        def placed_at(which):
            for at, (y, pair, xz) in enumerate(((y0, pair0, xz0), (y1, pair1, xz1))):
                for turn, ref in enumerate((y, pair.at[1], pair.at[0], xz)):
                    for c, first, start, n in quarter_rows(which ^ turn, shard):
                        row = (2 + at) * shard + first
                        outs[c][row : row + n] = ref[start : start + n]

        which = 2 * bits_ref[2] + bits_ref[6]
        for at in range(4):
            pl.when(which == at)(functools.partial(placed_at, at))

    return chain.call(
        kernel, "pack_far", (bits, *weights, *fars), [bf16(rows, d)] * 3, "s" + "v" * 9 + "-vvv", limit=4,
        aliases={1: 0, 2: 1, 3: 2},
    )


def feed_in(chain, xs, os, gs, wo, fc2, biases):
    rows, d = xs[0].shape
    columns = fc2.shape[0]
    shard = columns // 4

    def kernel(io, x0, x1, o0, o1, g0, g1, wo_ref, fc2_ref, *refs):
        b_refs, (h0, h1, dz0, dz1, b1_ref) = refs[:4], refs[4:]
        for x_ref, o_ref, h_ref in ((x0, o0, h0), (x1, o1, h1)):
            h_ref[...] = x_ref[...].astype(F32) + dot_nn(o_ref[...], wo_ref[: o_ref.shape[1]])
        for g_ref, dz_ref in ((g0, dz0), (g1, dz1)):
            dz_ref[...] = dot_nt(g_ref[...], fc2_ref[...])
        parts = [ref[row : row + 1, :shard].astype(F32) for ref, (_, row) in zip(b_refs, biases)]
        b1_ref[...] = jnp.concatenate(parts, axis=1)

    return chain.call(
        kernel, "feed_in", (*xs, *os, *gs, wo, fc2, *(a for a, _ in biases)),
        [f32(rows, d)] * 2 + [f32(rows, columns)] * 2 + [f32(1, columns)], "v" * 12 + "-vvvvv",
    )


def feed_far(chain, h, ob, dz, g, gain, bias, wo, fc1, b1):
    rows, d = h.shape
    columns = fc1.shape[0]
    width = columns // 2

    def kernel(io, part_ref, ob_ref, dz_ref, g_ref, gain_ref, bias_ref, wo_ref, fc1_ref, b1_ref,
               h_ref, du_ref, first_ref, second_ref, a2_ref, z_ref):
        feed_body(
            part_ref[...], ob_ref[...], dz_ref[...], wo_ref, gain_ref, bias_ref, fc1_ref, b1_ref[...], h_ref, a2_ref,
            z_ref, du_ref,
        )
        first_ref[...] = dot_tn(du_ref[:, :width], a2_ref[...])
        second_ref[...] = dot_tn(z_ref[:, :width], g_ref[...])

    return chain.call(
        kernel, "feed_far", (h, ob, dz, g, gain, bias, wo, fc1, b1),
        [f32(rows, d), bf16(rows, columns), f32(width, d), f32(width, d)], "v" * 9 + "-vvvv",
        scratch=[pltpu.VMEM((rows, d), BF16), pltpu.VMEM((rows, columns), BF16)],
    )


def feed_own(chain, h, ob, dz, g, gain, bias, wo, fc1, b1, far):
    rows, d = h.shape
    columns = fc1.shape[0]
    width = columns // 2
    shard = width // 2

    def kernel(io, part_ref, ob_ref, dz_ref, g_ref, gain_ref, bias_ref, wo_ref, fc1_ref, b1_ref, du1, first1, second1,
               h_ref, z_ref, du_ref, keep_ref, send_ref, sums_ref, a2_ref):
        feed_body(
            part_ref[...], ob_ref[...], dz_ref[...], wo_ref, gain_ref, bias_ref, fc1_ref, b1_ref[...], h_ref, a2_ref,
            z_ref, du_ref,
        )
        du = du_ref[:, :width]
        first = dot_tn(du, a2_ref[...]) + first1[...]
        second = dot_tn(z_ref[:, :width], g_ref[...]) + second1[...]
        for at, ref in enumerate((keep_ref, send_ref)):
            here = slice(at * shard, (at + 1) * shard)
            ref[0] = first[here].astype(BF16)
            ref[1] = second[here].astype(BF16)
        sums_ref[...] = jnp.sum(du.astype(F32), axis=0, keepdims=True) + jnp.sum(
            du1[:, :width].astype(F32), axis=0, keepdims=True
        )

    return chain.call(
        kernel, "feed_own", (h, ob, dz, g, gain, bias, wo, fc1, b1, *far),
        [f32(rows, d), bf16(rows, columns), bf16(rows, columns), bf16(2, shard, d), bf16(2, shard, d), f32(1, width)],
        "v" * 12 + "-vvvvvv", scratch=[pltpu.VMEM((rows, d), BF16)],
    )


def feed_result(chain, z, fc2, h):
    def kernel(io, z_ref, fc2_ref, h_ref, out_ref):
        out_ref[...] = (h_ref[...] + dot_nn(z_ref[...], fc2_ref[...])).astype(BF16)

    return chain.call(kernel, "feed_result", (z, fc2, h), [bf16(*h.shape)], "vvv-w", limit=8)[0]


def backward(chain, args, own):
    h, kt = args[2], args[8]
    rows, d = h.shape
    width = kt.shape[0]
    mols, pairs = rows // LEN, width // PAIR

    def kernel(io, du_ref, fc1_ref, h_ref, g_ref, gain_ref, wo_ref, p_ref, qt_ref, kt_ref, v_ref,
               gh_ref, dp_ref, dh_ref=None, sums_ref=None):
        da2 = dot_nn(du_ref[...], fc1_ref[...])
        xh, r = normalise(h_ref[...])
        dh = g_ref[:, :d].astype(F32) + norm_back(da2, gain_ref[...][None, :], xh, r)
        if own:
            dh_ref[...] = dh
            sums_ref[0:1] = jnp.sum(da2 * xh, axis=0, keepdims=True)
            sums_ref[1:2] = jnp.sum(da2, axis=0, keepdims=True)
            io.flush(2)
        gh = dh.astype(BF16)
        gh_ref[...] = gh
        dot = dot_nt(wo_ref[:width], gh).astype(BF16)
        every = [(m, i) for m in range(mols) for i in range(pairs)]
        lanes = lambda m: slice(LEN * m, LEN * (m + 1))
        rows_of = lambda i: slice(PAIR * i, PAIR * (i + 1))
        dps, dss, dos = {}, {}, {}
        for m, i in every:
            low, before = pair_window(i, width)
            dos[m, i] = pair_blocks(dot[rows_of(i), lanes(m)])
            dps[m, i] = dot_nn(v_ref[lanes(m), low : low + 2 * LEN], placed(dos[m, i], before))
        for m, i in every:
            dv = dot_nt(dos[m, i], p_ref[m, i])
            dp_ref[pl.ds(2 * width + PAIR * i, PAIR), lanes(m)] = dv.astype(BF16)
        for m, i in every:
            p = p_ref[m, i].astype(F32)
            t = dps[m, i] * p
            dss[m, i] = (t - p * jnp.sum(t, axis=0, keepdims=True)).astype(BF16)
        for m, i in every:
            dq = diagonal(dot_nn(kt_ref[rows_of(i), lanes(m)], dss[m, i])) * SCALE
            dp_ref[rows_of(i), lanes(m)] = dq.astype(BF16)
            dk = dot_nt(pair_blocks(qt_ref[rows_of(i), lanes(m)]), dss[m, i]) * SCALE
            dp_ref[pl.ds(width + PAIR * i, PAIR), lanes(m)] = dk.astype(BF16)

    outs = [bf16(rows, d), bf16(3 * width, rows)] + ([f32(rows, d), f32(8, d)] if own else [])
    return chain.call(
        kernel, "attention_backward", args, outs, "v" * 10 + ("-vvvv" if own else "-vv"),
    )


def weight_grads(chain, name, shard, at, lefts, rights):
    d = rights[0][0].shape[1]
    args, count = [], len(lefts)
    for (u0, u1, _), (v0, v1) in zip(lefts, rights):
        args += [u0, u1, v0, v1]

    def kernel(io, *refs):
        out_ref = refs[-1]
        for c in range(count):
            u0, u1, v0, v1 = refs[4 * c : 4 * c + 4]
            rows = slice(lefts[c][2] + at * shard, lefts[c][2] + (at + 1) * shard)
            left = jnp.concatenate([u0[rows], u1[rows]], axis=1)
            right = jnp.concatenate([v0[...], v1[...]], axis=0)
            out_ref[c] = dot_nn(left, right).astype(BF16)

    return chain.call(kernel, name, args, [bf16(count, shard, d)], "v" * len(args) + "-v")[0]


def input_grads(chain, dps, w, xs, sums, bias):
    rows, d = xs[0].shape

    def kernel(io, dp0, dp1, w_ref, x0, x1, sums_ref, bias_ref, mine_ref, theirs_ref):
        w = w_ref[...].reshape(dp0.shape[0], d)
        theirs = dot_tn(dp1[...], w)
        theirs_ref[:rows] = theirs.astype(BF16)
        mine = dot_tn(dp0[...], w)
        mine_ref[...] = mine
        xh0, _ = normalise(x0[...].astype(F32))
        xh1, _ = normalise(x1[...].astype(F32))
        bias = bias_ref[...]
        vec = [
            jnp.sum(mine * xh0, axis=0, keepdims=True) + jnp.sum(theirs * xh1, axis=0, keepdims=True),
            jnp.sum(mine, axis=0, keepdims=True) + jnp.sum(theirs, axis=0, keepdims=True),
            sums_ref[0:2],
            jnp.concatenate([bias, jnp.zeros((1, d - bias.shape[1]), F32)], axis=1),
            jnp.zeros((11, d), F32),
        ]
        theirs_ref[rows:] = jnp.concatenate(vec, axis=0).astype(BF16)

    return chain.call(
        kernel, "input_grads", (*dps, w, *xs, sums, bias), [f32(rows, d), bf16(rows + 16, d)], "vvvvvvv-vv"
    )


def input_norm(chain, x, gain, mine, got, dh):
    rows, d = x.shape

    def kernel(io, x_ref, gain_ref, mine_ref, got_ref, dh_ref, out_ref):
        xh, r = normalise(x_ref[...].astype(F32))
        da1 = mine_ref[...] + got_ref[:rows].astype(F32)
        out_ref[...] = (dh_ref[...] + norm_back(da1, gain_ref[...][None, :], xh, r)).astype(BF16)

    return chain.call(
        kernel, "input_norm", (x, gain, mine, got, dh), [bf16(rows, d)], "vvvvv-w", limit=8
    )[0]


def plus(*terms):
    total = terms[0].astype(F32)
    for term in terms[1:]:
        total = total + term.astype(F32)
    return total.astype(BF16)


def vector_rows(chain, mine, got):
    rows, d = mine.shape

    def kernel(io, mine_ref, got_ref, out_ref):
        a, b = mine_ref[rows - 16 :], got_ref[rows - 16 :]
        same = lax.broadcasted_iota(jnp.int32, (16, d), 0) < 4
        out_ref[...] = plus(a, jnp.where(same, b.astype(F32), 0.0))

    return chain.call(kernel, "vector_rows", (mine, got), [bf16(16, d)], "vv-v", limit=4)[0]


def vector_cores(chain, mine, got, shard):
    def kernel(io, mine_ref, got_ref, out_ref):
        a, b = mine_ref[...].astype(F32), got_ref[...].astype(F32)
        turned = jnp.concatenate([b[:, shard : 2 * shard], b[:, :shard], b[:, 2 * shard :]], axis=1)
        same = lax.broadcasted_iota(jnp.int32, a.shape, 0) < 4
        out_ref[...] = plus(a, jnp.where(same, b, turned))

    return chain.call(kernel, "vector_cores", (mine, got), [bf16(*mine.shape)], "vv-v", limit=4)[0]


def sum_half(chain, bits, mine, got, apart):
    def kernel(io, bits_ref, mine_ref, got_ref, *outs):
        half, quarter = 1 - bits_ref[0], bits_ref[1]
        on_ref, kept_ref = outs if apart else (outs[0].at[0], outs[0].at[1])
        on_ref[...] = mine_ref[half, 1 - quarter] + got_ref[half, 1 - quarter]
        kept_ref[...] = mine_ref[half, quarter] + got_ref[half, quarter]

    rows, d = mine.shape[2:]
    outs = [bf16(rows, d)] * 2 if apart else [bf16(2, rows, d)]
    return chain.call(kernel, "sum_half", (bits, mine, got), outs, "svv-" + "v" * len(outs), limit=8)


def sum_quarter(chain, bits, mine, got, kept, *more, vec=()):
    rows, d = mine.shape[2:]
    arrays = [a[0] if isinstance(a, tuple) else a for a in more]

    def kernel(io, bits_ref, mine_ref, got_ref, *refs):
        *refs, out_ref = refs
        half = bits_ref[0]
        quarter = bits_ref[1] if kept else 1 - bits_ref[1]
        terms = [ref[a[1]] if isinstance(a, tuple) else ref[...] for a, ref in zip(more, refs)]
        out_ref[:rows] = plus(mine_ref[half, quarter], got_ref[half, quarter], *terms)
        if vec:
            out_ref[rows:] = refs[-1][...]

    args = (bits, mine, got, *arrays, *vec)
    return chain.call(
        kernel, "sum_quarter", args, [bf16(rows + (16 if vec else 0), d)], "s" + "v" * (len(args) - 1) + "-v",
        limit=8,
    )[0]


def sum_quarter_apart(chain, bits, mine, got, *more):
    rows, d = mine.shape[2:]
    arrays = [a[0] if isinstance(a, tuple) else a for a in more]

    def kernel(io, bits_ref, mine_ref, got_ref, *refs):
        *refs, upper_ref, lower_ref = refs
        half, quarter = bits_ref[0], bits_ref[1]
        terms = [ref[a[1]] if isinstance(a, tuple) else ref[...] for a, ref in zip(more, refs)]
        total = plus(mine_ref[half, quarter], got_ref[half, quarter], *terms)
        upper_ref[...] = total[: rows // 2]
        lower_ref[...] = total[rows // 2 :]

    args = (bits, mine, got, *arrays)
    return chain.call(
        kernel, "sum_quarter", args, [bf16(rows // 2, d)] * 2, "s" + "v" * (len(args) - 1) + "-vv", limit=8
    )


def side_by_side(chain, a, b, apart):
    rows, d = a.shape

    def kernel(io, a_ref, b_ref, *outs):
        first, second = outs if apart else (outs[0].at[:rows], outs[0].at[rows:])
        first[...] = a_ref[...]
        second[...] = b_ref[...]

    outs = [bf16(rows, d)] * 2 if apart else [bf16(2 * rows, d)]
    return chain.call(kernel, "side_by_side", (a, b), outs, "vv-" + "v" * len(outs), limit=8)


def sum_pairs(chain, *pairs):
    rows = [a.shape[0] for a, _ in pairs]

    def kernel(io, *refs):
        *refs, out_ref = refs
        start = 0
        for a_ref, b_ref in zip(refs[::2], refs[1::2]):
            out_ref[start : start + a_ref.shape[0]] = a_ref[...] + b_ref[...]
            start += a_ref.shape[0]

    args = [a for pair in pairs for a in pair]
    return chain.call(
        kernel, "sum_pairs", args, [bf16(sum(rows), args[0].shape[1])], "v" * len(args) + "-v", limit=8
    )[0]


def place_sums(chain, bits, quarters, rows, targets, outs, whole=(), vec=(), skip=0):
    d = quarters[0][0].shape[1]
    n = len(outs)
    arrays = []
    for a, *_ in quarters:
        if not any(a is b for b in arrays):
            arrays.append(a)
    which = [next(k for k, b in enumerate(arrays) if b is a) for a, *_ in quarters]

    def kernel(io, bits_ref, *refs):
        refs, (buf, sems) = refs[:-2], refs[-2:]
        ins = [refs[k] for k in which]
        refs = refs[len(arrays) + len(whole) :]
        out_refs, vec_refs = refs[:n], refs[n:]

        def each(step):
            for j, (_, _, half, quarter) in enumerate(quarters):
                if j < skip:
                    continue
                half = 1 - bits_ref[0] if half else bits_ref[0]
                quarter = 1 - bits_ref[1] if quarter else bits_ref[1]
                for at, (out, index, first) in enumerate(targets):
                    ref = out_refs[out]
                    ref = ref if index is None else ref.at[index]
                    ref = ref.at[first : first + rows]
                    copy = pltpu.make_async_copy(buf.at[j], ref, sems.at[j])
                    pl.when(2 * half + quarter == at)(functools.partial(step, copy))

        starts = [start for _, start, _, _ in quarters]
        for j, ref in enumerate(ins):
            if j >= skip:
                buf[j] = ref[starts[j] : starts[j] + rows].astype(F32)
        each(lambda copy: copy.start())
        if vec:
            a, b, c, e = (ref[x + rows : x + rows + 16].astype(F32) for ref, x in zip(ins, starts))
            total = jnp.where(bits_ref[5] == 0, (a + b) + (c + e), (a + c) + (b + e))
            for at, (length, ref) in enumerate(zip(vec, vec_refs)):
                ref[...] = total[at, :length]
            io.flush(*range(n, n + len(vec)))
        each(lambda copy: copy.wait())

    return chain.call(
        kernel, "place_sums", (bits, *arrays, *whole), [*outs, *(f32(length) for length in vec)],
        "s" + "v" * len(arrays) + "p" * len(whole) + "-" + "r" * n + "w" * len(vec), limit=8, last=bool(vec),
        aliases={1 + len(arrays) + j: j for j in range(len(whole))},
        scratch=[pltpu.VMEM((len(quarters), rows, d), F32), pltpu.SemaphoreType.DMA((len(quarters),))],
    )


def local(
    n_dp, n_tensor, tokens, node_counts, edge_counts, ln1_gain, ln1_bias, qkv_weight, out_weight,
    ln2_gain, ln2_bias, fc1_weight, fc1_bias, fc2_weight, out_grad,
):
    d = tokens.shape[1]
    shard = out_weight.shape[0]
    width = 2 * shard
    mols = tokens.shape[0] // LEN
    dp_at = lax.axis_index("dp")
    tensor_at = lax.axis_index("tensor")
    core = tensor_at % 2
    bit0 = dp_at % 2
    bit1 = (dp_at // 2) % 2
    bits = jnp.stack(
        [jnp.where(core == 0, bit0, bit1), jnp.where(core == 0, bit1, bit0), bit0, tensor_at * mols,
         (tensor_at ^ 2) * mols, core, bit1]
    ).astype(jnp.int32)
    chain = Chain()

    def swap_core(a):
        return lax.ppermute(a, "tensor", [(t, t ^ 1) for t in range(n_tensor)])

    def swap_y(a):
        return lax.ppermute(a, "tensor", [(t, t ^ 2) for t in range(n_tensor)])

    def swap_dp(a, mask0, mask1):
        pairs = [
            (p * n_tensor + t, (p ^ (mask1 if t % 2 else mask0)) * n_tensor + t)
            for p in range(n_dp)
            for t in range(n_tensor)
        ]
        return lax.ppermute(a, ("dp", "tensor"), pairs)

    swap_first = lambda a: swap_dp(a, 1, 2)
    swap_second = lambda a: swap_dp(a, 2, 1)
    far_masks = [1 << k for k in range(2, n_dp.bit_length() - 1)]

    w_got = swap_core(qkv_weight)
    x_got, far_g = swap_y(tokens), swap_y(out_grad)
    picked = pick(chain, bits, out_weight, fc1_weight, fc2_weight, fc1_bias)
    far_y = swap_y(picked)
    near, others = load(
        chain, out_weight, fc1_weight, fc2_weight, picked,
        (tokens, out_grad, ln1_gain, ln1_bias, ln2_gain, ln2_bias),
    )
    near = (near, swap_core(near))
    tokens, out_grad, ln1_gain, ln1_bias, ln2_gain, ln2_bias = others

    counts = (node_counts, edge_counts)
    norm1 = (ln1_gain, ln1_bias)
    a1_0, qt_0, kt_0, v_0, p_0, ot_0, o_0, w_qkv = attention(
        chain, bits, 3, *counts, tokens, *norm1, (qkv_weight, w_got)
    )
    far_o = swap_y(o_0)
    far_y, short = hold(chain, far_y, d)
    far_x, far_z = swap_dp(short, 1, 1), swap_dp(short, 2, 2)
    far_z, pair = pair_up(chain, far_x, far_z)
    far_xz = swap_dp(far_z, 1, 1)
    a1_1, qt_1, kt_1, v_1, p_1, ot_1, o_1, wo, fc1, fc2 = attention(
        chain, bits, 4, *counts, x_got, *norm1, w_qkv, near=near
    )
    o_got = swap_y(o_1)
    spacer(chain)
    fars = (far_y, pair, far_xz)
    fars += tuple(swap_core(a) for a in fars)
    norm2 = (ln2_gain, ln2_bias)
    wo, fc1, fc2 = pack_far(chain, bits, (wo, fc1, fc2), fars)
    low, far_low = 3 * shard, 3 * shard // 4
    biases = ((near[0], low), (near[1], low), (fars[0], far_low), (fars[3], far_low))

    part_0, part_1, dz_0, dz_1, b1 = feed_in(
        chain, (tokens, x_got), (o_0, o_1), (out_grad, far_g), wo, fc2, biases
    )

    class Sum:
        def __init__(self, count, keep, got, apart, early):
            self.size = count * shard // 4
            self.apart, self.early = apart, early
            view = lambda a: a.reshape(2, 2, self.size, d)
            self.parts = (view(keep), view(got))

        def first(self):
            sent = sum_half(chain, bits, *self.parts, self.apart)
            got = [swap_first(a) for a in sent]
            self.on, self.kept = got if self.apart else ((got[0], 0), (got[0], 1))

        def second(self):
            self.got = swap_second(sum_quarter(chain, bits, *self.parts, False, self.on))

        def third(self, *vec):
            self.sum = sum_quarter(chain, bits, *self.parts, True, self.kept, self.got, vec=vec)
            self.got = swap_dp(self.sum, far_masks[0], far_masks[0])

        def third_apart(self):
            self.sums = sum_quarter_apart(chain, bits, *self.parts, self.kept, self.got)
            self.gots = [swap_dp(a, far_masks[0], far_masks[0]) for a in self.sums]
            self.halves = [None, None]

        def fourth_apart(self, at, *vec):
            self.sum, self.got = self.sums[at], self.gots[at]
            self.fourth(*vec)
            self.halves[at] = self.quarters

        def fourth(self, *vec):
            a = sum_pairs(chain, (self.sum, self.got), *vec)
            for mask in far_masks[1:]:
                a = sum_pairs(chain, (a, swap_dp(a, mask, mask)))
            b = swap_second(a)
            if self.early == 1:
                self.quarters = [(a, 0, 0, 0), (b, 0, 0, 1), (swap_first(a), 0, 1, 0), (swap_first(b), 0, 1, 1)]
            self.last = (a, b)

        def fifth(self):
            if self.early == 0:
                (a,) = side_by_side(chain, *self.last, False)
                b = swap_first(a)
                rows = a.shape[0] // 2
                self.quarters = [(a, 0, 0, 0), (a, rows, 0, 1), (b, 0, 1, 0), (b, rows, 1, 1)]
            if self.early == 3:
                a, b = self.last
                sent = lax.optimization_barrier((a, chain.token))[0]
                self.quarters = [(a, 0, 0, 0), (b, 0, 0, 1), (swap_first(sent), 0, 1, 0), (swap_first(b), 0, 1, 1)]
            if self.early == 2:
                a, b = side_by_side(chain, *self.last, True)
                self.quarters = [(a, 0, 0, 0), (b, 0, 0, 1), (swap_first(a), 0, 1, 0), (swap_first(b), 0, 1, 1)]

    h_1, du_1, *far_r = feed_far(chain, part_1, far_o, dz_1, far_g, *norm2, wo, fc1, b1)
    gh_1, dp_1 = backward(chain, (du_1, fc1, h_1, far_g, ln2_gain, wo, p_1, qt_1, kt_1, v_1), False)
    h_0, z_0, du_0, keep_r, send_r, bias_sums = feed_own(
        chain, part_0, o_got, dz_0, out_grad, *norm2, wo, fc1, b1, (du_1, *far_r)
    )
    gh_0, dp_0, dh, sums = backward(chain, (du_0, fc1, h_0, out_grad, ln2_gain, wo, p_0, qt_0, kt_0, v_0), True)
    r = Sum(2, keep_r, swap_core(send_r), True, 1)
    r.first()
    a1s = (a1_0, a1_1)
    lefts = [(dp_0, dp_1, c * width) for c in range(3)] + [(ot_0, ot_1, 0)]
    rights = [a1s] * 3 + [(gh_0, gh_1)]
    got_q = swap_core(weight_grads(chain, "weight_grads", shard, 1, lefts, rights))
    q = Sum(4, weight_grads(chain, "weight_grads", shard, 0, lefts, rights), got_q, True, 3)
    r.second()
    q.first()
    r.third()
    q.second()
    da1_mine, da1_theirs = input_grads(chain, (dp_0, dp_1), w_qkv, (tokens, x_got), sums, bias_sums)
    da1_got = swap_y(da1_theirs)
    r.fourth()
    q.third()
    vec = vector_rows(chain, da1_theirs, da1_got)
    vec_got = swap_core(vec)
    r.fifth()
    halves = [(c, None, half * shard // 2) for c in range(2) for half in range(2)]
    grad_fc1, grad_fc2 = place_sums(chain, bits, r.quarters, r.size, halves, [f32(shard, d)] * 2)
    vec = vector_cores(chain, vec, vec_got, shard)
    vec_got = swap_dp(vec, far_masks[0], far_masks[0])
    q.fourth((vec, vec_got))
    grad_tokens = input_norm(chain, tokens, ln1_gain, da1_mine, da1_got, dh)
    result = feed_result(chain, z_0, fc2, h_0)
    q.fifth()
    each = [(0, 0, 0), (0, 1, 0), (0, 2, 0), (1, None, 0)]
    outs = [f32(3, shard, d), f32(shard, d)]
    grads = place_sums(chain, bits, q.quarters[:3], q.size, each, outs)
    grad_qkv, grad_out, gain1, bias1, gain2, bias2, grad_b = place_sums(
        chain, bits, q.quarters, q.size, each, outs, grads, (d, d, d, d, shard), 3
    )
    return (
        result, grad_tokens, gain1, bias1, grad_qkv, grad_out, gain2, bias2, grad_fc1, grad_b, grad_fc2,
    )


def solution(mesh):
    tokens = P(("dp", "tensor"), None)
    rows = P("tensor", None)
    qkv = P(None, "tensor", None)
    in_specs = (
        tokens, P("dp"), P("dp"), P(), P(), qkv, rows, P(), P(), rows, P("tensor"), rows, tokens,
    )
    out_specs = (tokens, tokens, P(), P(), qkv, rows, P(), P(), rows, P("tensor"), rows)
    step = functools.partial(local, mesh.shape["dp"], mesh.shape["tensor"])
    return jax.shard_map(step, mesh=mesh, in_specs=in_specs, out_specs=out_specs, check_vma=False)
```
